32 devices in a mesh: head: 8 (over z, x), blk: 4 (over y, core).
Axes of the slice: x: 2, y: 2, z: 4, core: 2. Of those that a mesh axis runs over, the one named last changes fastest.
Arguments:
- tokens: bfloat16 [2, 2048, 1024], P(None, ('head', 'blk')), may hold values from -6 to 6
- cotangent: bfloat16 [2, 2048, 1024], P(None, ('head', 'blk')), may hold values from -6 to 6
- w_qkv: bfloat16 [1024, 3072], P(('head', 'blk')), may hold values from -0.1875 to 0.1875
- w_out: bfloat16 [1024, 1024], P(('head', 'blk')), may hold values from -4 to 4
- w_gate: bfloat16 [1024, 4096], P(('head', 'blk')), may hold values from -0.1875 to 0.1875
- w_up: bfloat16 [1024, 4096], P(('head', 'blk')), may hold values from -0.1875 to 0.1875
- w_down: bfloat16 [4096, 1024], P(('head', 'blk')), may hold values from -0.09375 to 0.09375
- norm_attn: bfloat16 [1024], P(('head', 'blk')), may hold values from 0.5 to 1.5
- norm_ffn: bfloat16 [1024], P(('head', 'blk')), may hold values from 0.5 to 1.5
- q_gain: bfloat16 [1024], P(('head', 'blk')), may hold values from 0.5 to 1.5
- k_gain: bfloat16 [1024], P(('head', 'blk')), may hold values from 0.5 to 1.5
- var_bias: float32 [16, 2], replicated, may hold values from -4 to 4
- doc_lengths: int32 [2, 8], replicated, may hold values from 1 to 1024, 2048 in all within a row
- variate: int32 [2, 2048], P(None, ('head', 'blk')), may hold values from 0 to 3
- times: int32 [2, 2048], P(None, ('head', 'blk')), may hold values from 0 to 1023
Outputs:
- out: bfloat16 [2, 2048, 1024], P(None, ('head', 'blk'))
- grad_tokens: bfloat16 [2, 2048, 1024], P(None, ('head', 'blk'))
- grad_w_qkv: float32 [1024, 3072], P(('head', 'blk'))
- grad_w_out: float32 [1024, 1024], P(('head', 'blk'))
- grad_w_gate: float32 [1024, 4096], P(('head', 'blk'))
- grad_w_up: float32 [1024, 4096], P(('head', 'blk'))
- grad_w_down: float32 [4096, 1024], P(('head', 'blk'))
- grad_norm_attn: float32 [1024], P(('head', 'blk'))
- grad_norm_ffn: float32 [1024], P(('head', 'blk'))
- grad_q_gain: float32 [1024], P(('head', 'blk'))
- grad_k_gain: float32 [1024], P(('head', 'blk'))
- grad_var_bias: float32 [16, 2], replicated
The draws below stay inside these ranges and needn't reach their ends.
Inputs may be any that keep to these rules, and one draw needn't show every extreme that they name: `doc_lengths`: each row holds the lengths of the consecutive documents of one micro-batch and sums to 2048.
All inputs are finite; a program needn't handle non-finite values.
Results may differ from the reference program's by a relative error of at most 0.025.
Values may be sent and summed in bfloat16 or wider, within the bound.
A program may use at most 320 MiB of HBM per device.

```python
import math
import jax
import jax.numpy as jnp
import numpy as np
from jax import lax

D = 1024
HEADS = 16
HDIM = 64
FF = 4096
MB = 2
VARIATES = 4
S = 2048
DOC_MAX = 1024
NDOC = 8


def with_ends(values, rng, smallest, largest):
    longest = values.shape.index(max(values.shape))
    spots = []
    for shift in (0, 1):
        where = [jax.random.randint(jax.random.fold_in(rng, axis), (), 0, length) for axis, length in enumerate(values.shape)]
        where[longest] = (where[longest] + shift) % values.shape[longest]
        spots.append(tuple(where))
    return values.at[spots[0]].set(smallest).at[spots[1]].set(largest)


def block_levels(key, dims, split, low, largest):
    factor_of, own = 1.0, jax.random.fold_in(key, 6)
    for position, shards_of in split:
        steps = jnp.exp(jax.random.uniform(jax.random.fold_in(own, position), (shards_of,), jnp.float32, low / len(split), largest / len(split)))
        factor_of = factor_of * jnp.repeat(steps, dims[position] // shards_of).reshape([-1 if axis == position else 1 for axis in range(len(dims))])
    return factor_of


def split_up(amount, total, limit, skew):
    portions = [(1 << 20) // math.isqrt(standing ** skew) + 1 for standing in range(2, amount + 1)]
    spare, given = total - limit - (amount - 1), [1] * (amount - 1)
    while spare > 0:
        candidates = [i for i in range(amount - 1) if given[i] < limit]
        mass, remaining = sum([portions[i] for i in candidates]), spare
        for i in candidates:
            extra = min(limit - given[i], max(1, remaining * portions[i] // mass), spare)
            given[i] = given[i] + extra
            spare = spare - extra
    return np.array([limit] + given)


def uneven_parts(stream_key, amount, total, reach, lean):
    if amount == 2:
        one = jax.random.randint(stream_key, (), max(1, total - reach), min(reach, total - 1) + 1)
        return jnp.stack([one, total - one])
    lengths = jnp.asarray(split_up(amount, total, reach, lean), jnp.int32)
    pairs = (amount - 1) // 2
    donor, receiver = lengths[1:1 + 2 * pairs:2], lengths[2:2 + 2 * pairs:2]
    room = jnp.minimum(donor - 1, reach - receiver)
    shifted = jax.random.randint(jax.random.fold_in(stream_key, 1), (pairs,), 0, 1 << 20) % (room + 1)
    lengths = lengths.at[1:1 + 2 * pairs:2].set(donor - shifted).at[2:2 + 2 * pairs:2].set(receiver + shifted)
    return lengths[jax.random.permutation(jax.random.fold_in(stream_key, 2), amount)]


def scatter_about(key, extent, width, bound, shards=(), kind=jnp.bfloat16):
    values = width * jax.random.normal(key, extent, jnp.float32)
    if shards:
        values = values * block_levels(key, extent, shards, -0.22, 0.18)
    return jnp.clip(values, -bound, bound).astype(kind)


def setup_inputs(seed: int = 0) -> dict:
    arg_keys = jax.random.split(jax.random.key(seed), 16)
    return {
        "tokens": scatter_about(arg_keys[0], (MB, S, D), 1.0, 6.0, ((1, 32),)),
        "cotangent": scatter_about(arg_keys[1], (MB, S, D), 1.0, 6.0, ((1, 32),)),
        "w_qkv": scatter_about(arg_keys[2], (D, 3 * D), D ** -0.5, 0.1875, ((0, 32),)),
        "w_out": scatter_about(arg_keys[3], (D, D), 2 ** -0.5, 4.0, ((0, 32),)),
        "w_gate": scatter_about(arg_keys[4], (D, FF), D ** -0.5, 0.1875, ((0, 32),)),
        "w_up": scatter_about(arg_keys[5], (D, FF), D ** -0.5, 0.1875, ((0, 32),)),
        "w_down": scatter_about(arg_keys[6], (FF, D), FF ** -0.5, 0.09375, ((0, 32),)),
        "norm_attn": jnp.clip(1.0 + 0.1 * jax.random.normal(arg_keys[7], (D,), jnp.float32), 0.5, 1.5).astype(jnp.bfloat16),
        "norm_ffn": jnp.clip(1.0 + 0.1 * jax.random.normal(arg_keys[8], (D,), jnp.float32), 0.5, 1.5).astype(jnp.bfloat16),
        "q_gain": jnp.clip(1.0 + 0.1 * jax.random.normal(arg_keys[9], (D,), jnp.float32), 0.5, 1.5).astype(jnp.bfloat16),
        "k_gain": jnp.clip(1.0 + 0.1 * jax.random.normal(arg_keys[10], (D,), jnp.float32), 0.5, 1.5).astype(jnp.bfloat16),
        "var_bias": scatter_about(arg_keys[11], (HEADS, 2), 1.0, 4.0, (), jnp.float32),
        "doc_lengths": jax.vmap(lambda own: uneven_parts(own, NDOC, S, DOC_MAX, 1))(jax.random.split(arg_keys[12], MB)).reshape((MB, NDOC)).astype(jnp.int32),
        "variate": with_ends(jax.random.randint(arg_keys[13], (MB, S), 0, VARIATES), jax.random.fold_in(arg_keys[13], 1), 0, VARIATES - 1).astype(jnp.int32),
        "times": with_ends(jax.random.randint(arg_keys[14], (MB, S), 0, 1024), jax.random.fold_in(arg_keys[14], 1), 0, 1023).astype(jnp.int32),
    }


EPS = 1e-06
THETA = 10000.0
NEGATIVE = -1e+30
HIGH = lax.Precision.HIGHEST
QUERY_BLOCK = 128

@jax.custom_vjp
def low(v):
    return lax.optimization_barrier(v.astype(jnp.bfloat16)).astype(jnp.float32)

@jax.custom_vjp
def low_back(v):
    return v

def low_keep(v):
    return (low(v), None)

def low_pass(kept, grad):
    return (grad,)

def back_keep(v):
    return (v, None)

def back_low(kept, grad):
    return (low(grad),)
low.defvjp(low_keep, low_pass)
low_back.defvjp(back_keep, back_low)

def inverse_rms(values_in):
    return lax.rsqrt(lax.optimization_barrier(jnp.mean(values_in * values_in, axis=-1, keepdims=True)) + EPS)

def rotate(values_in, time_index, sign_value):
    half_dim = values_in.shape[-1] // 2
    frequency = THETA ** (-2.0 * jnp.arange(half_dim, dtype=jnp.float32) / values_in.shape[-1])
    angles = time_index.astype(jnp.float32)[:, None] * frequency[None, :]
    cosine = jnp.cos(angles)[:, None, :]
    sine_part = sign_value * jnp.sin(angles)[:, None, :]
    first_half = values_in[..., :half_dim]
    second_half = values_in[..., half_dim:]
    return jnp.concatenate([first_half * cosine - second_half * sine_part, first_half * sine_part + second_half * cosine], axis=-1)

def attention(queries, keys, values, documents, variates, var_bias):
    seq_len = queries.shape[0]
    block_len = min(QUERY_BLOCK, seq_len)
    att_scale = 1.0 / math.sqrt(HDIM)

    def one_block(first_row):
        block_query = lax.dynamic_slice_in_dim(queries, first_row, block_len, 0)
        block_doc = lax.dynamic_slice_in_dim(documents, first_row, block_len, 0)
        block_var = lax.dynamic_slice_in_dim(variates, first_row, block_len, 0)
        scores = jnp.einsum('qhd,khd->qhk', block_query, keys, precision=HIGH) * att_scale
        same_var = block_var[:, None] == variates[None, :]
        same_doc = block_doc[:, None] == documents[None, :]
        scores = scores + jnp.where(same_var[:, None, :], var_bias[:, 0][None, :, None], var_bias[:, 1][None, :, None])
        scores = low_back(scores)
        scores = jnp.where(same_doc[:, None, :], scores, NEGATIVE)
        probs = jax.nn.softmax(scores, axis=-1)
        return jnp.einsum('qhk,khd->qhd', low(probs), values, precision=HIGH)
    starts = jnp.arange(0, seq_len, block_len, dtype=jnp.int32)
    blocks = lax.map(jax.checkpoint(one_block), starts)
    return blocks.reshape(seq_len, HEADS, HDIM)

def layer(inputs, weights, time_row, var_row, documents):
    w_qkv, w_out, w_gate, w_up, w_down, norm_attn, norm_ffn, q_gain, k_gain, var_bias = weights
    seq_len = inputs.shape[0]
    normed_one = low(inputs * inverse_rms(inputs) * norm_attn)
    qkv_all = low_back(jnp.dot(normed_one, w_qkv, precision=HIGH)).reshape(seq_len, HEADS, 3 * HDIM)
    query_raw = qkv_all[..., :HDIM]
    key_raw = qkv_all[..., HDIM:2 * HDIM]
    value_raw = qkv_all[..., 2 * HDIM:]
    queries = low(low_back(rotate(query_raw * inverse_rms(query_raw) * q_gain.reshape(HEADS, HDIM), time_row, 1.0)))
    keys = low(low_back(rotate(key_raw * inverse_rms(key_raw) * k_gain.reshape(HEADS, HDIM), time_row, 1.0)))
    values = low(low_back(value_raw))
    attended = low(low_back(attention(queries, keys, values, documents, var_row, var_bias))).reshape(seq_len, D)
    resid_one = inputs + low_back(jnp.dot(attended, w_out, precision=HIGH))
    normed_two = low(resid_one * inverse_rms(resid_one) * norm_ffn)
    gate_pre = low_back(jnp.dot(normed_two, w_gate, precision=HIGH))
    up_pre = low_back(jnp.dot(normed_two, w_up, precision=HIGH))
    hidden_act = low(jax.nn.silu(gate_pre) * up_pre)
    return resid_one + low_back(jnp.dot(hidden_act, w_down, precision=HIGH))

def reference(tokens, cotangent, w_qkv, w_out, w_gate, w_up, w_down, norm_attn, norm_ffn, q_gain, k_gain, var_bias, doc_lengths, variate, times):
    params = (w_qkv.astype(jnp.float32), w_out.astype(jnp.float32), w_gate.astype(jnp.float32), w_up.astype(jnp.float32), w_down.astype(jnp.float32), norm_attn.astype(jnp.float32), norm_ffn.astype(jnp.float32), q_gain.astype(jnp.float32), k_gain.astype(jnp.float32), var_bias.astype(jnp.float32))
    positions = jnp.arange(S, dtype=jnp.int32)
    outputs_list = []
    inputs_list = []
    totals = None
    for batch_id in range(MB):
        doc_ends = jnp.cumsum(doc_lengths[batch_id]).astype(jnp.int32)
        documents = lax.optimization_barrier(jnp.sum((positions[:, None] >= doc_ends[None, :]).astype(jnp.int32), axis=1))
        time_row = times[batch_id]
        var_row = variate[batch_id]

        def forward_fn(inputs, weights):
            return layer(inputs, weights, time_row, var_row, documents)
        result, pullback = jax.vjp(forward_fn, tokens[batch_id].astype(jnp.float32), params)
        grad_inputs, grad_weights = pullback(cotangent[batch_id].astype(jnp.float32))
        outputs_list.append(result.astype(jnp.bfloat16))
        inputs_list.append(grad_inputs.astype(jnp.bfloat16))
        if totals is None:
            totals = grad_weights
        else:
            totals = tuple((first_term + second_term for first_term, second_term in zip(totals, grad_weights)))
    return (jnp.stack(outputs_list), jnp.stack(inputs_list), totals[0], totals[1], totals[2], totals[3], totals[4], totals[5], totals[6], totals[7], totals[8], totals[9])
```

```python
import math

import jax
import jax.numpy as jnp
import numpy as np
from jax import lax
from jax.experimental import pallas as pl
from jax.experimental.pallas import tpu as pltpu
from jax.sharding import PartitionSpec as P

EPS = 1e-06
THETA = 10000.0
NEGATIVE = -1e30
KEY_BLOCK = 1024


def inverse_rms(values_in):
    return lax.rsqrt(jnp.mean(values_in * values_in, axis=-1, keepdims=True) + EPS)


def rotate(values_in, time_index, sign_value):
    half_dim = values_in.shape[-1] // 2
    frequency = THETA ** (-2.0 * jnp.arange(half_dim, dtype=jnp.float32) / values_in.shape[-1])
    angles = time_index.astype(jnp.float32)[:, None] * frequency[None, :]
    cosine = jnp.cos(angles)[:, None, :]
    sine_part = sign_value * jnp.sin(angles)[:, None, :]
    first_half = values_in[..., :half_dim]
    second_half = values_in[..., half_dim:]
    return jnp.concatenate(
        [
            first_half * cosine - second_half * sine_part,
            first_half * sine_part + second_half * cosine,
        ],
        axis=-1,
    )


def norm_back(grad_in, value_in, scale_in, gain_in):
    weighted = grad_in * gain_in
    scale_cube = scale_in * scale_in * scale_in
    return scale_in * weighted - value_in * scale_cube * jnp.mean(
        weighted * value_in, axis=-1, keepdims=True
    )


def row_contract(left_mat, right_mat):
    return lax.dot_general(
        left_mat, right_mat, (((0,), (0,)), ((), ())), preferred_element_type=jnp.float32
    )


def col_contract(left_mat, right_mat):
    return lax.dot_general(
        left_mat, right_mat, (((1,), (1,)), ((), ())), preferred_element_type=jnp.float32
    )


def document_of(positions, doc_ends):
    return jnp.sum((positions[:, None] >= doc_ends[None, :]).astype(jnp.int32), axis=1)


def key_positions(first_row, row_total, per_group, row_count, blk_n):
    row_index = first_row + jnp.arange(row_total, dtype=jnp.int32)
    source_blk = row_index // per_group
    within = row_index % per_group
    return (within // row_count * blk_n + source_blk) * row_count + within % row_count


def block_scores(queries, key_part, same_var, same_doc, bias_same, bias_other, att_scale):
    raw_scores = (
        jnp.einsum("qhd,khd->qhk", queries, key_part, preferred_element_type=jnp.float32)
        * att_scale
    )
    bias_terms = jnp.where(
        same_var[:, None, :], bias_same[None, :, None], bias_other[None, :, None]
    )
    return jnp.where(same_doc[:, None, :], raw_scores + bias_terms, NEGATIVE)


def forward_block(
    state_in, queries, key_part, value_part, same_var, same_doc, bias_same, bias_other, att_scale
):
    best_prev, total_prev, accum_prev = state_in
    scores = block_scores(queries, key_part, same_var, same_doc, bias_same, bias_other, att_scale)
    best_next = jnp.maximum(best_prev, jnp.max(scores, axis=-1))
    factor = jnp.exp(best_prev - best_next)
    weights = jnp.where(same_doc[:, None, :], jnp.exp(scores - best_next[..., None]), 0.0)
    total_next = total_prev * factor + jnp.sum(weights, axis=-1)
    accum_next = accum_prev * factor[..., None] + jnp.einsum(
        "qhk,khd->qhd", weights.astype(jnp.bfloat16), value_part, preferred_element_type=jnp.float32
    )
    return (best_next, total_next, accum_next)


def flatten_all(grads_in):
    return tuple((member.reshape(-1) for member in grads_in))


def unflatten_all(flat_in, grads_like):
    return tuple(
        (flat.reshape((-1,) + member.shape[1:]) for flat, member in zip(flat_in, grads_like))
    )


def on_device(
    tokens,
    cotangent,
    w_qkv,
    w_out,
    w_gate,
    w_up,
    w_down,
    norm_attn,
    norm_ffn,
    q_gain,
    k_gain,
    var_bias,
    doc_lengths,
    variate,
    times,
):
    heads_n = lax.axis_size("head")
    blk_n = lax.axis_size("blk")
    head_rank = lax.axis_index("head")
    blk_rank = lax.axis_index("blk")
    batch_count, row_count, model_width = tokens.shape
    head_count = var_bias.shape[0]
    head_dim = model_width // head_count
    local_heads = head_count // heads_n
    query_rows = heads_n * row_count
    key_rows = blk_n * query_rows
    key_block = min(KEY_BLOCK, key_rows)
    block_count = key_rows // key_block
    att_scale = 1.0 / math.sqrt(head_dim)
    gathered = (
        lax.all_gather(w_qkv, ("head", "blk"), axis=0, tiled=True),
        lax.all_gather(w_out, ("head", "blk"), axis=0, tiled=True),
        lax.all_gather(w_gate, ("head", "blk"), axis=0, tiled=True),
        lax.all_gather(w_up, ("head", "blk"), axis=0, tiled=True),
        lax.all_gather(w_down, ("head", "blk"), axis=0, tiled=True),
        lax.all_gather(norm_attn, ("head", "blk"), axis=0, tiled=True),
        lax.all_gather(norm_ffn, ("head", "blk"), axis=0, tiled=True),
        lax.all_gather(q_gain, ("head", "blk"), axis=0, tiled=True),
        lax.all_gather(k_gain, ("head", "blk"), axis=0, tiled=True),
    )
    wqkv_all, wout_all, wgate_all, wup_all, wdown_all = gathered[:5]
    gain_attn = gathered[5].astype(jnp.float32)
    gain_ffn = gathered[6].astype(jnp.float32)
    gain_query = gathered[7].astype(jnp.float32).reshape(head_count, head_dim)
    gain_key = gathered[8].astype(jnp.float32).reshape(head_count, head_dim)
    local_bias = lax.dynamic_slice_in_dim(var_bias, head_rank * local_heads, local_heads, 0)
    bias_same = local_bias[:, 0]
    bias_other = local_bias[:, 1]
    query_index = jnp.arange(query_rows, dtype=jnp.int32)
    query_pos = (query_index // row_count * blk_n + blk_rank) * row_count + query_index % row_count
    ends_all = jnp.cumsum(doc_lengths, axis=1)
    outputs_list = []
    inputs_list = []
    totals = None
    bias_accum = jnp.zeros((local_heads, 2), jnp.float32)
    for batch_id in range(batch_count):
        doc_ends = ends_all[batch_id]
        time_row = times[batch_id]
        inputs_f = tokens[batch_id].astype(jnp.float32)
        scale_one = inverse_rms(inputs_f)
        normed_one = (inputs_f * scale_one * gain_attn).astype(jnp.bfloat16)
        qkv_all = jnp.dot(normed_one, wqkv_all, preferred_element_type=jnp.float32).reshape(
            row_count, head_count, 3 * head_dim
        )
        query_raw = qkv_all[..., :head_dim]
        key_raw = qkv_all[..., head_dim : 2 * head_dim]
        value_raw = qkv_all[..., 2 * head_dim :]
        query_scale = inverse_rms(query_raw)
        key_scale = inverse_rms(key_raw)
        query_rot = rotate(query_raw * query_scale * gain_query, time_row, 1.0)
        key_rot = rotate(key_raw * key_scale * gain_key, time_row, 1.0)
        packed = jnp.concatenate([query_rot, key_rot, value_raw], axis=-1).astype(jnp.bfloat16)
        variate_rep = jnp.broadcast_to(
            variate[batch_id].astype(jnp.bfloat16)[:, None], (row_count, head_count)
        )
        packed_heads, variate_heads = (
            lax.all_to_all(packed, "head", split_axis=1, concat_axis=0, tiled=True),
            lax.all_to_all(variate_rep, "head", split_axis=1, concat_axis=0, tiled=True),
        )
        queries = packed_heads[..., :head_dim]
        key_values = packed_heads[..., head_dim:]
        query_var = variate_heads[:, 0]
        query_doc = document_of(query_pos, doc_ends)
        initial = (
            jnp.full((query_rows, local_heads), NEGATIVE, jnp.float32),
            jnp.zeros((query_rows, local_heads), jnp.float32),
            jnp.zeros((query_rows, local_heads, head_dim), jnp.float32),
        )
        kv_piece = lax.all_gather(key_values, "blk", axis=0, tiled=True)
        var_piece = lax.all_gather(query_var, "blk", axis=0, tiled=True)
        piece_rows = kv_piece.shape[0]

        def one_block(state_blk, kv_block, var_block, block_start):
            key_doc = document_of(
                key_positions(block_start, kv_block.shape[0], query_rows, row_count, blk_n),
                doc_ends,
            )
            same_doc = query_doc[:, None] == key_doc[None, :]
            same_var = query_var[:, None] == var_block[None, :]
            return forward_block(
                state_blk,
                queries,
                kv_block[..., :head_dim],
                kv_block[..., head_dim:],
                same_var,
                same_doc,
                bias_same,
                bias_other,
                att_scale,
            )

        def loop_step(turn_index, state_loop):
            kv_block = lax.dynamic_slice_in_dim(kv_piece, turn_index * key_block, key_block, 0)
            var_block = lax.dynamic_slice_in_dim(var_piece, turn_index * key_block, key_block, 0)
            return one_block(state_loop, kv_block, var_block, turn_index * key_block)

        attn_state = lax.fori_loop(0, piece_rows // key_block, loop_step, initial)
        best_score, total_weight, accum = attn_state
        attn_heads = accum / total_weight[..., None]
        log_total = best_score + jnp.log(total_weight)
        attn_tok = lax.all_to_all(
            attn_heads.astype(jnp.bfloat16), "head", split_axis=0, concat_axis=1, tiled=True
        ).reshape(row_count, model_width)
        resid_one = inputs_f + jnp.dot(attn_tok, wout_all, preferred_element_type=jnp.float32)
        scale_two = inverse_rms(resid_one)
        normed_two = (resid_one * scale_two * gain_ffn).astype(jnp.bfloat16)
        gate_pre = jnp.dot(normed_two, wgate_all, preferred_element_type=jnp.float32)
        up_pre = jnp.dot(normed_two, wup_all, preferred_element_type=jnp.float32)
        sigmoid_gate = jax.nn.sigmoid(gate_pre)
        silu_gate = gate_pre * sigmoid_gate
        hidden_act = (silu_gate * up_pre).astype(jnp.bfloat16)
        result = resid_one + jnp.dot(hidden_act, wdown_all, preferred_element_type=jnp.float32)
        outputs_list.append(result.astype(jnp.bfloat16))
        grad_out = cotangent[batch_id].astype(jnp.float32)
        grad_ffn = grad_out.astype(jnp.bfloat16)
        grad_down = row_contract(hidden_act, grad_ffn)
        grad_hidden = col_contract(grad_ffn, wdown_all)
        grad_gate = (
            grad_hidden * up_pre * sigmoid_gate * (1.0 + gate_pre * (1.0 - sigmoid_gate))
        ).astype(jnp.bfloat16)
        grad_up = (grad_hidden * silu_gate).astype(jnp.bfloat16)
        grad_wgate = row_contract(normed_two, grad_gate)
        grad_wup = row_contract(normed_two, grad_up)
        grad_normed = col_contract(grad_gate, wgate_all) + col_contract(grad_up, wup_all)
        grad_gffn = jnp.sum(grad_normed * resid_one * scale_two, axis=0)
        grad_resid = grad_out + norm_back(grad_normed, resid_one, scale_two, gain_ffn)
        grad_branch = grad_resid.astype(jnp.bfloat16)
        grad_wout = row_contract(attn_tok, grad_branch)
        grad_attn = (
            col_contract(grad_branch, wout_all)
            .astype(jnp.bfloat16)
            .reshape(row_count, head_count, head_dim)
        )
        grad_heads = lax.all_to_all(grad_attn, "head", split_axis=1, concat_axis=0, tiled=True)
        delta_row = jnp.sum(grad_heads.astype(jnp.float32) * attn_heads, axis=-1)
        keys_all, key_var_all = (
            lax.all_gather(key_values, "blk", axis=0, tiled=True),
            lax.all_gather(query_var, "blk", axis=0, tiled=True),
        )
        keys_blocks = keys_all.reshape(block_count, key_block, local_heads, 2 * head_dim)
        var_blocks = key_var_all.reshape(block_count, key_block)
        block_starts = jnp.arange(block_count, dtype=jnp.int32) * key_block

        def back_step(carry_back, block_in):
            grad_query, bias_grad = carry_back
            kv_block, var_block, block_start = block_in
            key_doc = document_of(
                key_positions(block_start, key_block, query_rows, row_count, blk_n), doc_ends
            )
            same_doc = query_doc[:, None] == key_doc[None, :]
            same_var = query_var[:, None] == var_block[None, :]
            key_part = kv_block[..., :head_dim]
            value_part = kv_block[..., head_dim:]
            scores = block_scores(
                queries, key_part, same_var, same_doc, bias_same, bias_other, att_scale
            )
            probs = jnp.where(same_doc[:, None, :], jnp.exp(scores - log_total[..., None]), 0.0)
            grad_probs = jnp.einsum(
                "qhd,khd->qhk", grad_heads, value_part, preferred_element_type=jnp.float32
            )
            grad_scores = (probs * (grad_probs - delta_row[..., None])).astype(jnp.bfloat16)
            grad_scores_f = grad_scores.astype(jnp.float32)
            same_sum = jnp.sum(jnp.where(same_var[:, None, :], grad_scores_f, 0.0), axis=(0, 2))
            other_sum = jnp.sum(jnp.where(same_var[:, None, :], 0.0, grad_scores_f), axis=(0, 2))
            bias_grad = bias_grad + jnp.stack([same_sum, other_sum], axis=-1)
            grad_query = grad_query + att_scale * jnp.einsum(
                "qhk,khd->qhd", grad_scores, key_part, preferred_element_type=jnp.float32
            )
            grad_key = att_scale * jnp.einsum(
                "qhk,qhd->khd", grad_scores, queries, preferred_element_type=jnp.float32
            )
            grad_value = jnp.einsum(
                "qhk,qhd->khd",
                probs.astype(jnp.bfloat16),
                grad_heads,
                preferred_element_type=jnp.float32,
            )
            return ((grad_query, bias_grad), jnp.concatenate([grad_key, grad_value], axis=-1))

        carry_start = (
            jnp.zeros((query_rows, local_heads, head_dim), jnp.float32),
            jnp.zeros((local_heads, 2), jnp.float32),
        )
        (grad_query, bias_part), grad_kv_parts = lax.scan(
            back_step, carry_start, (keys_blocks, var_blocks, block_starts)
        )
        bias_accum = bias_accum + bias_part
        grad_kv_own = lax.psum_scatter(
            grad_kv_parts.reshape(key_rows, local_heads, 2 * head_dim).astype(jnp.bfloat16),
            "blk",
            scatter_dimension=0,
            tiled=True,
        )
        grad_packed = jnp.concatenate([grad_query.astype(jnp.bfloat16), grad_kv_own], axis=-1)
        grad_tok = lax.all_to_all(
            grad_packed, "head", split_axis=0, concat_axis=1, tiled=True
        ).astype(jnp.float32)
        grad_qrot = rotate(grad_tok[..., :head_dim], time_row, -1.0)
        grad_krot = rotate(grad_tok[..., head_dim : 2 * head_dim], time_row, -1.0)
        grad_gquery = jnp.sum(grad_qrot * query_raw * query_scale, axis=0)
        grad_gkey = jnp.sum(grad_krot * key_raw * key_scale, axis=0)
        grad_qraw = norm_back(grad_qrot, query_raw, query_scale, gain_query)
        grad_kraw = norm_back(grad_krot, key_raw, key_scale, gain_key)
        grad_qkv = (
            jnp.concatenate([grad_qraw, grad_kraw, grad_tok[..., 2 * head_dim :]], axis=-1)
            .reshape(row_count, 3 * model_width)
            .astype(jnp.bfloat16)
        )
        grad_wqkv = row_contract(normed_one, grad_qkv)
        grad_normed_one = col_contract(grad_qkv, wqkv_all)
        grad_gattn = jnp.sum(grad_normed_one * inputs_f * scale_one, axis=0)
        grad_in = grad_resid + norm_back(grad_normed_one, inputs_f, scale_one, gain_attn)
        inputs_list.append(grad_in.astype(jnp.bfloat16))
        batch_grads = (
            grad_wqkv,
            grad_wout,
            grad_wgate,
            grad_wup,
            grad_down,
            grad_gattn,
            grad_gffn,
            grad_gquery.reshape(model_width),
            grad_gkey.reshape(model_width),
        )
        if totals is None:
            totals = batch_grads
        else:
            totals = tuple(
                (first_term + second_term for first_term, second_term in zip(totals, batch_grads))
            )
    flat_totals = flatten_all(totals)
    summed_flat = (
        lax.psum_scatter(flat_totals[0], ("head", "blk"), scatter_dimension=0, tiled=True),
        lax.psum_scatter(flat_totals[1], ("head", "blk"), scatter_dimension=0, tiled=True),
        lax.psum_scatter(flat_totals[2], ("head", "blk"), scatter_dimension=0, tiled=True),
        lax.psum_scatter(flat_totals[3], ("head", "blk"), scatter_dimension=0, tiled=True),
        lax.psum_scatter(flat_totals[4], ("head", "blk"), scatter_dimension=0, tiled=True),
        lax.psum_scatter(flat_totals[5], ("head", "blk"), scatter_dimension=0, tiled=True),
        lax.psum_scatter(flat_totals[6], ("head", "blk"), scatter_dimension=0, tiled=True),
        lax.psum_scatter(flat_totals[7], ("head", "blk"), scatter_dimension=0, tiled=True),
        lax.psum_scatter(flat_totals[8], ("head", "blk"), scatter_dimension=0, tiled=True),
    )
    totals = unflatten_all(summed_flat, totals)
    bias_full = lax.dynamic_update_slice_in_dim(
        jnp.zeros((head_count, 2), jnp.float32), bias_accum, head_rank * local_heads, 0
    )
    grad_bias = lax.psum(bias_full, ("head", "blk"))
    return (
        jnp.stack(outputs_list),
        jnp.stack(inputs_list),
        totals[0],
        totals[1],
        totals[2],
        totals[3],
        totals[4],
        totals[5],
        totals[6],
        totals[7],
        totals[8],
        grad_bias,
    )


AXES = ("zh", "zl", "x", "y", "c")
VMEM_BYTES = 58 * 2**20


class Net:
    def __init__(self, send_sems, recv_sems, local_sems):
        self.me = {name: lax.axis_index(name) for name in AXES}
        self.send_sems, self.recv_sems, self.local_sems = send_sems, recv_sems, local_sems
        self.used = 0
        self.local_used = 0
        self.copies = []
        self.locals = []

    def target(self, flips):
        return tuple(1 - self.me[a] if a in flips else self.me[a] for a in AXES)

    def index(self, names, flips=()):
        total = 0
        for a in names:
            total = total * 2 + (1 - self.me[a] if a in flips else self.me[a])
        return total

    def barrier(self, partners):
        sem = pltpu.get_barrier_semaphore()
        for flips in partners:
            pl.semaphore_signal(
                sem, inc=1, device_id=self.target(flips), device_id_type=pl.DeviceIdType.MESH
            )
        pl.semaphore_wait(sem, len(partners))

    def send(self, source, dest, flips):
        copy = pltpu.make_async_remote_copy(
            src_ref=source,
            dst_ref=dest,
            send_sem=self.send_sems.at[self.used],
            recv_sem=self.recv_sems.at[self.used],
            device_id=self.target(flips),
            device_id_type=pl.DeviceIdType.MESH,
        )
        self.used += 1
        copy.start()
        self.copies.append(copy)
        return copy

    def local(self, source, dest):
        copy = pltpu.make_async_copy(source, dest, self.local_sems.at[self.local_used])
        self.local_used += 1
        copy.start()
        return copy

    def finish(self):
        for copy in self.copies:
            copy.wait_send()


CHIP_FLIPS = [
    tuple(a for a, bit in zip(("zl", "x", "y"), ((m >> 2) & 1, (m >> 1) & 1, m & 1)) if bit)
    for m in range(1, 8)
]


class Tree:
    def __init__(self, net, region, dims):
        self.net, self.region, self.dims = net, region, dims
        self.arrive = {}
        self.sibling = []

    def push(self, flips, source=None):
        net = self.net
        source = self.region(flips) if source is None else source
        level = max([self.dims.index(a) for a in flips], default=-1)
        for d in self.dims[level + 1 :]:
            copy = net.send(source, self.region(flips), (d,))
            self.arrive[tuple(sorted(flips + (d,)))] = copy
        self.sibling.append(net.send(source, self.region(flips), ("c",)))

    def take(self, flips):
        self.arrive[tuple(sorted(flips))].wait_recv()
        self.push(flips)

    def order(self):
        masks = []
        for m in range(1, 2 ** len(self.dims)):
            masks.append(tuple(d for i, d in enumerate(self.dims) if (m >> i) & 1))
        return masks

    def end(self):
        for copy in self.sibling:
            copy.wait_recv()


def gather_kernel(
    tok, cot, wqkv, wout, wgate, wup, wdown, small,
    x_out, wh_out, wgu_out, wd_out, wo_out, gf_out, sm_out,
    wp, wl, gp, gl, send_sems, recv_sems, local_sems,
):
    net = Net(send_sems, recv_sems, local_sems)
    me = net.me
    zh, zl, x, y, c = (me[a] for a in AXES)
    net.barrier(CHIP_FLIPS + [("c",), ("zh",)])
    locals_ = []

    def x_region(part):
        def region(flips):
            z_part = zh if part == 0 else 1 - zh
            return x_out.at[z_part * 16 + net.index(AXES[1:], flips)]

        return region

    def wo_region(flips):
        return wo_out.at[:, net.index(AXES[1:], flips)]

    def gf_region(flips):
        return gf_out.at[net.index(("zl", "x", "c"), flips)]

    mine = net.index(AXES)
    x_own = Tree(net, x_region(0), ("y", "zl", "x"))
    x_far = Tree(net, x_region(1), ("y", "zl", "x"))
    wo_tree = Tree(net, wo_region, ("y", "zl", "x"))
    gf_tree = Tree(net, gf_region, ("zl", "x"))
    swap = net.send(tok.at[1 - zh], x_out.at[mine], ("zh",))
    x_own.push((), tok.at[zh])
    sm_zh = net.send(small, sm_out.at[zh, zl, x, y, c], ("zh",))
    wo_zh = net.send(wout, wo_out.at[zh, net.index(AXES[1:])], ("zh",))
    wd_zh = net.send(wdown, wd_out.at[zh, y], ("zh",))
    for zz in range(2):
        for xx in range(2):
            for cc in range(2):
                for zhh in range(2):
                    for yy in range(2):
                        col = 128 * (zhh * 16 + zz * 8 + xx * 4 + yy * 2 + cc)
                        lane = 128 * (zhh * 2 + yy)
                        gp[zz * 2 + xx, 0, cc, :, lane : lane + 128] = wgate[:, col : col + 128]
                        gp[zz * 2 + xx, 1, cc, :, lane : lane + 128] = wup[:, col : col + 128]
    my_pair = net.index(("zl", "x"))
    g_arrive = []
    for flips in (("x",), ("zl",), ("zl", "x")):
        g_arrive.append(net.send(gp.at[net.index(("zl", "x"), flips)], gl.at[my_pair], flips))
    g_own = net.local(gp.at[my_pair], gl.at[my_pair])
    heads = 16
    for h in range(heads):
        wp[h // 2, h % 2] = wqkv[:, 192 * h : 192 * (h + 1)]
    w_arrive = []
    my_chip = net.index(("zl", "x", "y"))
    for flips in CHIP_FLIPS:
        w_arrive.append(net.send(wp.at[net.index(("zl", "x", "y"), flips)], wl.at[my_chip], flips))
    w_own = net.local(wp.at[my_chip], wl.at[my_chip])
    wd_y = net.send(wdown, wd_out.at[zh, y], ("y",))
    locals_.append(net.local(tok.at[zh], x_out.at[mine]))
    sm_own = net.local(small, sm_out.at[zh, zl, x, y, c])
    wo_own = net.local(wout, wo_out.at[zh, net.index(AXES[1:])])
    locals_.append(net.local(wdown, wd_out.at[zh, y]))
    locals_.append(net.local(cot, gf_region(())))
    x_own.take(("y",))
    x_own.take(("zl",))
    g_own.wait()
    for copy in g_arrive:
        copy.wait_recv()
    g_c, g_keep = [], []
    for k in range(2):
        place = wgu_out.at[k, zh, :, y, c]
        g_c.append(net.send(gl.at[:, k, 1 - c], place, ("c",)))
        g_keep.append(net.local(gl.at[:, k, c], place))
    w_own.wait()
    for copy in w_arrive:
        copy.wait_recv()
    w_c = net.send(wl.at[:, 1 - c], wh_out.at[zh, :, c], ("c",))
    w_keep = net.local(wl.at[:, c], wh_out.at[zh, :, c])
    swap.wait_recv()
    x_far.push(())
    g_zh, g_y = [], []

    def g_piece(k, half):
        return wgu_out.at[k // 2, half, pl.ds(2 * (k % 2), 2), y]

    for k in range(4):
        if k % 2 == 0:
            g_keep[k // 2].wait()
            g_c[k // 2].wait_recv()
        g_zh.append(net.send(g_piece(k, zh), g_piece(k, zh), ("zh",)))
        g_y.append(net.send(g_piece(k, zh), g_piece(k, zh), ("y",)))
    w_keep.wait()
    w_c.wait_recv()
    w_zh = net.send(wh_out.at[zh], wh_out.at[zh], ("zh",))
    x_own.take(("y", "zl"))
    x_far.take(("y",))
    x_far.take(("zl",))
    x_far.take(("y", "zl"))
    sm_own.wait()
    sm_zh.wait_recv()
    sm_c = net.send(sm_out.at[:, zl, x, y, c], sm_out.at[:, zl, x, y, c], ("c",))
    gf_tree.push((), cot)
    wo_own.wait()
    wo_zh.wait_recv()
    wo_tree.push(())
    x_own.take(("x",))
    x_own.take(("y", "x"))
    sm_c.wait_recv()
    sm_y = net.send(sm_out.at[:, zl, x, y], sm_out.at[:, zl, x, y], ("y",))
    gf_tree.take(("zl",))
    wd_zh.wait_recv()
    wd_fwd = net.send(wd_out.at[1 - zh, y], wd_out.at[1 - zh, y], ("y",))
    wo_tree.take(("y",))
    x_own.take(("zl", "x"))
    x_own.take(("y", "zl", "x"))
    sm_y.wait_recv()
    sm_zl = net.send(sm_out.at[:, zl, x], sm_out.at[:, zl, x], ("zl",))
    wo_tree.take(("zl",))
    wo_tree.take(("y", "zl"))
    g_fwd = []

    def g_pass(k):
        g_zh[k].wait_recv()
        g_fwd.append(net.send(g_piece(k, 1 - zh), g_piece(k, 1 - zh), ("y",)))

    g_pass(0)
    x_far.take(("x",))
    x_far.take(("y", "x"))
    sm_zl.wait_recv()
    sm_x = net.send(sm_out.at[:, :, x], sm_out.at[:, :, x], ("x",))
    g_pass(1)
    x_far.take(("zl", "x"))
    x_far.take(("y", "zl", "x"))
    gf_tree.take(("x",))
    gf_tree.take(("zl", "x"))
    g_pass(2)
    for flips in (("x",), ("y", "x"), ("zl", "x"), ("y", "zl", "x")):
        wo_tree.take(flips)
    g_pass(3)
    for copy in [sm_x, w_zh, wd_y, wd_fwd] + g_y + g_fwd:
        copy.wait_recv()
    for tree in (x_own, x_far, wo_tree, gf_tree):
        tree.end()
    for copy in locals_:
        copy.wait()
    net.finish()


def gather_all(tok, cot, wqkv, wout, wgate, wup, wdown, small):
    bf = jnp.bfloat16
    any_spec = pl.BlockSpec(memory_space=pl.ANY)
    vm = pl.BlockSpec(memory_space=pltpu.VMEM)
    shapes = [
        jax.ShapeDtypeStruct((32, 64, 1024), bf),
        jax.ShapeDtypeStruct((2, 8, 2, 32, 192), bf),
        jax.ShapeDtypeStruct((2, 2, 4, 2, 2, 32, 512), bf),
        jax.ShapeDtypeStruct((2, 2, 128, 1024), bf),
        jax.ShapeDtypeStruct((2, 16, 32, 1024), bf),
        jax.ShapeDtypeStruct((8, 128, 1024), bf),
        jax.ShapeDtypeStruct((2, 2, 2, 2, 2, 8, 128), jnp.float32),
    ]
    return pl.pallas_call(
        gather_kernel,
        out_shape=shapes,
        in_specs=[any_spec, any_spec, vm, any_spec, vm, vm, any_spec, any_spec],
        out_specs=[any_spec] * 7,
        scratch_shapes=[
            pltpu.VMEM((8, 2, 32, 192), bf),
            pltpu.VMEM((8, 2, 32, 192), bf),
            pltpu.VMEM((4, 2, 2, 32, 512), bf),
            pltpu.VMEM((4, 2, 2, 32, 512), bf),
            pltpu.SemaphoreType.DMA((104,)),
            pltpu.SemaphoreType.DMA((104,)),
            pltpu.SemaphoreType.DMA((16,)),
        ],
        compiler_params=pltpu.CompilerParams(
            collective_id=1, has_side_effects=True, vmem_limit_bytes=VMEM_BYTES
        ),
        name="gather_all",
    )(tok, cot, wqkv, wout, wgate, wup, wdown, small)


HEAD_ROWS = 256
KEY_CHUNK = 512


def lane_iota(rows, lanes=128):
    return lax.broadcasted_iota(jnp.int32, (rows, lanes), 1)


def pieces(value):
    first = value.astype(jnp.bfloat16).astype(jnp.float32)
    second = (value - first).astype(jnp.bfloat16).astype(jnp.float32)
    return first, second, value - first - second


def swap_halves(values):
    lane = lane_iota(values.shape[0])
    return jnp.where(lane % 64 < 32, pltpu.roll(values, 96, 1), pltpu.roll(values, 32, 1))


def pair_mean(values):
    lane = lane_iota(values.shape[0])
    low = jnp.sum(jnp.where(lane < 64, values, 0.0), axis=1, keepdims=True)
    high = jnp.sum(jnp.where(lane < 64, 0.0, values), axis=1, keepdims=True)
    return jnp.where(lane < 64, low, high) * (1.0 / 64.0)


def angles_of(packed):
    lane = lane_iota(packed.shape[0])
    turned = pltpu.roll(packed, 64, 1)
    return jnp.where(lane < 64, packed, turned), jnp.where(lane < 64, turned, packed)


def doc_bounds(lengths, batch):
    starts, ends, total = [], [], jnp.int32(0)
    for j in range(lengths.shape[1]):
        starts.append(total)
        total = total + lengths[batch, j]
        ends.append(total)
    return starts, ends


def key_range(starts, ends, first, last):
    low, high = jnp.int32(0), ends[-1]
    for s in starts:
        low = jnp.where(s <= first, s, low)
    for e in reversed(ends):
        high = jnp.where(e > last, e, high)
    return low, high


def attend_kernel(
    lengths, bias, x_ref, wh_ref, rows_ref, gain_ref, qk_gain_ref, freq_ref,
    att_out, o_out, qf_out, kf_out, vf_out, raw_out, cs_out, feat,
):
    tokens_n = x_ref.shape[0]
    batch = lax.axis_index("zh")
    head = ((lax.axis_index("zl") * 2 + lax.axis_index("x")) * 2 + lax.axis_index("y")) * 2
    head = head + lax.axis_index("c")
    starts, ends = doc_bounds(lengths, batch)
    step = 128

    sub = lax.broadcasted_iota(jnp.int32, (8, step), 0)
    start_col = jnp.zeros((8, step), jnp.int32)
    end_col = jnp.zeros((8, step), jnp.int32)
    for j in range(8):
        start_col = jnp.where(sub == j, starts[j], start_col)
        end_col = jnp.where(sub == j, ends[j], end_col)
    same_bias = jnp.full((8, step), bias[head, 0], jnp.float32)
    other_bias = jnp.full((8, step), bias[head, 1], jnp.float32)
    other_parts = pieces(other_bias)
    diff_parts = pieces(same_bias - other_bias)
    zero = jnp.zeros((8, step), jnp.float32)
    const_q = jnp.where(sub == 0, -256.0, 0.0)
    for i, part in enumerate(other_parts):
        const_q = jnp.where(sub == i + 1, part, const_q)
    const_k = jnp.where(sub < 4, 1.0, 0.0)
    ones_k = jnp.where(sub < 3, 1.0, 0.0)

    @pl.loop(0, tokens_n // step)
    def _(i):
        col = pl.ds(pl.multiple_of(i * step, step), step)
        pos = lax.broadcasted_iota(jnp.int32, (8, step), 1) + i * step
        doc = jnp.where((pos >= start_col) & (pos < end_col), 1.0, 0.0)
        var_row = jnp.broadcast_to(rows_ref[0:1, col], (8, step))
        var = jnp.where(var_row == sub.astype(jnp.float32), 1.0, 0.0)
        rows = [doc * 256.0, const_q] + [var * part for part in diff_parts] + [zero, zero, zero]
        rows += [doc, const_k, var, var, var, ones_k, zero, zero]
        feat[col, :] = jnp.concatenate(rows, axis=0).T
        angle = jnp.broadcast_to(rows_ref[1:2, col], (32, step)) * freq_ref[...]
        cosine, sine = jnp.cos(angle), jnp.sin(angle)
        cs_out[col, :] = jnp.concatenate([cosine, cosine, -sine, sine], axis=0).T

    rows_n = HEAD_ROWS

    @pl.loop(0, tokens_n // rows_n)
    def _(i):
        row = pl.ds(pl.multiple_of(i * rows_n, rows_n), rows_n)
        value = x_ref[row, :].astype(jnp.float32)
        scale = lax.rsqrt(jnp.mean(value * value, axis=1, keepdims=True) + EPS)
        normed = (value * scale * gain_ref[...]).astype(jnp.bfloat16)
        qkv = jnp.dot(normed, wh_ref[...], preferred_element_type=jnp.float32)
        raw = qkv[:, :128]
        raw_out[row, :] = raw
        scaled = raw * lax.rsqrt(pair_mean(raw * raw) + EPS) * qk_gain_ref[...]
        cosine, sine = angles_of(cs_out[row, :])
        turned = (scaled * cosine + swap_halves(scaled) * sine).astype(jnp.bfloat16)
        turned = turned.astype(jnp.float32)
        lane = lane_iota(rows_n)
        marks = feat[row, :]
        qf_out[row, :] = jnp.where(
            lane < 64, turned * 0.125, pltpu.roll(marks, 64, 1)
        ).astype(jnp.bfloat16)
        kf_out[row, :] = jnp.where(lane < 64, pltpu.roll(turned, 64, 1), marks).astype(jnp.bfloat16)
        third = jnp.concatenate([qkv[:, 128:192], jnp.zeros((rows_n, 64), jnp.float32)], axis=1)
        vf_out[row, :] = jnp.where((lane >= 64) & (lane < 67), 1.0, third).astype(jnp.bfloat16)

    for i in range(tokens_n // rows_n):
        row = pl.ds(i * rows_n, rows_n)
        low, high = key_range(starts, ends, i * rows_n, (i + 1) * rows_n - 1)
        query = qf_out[row, :]

        def one_chunk(k, total):
            col = pl.ds(pl.multiple_of(k * KEY_CHUNK, KEY_CHUNK), KEY_CHUNK)
            scores = lax.dot_general(
                query, kf_out[col, :], (((1,), (1,)), ((), ())), preferred_element_type=jnp.float32
            )
            weights = jnp.exp(scores).astype(jnp.bfloat16)
            return total + jnp.dot(weights, vf_out[col, :], preferred_element_type=jnp.float32)

        total = lax.fori_loop(
            low // KEY_CHUNK,
            (high + KEY_CHUNK - 1) // KEY_CHUNK,
            one_chunk,
            jnp.zeros((rows_n, 128), jnp.float32),
        )
        weight = total[:, 64:65]
        result = total / weight
        lane = lane_iota(rows_n)
        o_out[row, :] = jnp.where(lane < 64, result, jnp.log(weight))
        att_out[row, :] = result[:, :64].astype(jnp.bfloat16)


def attend(lengths, bias, x_all, wh, rows, gain, qk_gain, freq):
    bf, f32 = jnp.bfloat16, jnp.float32
    n = x_all.shape[0]
    sm = pl.BlockSpec(memory_space=pltpu.SMEM)
    vm = pl.BlockSpec(memory_space=pltpu.VMEM)
    return pl.pallas_call(
        attend_kernel,
        out_shape=[
            jax.ShapeDtypeStruct((n, 64), bf),
            jax.ShapeDtypeStruct((n, 128), f32),
            jax.ShapeDtypeStruct((n, 128), bf),
            jax.ShapeDtypeStruct((n, 128), bf),
            jax.ShapeDtypeStruct((n, 128), bf),
            jax.ShapeDtypeStruct((n, 128), f32),
            jax.ShapeDtypeStruct((n, 128), f32),
        ],
        in_specs=[sm, sm] + [vm] * 6,
        out_specs=[vm] * 7,
        scratch_shapes=[pltpu.VMEM((n, 128), f32)],
        compiler_params=pltpu.CompilerParams(vmem_limit_bytes=VMEM_BYTES),
        name="attend",
    )(lengths, bias, x_all, wh, rows, gain, qk_gain, freq)


def attend_back_kernel(
    lengths, x_ref, wh_ref, g_ref, o_ref, qf_ref, kf_ref, vf_ref, raw_ref, cs_ref, gain_ref,
    qk_gain_ref, gn_out, gw_out, small_out, qb, gb, gk, gv, gqkv, normed_s, bias_s, gain_s,
):
    tokens_n = x_ref.shape[0]
    batch = lax.axis_index("zh")
    head = ((lax.axis_index("zl") * 2 + lax.axis_index("x")) * 2 + lax.axis_index("y")) * 2
    head = head + lax.axis_index("c")
    starts, ends = doc_bounds(lengths, batch)
    rows_n = HEAD_ROWS
    lane = lane_iota(rows_n)
    gk[...] = jnp.zeros_like(gk)
    gv[...] = jnp.zeros_like(gv)
    bias_s[...] = jnp.zeros_like(bias_s)
    gain_s[...] = jnp.zeros_like(gain_s)

    @pl.loop(0, tokens_n // rows_n)
    def _(i):
        row = pl.ds(pl.multiple_of(i * rows_n, rows_n), rows_n)
        value = x_ref[row, :].astype(jnp.float32)
        scale = lax.rsqrt(jnp.mean(value * value, axis=1, keepdims=True) + EPS)
        normed_s[row, :] = (value * scale * gain_ref[...]).astype(jnp.bfloat16)
        kept = o_ref[row, :]
        grad = jnp.concatenate(
            [g_ref[row, :].astype(jnp.float32), jnp.zeros((rows_n, 64), jnp.float32)], axis=1
        )
        delta = jnp.sum(jnp.where(lane < 64, grad * kept, 0.0), axis=1, keepdims=True)
        log_total = kept[:, 64:65]
        query = qf_ref[row, :].astype(jnp.float32)
        for j, part in enumerate(pieces(log_total)):
            query = jnp.where(lane == 64 + 40 + j, -part, query)
        qb[row, :] = query.astype(jnp.bfloat16)
        for j, part in enumerate(pieces(delta)):
            grad = jnp.where(lane == 64 + j, -part, grad)
        gb[row, :] = grad.astype(jnp.bfloat16)

    for i in range(tokens_n // rows_n):
        row = pl.ds(i * rows_n, rows_n)
        low, high = key_range(starts, ends, i * rows_n, (i + 1) * rows_n - 1)
        query, grad = qb[row, :], gb[row, :]

        def one_chunk(k, total):
            col = pl.ds(pl.multiple_of(k * KEY_CHUNK, KEY_CHUNK), KEY_CHUNK)
            key = kf_ref[col, :]
            last = (((1,), (1,)), ((), ()))
            first = (((0,), (0,)), ((), ()))
            scores = lax.dot_general(query, key, last, preferred_element_type=jnp.float32)
            probs = jnp.exp(scores)
            centred = lax.dot_general(grad, vf_ref[col, :], last, preferred_element_type=jnp.float32)
            back = (probs * centred).astype(jnp.bfloat16)
            gv[col, :] += lax.dot_general(
                probs.astype(jnp.bfloat16), grad, first, preferred_element_type=jnp.float32
            )
            gk[col, :] += lax.dot_general(back, query, first, preferred_element_type=jnp.float32)
            return total + jnp.dot(back, key, preferred_element_type=jnp.float32)

        total = lax.fori_loop(
            low // KEY_CHUNK,
            (high + KEY_CHUNK - 1) // KEY_CHUNK,
            one_chunk,
            jnp.zeros((rows_n, 128), jnp.float32),
        )
        gqkv[row, :128] = jnp.where(lane < 64, total * 0.125, 0.0).astype(jnp.bfloat16)
        kept = kf_ref[row, :].astype(jnp.float32)
        same = jnp.where((lane >= 80) & (lane < 88), total * kept, 0.0)
        every = jnp.where(lane == 72, total, 0.0)
        bias_s[0:1, :] += jnp.sum(same, axis=0, keepdims=True)
        bias_s[1:2, :] += jnp.sum(every, axis=0, keepdims=True)

    @pl.loop(0, tokens_n // rows_n)
    def _(i):
        row = pl.ds(pl.multiple_of(i * rows_n, rows_n), rows_n)
        raw = raw_ref[row, :]
        scale = lax.rsqrt(pair_mean(raw * raw) + EPS)
        cosine, sine = angles_of(cs_ref[row, :])
        key_part = pltpu.roll(gk[row, :].astype(jnp.bfloat16).astype(jnp.float32), 64, 1)
        grad = jnp.where(lane < 64, gqkv[row, :128].astype(jnp.float32), key_part)
        turned = grad * cosine - swap_halves(grad) * sine
        gain_s[0:1, :] += jnp.sum(turned * raw * scale, axis=0, keepdims=True)
        weighted = turned * qk_gain_ref[...]
        back = scale * weighted - raw * (scale * scale * scale) * pair_mean(weighted * raw)
        gqkv[row, :] = jnp.concatenate([back, gv[row, :][:, :64]], axis=1).astype(jnp.bfloat16)

    @pl.loop(0, tokens_n // rows_n)
    def _(i):
        row = pl.ds(pl.multiple_of(i * rows_n, rows_n), rows_n)
        grad = lax.dot_general(
            gqkv[row, :], wh_ref[...], (((1,), (1,)), ((), ())), preferred_element_type=jnp.float32
        )
        gn_out[row, :] = grad.astype(jnp.bfloat16)
        value = x_ref[row, :].astype(jnp.float32)
        scale = lax.rsqrt(jnp.mean(value * value, axis=1, keepdims=True) + EPS)
        term = grad * value * scale
        small_out[0:1, :] = jnp.where(i == 0, 0.0, small_out[0:1, :]) + jnp.sum(
            term, axis=0, keepdims=True
        )

    gw_out[...] = lax.dot_general(
        normed_s[...], gqkv[...], (((0,), (0,)), ((), ())), preferred_element_type=jnp.float32
    ).astype(jnp.bfloat16)
    one = lane_iota(1)
    both = gain_s[0:1, :]
    turned = pltpu.roll(jnp.broadcast_to(both, (8, 128)), 64, 1)[0:1, :]
    wide = lane_iota(1, 1024)
    query_gain = jnp.concatenate([jnp.where(one < 64, both, turned)] * 8, axis=1)
    key_gain = jnp.concatenate([jnp.where(one < 64, turned, both)] * 8, axis=1)
    small_out[1:2, :] = jnp.zeros((1, 1024), jnp.float32)
    small_out[2:3, :] = jnp.where(wide // 64 == head, query_gain, 0.0)
    small_out[3:4, :] = jnp.where(wide // 64 == head, key_gain, 0.0)
    same = jnp.sum(bias_s[0:1, :], axis=1, keepdims=True)
    every = jnp.sum(bias_s[1:2, :], axis=1, keepdims=True)
    row_bias = jnp.where(wide == 2 * head, same, 0.0)
    small_out[4:5, :] = jnp.where(wide == 2 * head + 1, every - same, row_bias)
    small_out[5:8, :] = jnp.zeros((3, 1024), jnp.float32)


def attend_back(lengths, x_all, wh, grad, kept, qf, kf, vf, raw, cs, gain, qk_gain):
    bf, f32 = jnp.bfloat16, jnp.float32
    n = x_all.shape[0]
    sm = pl.BlockSpec(memory_space=pltpu.SMEM)
    vm = pl.BlockSpec(memory_space=pltpu.VMEM)
    return pl.pallas_call(
        attend_back_kernel,
        out_shape=[
            jax.ShapeDtypeStruct((n, 1024), bf),
            jax.ShapeDtypeStruct((1024, 192), bf),
            jax.ShapeDtypeStruct((8, 1024), f32),
        ],
        in_specs=[sm] + [vm] * 11,
        out_specs=[vm] * 3,
        scratch_shapes=[
            pltpu.VMEM((n, 128), bf),
            pltpu.VMEM((n, 128), bf),
            pltpu.VMEM((n, 128), f32),
            pltpu.VMEM((n, 128), f32),
            pltpu.VMEM((n, 192), bf),
            pltpu.VMEM((n, 1024), bf),
            pltpu.VMEM((8, 128), f32),
            pltpu.VMEM((8, 128), f32),
        ],
        compiler_params=pltpu.CompilerParams(vmem_limit_bytes=VMEM_BYTES),
        name="attend_back",
    )(lengths, x_all, wh, grad, kept, qf, kf, vf, raw, cs, gain, qk_gain)


def middle_kernel(
    att, tok, cot, wo, wgu, wd, gf, gain_ref,
    out_ref, gatt_out, gres_out, gwgu_out, gwd_out, gwo_out, small_out,
    lb, ap, at2, at3, att_s, n2, gh, hid, ggu, kept, sent, landed, red_send, red_land,
    ga3, ga2, ag1, ls, lb2, out_acc, send_sems, recv_sems, local_sems,
):
    bf, f32 = jnp.bfloat16, jnp.float32
    last = (((1,), (1,)), ((), ()))
    first = (((0,), (0,)), ((), ()))
    net = Net(send_sems, recv_sems, local_sems)
    zh, zl, x, y, c = (net.me[a] for a in AXES)
    net.barrier(CHIP_FLIPS + [("c",), ("zh",)])
    chips = ("zl", "x", "y")
    my_chip = net.index(chips)
    lane = lane_iota(64)

    step = net.send(att.at[:, 1 - c], lb, ("c",))
    for p in range(4):
        gh[p] = lax.dot_general(gf[p], wd[...], last, preferred_element_type=f32).astype(gh.dtype)
    step.wait_recv()

    @pl.loop(0, 16)
    def _(i):
        own = jnp.concatenate([att[i, c]] * 2, axis=1)
        other = jnp.concatenate([lb[i]] * 2, axis=1)
        ap[i // 8, i % 8] = jnp.where((lane < 64) == (c == 0), own, other)

    arrive = []
    for flips in CHIP_FLIPS:
        arrive.append(net.send(ap.at[:, net.index(chips, flips)], at2.at[my_chip], flips))
    net_own = net.local(ap.at[:, my_chip], at2.at[my_chip])
    net_own.wait()
    for copy in arrive:
        copy.wait_recv()
    step = net.send(at2.at[:, 1 - zh], at3, ("zh",))
    for k in range(8):
        att_s[pl.ds(pl.multiple_of(zh * 64, 64), 64), 128 * k : 128 * (k + 1)] = at2[k, zh]
    step.wait_recv()
    for k in range(8):
        att_s[pl.ds(pl.multiple_of(64 - zh * 64, 64), 64), 128 * k : 128 * (k + 1)] = at3[k]

    resid = tok[...].astype(f32) + jnp.dot(att_s[...], wo[...], preferred_element_type=f32)
    scale = lax.rsqrt(jnp.mean(resid * resid, axis=1, keepdims=True) + EPS)
    gain = gain_ref[...]
    my_pair = net.index(("zl", "x"))
    n2[my_pair, c] = (resid * scale * gain).astype(bf)
    group = [("zl",), ("x",), ("zl", "x")]
    to_sibling = [net.send(n2.at[my_pair, c], n2.at[my_pair, c], ("c",))]
    from_chips = [net.send(n2.at[my_pair, c], n2.at[my_pair, c], flips) for flips in group]

    def feed(pair):
        rows = n2[pair].reshape(256, 1024)
        gate = jnp.dot(rows, wgu[0], preferred_element_type=f32)
        up = jnp.dot(rows, wgu[1], preferred_element_type=f32)
        sig = 1.0 / (1.0 + jnp.exp(-gate))
        silu = gate * sig
        hid[pair] = (silu * up).astype(bf)
        back = gh[pair]
        ggu[0, pair] = (back * up * sig * (1.0 + gate * (1.0 - sig))).astype(bf)
        ggu[1, pair] = (back * silu).astype(bf)

    def back_product(pair):
        total = lax.dot_general(ggu[0, pair], wgu[0], last, preferred_element_type=f32)
        return total + lax.dot_general(ggu[1, pair], wgu[1], last, preferred_element_type=f32)

    def out_product(pair):
        return jnp.dot(hid[pair], wd[...], preferred_element_type=f32)

    def share(kind, slot, value):
        kept[kind, slot, 0] = value[:128]
        kept[kind, slot, 1] = value[128:]
        sent[kind, slot] = kept[kind, slot, 1 - c].astype(bf)
        return net.send(sent.at[kind, slot], landed.at[kind, slot], ("c",))

    pairs = [my_pair] + [net.index(("zl", "x"), flips) for flips in group]
    halves = {}
    reduced = {0: [], 1: []}

    def finish_half(kind, slot):
        halves[kind, slot].wait_recv()
        total = kept[kind, slot, c] + landed[kind, slot].astype(f32)
        if slot == 0:
            kept[kind, slot, c] = total
        else:
            red_send[kind, slot - 1] = total.astype(bf)
            reduced[kind].append(
                net.send(red_send.at[kind, slot - 1], red_land.at[kind, slot - 1], group[slot - 1])
            )

    to_sibling[0].wait_recv()
    feed(pairs[0])
    halves[0, 0] = share(0, 0, back_product(pairs[0]))
    for k in range(3):
        from_chips[k].wait_recv()
        to_sibling.append(net.send(n2.at[pairs[k + 1], c], n2.at[pairs[k + 1], c], ("c",)))
    for k in range(3):
        to_sibling[k + 1].wait_recv()
        feed(pairs[k + 1])
        halves[0, k + 1] = share(0, k + 1, back_product(pairs[k + 1]))
        if k > 0:
            finish_half(0, k)
    finish_half(0, 3)
    finish_half(0, 0)
    for k in (1, 2, 3, 0):
        halves[1, k] = share(1, k, out_product(pairs[k]))
    for k in (1, 2, 3, 0):
        finish_half(1, k)

    gwd_out[...] = lax.dot_general(
        hid[...].reshape(1024, 512), gf[...].reshape(1024, 1024), first, preferred_element_type=f32
    ).astype(bf)
    for k in range(2):
        gwgu_out[k] = lax.dot_general(
            n2[...].reshape(1024, 1024), ggu[k].reshape(1024, 512), first, preferred_element_type=f32
        ).astype(bf)

    for copy in reduced[0]:
        copy.wait_recv()
    total = kept[0, 0, c]
    for k in range(3):
        total = total + red_land[0, k].astype(f32)
    small_out[...] = jnp.zeros_like(small_out)
    small_out[1:2, :] = jnp.sum(total * resid * scale, axis=0, keepdims=True)
    weighted = total * gain
    mean = jnp.mean(weighted * resid, axis=1, keepdims=True)
    grad_resid = cot[...].astype(f32) + scale * weighted - resid * (scale * scale * scale) * mean
    gres_out[...] = grad_resid
    branch = grad_resid.astype(bf)
    grad_att = lax.dot_general(branch, wo[...], last, preferred_element_type=f32).astype(bf)
    for k in range(8):
        for b in range(2):
            ga3[b, k] = grad_att[64 * b : 64 * (b + 1), 128 * k : 128 * (k + 1)]
    step = net.send(ga3.at[1 - zh], ga2.at[zh], ("zh",))
    gwo_out[...] = lax.dot_general(att_s[...], branch, first, preferred_element_type=f32).astype(bf)
    ga2[zh] = ga3[zh]
    step.wait_recv()
    arrive = []
    for flips in CHIP_FLIPS:
        arrive.append(net.send(ga2.at[:, net.index(chips, flips)], ag1.at[:, my_chip], flips))
    net_own = net.local(ga2.at[:, my_chip], ag1.at[:, my_chip])
    for copy in reduced[1]:
        copy.wait_recv()
    total = kept[1, 0, c] + resid
    for k in range(3):
        total = total + red_land[1, k].astype(f32)
    out_ref[...] = total.astype(bf)
    net_own.wait()
    for copy in arrive:
        copy.wait_recv()

    @pl.loop(0, 16)
    def _(i):
        both = ag1[i // 8, i % 8]
        low, high = both[:, :64], both[:, 64:]
        low32, high32 = low.astype(f32), high.astype(f32)
        ls[i] = jnp.where(c == 0, high32, low32).astype(bf)
        lb2[i] = jnp.where(c == 0, low32, high32).astype(bf)

    step = net.send(ls, gatt_out.at[:, c], ("c",))
    keep = net.local(lb2, gatt_out.at[:, c])
    keep.wait()
    step.wait_recv()
    net.finish()


def middle(att, tok, cot, wo, wgu, wd, gf, gain):
    bf, f32 = jnp.bfloat16, jnp.float32
    vm = pl.BlockSpec(memory_space=pltpu.VMEM)
    return pl.pallas_call(
        middle_kernel,
        out_shape=[
            jax.ShapeDtypeStruct((128, 1024), bf),
            jax.ShapeDtypeStruct((16, 2, 64, 64), bf),
            jax.ShapeDtypeStruct((128, 1024), f32),
            jax.ShapeDtypeStruct((2, 1024, 512), bf),
            jax.ShapeDtypeStruct((512, 1024), bf),
            jax.ShapeDtypeStruct((1024, 1024), bf),
            jax.ShapeDtypeStruct((8, 1024), f32),
        ],
        in_specs=[vm] * 8,
        out_specs=[vm] * 7,
        scratch_shapes=[
            pltpu.VMEM((16, 64, 64), bf),
            pltpu.VMEM((2, 8, 64, 128), bf),
            pltpu.VMEM((8, 2, 64, 128), bf),
            pltpu.VMEM((8, 64, 128), bf),
            pltpu.VMEM((128, 1024), bf),
            pltpu.VMEM((4, 2, 128, 1024), bf),
            pltpu.VMEM((4, 256, 512), f32),
            pltpu.VMEM((4, 256, 512), bf),
            pltpu.VMEM((2, 4, 256, 512), bf),
            pltpu.VMEM((2, 4, 2, 128, 1024), f32),
            pltpu.VMEM((2, 4, 128, 1024), bf),
            pltpu.VMEM((2, 4, 128, 1024), bf),
            pltpu.VMEM((2, 3, 128, 1024), bf),
            pltpu.VMEM((2, 3, 128, 1024), bf),
            pltpu.VMEM((2, 8, 64, 128), bf),
            pltpu.VMEM((2, 8, 64, 128), bf),
            pltpu.VMEM((2, 8, 64, 128), bf),
            pltpu.VMEM((16, 64, 64), bf),
            pltpu.VMEM((16, 64, 64), bf),
            pltpu.VMEM((8, 128), f32),
            pltpu.SemaphoreType.DMA((48,)),
            pltpu.SemaphoreType.DMA((48,)),
            pltpu.SemaphoreType.DMA((4,)),
        ],
        compiler_params=pltpu.CompilerParams(
            collective_id=2, has_side_effects=True, vmem_limit_bytes=VMEM_BYTES
        ),
        name="middle",
    )(att, tok, cot, wo, wgu, wd, gf, gain)


class Reduce:
    MASKS = [("x", "zl", "y"), ("x", "zl"), ("x", "y"), ("x",), ("zl", "y"), ("zl",), ("y",), ()]

    def __init__(self, net, parts, landing, sends, arrivals):
        self.net, self.parts, self.landing = net, parts, landing
        self.sends, self.arrivals = sends, arrivals
        self.c = net.me["c"]
        self.from_sibling, self.incoming = {}, {}

    def chip(self, mask):
        return self.net.index(("zl", "x", "y"), mask)

    def begin(self, masks):
        for mask in masks:
            slot = self.MASKS.index(mask)
            self.from_sibling[mask] = self.net.send(
                self.parts.at[:, self.chip(mask), 1 - self.c], self.landing.at[slot], ("c",)
            )

    def total(self, mask, upto):
        slot = self.MASKS.index(mask)
        value = self.parts[:, self.chip(mask), self.c].astype(jnp.float32)
        value = value + self.landing[slot].astype(jnp.float32)
        for stage in upto:
            value = value + self.arrivals[self.place(mask, stage)].astype(jnp.float32)
        return value

    def place(self, mask, stage):
        order = {"x": [("zl", "y"), ("zl",), ("y",), ()], "zl": [("y",), ()], "y": [()]}[stage]
        return {"x": 0, "zl": 4, "y": 6}[stage] + order.index(mask)

    def forward(self, mask):
        stage = mask[0]
        rest = mask[1:]
        before = {"x": (), "zl": ("x",), "y": ("x", "zl")}[stage]
        for earlier in before:
            self.incoming[mask, earlier].wait_recv()
        if not before:
            self.from_sibling[mask].wait_recv()
        elif mask in self.from_sibling:
            self.from_sibling[mask].wait_recv()
        slot = self.place(rest, stage)
        self.sends[slot] = self.total(mask, before).astype(jnp.bfloat16)
        self.incoming[rest, stage] = self.net.send(
            self.sends.at[slot], self.arrivals.at[slot], (stage,)
        )

    def result(self):
        self.from_sibling[()].wait_recv()
        for stage in ("x", "zl", "y"):
            self.incoming[(), stage].wait_recv()
        return self.total((), ("x", "zl", "y"))


def reduce_kernel(
    gn, gw, gwgu, gwd, gwo, small_a, small_b, tok, gres, gain_ref,
    gtok_out, gwqkv_out, gwo_out, gwg_out, gwu_out, gwd_out, small_out,
    n_land, n_send, n_arr, n_half, n_half_land, grad_s,
    o_land, o_send, o_arr, o_half, o_half_land, o_keep,
    y_wgu, y_wd, h_wgu, h_wd, h_wgu_land, h_wd_land, f_sum, f1, f2,
    w_land, w_t, w_p, w_q, s_acc, s_land, send_sems, recv_sems, local_sems,
):
    bf, f32 = jnp.bfloat16, jnp.float32
    net = Net(send_sems, recv_sems, local_sems)
    zh, zl, x, y, c = (net.me[a] for a in AXES)
    chips = ("zl", "x", "y")
    my_chip = net.index(chips)
    my_pair = net.index(("zl", "x"))
    net.barrier(CHIP_FLIPS + [("c",), ("zh",)])
    tree_n = Reduce(net, gn, n_land, n_send, n_arr)
    tree_o = Reduce(net, gwo, o_land, o_send, o_arr)

    y_far = [net.send(gwgu.at[k, 1 - zh, :, 1 - y], y_wgu.at[k, 1], ("y",)) for k in range(2)]
    y_far.append(net.send(gwd.at[1 - zh, 1 - y], y_wd.at[1], ("y",)))
    tree_n.begin(Reduce.MASKS[:4])
    w_zh = net.send(gw.at[1 - zh], w_land, ("zh",))
    tree_o.begin(Reduce.MASKS)
    tree_n.begin(Reduce.MASKS[4:])
    rounds = ("c", "x", "y", "zl", "zh")
    s_acc[0] = small_a[...] + small_b[...]
    s_step = net.send(s_acc.at[0], s_land.at[0], (rounds[0],))

    def small_round(step, k):
        step.wait_recv()
        total = s_acc[k] + s_land[k]
        if k == 4:
            small_out[...] = total
            return None
        s_acc[k + 1] = total
        return net.send(s_acc.at[k + 1], s_land.at[k + 1], (rounds[k + 1],))

    for mask in Reduce.MASKS[:4]:
        tree_n.forward(mask)
    y_near = [net.send(gwgu.at[k, zh, :, 1 - y], y_wgu.at[k, 0], ("y",)) for k in range(2)]
    y_near.append(net.send(gwd.at[zh, 1 - y], y_wd.at[0], ("y",)))
    for mask in Reduce.MASKS[:4]:
        tree_o.forward(mask)
    s_step = small_round(s_step, 0)
    h_steps = []
    for k in range(2):
        y_far[k].wait_recv()
        h_wgu[k] = (gwgu[k, 1 - zh, :, y].astype(f32) + y_wgu[k, 1].astype(f32)).astype(bf)
        h_steps.append(net.send(h_wgu.at[k], h_wgu_land.at[k], ("zh",)))
    y_far[2].wait_recv()
    h_wd[...] = (gwd[1 - zh, y].astype(f32) + y_wd[1].astype(f32)).astype(bf)
    h_steps.append(net.send(h_wd, h_wd_land, ("zh",)))
    s_step = small_round(s_step, 1)
    w_zh.wait_recv()
    w_t[...] = (gw[zh].astype(f32) + w_land[...].astype(f32)).astype(bf)
    w_c = net.send(w_t.at[:, 1 - c], w_p.at[:, c], ("c",))
    w_keep = net.local(w_t.at[:, c], w_p.at[:, c])
    tree_n.forward(("zl", "y"))
    tree_n.forward(("zl",))
    w_keep.wait()
    w_c.wait_recv()
    w_steps = []
    for flips in CHIP_FLIPS:
        w_steps.append(net.send(w_p.at[net.index(chips, flips)], w_q.at[my_chip], flips))
    w_own = net.local(w_p.at[my_chip], w_q.at[my_chip])
    s_step = small_round(s_step, 2)
    tree_o.forward(("zl", "y"))
    tree_o.forward(("zl",))
    tree_n.forward(("y",))
    tree_o.forward(("y",))
    s_step = small_round(s_step, 3)

    total = tree_n.result()
    grad_s[0] = total[0]
    grad_s[1] = total[1]
    n_half[...] = grad_s[1 - zh].astype(bf)
    n_step = net.send(n_half, n_half_land, ("zh",))
    total = tree_o.result()
    o_keep[0] = total[0]
    o_keep[1] = total[1]
    o_half[...] = o_keep[1 - zh].astype(bf)
    o_step = net.send(o_half, o_half_land, ("zh",))
    n_step.wait_recv()
    grad_s[1 - zh] = n_half_land[...].astype(f32)
    gain = gain_ref[...]
    for b in range(2):
        value = tok[b].astype(f32)
        scale = lax.rsqrt(jnp.mean(value * value, axis=1, keepdims=True) + EPS)
        weighted = grad_s[b] * gain
        mean = jnp.mean(weighted * value, axis=1, keepdims=True)
        back = scale * weighted - value * (scale * scale * scale) * mean
        gtok_out[b] = (gres[b] + back).astype(bf)
    o_step.wait_recv()
    gwo_out[...] = o_keep[zh] + o_half_land[...].astype(f32)
    s_step = small_round(s_step, 4)
    w_own.wait()
    for copy in w_steps:
        copy.wait_recv()
    for h in range(16):
        gwqkv_out[:, 192 * h : 192 * (h + 1)] = w_q[h // 2, h % 2].astype(f32)

    f_steps = []
    for k in range(2):
        y_near[k].wait_recv()
        h_steps[k].wait_recv()
        for j in range(4):
            rows = gwgu[k, zh, j, y].astype(f32) + y_wgu[k, 0, j].astype(f32)
            rows = rows + h_wgu_land[k, j].astype(f32)
            f_sum[k, j, 0] = rows[:32].astype(bf)
            f_sum[k, j, 1] = rows[32:].astype(bf)
        for flips in (("x",), ("zl",), ("zl", "x")):
            f_steps.append(
                net.send(f_sum.at[k, net.index(("zl", "x"), flips)], f1.at[k, my_pair], flips)
            )
        f1[k, my_pair] = f_sum[k, my_pair]
    y_near[2].wait_recv()
    h_steps[2].wait_recv()
    gwd_out[...] = gwd[zh, y].astype(f32) + y_wd[0].astype(f32) + h_wd_land[...].astype(f32)
    f_c = []
    for k in range(2):
        for j in range(3):
            f_steps[3 * k + j].wait_recv()
        f_c.append(net.send(f1.at[k, :, 1 - c], f2.at[k, :, c], ("c",)))
        f2[k, :, c] = f1[k, :, c]
    for k, out in ((0, gwg_out), (1, gwu_out)):
        f_c[k].wait_recv()
        for pair in range(4):
            for cc in range(2):
                for part in range(4):
                    idx = (part // 2) * 16 + pair * 4 + (part % 2) * 2 + cc
                    out[:, 128 * idx : 128 * (idx + 1)] = f2[
                        k, pair, cc, :, 128 * part : 128 * (part + 1)
                    ].astype(f32)
    net.finish()


def reduce_all(gn, gw, gwgu, gwd, gwo, small_a, small_b, tok, gres, gain):
    bf, f32 = jnp.bfloat16, jnp.float32
    vm = pl.BlockSpec(memory_space=pltpu.VMEM)
    V = pltpu.VMEM
    return pl.pallas_call(
        reduce_kernel,
        out_shape=[
            jax.ShapeDtypeStruct((2, 64, 1024), bf),
            jax.ShapeDtypeStruct((32, 3072), f32),
            jax.ShapeDtypeStruct((32, 1024), f32),
            jax.ShapeDtypeStruct((32, 4096), f32),
            jax.ShapeDtypeStruct((32, 4096), f32),
            jax.ShapeDtypeStruct((128, 1024), f32),
            jax.ShapeDtypeStruct((8, 1024), f32),
        ],
        in_specs=[vm] * 10,
        out_specs=[vm] * 7,
        scratch_shapes=[
            V((8, 2, 64, 1024), bf),
            V((7, 2, 64, 1024), bf),
            V((7, 2, 64, 1024), bf),
            V((64, 1024), bf),
            V((64, 1024), bf),
            V((2, 64, 1024), f32),
            V((8, 2, 32, 1024), bf),
            V((7, 2, 32, 1024), bf),
            V((7, 2, 32, 1024), bf),
            V((32, 1024), bf),
            V((32, 1024), bf),
            V((2, 32, 1024), f32),
            V((2, 2, 4, 64, 512), bf),
            V((2, 128, 1024), bf),
            V((2, 4, 64, 512), bf),
            V((128, 1024), bf),
            V((2, 4, 64, 512), bf),
            V((128, 1024), bf),
            V((2, 4, 2, 32, 512), bf),
            V((2, 4, 2, 32, 512), bf),
            V((2, 4, 2, 32, 512), bf),
            V((8, 2, 32, 192), bf),
            V((8, 2, 32, 192), bf),
            V((8, 2, 32, 192), bf),
            V((8, 2, 32, 192), bf),
            V((5, 8, 1024), f32),
            V((5, 8, 1024), f32),
            pltpu.SemaphoreType.DMA((72,)),
            pltpu.SemaphoreType.DMA((72,)),
            pltpu.SemaphoreType.DMA((4,)),
        ],
        compiler_params=pltpu.CompilerParams(
            collective_id=3, has_side_effects=True, vmem_limit_bytes=VMEM_BYTES
        ),
        name="reduce_all",
    )(gn, gw, gwgu, gwd, gwo, small_a, small_b, tok, gres, gain)


def frequencies():
    index = np.arange(32, dtype=np.float32)
    return np.broadcast_to((THETA ** (-2.0 * index / 64.0)).astype(np.float32)[:, None], (32, 128))


def on_device_cube(
    tokens,
    cotangent,
    w_qkv,
    w_out,
    w_gate,
    w_up,
    w_down,
    norm_attn,
    norm_ffn,
    q_gain,
    k_gain,
    var_bias,
    doc_lengths,
    variate,
    times,
):
    f32 = jnp.float32
    place = {name: lax.axis_index(name) for name in AXES}
    rank = jnp.int32(0)
    for name in AXES:
        rank = rank * 2 + place[name]
    gains = jnp.concatenate([norm_attn, norm_ffn, q_gain, k_gain]).astype(f32)
    small = jnp.stack([variate.reshape(128).astype(f32), times.reshape(128).astype(f32), gains])
    small = jnp.concatenate([small, jnp.zeros((5, 128), f32)])
    x_all, wh, wgu, wd, wo, gf, small_all = gather_all(
        tokens, cotangent.reshape(128, 1024), w_qkv, w_out, w_gate, w_up, w_down, small
    )
    x_all = x_all.reshape(2048, 1024)
    wh = wh.reshape(1024, 192)
    small_all = small_all.reshape(32, 8, 128)
    rows = lax.dynamic_slice(small_all, (0, 0, place["zh"] * 64), (32, 2, 64))
    rows = rows.transpose(1, 0, 2).reshape(2, 2048)
    all_gains = small_all[:, 2].reshape(32, 4, 32).transpose(1, 0, 2).reshape(4, 1024)
    head = rank % 16
    qk_gain = lax.dynamic_slice(all_gains, (2, head * 64), (2, 64)).reshape(1, 128)
    gain_attn, gain_ffn = all_gains[0:1], all_gains[1:2]
    att, kept, qf, kf, vf, raw, cs = attend(
        doc_lengths, var_bias, x_all, wh, rows, gain_attn, qk_gain, jnp.asarray(frequencies())
    )
    out, gatt, gres, gwgu, gwd, gwo, small_m = middle(
        att.reshape(16, 2, 64, 64),
        tokens.reshape(128, 1024),
        cotangent.reshape(128, 1024),
        wo.reshape(1024, 1024),
        wgu.reshape(2, 1024, 512),
        wd.reshape(512, 1024),
        gf.reshape(4, 256, 1024),
        gain_ffn,
    )
    gn, gw, small_b = attend_back(
        doc_lengths, x_all, wh, gatt.reshape(2048, 64), kept, qf, kf, vf, raw, cs,
        gain_attn, qk_gain,
    )
    gtok, gwqkv, gwo, gwg, gwu, gwd, small = reduce_all(
        gn.reshape(2, 8, 2, 64, 1024),
        gw.reshape(2, 8, 2, 32, 192),
        gwgu.reshape(2, 2, 4, 2, 64, 512),
        gwd.reshape(2, 2, 128, 1024),
        gwo.reshape(2, 8, 2, 32, 1024),
        small_m,
        small_b,
        tokens,
        gres.reshape(2, 64, 1024),
        gain_attn,
    )
    mine = lax.dynamic_slice(small, (0, rank * 32), (4, 32))
    return (
        out.reshape(2, 64, 1024),
        gtok,
        gwqkv,
        gwo,
        gwg,
        gwu,
        gwd,
        mine[0],
        mine[1],
        mine[2],
        mine[3],
        small[4, :32].reshape(16, 2),
    )


def run_parts(mesh, body, split):
    rows, cut = P(split, None), P(split)
    part = P(None, split, None)
    return jax.shard_map(
        body,
        mesh=mesh,
        in_specs=(part, part) + (rows,) * 5 + (cut,) * 4 + (P(), P(), P(None, split), P(None, split)),
        out_specs=(part, part) + (rows,) * 5 + (cut,) * 4 + (P(),),
        check_vma=False,
    )


def solution(mesh):
    sizes = (mesh.shape["head"], mesh.shape["blk"])
    general = run_parts(mesh, on_device, ("head", "blk"))
    if sizes != (8, 4):
        return general
    cube = jax.sharding.Mesh(mesh.devices.reshape(2, 2, 2, 2, 2), AXES)
    special = run_parts(cube, on_device_cube, AXES)

    def chosen(*arrays):
        tokens, w_gate, var_bias, lengths = arrays[0], arrays[4], arrays[11], arrays[12]
        shapes = (tokens.shape, w_gate.shape, var_bias.shape, lengths.shape)
        if shapes == ((2, 2048, 1024), (1024, 4096), (16, 2), (2, 8)):
            return special(*arrays)
        return general(*arrays)

    return chosen
```

```python
import math
from types import SimpleNamespace

import jax
import jax.numpy as jnp
import numpy as np
from jax import lax
from jax.experimental import pallas as pl
from jax.experimental.pallas import tpu as pltpu
from jax.sharding import PartitionSpec as P

EPS = 1e-06
THETA = 10000.0
NEGATIVE = -1e30
KEY_BLOCK = 1024


def inverse_rms(values_in):
    return lax.rsqrt(jnp.mean(values_in * values_in, axis=-1, keepdims=True) + EPS)


def rotate(values_in, time_index, sign_value):
    half_dim = values_in.shape[-1] // 2
    frequency = THETA ** (-2.0 * jnp.arange(half_dim, dtype=jnp.float32) / values_in.shape[-1])
    angles = time_index.astype(jnp.float32)[:, None] * frequency[None, :]
    cosine = jnp.cos(angles)[:, None, :]
    sine_part = sign_value * jnp.sin(angles)[:, None, :]
    first_half = values_in[..., :half_dim]
    second_half = values_in[..., half_dim:]
    return jnp.concatenate(
        [
            first_half * cosine - second_half * sine_part,
            first_half * sine_part + second_half * cosine,
        ],
        axis=-1,
    )


def norm_back(grad_in, value_in, scale_in, gain_in):
    weighted = grad_in * gain_in
    scale_cube = scale_in * scale_in * scale_in
    return scale_in * weighted - value_in * scale_cube * jnp.mean(
        weighted * value_in, axis=-1, keepdims=True
    )


def row_contract(left_mat, right_mat):
    return lax.dot_general(
        left_mat, right_mat, (((0,), (0,)), ((), ())), preferred_element_type=jnp.float32
    )


def col_contract(left_mat, right_mat):
    return lax.dot_general(
        left_mat, right_mat, (((1,), (1,)), ((), ())), preferred_element_type=jnp.float32
    )


def document_of(positions, doc_ends):
    return jnp.sum((positions[:, None] >= doc_ends[None, :]).astype(jnp.int32), axis=1)


def key_positions(first_row, row_total, per_group, row_count, blk_n):
    row_index = first_row + jnp.arange(row_total, dtype=jnp.int32)
    source_blk = row_index // per_group
    within = row_index % per_group
    return (within // row_count * blk_n + source_blk) * row_count + within % row_count


def block_scores(queries, key_part, same_var, same_doc, bias_same, bias_other, att_scale):
    raw_scores = (
        jnp.einsum("qhd,khd->qhk", queries, key_part, preferred_element_type=jnp.float32)
        * att_scale
    )
    bias_terms = jnp.where(
        same_var[:, None, :], bias_same[None, :, None], bias_other[None, :, None]
    )
    return jnp.where(same_doc[:, None, :], raw_scores + bias_terms, NEGATIVE)


def forward_block(
    state_in, queries, key_part, value_part, same_var, same_doc, bias_same, bias_other, att_scale
):
    best_prev, total_prev, accum_prev = state_in
    scores = block_scores(queries, key_part, same_var, same_doc, bias_same, bias_other, att_scale)
    best_next = jnp.maximum(best_prev, jnp.max(scores, axis=-1))
    factor = jnp.exp(best_prev - best_next)
    weights = jnp.where(same_doc[:, None, :], jnp.exp(scores - best_next[..., None]), 0.0)
    total_next = total_prev * factor + jnp.sum(weights, axis=-1)
    accum_next = accum_prev * factor[..., None] + jnp.einsum(
        "qhk,khd->qhd", weights.astype(jnp.bfloat16), value_part, preferred_element_type=jnp.float32
    )
    return (best_next, total_next, accum_next)


def flatten_all(grads_in):
    return tuple((member.reshape(-1) for member in grads_in))


def unflatten_all(flat_in, grads_like):
    return tuple(
        (flat.reshape((-1,) + member.shape[1:]) for flat, member in zip(flat_in, grads_like))
    )


def on_device(
    tokens,
    cotangent,
    w_qkv,
    w_out,
    w_gate,
    w_up,
    w_down,
    norm_attn,
    norm_ffn,
    q_gain,
    k_gain,
    var_bias,
    doc_lengths,
    variate,
    times,
):
    heads_n = lax.axis_size("head")
    blk_n = lax.axis_size("blk")
    head_rank = lax.axis_index("head")
    blk_rank = lax.axis_index("blk")
    batch_count, row_count, model_width = tokens.shape
    head_count = var_bias.shape[0]
    head_dim = model_width // head_count
    local_heads = head_count // heads_n
    query_rows = heads_n * row_count
    key_rows = blk_n * query_rows
    key_block = min(KEY_BLOCK, key_rows)
    block_count = key_rows // key_block
    att_scale = 1.0 / math.sqrt(head_dim)
    gathered = (
        lax.all_gather(w_qkv, ("head", "blk"), axis=0, tiled=True),
        lax.all_gather(w_out, ("head", "blk"), axis=0, tiled=True),
        lax.all_gather(w_gate, ("head", "blk"), axis=0, tiled=True),
        lax.all_gather(w_up, ("head", "blk"), axis=0, tiled=True),
        lax.all_gather(w_down, ("head", "blk"), axis=0, tiled=True),
        lax.all_gather(norm_attn, ("head", "blk"), axis=0, tiled=True),
        lax.all_gather(norm_ffn, ("head", "blk"), axis=0, tiled=True),
        lax.all_gather(q_gain, ("head", "blk"), axis=0, tiled=True),
        lax.all_gather(k_gain, ("head", "blk"), axis=0, tiled=True),
    )
    wqkv_all, wout_all, wgate_all, wup_all, wdown_all = gathered[:5]
    gain_attn = gathered[5].astype(jnp.float32)
    gain_ffn = gathered[6].astype(jnp.float32)
    gain_query = gathered[7].astype(jnp.float32).reshape(head_count, head_dim)
    gain_key = gathered[8].astype(jnp.float32).reshape(head_count, head_dim)
    local_bias = lax.dynamic_slice_in_dim(var_bias, head_rank * local_heads, local_heads, 0)
    bias_same = local_bias[:, 0]
    bias_other = local_bias[:, 1]
    query_index = jnp.arange(query_rows, dtype=jnp.int32)
    query_pos = (query_index // row_count * blk_n + blk_rank) * row_count + query_index % row_count
    ends_all = jnp.cumsum(doc_lengths, axis=1)
    outputs_list = []
    inputs_list = []
    totals = None
    bias_accum = jnp.zeros((local_heads, 2), jnp.float32)
    for batch_id in range(batch_count):
        doc_ends = ends_all[batch_id]
        time_row = times[batch_id]
        inputs_f = tokens[batch_id].astype(jnp.float32)
        scale_one = inverse_rms(inputs_f)
        normed_one = (inputs_f * scale_one * gain_attn).astype(jnp.bfloat16)
        qkv_all = jnp.dot(normed_one, wqkv_all, preferred_element_type=jnp.float32).reshape(
            row_count, head_count, 3 * head_dim
        )
        query_raw = qkv_all[..., :head_dim]
        key_raw = qkv_all[..., head_dim : 2 * head_dim]
        value_raw = qkv_all[..., 2 * head_dim :]
        query_scale = inverse_rms(query_raw)
        key_scale = inverse_rms(key_raw)
        query_rot = rotate(query_raw * query_scale * gain_query, time_row, 1.0)
        key_rot = rotate(key_raw * key_scale * gain_key, time_row, 1.0)
        packed = jnp.concatenate([query_rot, key_rot, value_raw], axis=-1).astype(jnp.bfloat16)
        variate_rep = jnp.broadcast_to(
            variate[batch_id].astype(jnp.bfloat16)[:, None], (row_count, head_count)
        )
        packed_heads, variate_heads = (
            lax.all_to_all(packed, "head", split_axis=1, concat_axis=0, tiled=True),
            lax.all_to_all(variate_rep, "head", split_axis=1, concat_axis=0, tiled=True),
        )
        queries = packed_heads[..., :head_dim]
        key_values = packed_heads[..., head_dim:]
        query_var = variate_heads[:, 0]
        query_doc = document_of(query_pos, doc_ends)
        initial = (
            jnp.full((query_rows, local_heads), NEGATIVE, jnp.float32),
            jnp.zeros((query_rows, local_heads), jnp.float32),
            jnp.zeros((query_rows, local_heads, head_dim), jnp.float32),
        )
        kv_piece = lax.all_gather(key_values, "blk", axis=0, tiled=True)
        var_piece = lax.all_gather(query_var, "blk", axis=0, tiled=True)
        piece_rows = kv_piece.shape[0]

        def one_block(state_blk, kv_block, var_block, block_start):
            key_doc = document_of(
                key_positions(block_start, kv_block.shape[0], query_rows, row_count, blk_n),
                doc_ends,
            )
            same_doc = query_doc[:, None] == key_doc[None, :]
            same_var = query_var[:, None] == var_block[None, :]
            return forward_block(
                state_blk,
                queries,
                kv_block[..., :head_dim],
                kv_block[..., head_dim:],
                same_var,
                same_doc,
                bias_same,
                bias_other,
                att_scale,
            )

        def loop_step(turn_index, state_loop):
            kv_block = lax.dynamic_slice_in_dim(kv_piece, turn_index * key_block, key_block, 0)
            var_block = lax.dynamic_slice_in_dim(var_piece, turn_index * key_block, key_block, 0)
            return one_block(state_loop, kv_block, var_block, turn_index * key_block)

        attn_state = lax.fori_loop(0, piece_rows // key_block, loop_step, initial)
        best_score, total_weight, accum = attn_state
        attn_heads = accum / total_weight[..., None]
        log_total = best_score + jnp.log(total_weight)
        attn_tok = lax.all_to_all(
            attn_heads.astype(jnp.bfloat16), "head", split_axis=0, concat_axis=1, tiled=True
        ).reshape(row_count, model_width)
        resid_one = inputs_f + jnp.dot(attn_tok, wout_all, preferred_element_type=jnp.float32)
        scale_two = inverse_rms(resid_one)
        normed_two = (resid_one * scale_two * gain_ffn).astype(jnp.bfloat16)
        gate_pre = jnp.dot(normed_two, wgate_all, preferred_element_type=jnp.float32)
        up_pre = jnp.dot(normed_two, wup_all, preferred_element_type=jnp.float32)
        sigmoid_gate = jax.nn.sigmoid(gate_pre)
        silu_gate = gate_pre * sigmoid_gate
        hidden_act = (silu_gate * up_pre).astype(jnp.bfloat16)
        result = resid_one + jnp.dot(hidden_act, wdown_all, preferred_element_type=jnp.float32)
        outputs_list.append(result.astype(jnp.bfloat16))
        grad_out = cotangent[batch_id].astype(jnp.float32)
        grad_ffn = grad_out.astype(jnp.bfloat16)
        grad_down = row_contract(hidden_act, grad_ffn)
        grad_hidden = col_contract(grad_ffn, wdown_all)
        grad_gate = (
            grad_hidden * up_pre * sigmoid_gate * (1.0 + gate_pre * (1.0 - sigmoid_gate))
        ).astype(jnp.bfloat16)
        grad_up = (grad_hidden * silu_gate).astype(jnp.bfloat16)
        grad_wgate = row_contract(normed_two, grad_gate)
        grad_wup = row_contract(normed_two, grad_up)
        grad_normed = col_contract(grad_gate, wgate_all) + col_contract(grad_up, wup_all)
        grad_gffn = jnp.sum(grad_normed * resid_one * scale_two, axis=0)
        grad_resid = grad_out + norm_back(grad_normed, resid_one, scale_two, gain_ffn)
        grad_branch = grad_resid.astype(jnp.bfloat16)
        grad_wout = row_contract(attn_tok, grad_branch)
        grad_attn = (
            col_contract(grad_branch, wout_all)
            .astype(jnp.bfloat16)
            .reshape(row_count, head_count, head_dim)
        )
        grad_heads = lax.all_to_all(grad_attn, "head", split_axis=1, concat_axis=0, tiled=True)
        delta_row = jnp.sum(grad_heads.astype(jnp.float32) * attn_heads, axis=-1)
        keys_all, key_var_all = (
            lax.all_gather(key_values, "blk", axis=0, tiled=True),
            lax.all_gather(query_var, "blk", axis=0, tiled=True),
        )
        keys_blocks = keys_all.reshape(block_count, key_block, local_heads, 2 * head_dim)
        var_blocks = key_var_all.reshape(block_count, key_block)
        block_starts = jnp.arange(block_count, dtype=jnp.int32) * key_block

        def back_step(carry_back, block_in):
            grad_query, bias_grad = carry_back
            kv_block, var_block, block_start = block_in
            key_doc = document_of(
                key_positions(block_start, key_block, query_rows, row_count, blk_n), doc_ends
            )
            same_doc = query_doc[:, None] == key_doc[None, :]
            same_var = query_var[:, None] == var_block[None, :]
            key_part = kv_block[..., :head_dim]
            value_part = kv_block[..., head_dim:]
            scores = block_scores(
                queries, key_part, same_var, same_doc, bias_same, bias_other, att_scale
            )
            probs = jnp.where(same_doc[:, None, :], jnp.exp(scores - log_total[..., None]), 0.0)
            grad_probs = jnp.einsum(
                "qhd,khd->qhk", grad_heads, value_part, preferred_element_type=jnp.float32
            )
            grad_scores = (probs * (grad_probs - delta_row[..., None])).astype(jnp.bfloat16)
            grad_scores_f = grad_scores.astype(jnp.float32)
            same_sum = jnp.sum(jnp.where(same_var[:, None, :], grad_scores_f, 0.0), axis=(0, 2))
            other_sum = jnp.sum(jnp.where(same_var[:, None, :], 0.0, grad_scores_f), axis=(0, 2))
            bias_grad = bias_grad + jnp.stack([same_sum, other_sum], axis=-1)
            grad_query = grad_query + att_scale * jnp.einsum(
                "qhk,khd->qhd", grad_scores, key_part, preferred_element_type=jnp.float32
            )
            grad_key = att_scale * jnp.einsum(
                "qhk,qhd->khd", grad_scores, queries, preferred_element_type=jnp.float32
            )
            grad_value = jnp.einsum(
                "qhk,qhd->khd",
                probs.astype(jnp.bfloat16),
                grad_heads,
                preferred_element_type=jnp.float32,
            )
            return ((grad_query, bias_grad), jnp.concatenate([grad_key, grad_value], axis=-1))

        carry_start = (
            jnp.zeros((query_rows, local_heads, head_dim), jnp.float32),
            jnp.zeros((local_heads, 2), jnp.float32),
        )
        (grad_query, bias_part), grad_kv_parts = lax.scan(
            back_step, carry_start, (keys_blocks, var_blocks, block_starts)
        )
        bias_accum = bias_accum + bias_part
        grad_kv_own = lax.psum_scatter(
            grad_kv_parts.reshape(key_rows, local_heads, 2 * head_dim).astype(jnp.bfloat16),
            "blk",
            scatter_dimension=0,
            tiled=True,
        )
        grad_packed = jnp.concatenate([grad_query.astype(jnp.bfloat16), grad_kv_own], axis=-1)
        grad_tok = lax.all_to_all(
            grad_packed, "head", split_axis=0, concat_axis=1, tiled=True
        ).astype(jnp.float32)
        grad_qrot = rotate(grad_tok[..., :head_dim], time_row, -1.0)
        grad_krot = rotate(grad_tok[..., head_dim : 2 * head_dim], time_row, -1.0)
        grad_gquery = jnp.sum(grad_qrot * query_raw * query_scale, axis=0)
        grad_gkey = jnp.sum(grad_krot * key_raw * key_scale, axis=0)
        grad_qraw = norm_back(grad_qrot, query_raw, query_scale, gain_query)
        grad_kraw = norm_back(grad_krot, key_raw, key_scale, gain_key)
        grad_qkv = (
            jnp.concatenate([grad_qraw, grad_kraw, grad_tok[..., 2 * head_dim :]], axis=-1)
            .reshape(row_count, 3 * model_width)
            .astype(jnp.bfloat16)
        )
        grad_wqkv = row_contract(normed_one, grad_qkv)
        grad_normed_one = col_contract(grad_qkv, wqkv_all)
        grad_gattn = jnp.sum(grad_normed_one * inputs_f * scale_one, axis=0)
        grad_in = grad_resid + norm_back(grad_normed_one, inputs_f, scale_one, gain_attn)
        inputs_list.append(grad_in.astype(jnp.bfloat16))
        batch_grads = (
            grad_wqkv,
            grad_wout,
            grad_wgate,
            grad_wup,
            grad_down,
            grad_gattn,
            grad_gffn,
            grad_gquery.reshape(model_width),
            grad_gkey.reshape(model_width),
        )
        if totals is None:
            totals = batch_grads
        else:
            totals = tuple(
                (first_term + second_term for first_term, second_term in zip(totals, batch_grads))
            )
    flat_totals = flatten_all(totals)
    summed_flat = (
        lax.psum_scatter(flat_totals[0], ("head", "blk"), scatter_dimension=0, tiled=True),
        lax.psum_scatter(flat_totals[1], ("head", "blk"), scatter_dimension=0, tiled=True),
        lax.psum_scatter(flat_totals[2], ("head", "blk"), scatter_dimension=0, tiled=True),
        lax.psum_scatter(flat_totals[3], ("head", "blk"), scatter_dimension=0, tiled=True),
        lax.psum_scatter(flat_totals[4], ("head", "blk"), scatter_dimension=0, tiled=True),
        lax.psum_scatter(flat_totals[5], ("head", "blk"), scatter_dimension=0, tiled=True),
        lax.psum_scatter(flat_totals[6], ("head", "blk"), scatter_dimension=0, tiled=True),
        lax.psum_scatter(flat_totals[7], ("head", "blk"), scatter_dimension=0, tiled=True),
        lax.psum_scatter(flat_totals[8], ("head", "blk"), scatter_dimension=0, tiled=True),
    )
    totals = unflatten_all(summed_flat, totals)
    bias_full = lax.dynamic_update_slice_in_dim(
        jnp.zeros((head_count, 2), jnp.float32), bias_accum, head_rank * local_heads, 0
    )
    grad_bias = lax.psum(bias_full, ("head", "blk"))
    return (
        jnp.stack(outputs_list),
        jnp.stack(inputs_list),
        totals[0],
        totals[1],
        totals[2],
        totals[3],
        totals[4],
        totals[5],
        totals[6],
        totals[7],
        totals[8],
        grad_bias,
    )


AXES = ("zh", "zl", "x", "y", "c")
CHIPS = ("zl", "x", "y")
VMEM_BYTES = 62 * 2**20
ROW_BLOCK = 256
SPAN = 512
LAST = (((1,), (1,)), ((), ()))
FIRST = (((0,), (0,)), ((), ()))
CHIP_FLIPS = [
    tuple(a for a, bit in zip(CHIPS, ((m >> 2) & 1, (m >> 1) & 1, m & 1)) if bit)
    for m in range(1, 8)
]
GROUP_FLIPS = [("zl",), ("x",), ("zl", "x")]


class Net:
    def __init__(self, send_sems, recv_sems, local_sems):
        self.me = {name: lax.axis_index(name) for name in AXES}
        self.send_sems, self.recv_sems, self.local_sems = send_sems, recv_sems, local_sems
        self.used = 0
        self.local_used = 0
        self.open = []

    def target(self, flips):
        return tuple(1 - self.me[a] if a in flips else self.me[a] for a in AXES)

    def index(self, names, flips=()):
        total = 0
        for a in names:
            total = total * 2 + (1 - self.me[a] if a in flips else self.me[a])
        return total

    def barrier(self, partners):
        sem = pltpu.get_barrier_semaphore()
        for flips in partners:
            pl.semaphore_signal(
                sem, inc=1, device_id=self.target(flips), device_id_type=pl.DeviceIdType.MESH
            )
        pl.semaphore_wait(sem, len(partners))

    def send(self, source, dest, flips):
        copy = pltpu.make_async_remote_copy(
            src_ref=source,
            dst_ref=dest,
            send_sem=self.send_sems.at[self.used],
            recv_sem=self.recv_sems.at[self.used],
            device_id=self.target(flips),
            device_id_type=pl.DeviceIdType.MESH,
        )
        self.used += 1
        copy.start()
        self.open.append(copy)
        return copy

    def local(self, source, dest):
        copy = pltpu.make_async_copy(source, dest, self.local_sems.at[self.local_used])
        self.local_used += 1
        copy.start()
        return copy

    def drain(self):
        for copy in self.open:
            copy.wait_send()
        self.open = []


class Gather:
    def __init__(self, net, region, dims):
        self.net, self.region, self.dims = net, region, dims
        self.arrive = {}
        self.sibling = {}

    def key(self, flips):
        return tuple(sorted(flips))

    def push(self, flips, source=None):
        source = self.region(flips) if source is None else source
        level = max([self.dims.index(a) for a in flips], default=-1)
        for d in self.dims[level + 1 :]:
            copy = self.net.send(source, self.region(flips), (d,))
            self.arrive[self.key(flips + (d,))] = copy
        self.sibling[self.key(flips)] = self.net.send(source, self.region(flips), ("c",))

    def take(self, *flips):
        self.arrive[self.key(flips)].wait_recv()
        self.push(flips)

    def ready(self, *flips):
        self.sibling[self.key(flips)].wait_recv()


class Reduce:
    def __init__(self, net, dims, part, land, send, arrive):
        self.net, self.dims = net, dims
        self.part, self.land, self.send_slot, self.arrive = part, land, send, arrive
        self.from_sibling, self.incoming = {}, {}
        a, b, d = dims
        self.masks = [(a, b, d), (a, b), (a, d), (a,), (b, d), (b,), (d,), ()]
        self.slots = {}
        for rest in [(b, d), (b,), (d,), ()]:
            self.slots[rest, a] = len(self.slots)
        for rest in [(d,), ()]:
            self.slots[rest, b] = len(self.slots)
        self.slots[(), d] = len(self.slots)

    def ordered(self, flips):
        return tuple(a for a in self.dims if a in flips)

    def begin(self, flips):
        mask = self.ordered(flips)
        self.from_sibling[mask] = self.net.send(
            self.part(mask, 1 - self.net.me["c"]), self.land(self.masks.index(mask)), ("c",)
        )

    def total(self, mask, before):
        value = self.part(mask, self.net.me["c"])[...].astype(jnp.float32)
        value = value + self.land(self.masks.index(mask))[...].astype(jnp.float32)
        for stage in before:
            value = value + self.arrive(self.slots[mask, stage])[...].astype(jnp.float32)
        return value

    def settle(self, mask, before):
        self.from_sibling[mask].wait_recv()
        for stage in before:
            self.incoming[mask, stage].wait_recv()
        return self.total(mask, before)

    def forward(self, flips):
        mask = self.ordered(flips)
        stage, rest = mask[0], mask[1:]
        value = self.settle(mask, self.dims[: self.dims.index(stage)])
        slot = self.slots[rest, stage]
        self.send_slot(slot)[...] = value.astype(jnp.bfloat16)
        self.incoming[rest, stage] = self.net.send(
            self.send_slot(slot), self.arrive(slot), (stage,)
        )

    def result(self):
        return self.settle((), self.dims)


def lane_iota(rows, lanes=128):
    return lax.broadcasted_iota(jnp.int32, (rows, lanes), 1)


def pieces(value):
    first = value.astype(jnp.bfloat16).astype(jnp.float32)
    second = (value - first).astype(jnp.bfloat16).astype(jnp.float32)
    return first, second, value - first - second


def swap_halves(values):
    lane = lane_iota(values.shape[0])
    return jnp.where(lane % 64 < 32, pltpu.roll(values, 96, 1), pltpu.roll(values, 32, 1))


def pair_mean(values):
    lane = lane_iota(values.shape[0])
    low = jnp.sum(jnp.where(lane < 64, values, 0.0), axis=1, keepdims=True)
    high = jnp.sum(jnp.where(lane < 64, 0.0, values), axis=1, keepdims=True)
    return jnp.where(lane < 64, low, high) * (1.0 / 64.0)


def angles_of(packed):
    lane = lane_iota(packed.shape[0])
    turned = pltpu.roll(packed, 64, 1)
    return jnp.where(lane < 64, packed, turned), jnp.where(lane < 64, turned, packed)


def row_scale(value):
    return lax.rsqrt(jnp.mean(value * value, axis=1, keepdims=True) + EPS)


def layer_inputs():
    return ["lengths", "bias", "tok", "cot", "wqkv", "wout", "wgate", "wup", "wdown"] + [
        "gains", "variate", "times", "freq",
    ]


def layer_outputs():
    bf, f32 = jnp.bfloat16, jnp.float32
    return {
        "out": ((128, 1024), bf),
        "gtok": ((2, 64, 1024), bf),
        "gwqkv": ((32, 3072), f32),
        "gwout": ((32, 1024), f32),
        "gwgate": ((32, 4096), f32),
        "gwup": ((32, 4096), f32),
        "gwdown": ((128, 1024), f32),
        "gsmall": ((8, 8, 128), f32),
    }


def layer_scratch():
    bf, f32 = jnp.bfloat16, jnp.float32
    return {
        "x": ((32, 64, 1024), bf),
        "wp": ((8, 2, 32, 192), bf),
        "wl": ((8, 2, 32, 192), bf),
        "wh": ((2, 8, 2, 32, 192), bf),
        "gp": ((4, 2, 2, 32, 512), bf),
        "gl": ((4, 2, 2, 32, 512), bf),
        "wgu": ((2, 2, 4, 2, 2, 32, 512), bf),
        "wd": ((2, 2, 128, 1024), bf),
        "wo": ((2, 16, 32, 1024), bf),
        "gf": ((8, 2, 64, 1024), bf),
        "tile": ((8, 128), f32),
        "sm": ((2, 2, 2, 2, 2, 8, 128), f32),
        "gain_s": ((4, 8, 128), f32),
        "feat": ((2048, 128), f32),
        "cs": ((2048, 128), f32),
        "raw": ((2048, 128), f32),
        "kept_o": ((2048, 128), f32),
        "qf": ((2048, 128), bf),
        "kf": ((2048, 128), bf),
        "vf": ((2048, 128), bf),
        "att": ((16, 2, 64, 64), bf),
        "lb": ((16, 64, 64), bf),
        "ap": ((2, 8, 64, 128), bf),
        "at2": ((8, 2, 64, 128), bf),
        "at3": ((8, 64, 128), bf),
        "att_s": ((128, 1024), bf),
        "resid": ((128, 1024), f32),
        "n2": ((8, 2, 64, 1024), bf),
        "gh": ((4, 256, 512), f32),
        "hid": ((4, 256, 512), bf),
        "ggu": ((2, 4, 256, 512), bf),
        "kept": ((8, 128, 1024), f32),
        "sent": ((8, 2, 64, 1024), bf),
        "landed": ((8, 2, 64, 1024), bf),
        "red_send": ((2, 3, 128, 1024), bf),
        "red_land": ((2, 3, 128, 1024), bf),
        "ga3": ((2, 8, 64, 128), bf),
        "ga2": ((2, 8, 64, 128), bf),
        "ag1": ((2, 8, 64, 128), bf),
        "gatt": ((16, 2, 64, 64), bf),
        "gwgu": ((2, 2, 4, 2, 64, 512), bf),
        "gwd": ((2, 2, 128, 1024), bf),
        "gwo": ((2, 8, 2, 32, 1024), bf),
        "gb": ((2048, 128), bf),
        "gq": ((2048, 128), bf),
        "gw": ((2, 8, 2, 32, 192), bf),
        "bias_s": ((8, 128), f32),
        "sums": ((8, 1024), f32),
        "n_half": ((64, 1024), bf),
        "n_half_land": ((64, 1024), bf),
        "o_arr": ((7, 2, 32, 1024), bf),
        "o_half": ((32, 1024), bf),
        "o_half_land": ((32, 1024), bf),
        "y_wgu": ((2, 2, 4, 64, 512), bf),
        "y_wd": ((2, 128, 1024), bf),
        "h_wgu": ((2, 4, 64, 512), bf),
        "h_wd": ((128, 1024), bf),
        "h_wgu_land": ((2, 4, 64, 512), bf),
        "h_wd_land": ((128, 1024), bf),
        "f2": ((2, 4, 2, 32, 512), bf),
        "w_land": ((8, 2, 32, 192), bf),
        "w_t": ((8, 2, 32, 192), bf),
        "s_acc": ((5, 8, 8, 128), f32),
        "s_land": ((5, 8, 8, 128), f32),
    }


N_COPIES = 232


def layer_kernel(*refs):
    names = layer_inputs() + list(layer_outputs()) + list(layer_scratch())
    r = SimpleNamespace(**dict(zip(names, refs)))
    send_sems, recv_sems, local_sems = refs[len(names) :]
    bf, f32 = jnp.bfloat16, jnp.float32
    net = Net(send_sems, recv_sems, local_sems)
    zh, zl, x, y, c = (net.me[a] for a in AXES)
    mine, in_half = net.index(AXES), net.index(AXES[1:])
    my_chip, my_pair = net.index(CHIPS), net.index(("zl", "x"))
    head = in_half
    net.barrier(CHIP_FLIPS + [("c",), ("zh",)])

    def x_region(part):
        def region(flips):
            return r.x.at[(zh if part == 0 else 1 - zh) * 16 + net.index(AXES[1:], flips)]

        return region

    x_own = Gather(net, x_region(0), ("zl", "y", "x"))
    x_far = Gather(net, x_region(1), ("zl", "x", "y"))
    wo_tree = Gather(net, lambda f: r.wo.at[:, net.index(AXES[1:], f)], ("y", "zl", "x"))
    gf_tree = Gather(net, lambda f: r.gf.at[net.index(("zl", "x", "c"), f)], ("zl", "x"))
    swap = net.send(r.tok.at[1 - zh], r.x.at[mine], ("zh",))
    x_own.push((), r.tok.at[zh])
    r.tile[...] = jnp.zeros_like(r.tile)
    r.tile[0:2, 0:64] = r.variate[...].astype(f32)
    r.tile[2:4, 0:64] = r.times[...].astype(f32)
    r.tile[4:5, :] = r.gains[...]
    sm_step = net.send(r.tile, r.sm.at[zh, zl, x, y, c], ("zh",))
    for h in range(16):
        r.wp[h // 2, h % 2] = r.wqkv[:, 192 * h : 192 * (h + 1)]
    w_arrive = []
    for flips in CHIP_FLIPS:
        w_arrive.append(net.send(r.wp.at[net.index(CHIPS, flips)], r.wl.at[my_chip], flips))
    r.x[mine] = r.tok[zh]
    r.sm[zh, zl, x, y, c] = r.tile[...]
    r.wl[my_chip] = r.wp[my_chip]
    for pair in range(4):
        for cc in range(2):
            for part in range(4):
                idx = (part // 2) * 16 + pair * 4 + (part % 2) * 2 + cc
                col, lane = 128 * idx, 128 * part
                r.gp[pair, 0, cc, :, lane : lane + 128] = r.wgate[:, col : col + 128]
                r.gp[pair, 1, cc, :, lane : lane + 128] = r.wup[:, col : col + 128]
    g_arrive = []
    for flips in GROUP_FLIPS:
        g_arrive.append(
            net.send(r.gp.at[net.index(("zl", "x"), flips)], r.gl.at[my_pair], flips)
        )
    r.gl[my_pair] = r.gp[my_pair]
    r.gf[net.index(("zl", "x", "c"))] = r.cot[...]
    r.wd[zh, y] = r.wdown[...]
    r.wo[zh, in_half] = r.wout[...]
    wo_zh = net.send(r.wout, r.wo.at[zh, in_half], ("zh",))

    sm_step.wait_recv()
    sm_step = net.send(r.sm.at[:, zl, x, y, c], r.sm.at[:, zl, x, y, c], ("c",))
    x_own.take("zl")
    x_own.take("y")
    sm_step.wait_recv()
    sm_step = net.send(r.sm.at[:, zl, x, y], r.sm.at[:, zl, x, y], ("y",))
    for copy in w_arrive:
        copy.wait_recv()
    w_c = net.send(r.wl.at[:, 1 - c], r.wh.at[zh, :, c], ("c",))
    r.wh[zh, :, c] = r.wl[:, c]
    swap.wait_recv()
    x_far.push(())
    sm_step.wait_recv()
    sm_step = net.send(r.sm.at[:, zl, x], r.sm.at[:, zl, x], ("zl",))
    x_own.take("zl", "y")
    w_c.wait_recv()
    w_zh = net.send(r.wh.at[zh], r.wh.at[zh], ("zh",))
    x_far.take("zl")
    sm_step.wait_recv()
    sm_step = net.send(r.sm.at[:, :, x], r.sm.at[:, :, x], ("x",))
    for copy in g_arrive:
        copy.wait_recv()
    g_c = []
    for k in range(2):
        g_c.append(net.send(r.gl.at[:, k, 1 - c], r.wgu.at[k, zh, :, y, c], ("c",)))
        r.wgu[k, zh, :, y, c] = r.gl[:, k, c]
    x_own.take("x")
    x_own.take("zl", "x")
    x_far.take("x")
    x_far.take("zl", "x")

    def g_piece(k, half):
        return r.wgu.at[k // 2, half, pl.ds(2 * (k % 2), 2), y]

    g_zh, g_y, g_fwd = [], [], []
    for k in range(4):
        if k % 2 == 0:
            g_c[k // 2].wait_recv()
        g_zh.append(net.send(g_piece(k, zh), g_piece(k, zh), ("zh",)))
    wd_zh = net.send(r.wdown, r.wd.at[zh, y], ("zh",))
    x_own.take("y", "x")
    x_far.take("y")
    sm_step.wait_recv()

    lane8 = lane_iota(8)
    for group in range(8):
        for which in range(4):
            row = jnp.zeros((8, 128), f32)
            for j in range(4):
                block = 4 * group + j
                held = r.sm[
                    block // 16, (block // 8) % 2, (block // 4) % 2, (block // 2) % 2, block % 2
                ]
                moved = held if j == which else pltpu.roll(held, (32 * (j - which)) % 128, 1)
                row = jnp.where(lane8 // 32 == j, moved, row)
            r.gain_s[which, group : group + 1] = row[4:5, :]
    gain_attn = jnp.concatenate([r.gain_s[0, k : k + 1] for k in range(8)], axis=1)
    gain_ffn = jnp.concatenate([r.gain_s[1, k : k + 1] for k in range(8)], axis=1)
    held_q = r.gain_s[2, pl.ds(my_chip, 1)]
    held_k = r.gain_s[3, pl.ds(my_chip, 1)]
    wide_q, wide_k = jnp.broadcast_to(held_q, (8, 128)), jnp.broadcast_to(held_k, (8, 128))
    wide_q = jnp.where(c == 0, wide_q, pltpu.roll(wide_q, 64, 1))
    wide_k = jnp.where(c == 0, pltpu.roll(wide_k, 64, 1), wide_k)
    qk_gain = jnp.where(lane8 < 64, wide_q, wide_k)[0:1, :]

    starts, ends, total = [], [], jnp.int32(0)
    for j in range(8):
        starts.append(total)
        total = total + r.lengths[zh, j]
        ends.append(total)
    sub = lax.broadcasted_iota(jnp.int32, (8, 128), 0)
    start_col = jnp.zeros((8, 128), jnp.int32)
    end_col = jnp.zeros((8, 128), jnp.int32)
    for j in range(8):
        start_col = jnp.where(sub == j, starts[j], start_col)
        end_col = jnp.where(sub == j, ends[j], end_col)
    same_bias = jnp.full((8, 128), r.bias[head, 0], f32)
    other_bias = jnp.full((8, 128), r.bias[head, 1], f32)
    diff_parts = pieces(same_bias - other_bias)
    zero = jnp.zeros((8, 128), f32)
    const_q = jnp.where(sub == 0, -256.0, 0.0)
    for i, part in enumerate(pieces(other_bias)):
        const_q = jnp.where(sub == i + 1, part, const_q)
    const_k = jnp.where(sub < 4, 1.0, 0.0)
    ones_k = jnp.where(sub < 3, 1.0, 0.0)

    @pl.loop(0, 16)
    def _(i):
        col = pl.ds(pl.multiple_of(i * 128, 128), 128)
        low = r.sm[i // 8, (i // 4) % 2, (i // 2) % 2, i % 2, 0]
        high = r.sm[i // 8, (i // 4) % 2, (i // 2) % 2, i % 2, 1]
        both = jnp.where(lane8 < 64, low, pltpu.roll(high, 64, 1))
        var_row = jnp.where(zh == 0, both[0:1, :], both[1:2, :])
        time_row = jnp.where(zh == 0, both[2:3, :], both[3:4, :])
        pos = lane8 + i * 128
        doc = jnp.where((pos >= start_col) & (pos < end_col), 1.0, 0.0)
        var = jnp.where(jnp.broadcast_to(var_row, (8, 128)) == sub.astype(f32), 1.0, 0.0)
        rows = [doc * 256.0, const_q] + [var * part for part in diff_parts] + [zero, zero, zero]
        rows += [doc, const_k, var, var, var, ones_k, zero, zero]
        r.feat[col, :] = jnp.concatenate(rows, axis=0).T
        angle = jnp.broadcast_to(time_row, (32, 128)) * r.freq[...]
        cosine, sine = jnp.cos(angle), jnp.sin(angle)
        r.cs[col, :] = jnp.concatenate([cosine, cosine, -sine, sine], axis=0).T

    x_own.take("zl", "y", "x")
    x_far.take("zl", "y")
    x_far.take("x", "y")
    x_far.take("zl", "x", "y")
    for k in range(4):
        g_y.append(net.send(g_piece(k, zh), g_piece(k, zh), ("y",)))
    gf_tree.push((), r.cot)
    wd_y = net.send(r.wdown, r.wd.at[zh, y], ("y",))
    w_zh.wait_recv()

    lane = lane_iota(ROW_BLOCK)

    def rows_at(part, flips):
        z_part = zh if part == 0 else 1 - zh
        start = ((z_part * 2 + net.index(("zl",), flips)) * 2 + net.index(("x",), flips)) * ROW_BLOCK
        return pl.ds(pl.multiple_of(start, ROW_BLOCK), ROW_BLOCK), pl.ds(start // 64, 4)

    def project(part, flips):
        tree = x_own if part == 0 else x_far
        tree.ready(*flips)
        tree.ready(*(flips + ("y",)))
        row, blocks = rows_at(part, flips)
        value = r.x[blocks].reshape(ROW_BLOCK, 1024).astype(f32)
        normed = (value * row_scale(value) * gain_attn).astype(bf)
        qkv = jnp.dot(normed, r.wh[...].reshape(1024, 192), preferred_element_type=f32)
        raw = qkv[:, :128]
        r.raw[row, :] = raw
        scaled = raw * lax.rsqrt(pair_mean(raw * raw) + EPS) * qk_gain
        cosine, sine = angles_of(r.cs[row, :])
        turned = (scaled * cosine + swap_halves(scaled) * sine).astype(bf).astype(f32)
        marks = r.feat[row, :]
        r.qf[row, :] = jnp.where(lane < 64, turned * 0.125, pltpu.roll(marks, 64, 1)).astype(bf)
        r.kf[row, :] = jnp.where(lane < 64, pltpu.roll(turned, 64, 1), marks).astype(bf)
        third = jnp.concatenate([qkv[:, 128:192], jnp.zeros((ROW_BLOCK, 64), f32)], axis=1)
        r.vf[row, :] = jnp.where((lane >= 64) & (lane < 67), 1.0, third).astype(bf)

    project(0, ())
    project(0, ("zl",))
    wo_zh.wait_recv()
    wo_tree.push(())
    project(1, ())
    project(1, ("zl",))
    gf_tree.take("zl")
    project(0, ("x",))
    project(0, ("zl", "x"))
    wo_tree.take("y")
    project(1, ("x",))
    project(1, ("zl", "x"))
    wo_tree.take("zl")
    wo_tree.take("zl", "y")

    lane_span = lane_iota(SPAN)

    def attend(i):
        row = pl.ds(i * SPAN, SPAN)
        query = r.qf[row, :]

        def one_chunk(k, total):
            col = pl.ds(pl.multiple_of(k * SPAN, SPAN), SPAN)
            scores = lax.dot_general(query, r.kf[col, :], LAST, preferred_element_type=f32)
            weights = jnp.exp(scores).astype(bf)
            return total + jnp.dot(weights, r.vf[col, :], preferred_element_type=f32)

        total = lax.fori_loop(0, 2048 // SPAN, one_chunk, jnp.zeros((SPAN, 128), f32))
        weight = total[:, 64:65]
        result = total / weight
        r.kept_o[row, :] = jnp.where(lane_span < 64, result, jnp.log(weight))
        r.att[4 * i : 4 * i + 4] = result[:, :64].astype(bf).reshape(4, 2, 64, 64)

    def g_pass(k):
        g_zh[k].wait_recv()
        g_fwd.append(net.send(g_piece(k, 1 - zh), g_piece(k, 1 - zh), ("y",)))

    attend(0)
    gf_tree.take("x")
    gf_tree.take("zl", "x")
    g_pass(0)
    attend(1)
    wo_tree.take("x")
    wo_tree.take("y", "x")
    g_pass(1)
    attend(2)
    wo_tree.take("zl", "x")
    wo_tree.take("zl", "y", "x")
    g_pass(2)
    attend(3)

    step = net.send(r.att.at[:, 1 - c], r.lb, ("c",))
    g_pass(3)
    wd_zh.wait_recv()
    wd_fwd = net.send(r.wd.at[1 - zh, y], r.wd.at[1 - zh, y], ("y",))
    step.wait_recv()
    lane64 = lane_iota(64)

    @pl.loop(0, 16)
    def _(i):
        own = jnp.concatenate([r.att[i, c]] * 2, axis=1)
        other = jnp.concatenate([r.lb[i]] * 2, axis=1)
        r.ap[i // 8, i % 8] = jnp.where((lane64 < 64) == (c == 0), own, other)

    arrive = []
    for flips in CHIP_FLIPS:
        arrive.append(
            net.send(r.ap.at[:, net.index(CHIPS, flips)], r.at2.at[my_chip], flips)
        )
    r.at2[my_chip] = r.ap[:, my_chip]
    def w_down():
        return r.wd[...].reshape(512, 1024)

    def w_o():
        return r.wo[...].reshape(1024, 1024)

    def w_in(k):
        return r.wgu[k].reshape(1024, 512)

    gf_tree.ready()
    gf_tree.ready("zl")
    gf_tree.ready("x")
    gf_tree.ready("zl", "x")
    wd_y.wait_recv()
    wd_fwd.wait_recv()
    for p in range(2):
        rows = r.gf[2 * p : 2 * p + 2].reshape(256, 1024)
        r.gh[p] = lax.dot_general(rows, w_down(), LAST, preferred_element_type=f32)
    for copy in arrive:
        copy.wait_recv()
    step = net.send(r.at2.at[:, 1 - zh], r.at3, ("zh",))
    for p in range(2, 4):
        rows = r.gf[2 * p : 2 * p + 2].reshape(256, 1024)
        r.gh[p] = lax.dot_general(rows, w_down(), LAST, preferred_element_type=f32)
    for k in range(8):
        r.att_s[pl.ds(pl.multiple_of(zh * 64, 64), 64), 128 * k : 128 * (k + 1)] = r.at2[k, zh]
    for flips in [(), ("y",), ("zl",), ("zl", "y"), ("x",), ("y", "x"), ("zl", "x"), ("zl", "y", "x")]:
        wo_tree.ready(*flips)
    step.wait_recv()
    for k in range(8):
        r.att_s[pl.ds(pl.multiple_of(64 - zh * 64, 64), 64), 128 * k : 128 * (k + 1)] = r.at3[k]

    resid = r.tok[...].reshape(128, 1024).astype(f32)
    resid = resid + jnp.dot(r.att_s[...], w_o(), preferred_element_type=f32)
    scale = row_scale(resid)
    r.resid[...] = resid
    mine8 = 2 * my_pair + c
    r.n2[mine8] = (resid * scale * gain_ffn).astype(bf).reshape(2, 64, 1024)
    to_sibling = [net.send(r.n2.at[mine8], r.n2.at[mine8], ("c",))]
    from_chips = [net.send(r.n2.at[mine8], r.n2.at[mine8], flips) for flips in GROUP_FLIPS]
    for copy in g_y + g_fwd:
        copy.wait_recv()

    def pair_rows(ref, pair):
        return ref[pl.ds(2 * pair, 2)].reshape(256, 1024)

    def feed(pair):
        rows = pair_rows(r.n2, pair)
        gate = jnp.dot(rows, w_in(0), preferred_element_type=f32)
        up = jnp.dot(rows, w_in(1), preferred_element_type=f32)
        sig = 1.0 / (1.0 + jnp.exp(-gate))
        silu = gate * sig
        r.hid[pair] = (silu * up).astype(bf)
        back = r.gh[pair]
        r.ggu[0, pair] = (back * up * sig * (1.0 + gate * (1.0 - sig))).astype(bf)
        r.ggu[1, pair] = (back * silu).astype(bf)

    def back_product(pair):
        total = lax.dot_general(r.ggu[0, pair], w_in(0), LAST, preferred_element_type=f32)
        return total + lax.dot_general(r.ggu[1, pair], w_in(1), LAST, preferred_element_type=f32)

    def out_product(pair):
        return jnp.dot(r.hid[pair], w_down(), preferred_element_type=f32)

    halves, reduced = {}, {0: [], 1: []}

    def share(kind, slot, value):
        at = 4 * kind + slot
        r.kept[at] = jnp.where(c == 0, value[:128], value[128:])
        r.sent[at] = jnp.where(c == 0, value[128:], value[:128]).astype(bf).reshape(2, 64, 1024)
        halves[at] = net.send(r.sent.at[at], r.landed.at[at], ("c",))

    def finish_half(kind, slot):
        at = 4 * kind + slot
        halves[at].wait_recv()
        total = r.kept[at] + r.landed[at].reshape(128, 1024).astype(f32)
        if slot == 0:
            r.kept[at] = total
        else:
            r.red_send[kind, slot - 1] = total.astype(bf)
            reduced[kind].append(
                net.send(
                    r.red_send.at[kind, slot - 1],
                    r.red_land.at[kind, slot - 1],
                    GROUP_FLIPS[slot - 1],
                )
            )

    pairs = [my_pair] + [net.index(("zl", "x"), flips) for flips in GROUP_FLIPS]
    to_sibling[0].wait_recv()
    feed(pairs[0])
    for k in range(3):
        from_chips[k].wait_recv()
        to_sibling.append(
            net.send(r.n2.at[2 * pairs[k + 1] + c], r.n2.at[2 * pairs[k + 1] + c], ("c",))
        )
    for k in range(3):
        to_sibling[k + 1].wait_recv()
        feed(pairs[k + 1])
        share(0, k + 1, back_product(pairs[k + 1]))
        if k > 0:
            finish_half(0, k)
    finish_half(0, 3)
    share(0, 0, back_product(pairs[0]))
    for k in (1, 2, 3):
        share(1, k, out_product(pairs[k]))
        if k > 1:
            finish_half(1, k - 1)
    finish_half(0, 0)
    finish_half(1, 3)
    for k in range(2):
        r.gwgu[k] = (
            lax.dot_general(
                r.n2[...].reshape(1024, 1024),
                r.ggu[k].reshape(1024, 512),
                FIRST,
                preferred_element_type=f32,
            )
            .astype(bf)
            .reshape(2, 4, 2, 64, 512)
        )
    y_far = [net.send(r.gwgu.at[k, 1 - zh, :, 1 - y], r.y_wgu.at[k, 1], ("y",)) for k in range(2)]
    share(1, 0, out_product(pairs[0]))
    net.drain()

    for copy in reduced[0]:
        copy.wait_recv()
    total = r.kept[0]
    for k in range(3):
        total = total + r.red_land[0, k].astype(f32)
    resid = r.resid[...]
    scale = row_scale(resid)
    r.sums[...] = jnp.zeros_like(r.sums)
    r.sums[1:2, :] = jnp.sum(total * resid * scale, axis=0, keepdims=True)
    weighted = total * gain_ffn
    mean = jnp.mean(weighted * resid, axis=1, keepdims=True)
    grad_resid = r.cot[...].reshape(128, 1024).astype(f32) + scale * weighted
    grad_resid = grad_resid - resid * (scale * scale * scale) * mean
    r.kept[7] = grad_resid
    branch = grad_resid.astype(bf)
    grad_att = lax.dot_general(branch, w_o(), LAST, preferred_element_type=f32).astype(bf)
    for k in range(8):
        for b in range(2):
            r.ga3[b, k] = grad_att[64 * b : 64 * (b + 1), 128 * k : 128 * (k + 1)]
    step = net.send(r.ga3.at[1 - zh], r.ga2.at[zh], ("zh",))
    r.ga2[zh] = r.ga3[zh]
    finish_half(1, 0)
    r.gwo[...] = (
        lax.dot_general(r.att_s[...], branch, FIRST, preferred_element_type=f32)
        .astype(bf)
        .reshape(2, 8, 2, 32, 1024)
    )
    step.wait_recv()
    arrive = []
    for flips in CHIP_FLIPS:
        arrive.append(
            net.send(r.ga2.at[:, net.index(CHIPS, flips)], r.ag1.at[:, my_chip], flips)
        )
    r.ag1[:, my_chip] = r.ga2[:, my_chip]
    r.gwd[...] = (
        lax.dot_general(
            r.hid[...].reshape(1024, 512),
            r.gf[...].reshape(1024, 1024),
            FIRST,
            preferred_element_type=f32,
        )
        .astype(bf)
        .reshape(2, 2, 128, 1024)
    )
    y_far.append(net.send(r.gwd.at[1 - zh, 1 - y], r.y_wd.at[1], ("y",)))
    for copy in reduced[1]:
        copy.wait_recv()
    total = r.kept[4] + resid
    for k in range(3):
        total = total + r.red_land[1, k].astype(f32)
    r.out[...] = total.astype(bf)
    for copy in arrive:
        copy.wait_recv()

    @pl.loop(0, 16)
    def _(i):
        both = r.ag1[i // 8, i % 8]
        low, high = both[:, :64].astype(f32), both[:, 64:].astype(f32)
        r.lb[i] = jnp.where(c == 0, high, low).astype(bf)
        r.gatt[i, c] = jnp.where(c == 0, low, high).astype(bf)

    step = net.send(r.lb, r.gatt.at[:, c], ("c",))
    y_near = [net.send(r.gwgu.at[k, zh, :, 1 - y], r.y_wgu.at[k, 0], ("y",)) for k in range(2)]
    y_near.append(net.send(r.gwd.at[zh, 1 - y], r.y_wd.at[0], ("y",)))
    r.feat[...] = jnp.zeros_like(r.feat)
    r.bias_s[...] = jnp.zeros_like(r.bias_s)
    r.gh[...] = jnp.zeros_like(r.gh)
    step.wait_recv()

    @pl.loop(0, 4)
    def _(i):
        row = pl.ds(pl.multiple_of(i * SPAN, SPAN), SPAN)
        kept = r.kept_o[row, :]
        grad = r.gatt[pl.ds(i * 4, 4)].reshape(SPAN, 64).astype(f32)
        grad = jnp.concatenate([grad, jnp.zeros((SPAN, 64), f32)], axis=1)
        delta = jnp.sum(jnp.where(lane_span < 64, grad * kept, 0.0), axis=1, keepdims=True)
        query = r.qf[row, :].astype(f32)
        for j, part in enumerate(pieces(kept[:, 64:65])):
            query = jnp.where(lane_span == 64 + 40 + j, -part, query)
        r.qf[row, :] = query.astype(bf)
        for j, part in enumerate(pieces(delta)):
            grad = jnp.where(lane_span == 64 + j, -part, grad)
        r.gb[row, :] = grad.astype(bf)

    grad_k, grad_v = r.feat, r.kept_o
    grad_v[...] = jnp.zeros_like(grad_v)
    tree_o = Reduce(
        net,
        ("x", "zl", "y"),
        lambda mask, core: r.gwo.at[:, net.index(CHIPS, mask), core],
        lambda slot: r.wo.at[0, pl.ds(2 * slot, 2)],
        lambda slot: r.wo.at[1, pl.ds(2 * slot, 2)],
        lambda slot: r.o_arr.at[slot],
    )
    for mask in tree_o.masks:
        tree_o.begin(mask)

    def attend_back(i):
        row = pl.ds(i * SPAN, SPAN)
        query, grad = r.qf[row, :], r.gb[row, :]

        def one_chunk(k, total):
            col = pl.ds(pl.multiple_of(k * SPAN, SPAN), SPAN)
            key = r.kf[col, :]
            scores = lax.dot_general(query, key, LAST, preferred_element_type=f32)
            probs = jnp.exp(scores)
            centred = lax.dot_general(grad, r.vf[col, :], LAST, preferred_element_type=f32)
            back = (probs * centred).astype(bf)
            grad_v[col, :] += lax.dot_general(
                probs.astype(bf), grad, FIRST, preferred_element_type=f32
            )
            grad_k[col, :] += lax.dot_general(back, query, FIRST, preferred_element_type=f32)
            return total + jnp.dot(back, key, preferred_element_type=f32)

        total = lax.fori_loop(0, 2048 // SPAN, one_chunk, jnp.zeros((SPAN, 128), f32))
        r.gq[row, :] = (total * 0.125).astype(bf)
        marks = r.kf[row, :].astype(f32)
        same = jnp.where((lane_span >= 80) & (lane_span < 88), total * marks, 0.0)
        every = jnp.where(lane_span == 72, total, 0.0)
        r.bias_s[0:1, :] += jnp.sum(same, axis=0, keepdims=True)
        r.bias_s[1:2, :] += jnp.sum(every, axis=0, keepdims=True)

    h_steps = []

    def half_gate_up(k):
        y_far[k].wait_recv()
        r.h_wgu[k] = (r.gwgu[k, 1 - zh, :, y].astype(f32) + r.y_wgu[k, 1].astype(f32)).astype(bf)
        h_steps.append(net.send(r.h_wgu.at[k], r.h_wgu_land.at[k], ("zh",)))

    half_gate_up(0)
    attend_back(0)
    half_gate_up(1)
    for mask in tree_o.masks[:4]:
        tree_o.forward(mask)
    attend_back(1)
    y_far[2].wait_recv()
    r.h_wd[...] = (r.gwd[1 - zh, y].astype(f32) + r.y_wd[1].astype(f32)).astype(bf)
    h_steps.append(net.send(r.h_wd, r.h_wd_land, ("zh",)))
    attend_back(2)
    tree_o.forward(("zl", "y"))
    tree_o.forward(("zl",))
    attend_back(3)
    tree_o.forward(("y",))

    def token_tree(part, dims):
        return Reduce(
            net,
            dims,
            lambda mask, core: r.x.at[part * 16 + 2 * net.index(CHIPS, mask) + core],
            lambda slot: r.landed.at[slot, part],
            lambda slot: r.sent.at[slot, part],
            lambda slot: r.n2.at[slot, part],
        )

    trees = [token_tree(0, ("x", "zl", "y")), token_tree(1, ("y", "zl", "x"))]

    def project_back(part, flips):
        start = (part * 4 + net.index(("zl", "x"), flips)) * ROW_BLOCK
        row, blocks = pl.ds(pl.multiple_of(start, ROW_BLOCK), ROW_BLOCK), pl.ds(start // 64, 4)
        raw = r.raw[row, :]
        scale = lax.rsqrt(pair_mean(raw * raw) + EPS)
        cosine, sine = angles_of(r.cs[row, :])
        key_part = pltpu.roll(grad_k[row, :].astype(bf).astype(f32), 64, 1)
        grad = jnp.where(lane < 64, r.gq[row, :].astype(f32), key_part)
        turned = grad * cosine - swap_halves(grad) * sine
        r.bias_s[2:3, :] += jnp.sum(turned * raw * scale, axis=0, keepdims=True)
        weighted = turned * qk_gain
        back = scale * weighted - raw * (scale * scale * scale) * pair_mean(weighted * raw)
        grad_qkv = jnp.concatenate([back, grad_v[row, :][:, :64]], axis=1).astype(bf)
        grad_normed = lax.dot_general(
            grad_qkv, r.wh[...].reshape(1024, 192), LAST, preferred_element_type=f32
        )
        value = r.x[blocks].reshape(ROW_BLOCK, 1024).astype(f32)
        shaped = value * row_scale(value)
        r.sums[0:1, :] += jnp.sum(grad_normed * shaped, axis=0, keepdims=True)
        normed = (shaped * gain_attn).astype(bf)
        term = lax.dot_general(normed, grad_qkv, FIRST, preferred_element_type=f32)
        r.gh[:, :, :192] += term.reshape(4, 256, 192)
        r.x[blocks] = grad_normed.astype(bf).reshape(4, 64, 1024)
        trees[part].begin(flips)
        trees[part].begin(flips + ("y",))

    project_back(0, ("zl", "x"))
    project_back(1, ("zl", "x"))
    project_back(0, ("x",))
    trees[0].forward(("zl", "x", "y"))
    trees[0].forward(("zl", "x"))
    trees[1].forward(("zl", "x", "y"))
    project_back(1, ("x",))
    trees[0].forward(("x", "y"))
    trees[0].forward(("x",))
    trees[1].forward(("x", "y"))
    project_back(1, ("zl",))
    project_back(0, ("zl",))
    trees[1].forward(("zl", "y"))
    project_back(1, ())
    trees[1].forward(("y",))
    project_back(0, ())

    one = lane_iota(8)
    both = jnp.broadcast_to(r.bias_s[2:3, :], (8, 128))
    turned = pltpu.roll(both, 64, 1)
    wide = lane_iota(1, 1024)
    query_gain = jnp.concatenate([jnp.where(one < 64, both, turned)[0:1]] * 8, axis=1)
    key_gain = jnp.concatenate([jnp.where(one < 64, turned, both)[0:1]] * 8, axis=1)
    r.sums[2:3, :] = jnp.where(wide // 64 == head, query_gain, 0.0)
    r.sums[3:4, :] = jnp.where(wide // 64 == head, key_gain, 0.0)
    same = jnp.sum(r.bias_s[0:1, :], axis=1, keepdims=True)
    every = jnp.sum(r.bias_s[1:2, :], axis=1, keepdims=True)
    row_bias = jnp.where(wide == 2 * head, same, 0.0)
    r.sums[4:5, :] = jnp.where(wide == 2 * head + 1, every - same, row_bias)
    for k in range(8):
        r.s_acc[0, k] = r.sums[:, 128 * k : 128 * (k + 1)]
    rounds = ("c", "x", "y", "zl", "zh")
    s_step = net.send(r.s_acc.at[0], r.s_land.at[0], (rounds[0],))

    def small_round(step, k):
        step.wait_recv()
        total = r.s_acc[k] + r.s_land[k]
        if k == 4:
            r.gsmall[...] = total
            return None
        r.s_acc[k + 1] = total
        return net.send(r.s_acc.at[k + 1], r.s_land.at[k + 1], (rounds[k + 1],))

    r.gw[...] = r.gh[:, :, :192].astype(bf).reshape(2, 8, 2, 32, 192)
    w_zh = net.send(r.gw.at[1 - zh], r.w_land, ("zh",))
    trees[0].forward(("zl", "y"))
    trees[0].forward(("zl",))
    trees[1].forward(("zl", "x"))
    trees[1].forward(("zl",))
    s_step = small_round(s_step, 0)
    trees[0].forward(("y",))
    trees[1].forward(("x",))
    s_step = small_round(s_step, 1)
    w_zh.wait_recv()
    r.w_t[...] = (r.gw[zh].astype(f32) + r.w_land[...].astype(f32)).astype(bf)
    w_c = net.send(r.w_t.at[:, 1 - c], r.wp.at[:, c], ("c",))
    r.wp[:, c] = r.w_t[:, c]
    r.kept[1, :64] = trees[0].result()
    r.kept[2, :64] = trees[1].result()
    r.n_half[...] = r.kept[2 - zh, :64].astype(bf)
    n_step = net.send(r.n_half, r.n_half_land, ("zh",))
    s_step = small_round(s_step, 2)
    w_c.wait_recv()
    w_steps = []
    for flips in CHIP_FLIPS:
        w_steps.append(net.send(r.wp.at[net.index(CHIPS, flips)], r.wl.at[my_chip], flips))
    r.wl[my_chip] = r.wp[my_chip]
    total = tree_o.result()
    r.kept[3, :32] = total[0]
    r.kept[4, :32] = total[1]
    r.o_half[...] = r.kept[4 - zh, :32].astype(bf)
    o_step = net.send(r.o_half, r.o_half_land, ("zh",))
    s_step = small_round(s_step, 3)

    f_steps = []
    for k in range(2):
        y_near[k].wait_recv()
        h_steps[k].wait_recv()
        for j in range(4):
            rows = r.gwgu[k, zh, j, y].astype(f32) + r.y_wgu[k, 0, j].astype(f32)
            rows = rows + r.h_wgu_land[k, j].astype(f32)
            r.gp[j, k, 0] = rows[:32].astype(bf)
            r.gp[j, k, 1] = rows[32:].astype(bf)
        for flips in GROUP_FLIPS:
            f_steps.append(
                net.send(
                    r.gp.at[net.index(("zl", "x"), flips), k], r.gl.at[my_pair, k], flips
                )
            )
        r.gl[my_pair, k] = r.gp[my_pair, k]
    y_near[2].wait_recv()
    h_steps[2].wait_recv()
    r.gwdown[...] = r.gwd[zh, y].astype(f32) + r.y_wd[0].astype(f32) + r.h_wd_land[...].astype(f32)
    f_c = []
    for k in range(2):
        for j in range(3):
            f_steps[3 * k + j].wait_recv()
        f_c.append(net.send(r.gl.at[:, k, 1 - c], r.f2.at[k, :, c], ("c",)))
        r.f2[k, :, c] = r.gl[:, k, c]

    n_step.wait_recv()
    r.kept[2 - zh, :64] = r.n_half_land[...].astype(f32)
    for b in range(2):
        value = r.tok[b].astype(f32)
        scale = row_scale(value)
        weighted = r.kept[1 + b, :64] * gain_attn
        mean = jnp.mean(weighted * value, axis=1, keepdims=True)
        back = scale * weighted - value * (scale * scale * scale) * mean
        r.gtok[b] = (r.kept[7, 64 * b : 64 * (b + 1), :] + back).astype(bf)
    for copy in w_steps:
        copy.wait_recv()
    for h in range(16):
        r.gwqkv[:, 192 * h : 192 * (h + 1)] = r.wl[h // 2, h % 2].astype(f32)
    o_step.wait_recv()
    r.gwout[...] = r.kept[3 + zh, :32] + r.o_half_land[...].astype(f32)
    for k, out in ((0, r.gwgate), (1, r.gwup)):
        f_c[k].wait_recv()
        for pair in range(4):
            for cc in range(2):
                for part in range(4):
                    idx = (part // 2) * 16 + pair * 4 + (part % 2) * 2 + cc
                    out[:, 128 * idx : 128 * (idx + 1)] = r.f2[
                        k, pair, cc, :, 128 * part : 128 * (part + 1)
                    ].astype(f32)
    small_round(s_step, 4)
    net.drain()


def layer(*arrays):
    sm = pl.BlockSpec(memory_space=pltpu.SMEM)
    vm = pl.BlockSpec(memory_space=pltpu.VMEM)
    outs = layer_outputs()
    return pl.pallas_call(
        layer_kernel,
        out_shape=[jax.ShapeDtypeStruct(*spec) for spec in outs.values()],
        in_specs=[sm, sm] + [vm] * (len(layer_inputs()) - 2),
        out_specs=[vm] * len(outs),
        scratch_shapes=[pltpu.VMEM(*spec) for spec in layer_scratch().values()]
        + [
            pltpu.SemaphoreType.DMA((N_COPIES,)),
            pltpu.SemaphoreType.DMA((N_COPIES,)),
            pltpu.SemaphoreType.DMA((2,)),
        ],
        compiler_params=pltpu.CompilerParams(
            collective_id=1, has_side_effects=True, vmem_limit_bytes=VMEM_BYTES
        ),
        name="layer",
    )(*arrays)


def frequencies():
    index = np.arange(32, dtype=np.float32)
    return np.broadcast_to((THETA ** (-2.0 * index / 64.0)).astype(np.float32)[:, None], (32, 128))


def on_device_cube(
    tokens,
    cotangent,
    w_qkv,
    w_out,
    w_gate,
    w_up,
    w_down,
    norm_attn,
    norm_ffn,
    q_gain,
    k_gain,
    var_bias,
    doc_lengths,
    variate,
    times,
):
    rank = jnp.int32(0)
    for name in AXES:
        rank = rank * 2 + lax.axis_index(name)
    gains = jnp.concatenate([norm_attn, norm_ffn, q_gain, k_gain]).astype(jnp.float32)
    out, gtok, gwqkv, gwout, gwgate, gwup, gwdown, small = layer(
        doc_lengths, var_bias, tokens, cotangent, w_qkv, w_out, w_gate, w_up, w_down,
        gains.reshape(1, 128), variate, times, jnp.asarray(frequencies()),
    )
    tile = lax.dynamic_slice(small, (rank // 4, 0, (rank % 4) * 32), (1, 8, 32))[0]
    return (
        out.reshape(2, 64, 1024),
        gtok,
        gwqkv,
        gwout,
        gwgate,
        gwup,
        gwdown,
        tile[0],
        tile[1],
        tile[2],
        tile[3],
        small[0, 4, :32].reshape(16, 2),
    )


def run_parts(mesh, body, split):
    rows, cut = P(split, None), P(split)
    part = P(None, split, None)
    return jax.shard_map(
        body,
        mesh=mesh,
        in_specs=(part, part) + (rows,) * 5 + (cut,) * 4 + (P(), P(), P(None, split), P(None, split)),
        out_specs=(part, part) + (rows,) * 5 + (cut,) * 4 + (P(),),
        check_vma=False,
    )


def solution(mesh):
    sizes = (mesh.shape["head"], mesh.shape["blk"])
    general = run_parts(mesh, on_device, ("head", "blk"))
    if sizes != (8, 4):
        return general
    cube = jax.sharding.Mesh(mesh.devices.reshape(2, 2, 2, 2, 2), AXES)
    special = run_parts(cube, on_device_cube, AXES)

    def chosen(*arrays):
        tokens, w_gate, var_bias, lengths = arrays[0], arrays[4], arrays[11], arrays[12]
        shapes = (tokens.shape, w_gate.shape, var_bias.shape, lengths.shape)
        if shapes == ((2, 2048, 1024), (1024, 4096), (16, 2), (2, 8)):
            return special(*arrays)
        return general(*arrays)

    return chosen
```

```python
import math
from types import SimpleNamespace

import jax
import jax.numpy as jnp
import numpy as np
from jax import lax
from jax.experimental import pallas as pl
from jax.experimental.pallas import tpu as pltpu
from jax.sharding import PartitionSpec as P

EPS = 1e-06
THETA = 10000.0
NEGATIVE = -1e30
KEY_BLOCK = 1024


def inverse_rms(values_in):
    return lax.rsqrt(jnp.mean(values_in * values_in, axis=-1, keepdims=True) + EPS)


def rotate(values_in, time_index, sign_value):
    half_dim = values_in.shape[-1] // 2
    frequency = THETA ** (-2.0 * jnp.arange(half_dim, dtype=jnp.float32) / values_in.shape[-1])
    angles = time_index.astype(jnp.float32)[:, None] * frequency[None, :]
    cosine = jnp.cos(angles)[:, None, :]
    sine_part = sign_value * jnp.sin(angles)[:, None, :]
    first_half = values_in[..., :half_dim]
    second_half = values_in[..., half_dim:]
    return jnp.concatenate(
        [
            first_half * cosine - second_half * sine_part,
            first_half * sine_part + second_half * cosine,
        ],
        axis=-1,
    )


def norm_back(grad_in, value_in, scale_in, gain_in):
    weighted = grad_in * gain_in
    scale_cube = scale_in * scale_in * scale_in
    return scale_in * weighted - value_in * scale_cube * jnp.mean(
        weighted * value_in, axis=-1, keepdims=True
    )


def row_contract(left_mat, right_mat):
    return lax.dot_general(
        left_mat, right_mat, (((0,), (0,)), ((), ())), preferred_element_type=jnp.float32
    )


def col_contract(left_mat, right_mat):
    return lax.dot_general(
        left_mat, right_mat, (((1,), (1,)), ((), ())), preferred_element_type=jnp.float32
    )


def document_of(positions, doc_ends):
    return jnp.sum((positions[:, None] >= doc_ends[None, :]).astype(jnp.int32), axis=1)


def key_positions(first_row, row_total, per_group, row_count, blk_n):
    row_index = first_row + jnp.arange(row_total, dtype=jnp.int32)
    source_blk = row_index // per_group
    within = row_index % per_group
    return (within // row_count * blk_n + source_blk) * row_count + within % row_count


def block_scores(queries, key_part, same_var, same_doc, bias_same, bias_other, att_scale):
    raw_scores = (
        jnp.einsum("qhd,khd->qhk", queries, key_part, preferred_element_type=jnp.float32)
        * att_scale
    )
    bias_terms = jnp.where(
        same_var[:, None, :], bias_same[None, :, None], bias_other[None, :, None]
    )
    return jnp.where(same_doc[:, None, :], raw_scores + bias_terms, NEGATIVE)


def forward_block(
    state_in, queries, key_part, value_part, same_var, same_doc, bias_same, bias_other, att_scale
):
    best_prev, total_prev, accum_prev = state_in
    scores = block_scores(queries, key_part, same_var, same_doc, bias_same, bias_other, att_scale)
    best_next = jnp.maximum(best_prev, jnp.max(scores, axis=-1))
    factor = jnp.exp(best_prev - best_next)
    weights = jnp.where(same_doc[:, None, :], jnp.exp(scores - best_next[..., None]), 0.0)
    total_next = total_prev * factor + jnp.sum(weights, axis=-1)
    accum_next = accum_prev * factor[..., None] + jnp.einsum(
        "qhk,khd->qhd", weights.astype(jnp.bfloat16), value_part, preferred_element_type=jnp.float32
    )
    return (best_next, total_next, accum_next)


def flatten_all(grads_in):
    return tuple((member.reshape(-1) for member in grads_in))


def unflatten_all(flat_in, grads_like):
    return tuple(
        (flat.reshape((-1,) + member.shape[1:]) for flat, member in zip(flat_in, grads_like))
    )


def on_device(
    tokens,
    cotangent,
    w_qkv,
    w_out,
    w_gate,
    w_up,
    w_down,
    norm_attn,
    norm_ffn,
    q_gain,
    k_gain,
    var_bias,
    doc_lengths,
    variate,
    times,
):
    heads_n = lax.axis_size("head")
    blk_n = lax.axis_size("blk")
    head_rank = lax.axis_index("head")
    blk_rank = lax.axis_index("blk")
    batch_count, row_count, model_width = tokens.shape
    head_count = var_bias.shape[0]
    head_dim = model_width // head_count
    local_heads = head_count // heads_n
    query_rows = heads_n * row_count
    key_rows = blk_n * query_rows
    key_block = min(KEY_BLOCK, key_rows)
    block_count = key_rows // key_block
    att_scale = 1.0 / math.sqrt(head_dim)
    gathered = (
        lax.all_gather(w_qkv, ("head", "blk"), axis=0, tiled=True),
        lax.all_gather(w_out, ("head", "blk"), axis=0, tiled=True),
        lax.all_gather(w_gate, ("head", "blk"), axis=0, tiled=True),
        lax.all_gather(w_up, ("head", "blk"), axis=0, tiled=True),
        lax.all_gather(w_down, ("head", "blk"), axis=0, tiled=True),
        lax.all_gather(norm_attn, ("head", "blk"), axis=0, tiled=True),
        lax.all_gather(norm_ffn, ("head", "blk"), axis=0, tiled=True),
        lax.all_gather(q_gain, ("head", "blk"), axis=0, tiled=True),
        lax.all_gather(k_gain, ("head", "blk"), axis=0, tiled=True),
    )
    wqkv_all, wout_all, wgate_all, wup_all, wdown_all = gathered[:5]
    gain_attn = gathered[5].astype(jnp.float32)
    gain_ffn = gathered[6].astype(jnp.float32)
    gain_query = gathered[7].astype(jnp.float32).reshape(head_count, head_dim)
    gain_key = gathered[8].astype(jnp.float32).reshape(head_count, head_dim)
    local_bias = lax.dynamic_slice_in_dim(var_bias, head_rank * local_heads, local_heads, 0)
    bias_same = local_bias[:, 0]
    bias_other = local_bias[:, 1]
    query_index = jnp.arange(query_rows, dtype=jnp.int32)
    query_pos = (query_index // row_count * blk_n + blk_rank) * row_count + query_index % row_count
    ends_all = jnp.cumsum(doc_lengths, axis=1)
    outputs_list = []
    inputs_list = []
    totals = None
    bias_accum = jnp.zeros((local_heads, 2), jnp.float32)
    for batch_id in range(batch_count):
        doc_ends = ends_all[batch_id]
        time_row = times[batch_id]
        inputs_f = tokens[batch_id].astype(jnp.float32)
        scale_one = inverse_rms(inputs_f)
        normed_one = (inputs_f * scale_one * gain_attn).astype(jnp.bfloat16)
        qkv_all = jnp.dot(normed_one, wqkv_all, preferred_element_type=jnp.float32).reshape(
            row_count, head_count, 3 * head_dim
        )
        query_raw = qkv_all[..., :head_dim]
        key_raw = qkv_all[..., head_dim : 2 * head_dim]
        value_raw = qkv_all[..., 2 * head_dim :]
        query_scale = inverse_rms(query_raw)
        key_scale = inverse_rms(key_raw)
        query_rot = rotate(query_raw * query_scale * gain_query, time_row, 1.0)
        key_rot = rotate(key_raw * key_scale * gain_key, time_row, 1.0)
        packed = jnp.concatenate([query_rot, key_rot, value_raw], axis=-1).astype(jnp.bfloat16)
        variate_rep = jnp.broadcast_to(
            variate[batch_id].astype(jnp.bfloat16)[:, None], (row_count, head_count)
        )
        packed_heads, variate_heads = (
            lax.all_to_all(packed, "head", split_axis=1, concat_axis=0, tiled=True),
            lax.all_to_all(variate_rep, "head", split_axis=1, concat_axis=0, tiled=True),
        )
        queries = packed_heads[..., :head_dim]
        key_values = packed_heads[..., head_dim:]
        query_var = variate_heads[:, 0]
        query_doc = document_of(query_pos, doc_ends)
        initial = (
            jnp.full((query_rows, local_heads), NEGATIVE, jnp.float32),
            jnp.zeros((query_rows, local_heads), jnp.float32),
            jnp.zeros((query_rows, local_heads, head_dim), jnp.float32),
        )
        kv_piece = lax.all_gather(key_values, "blk", axis=0, tiled=True)
        var_piece = lax.all_gather(query_var, "blk", axis=0, tiled=True)
        piece_rows = kv_piece.shape[0]

        def one_block(state_blk, kv_block, var_block, block_start):
            key_doc = document_of(
                key_positions(block_start, kv_block.shape[0], query_rows, row_count, blk_n),
                doc_ends,
            )
            same_doc = query_doc[:, None] == key_doc[None, :]
            same_var = query_var[:, None] == var_block[None, :]
            return forward_block(
                state_blk,
                queries,
                kv_block[..., :head_dim],
                kv_block[..., head_dim:],
                same_var,
                same_doc,
                bias_same,
                bias_other,
                att_scale,
            )

        def loop_step(turn_index, state_loop):
            kv_block = lax.dynamic_slice_in_dim(kv_piece, turn_index * key_block, key_block, 0)
            var_block = lax.dynamic_slice_in_dim(var_piece, turn_index * key_block, key_block, 0)
            return one_block(state_loop, kv_block, var_block, turn_index * key_block)

        attn_state = lax.fori_loop(0, piece_rows // key_block, loop_step, initial)
        best_score, total_weight, accum = attn_state
        attn_heads = accum / total_weight[..., None]
        log_total = best_score + jnp.log(total_weight)
        attn_tok = lax.all_to_all(
            attn_heads.astype(jnp.bfloat16), "head", split_axis=0, concat_axis=1, tiled=True
        ).reshape(row_count, model_width)
        resid_one = inputs_f + jnp.dot(attn_tok, wout_all, preferred_element_type=jnp.float32)
        scale_two = inverse_rms(resid_one)
        normed_two = (resid_one * scale_two * gain_ffn).astype(jnp.bfloat16)
        gate_pre = jnp.dot(normed_two, wgate_all, preferred_element_type=jnp.float32)
        up_pre = jnp.dot(normed_two, wup_all, preferred_element_type=jnp.float32)
        sigmoid_gate = jax.nn.sigmoid(gate_pre)
        silu_gate = gate_pre * sigmoid_gate
        hidden_act = (silu_gate * up_pre).astype(jnp.bfloat16)
        result = resid_one + jnp.dot(hidden_act, wdown_all, preferred_element_type=jnp.float32)
        outputs_list.append(result.astype(jnp.bfloat16))
        grad_out = cotangent[batch_id].astype(jnp.float32)
        grad_ffn = grad_out.astype(jnp.bfloat16)
        grad_down = row_contract(hidden_act, grad_ffn)
        grad_hidden = col_contract(grad_ffn, wdown_all)
        grad_gate = (
            grad_hidden * up_pre * sigmoid_gate * (1.0 + gate_pre * (1.0 - sigmoid_gate))
        ).astype(jnp.bfloat16)
        grad_up = (grad_hidden * silu_gate).astype(jnp.bfloat16)
        grad_wgate = row_contract(normed_two, grad_gate)
        grad_wup = row_contract(normed_two, grad_up)
        grad_normed = col_contract(grad_gate, wgate_all) + col_contract(grad_up, wup_all)
        grad_gffn = jnp.sum(grad_normed * resid_one * scale_two, axis=0)
        grad_resid = grad_out + norm_back(grad_normed, resid_one, scale_two, gain_ffn)
        grad_branch = grad_resid.astype(jnp.bfloat16)
        grad_wout = row_contract(attn_tok, grad_branch)
        grad_attn = (
            col_contract(grad_branch, wout_all)
            .astype(jnp.bfloat16)
            .reshape(row_count, head_count, head_dim)
        )
        grad_heads = lax.all_to_all(grad_attn, "head", split_axis=1, concat_axis=0, tiled=True)
        delta_row = jnp.sum(grad_heads.astype(jnp.float32) * attn_heads, axis=-1)
        keys_all, key_var_all = (
            lax.all_gather(key_values, "blk", axis=0, tiled=True),
            lax.all_gather(query_var, "blk", axis=0, tiled=True),
        )
        keys_blocks = keys_all.reshape(block_count, key_block, local_heads, 2 * head_dim)
        var_blocks = key_var_all.reshape(block_count, key_block)
        block_starts = jnp.arange(block_count, dtype=jnp.int32) * key_block

        def back_step(carry_back, block_in):
            grad_query, bias_grad = carry_back
            kv_block, var_block, block_start = block_in
            key_doc = document_of(
                key_positions(block_start, key_block, query_rows, row_count, blk_n), doc_ends
            )
            same_doc = query_doc[:, None] == key_doc[None, :]
            same_var = query_var[:, None] == var_block[None, :]
            key_part = kv_block[..., :head_dim]
            value_part = kv_block[..., head_dim:]
            scores = block_scores(
                queries, key_part, same_var, same_doc, bias_same, bias_other, att_scale
            )
            probs = jnp.where(same_doc[:, None, :], jnp.exp(scores - log_total[..., None]), 0.0)
            grad_probs = jnp.einsum(
                "qhd,khd->qhk", grad_heads, value_part, preferred_element_type=jnp.float32
            )
            grad_scores = (probs * (grad_probs - delta_row[..., None])).astype(jnp.bfloat16)
            grad_scores_f = grad_scores.astype(jnp.float32)
            same_sum = jnp.sum(jnp.where(same_var[:, None, :], grad_scores_f, 0.0), axis=(0, 2))
            other_sum = jnp.sum(jnp.where(same_var[:, None, :], 0.0, grad_scores_f), axis=(0, 2))
            bias_grad = bias_grad + jnp.stack([same_sum, other_sum], axis=-1)
            grad_query = grad_query + att_scale * jnp.einsum(
                "qhk,khd->qhd", grad_scores, key_part, preferred_element_type=jnp.float32
            )
            grad_key = att_scale * jnp.einsum(
                "qhk,qhd->khd", grad_scores, queries, preferred_element_type=jnp.float32
            )
            grad_value = jnp.einsum(
                "qhk,qhd->khd",
                probs.astype(jnp.bfloat16),
                grad_heads,
                preferred_element_type=jnp.float32,
            )
            return ((grad_query, bias_grad), jnp.concatenate([grad_key, grad_value], axis=-1))

        carry_start = (
            jnp.zeros((query_rows, local_heads, head_dim), jnp.float32),
            jnp.zeros((local_heads, 2), jnp.float32),
        )
        (grad_query, bias_part), grad_kv_parts = lax.scan(
            back_step, carry_start, (keys_blocks, var_blocks, block_starts)
        )
        bias_accum = bias_accum + bias_part
        grad_kv_own = lax.psum_scatter(
            grad_kv_parts.reshape(key_rows, local_heads, 2 * head_dim).astype(jnp.bfloat16),
            "blk",
            scatter_dimension=0,
            tiled=True,
        )
        grad_packed = jnp.concatenate([grad_query.astype(jnp.bfloat16), grad_kv_own], axis=-1)
        grad_tok = lax.all_to_all(
            grad_packed, "head", split_axis=0, concat_axis=1, tiled=True
        ).astype(jnp.float32)
        grad_qrot = rotate(grad_tok[..., :head_dim], time_row, -1.0)
        grad_krot = rotate(grad_tok[..., head_dim : 2 * head_dim], time_row, -1.0)
        grad_gquery = jnp.sum(grad_qrot * query_raw * query_scale, axis=0)
        grad_gkey = jnp.sum(grad_krot * key_raw * key_scale, axis=0)
        grad_qraw = norm_back(grad_qrot, query_raw, query_scale, gain_query)
        grad_kraw = norm_back(grad_krot, key_raw, key_scale, gain_key)
        grad_qkv = (
            jnp.concatenate([grad_qraw, grad_kraw, grad_tok[..., 2 * head_dim :]], axis=-1)
            .reshape(row_count, 3 * model_width)
            .astype(jnp.bfloat16)
        )
        grad_wqkv = row_contract(normed_one, grad_qkv)
        grad_normed_one = col_contract(grad_qkv, wqkv_all)
        grad_gattn = jnp.sum(grad_normed_one * inputs_f * scale_one, axis=0)
        grad_in = grad_resid + norm_back(grad_normed_one, inputs_f, scale_one, gain_attn)
        inputs_list.append(grad_in.astype(jnp.bfloat16))
        batch_grads = (
            grad_wqkv,
            grad_wout,
            grad_wgate,
            grad_wup,
            grad_down,
            grad_gattn,
            grad_gffn,
            grad_gquery.reshape(model_width),
            grad_gkey.reshape(model_width),
        )
        if totals is None:
            totals = batch_grads
        else:
            totals = tuple(
                (first_term + second_term for first_term, second_term in zip(totals, batch_grads))
            )
    flat_totals = flatten_all(totals)
    summed_flat = (
        lax.psum_scatter(flat_totals[0], ("head", "blk"), scatter_dimension=0, tiled=True),
        lax.psum_scatter(flat_totals[1], ("head", "blk"), scatter_dimension=0, tiled=True),
        lax.psum_scatter(flat_totals[2], ("head", "blk"), scatter_dimension=0, tiled=True),
        lax.psum_scatter(flat_totals[3], ("head", "blk"), scatter_dimension=0, tiled=True),
        lax.psum_scatter(flat_totals[4], ("head", "blk"), scatter_dimension=0, tiled=True),
        lax.psum_scatter(flat_totals[5], ("head", "blk"), scatter_dimension=0, tiled=True),
        lax.psum_scatter(flat_totals[6], ("head", "blk"), scatter_dimension=0, tiled=True),
        lax.psum_scatter(flat_totals[7], ("head", "blk"), scatter_dimension=0, tiled=True),
        lax.psum_scatter(flat_totals[8], ("head", "blk"), scatter_dimension=0, tiled=True),
    )
    totals = unflatten_all(summed_flat, totals)
    bias_full = lax.dynamic_update_slice_in_dim(
        jnp.zeros((head_count, 2), jnp.float32), bias_accum, head_rank * local_heads, 0
    )
    grad_bias = lax.psum(bias_full, ("head", "blk"))
    return (
        jnp.stack(outputs_list),
        jnp.stack(inputs_list),
        totals[0],
        totals[1],
        totals[2],
        totals[3],
        totals[4],
        totals[5],
        totals[6],
        totals[7],
        totals[8],
        grad_bias,
    )


AXES = ("zh", "zl", "x", "y", "c")
CHIPS = ("zl", "x", "y")
VMEM_BYTES = 62 * 2**20
ROW_BLOCK = 256
SPAN = 512
LAST = (((1,), (1,)), ((), ()))
FIRST = (((0,), (0,)), ((), ()))
CHIP_FLIPS = [
    tuple(a for a, bit in zip(CHIPS, ((m >> 2) & 1, (m >> 1) & 1, m & 1)) if bit)
    for m in range(1, 8)
]
GROUP_FLIPS = [("zl",), ("x",), ("zl", "x")]


class Net:
    def __init__(self, send_sems, recv_sems, local_sems):
        self.me = {name: lax.axis_index(name) for name in AXES}
        self.send_sems, self.recv_sems, self.local_sems = send_sems, recv_sems, local_sems
        self.used = 0
        self.local_used = 0
        self.open = []

    def target(self, flips):
        return tuple(1 - self.me[a] if a in flips else self.me[a] for a in AXES)

    def index(self, names, flips=()):
        total = 0
        for a in names:
            total = total * 2 + (1 - self.me[a] if a in flips else self.me[a])
        return total

    def barrier(self, partners):
        sem = pltpu.get_barrier_semaphore()
        for flips in partners:
            pl.semaphore_signal(
                sem, inc=1, device_id=self.target(flips), device_id_type=pl.DeviceIdType.MESH
            )
        pl.semaphore_wait(sem, len(partners))

    def send(self, source, dest, flips):
        copy = pltpu.make_async_remote_copy(
            src_ref=source,
            dst_ref=dest,
            send_sem=self.send_sems.at[self.used],
            recv_sem=self.recv_sems.at[self.used],
            device_id=self.target(flips),
            device_id_type=pl.DeviceIdType.MESH,
        )
        self.used += 1
        copy.start()
        self.open.append(copy)
        return copy

    def local(self, source, dest):
        copy = pltpu.make_async_copy(source, dest, self.local_sems.at[self.local_used])
        self.local_used += 1
        copy.start()
        return copy

    def settle(self, copies):
        for copy in copies:
            copy.wait_send()
        gone = [id(copy) for copy in copies]
        self.open = [copy for copy in self.open if id(copy) not in gone]

    def drain(self):
        for copy in self.open:
            copy.wait_send()
        self.open = []


class Gather:
    def __init__(self, net, region, dims):
        self.net, self.region, self.dims = net, region, dims
        self.arrive = {}
        self.sibling = {}

    def key(self, flips):
        return tuple(sorted(flips))

    def push(self, flips, source=None):
        source = self.region(flips) if source is None else source
        level = max([self.dims.index(a) for a in flips], default=-1)
        for d in self.dims[level + 1 :]:
            copy = self.net.send(source, self.region(flips), (d,))
            self.arrive[self.key(flips + (d,))] = copy
        self.sibling[self.key(flips)] = self.net.send(source, self.region(flips), ("c",))

    def take(self, *flips):
        self.arrive[self.key(flips)].wait_recv()
        self.push(flips)

    def ready(self, *flips):
        self.sibling[self.key(flips)].wait_recv()


class Reduce:
    def __init__(self, net, dims, part, land, send, arrive):
        self.net, self.dims = net, dims
        self.part, self.land, self.send_slot, self.arrive = part, land, send, arrive
        self.from_sibling, self.incoming = {}, {}
        a, b, d = dims
        self.masks = [(a, b, d), (a, b), (a, d), (a,), (b, d), (b,), (d,), ()]
        self.slots = {}
        for rest in [(b, d), (b,), (d,), ()]:
            self.slots[rest, a] = len(self.slots)
        for rest in [(d,), ()]:
            self.slots[rest, b] = len(self.slots)
        self.slots[(), d] = len(self.slots)

    def ordered(self, flips):
        return tuple(a for a in self.dims if a in flips)

    def begin(self, flips):
        mask = self.ordered(flips)
        self.from_sibling[mask] = self.net.send(
            self.part(mask, 1 - self.net.me["c"]), self.land(self.masks.index(mask)), ("c",)
        )

    def total(self, mask, before):
        value = self.part(mask, self.net.me["c"])[...].astype(jnp.float32)
        value = value + self.land(self.masks.index(mask))[...].astype(jnp.float32)
        for stage in before:
            value = value + self.arrive(self.slots[mask, stage])[...].astype(jnp.float32)
        return value

    def settle(self, mask, before):
        self.from_sibling[mask].wait_recv()
        for stage in before:
            self.incoming[mask, stage].wait_recv()
        return self.total(mask, before)

    def forward(self, flips):
        mask = self.ordered(flips)
        stage, rest = mask[0], mask[1:]
        value = self.settle(mask, self.dims[: self.dims.index(stage)])
        slot = self.slots[rest, stage]
        self.send_slot(slot)[...] = value.astype(jnp.bfloat16)
        self.incoming[rest, stage] = self.net.send(
            self.send_slot(slot), self.arrive(slot), (stage,)
        )

    def result(self):
        return self.settle((), self.dims)


def lane_iota(rows, lanes=128):
    return lax.broadcasted_iota(jnp.int32, (rows, lanes), 1)


def pieces(value):
    first = value.astype(jnp.bfloat16).astype(jnp.float32)
    second = (value - first).astype(jnp.bfloat16).astype(jnp.float32)
    return first, second, value - first - second


def swap_halves(values):
    lane = lane_iota(values.shape[0])
    return jnp.where(lane % 64 < 32, pltpu.roll(values, 96, 1), pltpu.roll(values, 32, 1))


def pair_mean(values):
    lane = lane_iota(values.shape[0])
    low = jnp.sum(jnp.where(lane < 64, values, 0.0), axis=1, keepdims=True)
    high = jnp.sum(jnp.where(lane < 64, 0.0, values), axis=1, keepdims=True)
    return jnp.where(lane < 64, low, high) * (1.0 / 64.0)


def angles_of(packed):
    lane = lane_iota(packed.shape[0])
    turned = pltpu.roll(packed, 64, 1)
    return jnp.where(lane < 64, packed, turned), jnp.where(lane < 64, turned, packed)


def row_scale(value):
    return lax.rsqrt(jnp.mean(value * value, axis=1, keepdims=True) + EPS)


def layer_inputs():
    return ["lengths", "bias", "tok", "cot", "wqkv", "wout", "wgate", "wup", "wdown"] + [
        "norm_attn", "norm_ffn", "q_gain", "k_gain", "variate", "times", "freq",
    ]


def layer_outputs():
    bf, f32 = jnp.bfloat16, jnp.float32
    return {
        "out": ((128, 1024), bf),
        "gtok": ((2, 64, 1024), bf),
        "gwqkv": ((32, 3072), f32),
        "gwout": ((32, 1024), f32),
        "gwgate": ((32, 4096), f32),
        "gwup": ((32, 4096), f32),
        "gwdown": ((128, 1024), f32),
        "gsmall": ((8, 8, 128), f32),
    }


def layer_scratch():
    bf, f32 = jnp.bfloat16, jnp.float32
    return {
        "x": ((32, 64, 1024), bf),
        "wp": ((8, 2, 32, 192), bf),
        "wl": ((8, 2, 32, 192), bf),
        "wh": ((2, 8, 2, 32, 192), bf),
        "gp": ((4, 2, 2, 32, 512), bf),
        "gl": ((4, 2, 2, 32, 512), bf),
        "wgu": ((2, 2, 4, 2, 2, 32, 512), bf),
        "wd": ((2, 2, 128, 1024), bf),
        "wo": ((2, 16, 32, 1024), bf),
        "gf": ((8, 2, 64, 1024), bf),
        "tile": ((8, 128), f32),
        "sm": ((2, 2, 2, 2, 2, 8, 128), f32),
        "gain_s": ((4, 8, 128), f32),
        "feat": ((2048, 128), f32),
        "cs": ((2048, 128), f32),
        "raw": ((2048, 128), f32),
        "kept_o": ((2048, 128), f32),
        "qf": ((2048, 128), bf),
        "kf": ((2048, 128), bf),
        "vf": ((2048, 128), bf),
        "att": ((16, 2, 64, 64), bf),
        "lb": ((16, 64, 64), bf),
        "ap": ((2, 8, 64, 128), bf),
        "at2": ((8, 2, 64, 128), bf),
        "at3": ((8, 64, 128), bf),
        "att_s": ((128, 1024), bf),
        "resid": ((128, 1024), f32),
        "n2": ((8, 2, 64, 1024), bf),
        "gate": ((4, 256, 512), f32),
        "up": ((4, 256, 512), f32),
        "hid": ((4, 256, 512), bf),
        "ggu": ((2, 4, 256, 512), bf),
        "kept": ((8, 128, 1024), f32),
        "sent": ((8, 2, 64, 1024), bf),
        "landed": ((8, 2, 64, 1024), bf),
        "red_send": ((2, 3, 128, 1024), bf),
        "red_land": ((2, 3, 128, 1024), bf),
        "branch": ((128, 1024), bf),
        "ga3": ((2, 8, 64, 128), bf),
        "ga2": ((2, 8, 64, 128), bf),
        "ag1": ((2, 8, 64, 128), bf),
        "gatt": ((16, 2, 64, 64), bf),
        "gwgu": ((2, 2, 4, 2, 64, 512), bf),
        "gwd": ((2, 2, 128, 1024), bf),
        "gwo": ((2, 8, 2, 32, 1024), bf),
        "gb": ((2048, 128), bf),
        "gq": ((2048, 128), bf),
        "gw": ((2, 8, 2, 32, 192), bf),
        "bias_s": ((8, 128), f32),
        "sums": ((8, 1024), f32),
        "n_half": ((64, 1024), bf),
        "n_half_land": ((64, 1024), bf),
        "o_arr": ((7, 2, 32, 1024), bf),
        "o_half": ((32, 1024), bf),
        "o_half_land": ((32, 1024), bf),
        "y_wgu": ((2, 2, 4, 64, 512), bf),
        "y_wd": ((2, 128, 1024), bf),
        "h_wgu": ((2, 4, 64, 512), bf),
        "h_wd": ((128, 1024), bf),
        "h_wgu_land": ((2, 4, 64, 512), bf),
        "h_wd_land": ((128, 1024), bf),
        "f2": ((2, 4, 2, 32, 512), bf),
        "w_land": ((8, 2, 32, 192), bf),
        "w_t": ((8, 2, 32, 192), bf),
        "s_acc": ((3, 8, 8, 128), f32),
        "s_land": ((9, 8, 8, 128), f32),
    }


N_COPIES = 232


def layer_kernel(*refs):
    names = layer_inputs() + list(layer_outputs()) + list(layer_scratch())
    r = SimpleNamespace(**dict(zip(names, refs)))
    send_sems, recv_sems, local_sems = refs[len(names) :]
    bf, f32 = jnp.bfloat16, jnp.float32
    net = Net(send_sems, recv_sems, local_sems)
    zh, zl, x, y, c = (net.me[a] for a in AXES)
    mine, in_half = net.index(AXES), net.index(AXES[1:])
    my_chip, my_pair = net.index(CHIPS), net.index(("zl", "x"))
    head = in_half
    net.barrier(CHIP_FLIPS + [("c",), ("zh",)])

    def x_region(part):
        def region(flips):
            return r.x.at[(zh if part == 0 else 1 - zh) * 16 + net.index(AXES[1:], flips)]

        return region

    x_own = Gather(net, x_region(0), ("zl", "y", "x"))
    x_far = Gather(net, x_region(1), ("zl", "x", "y"))
    wo_tree = Gather(net, lambda f: r.wo.at[:, net.index(AXES[1:], f)], ("zl", "y", "x"))
    gf_tree = Gather(net, lambda f: r.gf.at[net.index(("zl", "x", "c"), f)], ("zl", "x"))
    r.tile[...] = jnp.zeros_like(r.tile)
    r.tile[0:2, 0:64] = r.variate[...].astype(f32)
    r.tile[2:4, 0:64] = r.times[...].astype(f32)
    for k, gain in enumerate((r.norm_attn, r.norm_ffn, r.q_gain, r.k_gain)):
        r.tile[4 + k : 5 + k, 0:32] = gain[...].astype(f32)
    sm_step = net.send(r.tile, r.sm.at[zh, zl, x, y, c], ("zh",))
    swap = net.send(r.tok.at[1 - zh], r.x.at[mine], ("zh",))
    for h in range(16):
        r.wp[h // 2, h % 2] = r.wqkv[:, 192 * h : 192 * (h + 1)]
    w_arrive = []
    for flips in CHIP_FLIPS:
        w_arrive.append(net.send(r.wp.at[net.index(CHIPS, flips)], r.wl.at[my_chip], flips))
    x_own.push((), r.tok.at[zh])
    for pair in range(4):
        for cc in range(2):
            for part in range(4):
                idx = (part // 2) * 16 + pair * 4 + (part % 2) * 2 + cc
                col, lane = 128 * idx, 128 * part
                r.gp[pair, 0, cc, :, lane : lane + 128] = r.wgate[:, col : col + 128]
                r.gp[pair, 1, cc, :, lane : lane + 128] = r.wup[:, col : col + 128]
    g_arrive = []
    for flips in GROUP_FLIPS:
        g_arrive.append(
            net.send(r.gp.at[net.index(("zl", "x"), flips)], r.gl.at[my_pair], flips)
        )
    r.sm[zh, zl, x, y, c] = r.tile[...]
    r.wl[my_chip] = r.wp[my_chip]
    r.x[mine] = r.tok[zh]
    r.gl[my_pair] = r.gp[my_pair]
    r.gf[net.index(("zl", "x", "c"))] = r.cot[...]
    r.wd[zh, y] = r.wdown[...]
    r.wo[zh, in_half] = r.wout[...]

    sm_step.wait_recv()
    sm_step = net.send(r.sm.at[:, zl, x, y, c], r.sm.at[:, zl, x, y, c], ("c",))
    for copy in w_arrive:
        copy.wait_recv()
    w_c = net.send(r.wl.at[:, 1 - c], r.wh.at[zh, :, c], ("c",))
    r.wh[zh, :, c] = r.wl[:, c]
    sm_step.wait_recv()
    sm_step = net.send(r.sm.at[:, zl, x, y], r.sm.at[:, zl, x, y], ("y",))
    x_own.take("zl")
    x_own.take("y")
    w_c.wait_recv()
    w_zh = net.send(r.wh.at[zh], r.wh.at[zh], ("zh",))
    swap.wait_recv()
    x_far.push(())
    wo_zh = net.send(r.wout, r.wo.at[zh, in_half], ("zh",))
    sm_step.wait_recv()
    sm_step = net.send(r.sm.at[:, zl, x], r.sm.at[:, zl, x], ("zl",))
    x_own.take("zl", "y")
    x_own.take("x")
    x_far.take("zl")
    sm_step.wait_recv()
    sm_step = net.send(r.sm.at[:, :, x], r.sm.at[:, :, x], ("x",))
    def g_piece(k, half):
        return r.wgu.at[k // 2, half, pl.ds(2 * (k % 2), 2), y]

    g_c, g_zh, g_y, g_fwd = [], [], [], []

    for copy in g_arrive:
        copy.wait_recv()
    for k in range(2):
        g_c.append(net.send(r.gl.at[:, k, 1 - c], r.wgu.at[k, zh, :, y, c], ("c",)))
        r.wgu[k, zh, :, y, c] = r.gl[:, k, c]
    x_far.take("x")
    x_own.take("zl", "x")
    x_own.take("y", "x")
    wo_zh.wait_recv()
    wo_tree.push(())
    for k in range(4):
        if k % 2 == 0:
            g_c[k // 2].wait_recv()
        g_zh.append(net.send(g_piece(k, zh), g_piece(k, zh), ("zh",)))
    x_far.take("zl", "x")
    for k in range(4):
        g_y.append(net.send(g_piece(k, zh), g_piece(k, zh), ("y",)))
    sm_step.wait_recv()

    lane8 = lane_iota(8)
    for group in range(8):
        for which in range(4):
            row = jnp.zeros((8, 128), f32)
            for j in range(4):
                block = 4 * group + j
                held = r.sm[
                    block // 16, (block // 8) % 2, (block // 4) % 2, (block // 2) % 2, block % 2
                ]
                moved = held if j == 0 else pltpu.roll(held, 32 * j, 1)
                row = jnp.where(lane8 // 32 == j, moved, row)
            r.gain_s[which, group : group + 1] = row[4 + which : 5 + which, :]
    gain_attn = jnp.concatenate([r.gain_s[0, k : k + 1] for k in range(8)], axis=1)
    gain_ffn = jnp.concatenate([r.gain_s[1, k : k + 1] for k in range(8)], axis=1)
    held_q = r.gain_s[2, pl.ds(my_chip, 1)]
    held_k = r.gain_s[3, pl.ds(my_chip, 1)]
    wide_q, wide_k = jnp.broadcast_to(held_q, (8, 128)), jnp.broadcast_to(held_k, (8, 128))
    wide_q = jnp.where(c == 0, wide_q, pltpu.roll(wide_q, 64, 1))
    wide_k = jnp.where(c == 0, pltpu.roll(wide_k, 64, 1), wide_k)
    qk_gain = jnp.where(lane8 < 64, wide_q, wide_k)[0:1, :]

    starts, ends, total = [], [], jnp.int32(0)
    for j in range(8):
        starts.append(total)
        total = total + r.lengths[zh, j]
        ends.append(total)
    sub = lax.broadcasted_iota(jnp.int32, (8, 128), 0)
    start_col = jnp.zeros((8, 128), jnp.int32)
    end_col = jnp.zeros((8, 128), jnp.int32)
    for j in range(8):
        start_col = jnp.where(sub == j, starts[j], start_col)
        end_col = jnp.where(sub == j, ends[j], end_col)
    same_bias = jnp.full((8, 128), r.bias[0, head], f32)
    other_bias = jnp.full((8, 128), r.bias[1, head], f32)
    diff_parts = pieces(same_bias - other_bias)
    zero = jnp.zeros((8, 128), f32)
    const_q = jnp.where(sub == 0, -256.0, 0.0)
    for i, part in enumerate(pieces(other_bias)):
        const_q = jnp.where(sub == i + 1, part, const_q)
    const_k = jnp.where(sub < 4, 1.0, 0.0)
    ones_k = jnp.where(sub < 3, 1.0, 0.0)

    @pl.loop(0, 16)
    def _(i):
        col = pl.ds(pl.multiple_of(i * 128, 128), 128)
        low = r.sm[i // 8, (i // 4) % 2, (i // 2) % 2, i % 2, 0]
        high = r.sm[i // 8, (i // 4) % 2, (i // 2) % 2, i % 2, 1]
        both = jnp.where(lane8 < 64, low, pltpu.roll(high, 64, 1))
        var_row = jnp.where(zh == 0, both[0:1, :], both[1:2, :])
        time_row = jnp.where(zh == 0, both[2:3, :], both[3:4, :])
        pos = lane8 + i * 128
        doc = jnp.where((pos >= start_col) & (pos < end_col), 1.0, 0.0)
        var = jnp.where(jnp.broadcast_to(var_row, (8, 128)) == sub.astype(f32), 1.0, 0.0)
        rows = [doc * 256.0, const_q] + [var * part for part in diff_parts] + [zero, zero, zero]
        rows += [doc, const_k, var, var, var, ones_k, zero, zero]
        r.feat[col, :] = jnp.concatenate(rows, axis=0).T
        angle = jnp.broadcast_to(time_row, (32, 128)) * jnp.broadcast_to(r.freq[...], (32, 128))
        cosine, sine = jnp.cos(angle), jnp.sin(angle)
        r.cs[col, :] = jnp.concatenate([cosine, cosine, -sine, sine], axis=0).T

    lane = lane_iota(ROW_BLOCK)

    def arrived(part, *flips):
        tree = x_own if part == 0 else x_far
        tree.ready(*flips)
        tree.ready(*(flips + ("y",)))

    def project(j):
        part, far_x, far_zl = j // 4, (j // 2) % 2, j % 2
        at = ((zh + part - 2 * zh * part) * 2 + zl + far_zl - 2 * zl * far_zl) * 2
        at = (at + x + far_x - 2 * x * far_x) * ROW_BLOCK
        row = pl.ds(pl.multiple_of(at, ROW_BLOCK), ROW_BLOCK)
        blocks = pl.ds(at // 64, 4)
        value = r.x[blocks].reshape(ROW_BLOCK, 1024).astype(f32)
        normed = (value * row_scale(value) * gain_attn).astype(bf)
        qkv = jnp.dot(normed, r.wh[...].reshape(1024, 192), preferred_element_type=f32)
        raw = qkv[:, :128]
        r.raw[row, :] = raw
        scaled = raw * lax.rsqrt(pair_mean(raw * raw) + EPS) * qk_gain
        cosine, sine = angles_of(r.cs[row, :])
        turned = (scaled * cosine + swap_halves(scaled) * sine).astype(bf).astype(f32)
        marks = r.feat[row, :]
        r.qf[row, :] = jnp.where(lane < 64, turned * 0.125, pltpu.roll(marks, 64, 1)).astype(bf)
        r.kf[row, :] = jnp.where(lane < 64, pltpu.roll(turned, 64, 1), marks).astype(bf)
        third = jnp.concatenate([qkv[:, 128:192], jnp.zeros((ROW_BLOCK, 64), f32)], axis=1)
        r.vf[row, :] = jnp.where((lane >= 64) & (lane < 67), 1.0, third).astype(bf)

    w_zh.wait_recv()
    arrived(0)
    arrived(0, "zl")
    x_own.take("zl", "y", "x")
    x_far.take("y")
    x_far.take("zl", "y")
    arrived(0, "x")
    arrived(0, "zl", "x")
    pl.loop(0, 4)(project)
    x_far.take("x", "y")
    x_far.take("zl", "x", "y")
    arrived(1)
    arrived(1, "zl")
    arrived(1, "x")
    arrived(1, "zl", "x")
    pl.loop(4, 8)(project)
    wo_tree.take("zl")

    lane_span = lane_iota(SPAN)

    def attend(i):
        row = pl.ds(pl.multiple_of(i * SPAN, SPAN), SPAN)
        query = r.qf[row, :]

        def one_chunk(k, total):
            col = pl.ds(pl.multiple_of(k * SPAN, SPAN), SPAN)
            scores = lax.dot_general(query, r.kf[col, :], LAST, preferred_element_type=f32)
            weights = jnp.exp(scores).astype(bf)
            return total + jnp.dot(weights, r.vf[col, :], preferred_element_type=f32)

        total = lax.fori_loop(0, 2048 // SPAN, one_chunk, jnp.zeros((SPAN, 128), f32))
        weight = total[:, 64:65]
        result = total / weight
        r.kept_o[row, :] = jnp.where(lane_span < 64, result, jnp.log(weight))
        r.att[pl.ds(4 * i, 4)] = result[:, :64].astype(bf).reshape(4, 2, 64, 64)

    def g_pass(k):
        g_zh[k].wait_recv()
        g_fwd.append(net.send(g_piece(k, 1 - zh), g_piece(k, 1 - zh), ("y",)))

    pl.loop(0, 2)(attend)
    wo_tree.take("y")
    g_pass(0)
    pl.loop(2, 4)(attend)

    step = net.send(r.att.at[:, 1 - c], r.lb, ("c",))
    wo_tree.take("zl", "y")
    step.wait_recv()
    lane64 = lane_iota(64)

    @pl.loop(0, 16)
    def _(i):
        own = jnp.concatenate([r.att[i, c]] * 2, axis=1)
        other = jnp.concatenate([r.lb[i]] * 2, axis=1)
        r.ap[i // 8, i % 8] = jnp.where((lane64 < 64) == (c == 0), own, other)

    arrive = []
    for flips in CHIP_FLIPS:
        arrive.append(
            net.send(r.ap.at[:, net.index(CHIPS, flips)], r.at2.at[my_chip], flips)
        )
    r.at2[my_chip] = r.ap[:, my_chip]

    def w_down():
        return r.wd[...].reshape(512, 1024)

    def w_o():
        return r.wo[...].reshape(1024, 1024)

    def w_in(k):
        return r.wgu[k].reshape(1024, 512)

    for copy in arrive:
        copy.wait_recv()
    step = net.send(r.at2.at[:, 1 - zh], r.at3, ("zh",))
    wd_zh = net.send(r.wdown, r.wd.at[zh, y], ("zh",))
    for k in range(8):
        r.att_s[pl.ds(pl.multiple_of(zh * 64, 64), 64), 128 * k : 128 * (k + 1)] = r.at2[k, zh]
    gf_tree.push((), r.cot)
    g_pass(1)
    g_pass(2)
    wd_y = net.send(r.wdown, r.wd.at[zh, y], ("y",))
    wo_tree.take("x")
    wo_tree.take("y", "x")
    wo_tree.take("zl", "x")
    wo_tree.take("zl", "y", "x")
    g_pass(3)
    for flips in [(), ("y",), ("zl",), ("zl", "y"), ("x",), ("y", "x"), ("zl", "x"), ("zl", "y", "x")]:
        wo_tree.ready(*flips)
    step.wait_recv()
    for k in range(8):
        r.att_s[pl.ds(pl.multiple_of(64 - zh * 64, 64), 64), 128 * k : 128 * (k + 1)] = r.at3[k]

    resid = r.tok[...].reshape(128, 1024).astype(f32)
    resid = resid + jnp.dot(r.att_s[...], w_o(), preferred_element_type=f32)
    scale = row_scale(resid)
    r.resid[...] = resid
    mine8 = 2 * my_pair + c
    r.n2[mine8] = (resid * scale * gain_ffn).astype(bf).reshape(2, 64, 1024)
    to_sibling = [net.send(r.n2.at[mine8], r.n2.at[mine8], ("c",))]
    from_chips = [net.send(r.n2.at[mine8], r.n2.at[mine8], flips) for flips in GROUP_FLIPS]
    def pair_rows(ref, pair):
        return ref[pl.ds(2 * pair, 2)].reshape(256, 1024)

    def feed(pair):
        rows = pair_rows(r.n2, pair)
        r.gate[pair] = jnp.dot(rows, w_in(0), preferred_element_type=f32)
        r.up[pair] = jnp.dot(rows, w_in(1), preferred_element_type=f32)

    def feed_back(pair):
        back = lax.dot_general(pair_rows(r.gf, pair), w_down(), LAST, preferred_element_type=f32)
        gate, up = r.gate[pair], r.up[pair]
        sig = 1.0 / (1.0 + jnp.exp(-gate))
        silu = gate * sig
        r.hid[pair] = (silu * up).astype(bf)
        r.ggu[0, pair] = (back * up * sig * (1.0 + gate * (1.0 - sig))).astype(bf)
        r.ggu[1, pair] = (back * silu).astype(bf)

    def back_product(pair):
        total = lax.dot_general(r.ggu[0, pair], w_in(0), LAST, preferred_element_type=f32)
        return total + lax.dot_general(r.ggu[1, pair], w_in(1), LAST, preferred_element_type=f32)

    def out_product(pair):
        return jnp.dot(r.hid[pair], w_down(), preferred_element_type=f32)

    halves, reduced = {}, {0: [], 1: []}

    def pair_at(slot):
        far_zl, far_x = slot % 2, slot // 2
        return (zl + far_zl - 2 * zl * far_zl) * 2 + x + far_x - 2 * x * far_x

    def keep_half(at, value):
        r.kept[at] = jnp.where(c == 0, value[:128], value[128:])
        r.sent[at] = jnp.where(c == 0, value[128:], value[:128]).astype(bf).reshape(2, 64, 1024)

    def share(kind, slot):
        at = 4 * kind + slot
        halves[at] = net.send(r.sent.at[at], r.landed.at[at], ("c",))

    def finish_half(kind, slot):
        at = 4 * kind + slot
        halves[at].wait_recv()
        total = r.kept[at] + r.landed[at].reshape(128, 1024).astype(f32)
        if slot == 0:
            r.kept[at] = total
        else:
            r.red_send[kind, slot - 1] = total.astype(bf)
            reduced[kind].append(
                net.send(
                    r.red_send.at[kind, slot - 1],
                    r.red_land.at[kind, slot - 1],
                    GROUP_FLIPS[slot - 1],
                )
            )

    pairs = [my_pair] + [net.index(("zl", "x"), flips) for flips in GROUP_FLIPS]
    wd_zh.wait_recv()
    wd_fwd = net.send(r.wd.at[1 - zh, y], r.wd.at[1 - zh, y], ("y",))
    gf_tree.take("zl")
    for copy in g_y + g_fwd:
        copy.wait_recv()
    to_sibling[0].wait_recv()
    for k in range(3):
        from_chips[k].wait_recv()
        at = 2 * pairs[k + 1] + c
        to_sibling.append(net.send(r.n2.at[at], r.n2.at[at], ("c",)))
        if k == 0:
            to_sibling[1].wait_recv()
            pl.loop(0, 2)(lambda slot: feed(pair_at(slot)))
    gf_tree.take("x")
    gf_tree.take("zl", "x")
    to_sibling[2].wait_recv()
    to_sibling[3].wait_recv()
    pl.loop(2, 4)(lambda slot: feed(pair_at(slot)))
    gf_tree.ready()
    gf_tree.ready("zl")
    gf_tree.ready("x")
    gf_tree.ready("zl", "x")
    wd_y.wait_recv()
    wd_fwd.wait_recv()
    net.drain()

    def feed_both(slot):
        pair = pair_at(slot)
        feed_back(pair)
        keep_half(slot, back_product(pair))

    pl.loop(2, 4)(feed_both)
    share(0, 2)
    share(0, 3)
    pl.loop(0, 2)(feed_both)
    finish_half(0, 3)
    finish_half(0, 2)
    share(0, 1)
    share(0, 0)

    @pl.loop(0, 2)
    def _(k):
        r.gwgu[k] = (
            lax.dot_general(
                r.n2[...].reshape(1024, 1024),
                r.ggu[k].reshape(1024, 512),
                FIRST,
                preferred_element_type=f32,
            )
            .astype(bf)
            .reshape(2, 4, 2, 64, 512)
        )
    finish_half(0, 1)
    y_far = [net.send(r.gwgu.at[k, 1 - zh, :, 1 - y], r.y_wgu.at[k, 1], ("y",)) for k in range(2)]
    finish_half(0, 0)

    @pl.loop(0, 4)
    def _(slot):
        keep_half(4 + slot, out_product(pair_at(slot)))

    for k in range(4):
        share(1, k)
    for half in range(2):
        cols = slice(512 * half, 512 * (half + 1))
        r.gwd[:, :, :, cols] = (
            lax.dot_general(
                r.hid[...].reshape(1024, 512),
                r.gf[:, :, :, cols].reshape(1024, 512),
                FIRST,
                preferred_element_type=f32,
            )
            .astype(bf)
            .reshape(2, 2, 128, 512)
        )
    net.settle(list(halves.values()))

    h_steps = []

    def half_gate_up(k):
        y_far[k].wait_recv()
        r.h_wgu[k] = (r.gwgu[k, 1 - zh, :, y].astype(f32) + r.y_wgu[k, 1].astype(f32)).astype(bf)
        h_steps.append(net.send(r.h_wgu.at[k], r.h_wgu_land.at[k], ("zh",)))

    def half_down():
        y_far[2].wait_recv()
        r.h_wd[...] = (r.gwd[1 - zh, y].astype(f32) + r.y_wd[1].astype(f32)).astype(bf)
        h_steps.append(net.send(r.h_wd, r.h_wd_land, ("zh",)))

    for copy in reduced[0]:
        copy.wait_recv()
    total = r.kept[0]
    for k in range(3):
        total = total + r.red_land[0, k].astype(f32)
    resid = r.resid[...]
    scale = row_scale(resid)
    r.sums[...] = jnp.zeros_like(r.sums)
    r.sums[1:2, :] = jnp.sum(total * resid * scale, axis=0, keepdims=True)
    weighted = total * gain_ffn
    mean = jnp.mean(weighted * resid, axis=1, keepdims=True)
    grad_resid = r.cot[...].reshape(128, 1024).astype(f32) + scale * weighted
    grad_resid = grad_resid - resid * (scale * scale * scale) * mean
    r.kept[0] = grad_resid
    r.branch[...] = grad_resid.astype(bf)
    grad_att = lax.dot_general(r.branch[...], w_o(), LAST, preferred_element_type=f32).astype(bf)
    for k in range(8):
        for b in range(2):
            r.ga3[b, k] = grad_att[64 * b : 64 * (b + 1), 128 * k : 128 * (k + 1)]
    step = net.send(r.ga3.at[1 - zh], r.ga2.at[zh], ("zh",))
    r.ga2[zh] = r.ga3[zh]
    step.wait_recv()
    arrive = []
    for flips in CHIP_FLIPS:
        arrive.append(
            net.send(r.ga2.at[:, net.index(CHIPS, flips)], r.ag1.at[:, my_chip], flips)
        )
    r.ag1[:, my_chip] = r.ga2[:, my_chip]
    for j in range(8):
        cols = slice(128 * j, 128 * (j + 1))
        r.gwo[j // 4, 2 * (j % 4) : 2 * (j % 4) + 2] = (
            lax.dot_general(r.att_s[:, cols], r.branch[...], FIRST, preferred_element_type=f32)
            .astype(bf)
            .reshape(2, 2, 32, 1024)
        )
    for copy in arrive:
        copy.wait_recv()

    @pl.loop(0, 16)
    def _(i):
        both = r.ag1[i // 8, i % 8]
        low, high = both[:, :64].astype(f32), both[:, 64:].astype(f32)
        r.lb[i] = jnp.where(c == 0, high, low).astype(bf)
        r.gatt[i, c] = jnp.where(c == 0, low, high).astype(bf)

    for k in (3, 2, 1, 0):
        finish_half(1, k)
    step = net.send(r.lb, r.gatt.at[:, c], ("c",))
    half_gate_up(0)
    half_gate_up(1)
    y_far.append(net.send(r.gwd.at[1 - zh, 1 - y], r.y_wd.at[1], ("y",)))
    y_near = [net.send(r.gwgu.at[k, zh, :, 1 - y], r.y_wgu.at[k, 0], ("y",)) for k in range(2)]
    y_near.append(net.send(r.gwd.at[zh, 1 - y], r.y_wd.at[0], ("y",)))
    r.feat[...] = jnp.zeros_like(r.feat)
    r.bias_s[...] = jnp.zeros_like(r.bias_s)
    r.gate[...] = jnp.zeros_like(r.gate)
    step.wait_recv()

    @pl.loop(0, 4)
    def _(i):
        row = pl.ds(pl.multiple_of(i * SPAN, SPAN), SPAN)
        kept = r.kept_o[row, :]
        grad = r.gatt[pl.ds(i * 4, 4)].reshape(SPAN, 64).astype(f32)
        grad = jnp.concatenate([grad, jnp.zeros((SPAN, 64), f32)], axis=1)
        delta = jnp.sum(jnp.where(lane_span < 64, grad * kept, 0.0), axis=1, keepdims=True)
        query = r.qf[row, :].astype(f32)
        for j, part in enumerate(pieces(kept[:, 64:65])):
            query = jnp.where(lane_span == 64 + 40 + j, -part, query)
        r.qf[row, :] = query.astype(bf)
        for j, part in enumerate(pieces(delta)):
            grad = jnp.where(lane_span == 64 + j, -part, grad)
        r.gb[row, :] = grad.astype(bf)

    grad_k, grad_v = r.feat, r.kept_o
    grad_v[...] = jnp.zeros_like(grad_v)
    tree_o = Reduce(
        net,
        ("x", "zl", "y"),
        lambda mask, core: r.gwo.at[:, net.index(CHIPS, mask), core],
        lambda slot: r.wo.at[0, pl.ds(2 * slot, 2)],
        lambda slot: r.wo.at[1, pl.ds(2 * slot, 2)],
        lambda slot: r.o_arr.at[slot],
    )
    for mask in tree_o.masks:
        tree_o.begin(mask)

    def attend_back(i):
        row = pl.ds(pl.multiple_of(i * SPAN, SPAN), SPAN)
        query, grad = r.qf[row, :], r.gb[row, :]

        def one_chunk(k, total):
            col = pl.ds(pl.multiple_of(k * SPAN, SPAN), SPAN)
            key = r.kf[col, :]
            scores = lax.dot_general(query, key, LAST, preferred_element_type=f32)
            probs = jnp.exp(scores)
            centred = lax.dot_general(grad, r.vf[col, :], LAST, preferred_element_type=f32)
            back = (probs * centred).astype(bf)
            grad_v[col, :] += lax.dot_general(
                probs.astype(bf), grad, FIRST, preferred_element_type=f32
            )
            grad_k[col, :] += lax.dot_general(back, query, FIRST, preferred_element_type=f32)
            return total + jnp.dot(back, key, preferred_element_type=f32)

        total = lax.fori_loop(0, 2048 // SPAN, one_chunk, jnp.zeros((SPAN, 128), f32))
        r.gq[row, :] = (total * 0.125).astype(bf)
        marks = r.kf[row, :].astype(f32)
        same = jnp.where((lane_span >= 80) & (lane_span < 88), total * marks, 0.0)
        every = jnp.where(lane_span == 72, total, 0.0)
        r.bias_s[0:1, :] += jnp.sum(same, axis=0, keepdims=True)
        r.bias_s[1:2, :] += jnp.sum(every, axis=0, keepdims=True)

    half_down()
    pl.loop(0, 2)(attend_back)
    for mask in tree_o.masks[:4]:
        tree_o.forward(mask)
    pl.loop(2, 4)(attend_back)
    tree_o.forward(("zl", "y"))
    tree_o.forward(("zl",))

    def token_tree(part, dims):
        return Reduce(
            net,
            dims,
            lambda mask, core: r.x.at[part * 16 + 2 * net.index(CHIPS, mask) + core],
            lambda slot: r.landed.at[slot, part],
            lambda slot: r.sent.at[slot, part],
            lambda slot: r.n2.at[slot, part],
        )

    trees = [token_tree(0, ("x", "y", "zl")), token_tree(1, ("y", "x", "zl"))]

    def project_back(part, where):
        start = (part * 4 + where) * ROW_BLOCK
        row, blocks = pl.ds(pl.multiple_of(start, ROW_BLOCK), ROW_BLOCK), pl.ds(start // 64, 4)
        raw = r.raw[row, :]
        scale = lax.rsqrt(pair_mean(raw * raw) + EPS)
        cosine, sine = angles_of(r.cs[row, :])
        key_part = pltpu.roll(grad_k[row, :].astype(bf).astype(f32), 64, 1)
        grad = jnp.where(lane < 64, r.gq[row, :].astype(f32), key_part)
        turned = grad * cosine - swap_halves(grad) * sine
        r.bias_s[2:3, :] += jnp.sum(turned * raw * scale, axis=0, keepdims=True)
        weighted = turned * qk_gain
        back = scale * weighted - raw * (scale * scale * scale) * pair_mean(weighted * raw)
        grad_qkv = jnp.concatenate([back, grad_v[row, :][:, :64]], axis=1).astype(bf)
        grad_normed = lax.dot_general(
            grad_qkv, r.wh[...].reshape(1024, 192), LAST, preferred_element_type=f32
        )
        value = r.x[blocks].reshape(ROW_BLOCK, 1024).astype(f32)
        shaped = value * row_scale(value)
        r.sums[0:1, :] += jnp.sum(grad_normed * shaped, axis=0, keepdims=True)
        normed = (shaped * gain_attn).astype(bf)
        term = lax.dot_general(normed, grad_qkv, FIRST, preferred_element_type=f32)
        r.gate[:, :, :192] += term.reshape(4, 256, 192)
        r.x[blocks] = grad_normed.astype(bf).reshape(4, 64, 1024)

    f_steps, f_c = [], []

    def feed_sum(k):
        y_near[k].wait_recv()
        h_steps[k].wait_recv()
        for j in range(4):
            rows = r.gwgu[k, zh, j, y].astype(f32) + r.y_wgu[k, 0, j].astype(f32)
            rows = rows + r.h_wgu_land[k, j].astype(f32)
            r.gp[j, k, 0] = rows[:32].astype(bf)
            r.gp[j, k, 1] = rows[32:].astype(bf)
        for flips in GROUP_FLIPS:
            f_steps.append(
                net.send(r.gp.at[net.index(("zl", "x"), flips), k], r.gl.at[my_pair, k], flips)
            )
        r.gl[my_pair, k] = r.gp[my_pair, k]

    def feed_sibling(k):
        for j in range(3):
            f_steps[3 * k + j].wait_recv()
        f_c.append(net.send(r.gl.at[:, k, 1 - c], r.f2.at[k, :, c], ("c",)))
        r.f2[k, :, c] = r.gl[:, k, c]

    def two_back(*flips):
        where = net.index(("zl", "x"), flips)
        pl.loop(0, 2)(lambda part: project_back(part, where))
        for tree in trees:
            tree.begin(flips)
            tree.begin(flips + ("y",))

    two_back("zl", "x")
    tree_o.forward(("y",))
    two_back("x")
    trees[0].forward(("zl", "x", "y"))
    trees[0].forward(("zl", "x"))
    trees[1].forward(("zl", "x", "y"))
    two_back("zl")
    trees[0].forward(("x", "y"))
    trees[0].forward(("x",))
    trees[1].forward(("x", "y"))
    two_back()
    trees[1].forward(("zl", "y"))
    trees[1].forward(("y",))
    trees[0].forward(("zl", "y"))
    trees[1].forward(("zl", "x"))

    one = lane_iota(8)
    both = jnp.broadcast_to(r.bias_s[2:3, :], (8, 128))
    turned = pltpu.roll(both, 64, 1)
    wide = lane_iota(1, 1024)
    query_gain = jnp.concatenate([jnp.where(one < 64, both, turned)[0:1]] * 8, axis=1)
    key_gain = jnp.concatenate([jnp.where(one < 64, turned, both)[0:1]] * 8, axis=1)
    r.sums[2:3, :] = jnp.where(wide // 64 == head, query_gain, 0.0)
    r.sums[3:4, :] = jnp.where(wide // 64 == head, key_gain, 0.0)
    same = jnp.sum(r.bias_s[0:1, :], axis=1, keepdims=True)
    every = jnp.sum(r.bias_s[1:2, :], axis=1, keepdims=True)
    row_bias = jnp.where(wide == head, same, 0.0)
    r.sums[4:5, :] = jnp.where(wide == 16 + head, every - same, row_bias)
    for k in range(8):
        r.s_acc[0, k] = r.sums[:, 128 * k : 128 * (k + 1)]
    s_steps = [net.send(r.s_acc.at[0], r.s_land.at[k], f) for k, f in enumerate(CHIP_FLIPS)]

    r.gw[...] = r.gate[:, :, :192].astype(bf).reshape(2, 8, 2, 32, 192)
    w_zh = net.send(r.gw.at[1 - zh], r.w_land, ("zh",))
    trees[0].forward(("y",))
    trees[1].forward(("x",))
    for copy in reduced[1]:
        copy.wait_recv()
    total = r.kept[4] + r.resid[...]
    for k in range(3):
        total = total + r.red_land[1, k].astype(f32)
    r.out[...] = total.astype(bf)
    total = tree_o.result()
    r.kept[3, :32] = total[0]
    r.kept[4, :32] = total[1]
    r.o_half[...] = r.kept[4 - zh, :32].astype(bf)
    o_step = net.send(r.o_half, r.o_half_land, ("zh",))
    trees[0].forward(("zl",))
    trees[1].forward(("zl",))
    feed_sum(0)
    feed_sum(1)
    total = r.s_acc[0]
    for k, copy in enumerate(s_steps):
        copy.wait_recv()
        total = total + r.s_land[k]
    r.s_acc[1] = total
    s_step = net.send(r.s_acc.at[1], r.s_land.at[7], ("zh",))
    w_zh.wait_recv()
    r.w_t[...] = (r.gw[zh].astype(f32) + r.w_land[...].astype(f32)).astype(bf)
    w_c = net.send(r.w_t.at[:, 1 - c], r.wp.at[:, c], ("c",))
    r.wp[:, c] = r.w_t[:, c]
    r.kept[1, :64] = trees[0].result()
    r.kept[2, :64] = trees[1].result()
    r.n_half[...] = r.kept[2 - zh, :64].astype(bf)
    n_step = net.send(r.n_half, r.n_half_land, ("zh",))
    w_c.wait_recv()
    w_steps = []
    for flips in CHIP_FLIPS:
        w_steps.append(net.send(r.wp.at[net.index(CHIPS, flips)], r.wl.at[my_chip], flips))
    r.wl[my_chip] = r.wp[my_chip]
    s_step.wait_recv()
    r.s_acc[2] = r.s_acc[1] + r.s_land[7]
    s_step = net.send(r.s_acc.at[2], r.s_land.at[8], ("c",))

    y_near[2].wait_recv()
    h_steps[2].wait_recv()
    r.gwdown[...] = r.gwd[zh, y].astype(f32) + r.y_wd[0].astype(f32) + r.h_wd_land[...].astype(f32)
    feed_sibling(0)
    feed_sibling(1)
    n_step.wait_recv()
    r.kept[2 - zh, :64] = r.n_half_land[...].astype(f32)
    for b in range(2):
        value = r.tok[b].astype(f32)
        scale = row_scale(value)
        weighted = r.kept[1 + b, :64] * gain_attn
        mean = jnp.mean(weighted * value, axis=1, keepdims=True)
        back = scale * weighted - value * (scale * scale * scale) * mean
        r.gtok[b] = (r.kept[0, 64 * b : 64 * (b + 1), :] + back).astype(bf)
    for copy in w_steps:
        copy.wait_recv()
    for h in range(16):
        r.gwqkv[:, 192 * h : 192 * (h + 1)] = r.wl[h // 2, h % 2].astype(f32)
    o_step.wait_recv()
    r.gwout[...] = r.kept[3 + zh, :32] + r.o_half_land[...].astype(f32)
    for k, out in ((0, r.gwgate), (1, r.gwup)):
        f_c[k].wait_recv()
        for pair in range(4):
            for cc in range(2):
                for part in range(4):
                    idx = (part // 2) * 16 + pair * 4 + (part % 2) * 2 + cc
                    out[:, 128 * idx : 128 * (idx + 1)] = r.f2[
                        k, pair, cc, :, 128 * part : 128 * (part + 1)
                    ].astype(f32)
    s_step.wait_recv()
    r.gsmall[...] = r.s_acc[2] + r.s_land[8]
    net.drain()


def layer(*arrays):
    sm = pl.BlockSpec(memory_space=pltpu.SMEM)
    vm = pl.BlockSpec(memory_space=pltpu.VMEM)
    outs = layer_outputs()
    return pl.pallas_call(
        layer_kernel,
        out_shape=[jax.ShapeDtypeStruct(*spec) for spec in outs.values()],
        in_specs=[sm, sm] + [vm] * (len(layer_inputs()) - 2),
        out_specs=[vm] * len(outs),
        scratch_shapes=[pltpu.VMEM(*spec) for spec in layer_scratch().values()]
        + [
            pltpu.SemaphoreType.DMA((N_COPIES,)),
            pltpu.SemaphoreType.DMA((N_COPIES,)),
            pltpu.SemaphoreType.DMA((2,)),
        ],
        compiler_params=pltpu.CompilerParams(
            collective_id=1, has_side_effects=True, vmem_limit_bytes=VMEM_BYTES
        ),
        name="layer",
    )(*arrays)


def give_out_kernel(small, *refs):
    n = (len(refs) - 5) // 2
    gains, bias = refs[2 * n : 2 * n + 4], refs[-1]
    for source, dest in zip(refs[:n], refs[n : 2 * n]):
        dest[...] = source[...]
    rank = jnp.int32(0)
    for name in AXES:
        rank = rank * 2 + lax.axis_index(name)
    held = small[rank // 4]
    mine = held
    for k in range(1, 4):
        mine = jnp.where(rank % 4 == k, pltpu.roll(held, 128 - 32 * k, 1), mine)
    for k, gain in enumerate(gains):
        gain[...] = mine[k : k + 1, :32]
    first = small[0]
    bias[0:1, :] = first[4:5, :16]
    bias[1:2, :] = pltpu.roll(first, 112, 1)[4:5, :16]


def give_out(small, *large):
    f32 = jnp.float32
    vm = pl.BlockSpec(memory_space=pltpu.VMEM)
    n = len(large)
    return pl.pallas_call(
        give_out_kernel,
        out_shape=[jax.ShapeDtypeStruct(a.shape, a.dtype) for a in large]
        + [jax.ShapeDtypeStruct((1, 32), f32)] * 4
        + [jax.ShapeDtypeStruct((2, 16), f32)],
        in_specs=[vm] * (n + 1),
        out_specs=[vm] * (n + 5),
        name="give_out",
    )(small, *large)


def frequencies():
    index = np.arange(32, dtype=np.float32)
    return (THETA ** (-2.0 * index / 64.0)).astype(np.float32)[:, None]


def on_device_cube(
    tokens,
    cotangent,
    w_qkv,
    w_out,
    w_gate,
    w_up,
    w_down,
    norm_attn,
    norm_ffn,
    q_gain,
    k_gain,
    var_bias,
    doc_lengths,
    variate,
    times,
):
    results = layer(
        doc_lengths, var_bias.T, tokens, cotangent, w_qkv, w_out, w_gate, w_up, w_down,
        *(gain.reshape(1, 32) for gain in (norm_attn, norm_ffn, q_gain, k_gain)),
        variate, times, jnp.asarray(frequencies()),
    )
    *large, small = results
    out, gtok, gwqkv, gwout, gwgate, gwup, gwdown, *gains, bias = give_out(small, *large)
    return (
        out.reshape(2, 64, 1024),
        gtok,
        gwqkv,
        gwout,
        gwgate,
        gwup,
        gwdown,
        *(gain.reshape(32) for gain in gains),
        bias.T,
    )


def run_parts(mesh, body, split):
    rows, cut = P(split, None), P(split)
    part = P(None, split, None)
    return jax.shard_map(
        body,
        mesh=mesh,
        in_specs=(part, part) + (rows,) * 5 + (cut,) * 4 + (P(), P(), P(None, split), P(None, split)),
        out_specs=(part, part) + (rows,) * 5 + (cut,) * 4 + (P(),),
        check_vma=False,
    )


def solution(mesh):
    sizes = (mesh.shape["head"], mesh.shape["blk"])
    general = run_parts(mesh, on_device, ("head", "blk"))
    if sizes != (8, 4):
        return general
    cube = jax.sharding.Mesh(mesh.devices.reshape(2, 2, 2, 2, 2), AXES)
    special = run_parts(cube, on_device_cube, AXES)

    def chosen(*arrays):
        tokens, w_gate, var_bias, lengths = arrays[0], arrays[4], arrays[11], arrays[12]
        shapes = (tokens.shape, w_gate.shape, var_bias.shape, lengths.shape)
        if shapes == ((2, 2048, 1024), (1024, 4096), (16, 2), (2, 8)):
            return special(*arrays)
        return general(*arrays)

    return chosen
```

```python
import math
from types import SimpleNamespace

import jax
import jax.numpy as jnp
import numpy as np
from jax import lax
from jax.experimental import pallas as pl
from jax.experimental.pallas import tpu as pltpu
from jax.sharding import PartitionSpec as P

EPS = 1e-06
THETA = 10000.0
NEGATIVE = -1e30
KEY_BLOCK = 1024


def inverse_rms(values_in):
    return lax.rsqrt(jnp.mean(values_in * values_in, axis=-1, keepdims=True) + EPS)


def rotate(values_in, time_index, sign_value):
    half_dim = values_in.shape[-1] // 2
    frequency = THETA ** (-2.0 * jnp.arange(half_dim, dtype=jnp.float32) / values_in.shape[-1])
    angles = time_index.astype(jnp.float32)[:, None] * frequency[None, :]
    cosine = jnp.cos(angles)[:, None, :]
    sine_part = sign_value * jnp.sin(angles)[:, None, :]
    first_half = values_in[..., :half_dim]
    second_half = values_in[..., half_dim:]
    return jnp.concatenate(
        [
            first_half * cosine - second_half * sine_part,
            first_half * sine_part + second_half * cosine,
        ],
        axis=-1,
    )


def norm_back(grad_in, value_in, scale_in, gain_in):
    weighted = grad_in * gain_in
    scale_cube = scale_in * scale_in * scale_in
    return scale_in * weighted - value_in * scale_cube * jnp.mean(
        weighted * value_in, axis=-1, keepdims=True
    )


def row_contract(left_mat, right_mat):
    return lax.dot_general(
        left_mat, right_mat, (((0,), (0,)), ((), ())), preferred_element_type=jnp.float32
    )


def col_contract(left_mat, right_mat):
    return lax.dot_general(
        left_mat, right_mat, (((1,), (1,)), ((), ())), preferred_element_type=jnp.float32
    )


def document_of(positions, doc_ends):
    return jnp.sum((positions[:, None] >= doc_ends[None, :]).astype(jnp.int32), axis=1)


def key_positions(first_row, row_total, per_group, row_count, blk_n):
    row_index = first_row + jnp.arange(row_total, dtype=jnp.int32)
    source_blk = row_index // per_group
    within = row_index % per_group
    return (within // row_count * blk_n + source_blk) * row_count + within % row_count


def block_scores(queries, key_part, same_var, same_doc, bias_same, bias_other, att_scale):
    raw_scores = (
        jnp.einsum("qhd,khd->qhk", queries, key_part, preferred_element_type=jnp.float32)
        * att_scale
    )
    bias_terms = jnp.where(
        same_var[:, None, :], bias_same[None, :, None], bias_other[None, :, None]
    )
    return jnp.where(same_doc[:, None, :], raw_scores + bias_terms, NEGATIVE)


def forward_block(
    state_in, queries, key_part, value_part, same_var, same_doc, bias_same, bias_other, att_scale
):
    best_prev, total_prev, accum_prev = state_in
    scores = block_scores(queries, key_part, same_var, same_doc, bias_same, bias_other, att_scale)
    best_next = jnp.maximum(best_prev, jnp.max(scores, axis=-1))
    factor = jnp.exp(best_prev - best_next)
    weights = jnp.where(same_doc[:, None, :], jnp.exp(scores - best_next[..., None]), 0.0)
    total_next = total_prev * factor + jnp.sum(weights, axis=-1)
    accum_next = accum_prev * factor[..., None] + jnp.einsum(
        "qhk,khd->qhd", weights.astype(jnp.bfloat16), value_part, preferred_element_type=jnp.float32
    )
    return (best_next, total_next, accum_next)


def flatten_all(grads_in):
    return tuple((member.reshape(-1) for member in grads_in))


def unflatten_all(flat_in, grads_like):
    return tuple(
        (flat.reshape((-1,) + member.shape[1:]) for flat, member in zip(flat_in, grads_like))
    )


def on_device(
    tokens,
    cotangent,
    w_qkv,
    w_out,
    w_gate,
    w_up,
    w_down,
    norm_attn,
    norm_ffn,
    q_gain,
    k_gain,
    var_bias,
    doc_lengths,
    variate,
    times,
):
    heads_n = lax.axis_size("head")
    blk_n = lax.axis_size("blk")
    head_rank = lax.axis_index("head")
    blk_rank = lax.axis_index("blk")
    batch_count, row_count, model_width = tokens.shape
    head_count = var_bias.shape[0]
    head_dim = model_width // head_count
    local_heads = head_count // heads_n
    query_rows = heads_n * row_count
    key_rows = blk_n * query_rows
    key_block = min(KEY_BLOCK, key_rows)
    block_count = key_rows // key_block
    att_scale = 1.0 / math.sqrt(head_dim)
    gathered = (
        lax.all_gather(w_qkv, ("head", "blk"), axis=0, tiled=True),
        lax.all_gather(w_out, ("head", "blk"), axis=0, tiled=True),
        lax.all_gather(w_gate, ("head", "blk"), axis=0, tiled=True),
        lax.all_gather(w_up, ("head", "blk"), axis=0, tiled=True),
        lax.all_gather(w_down, ("head", "blk"), axis=0, tiled=True),
        lax.all_gather(norm_attn, ("head", "blk"), axis=0, tiled=True),
        lax.all_gather(norm_ffn, ("head", "blk"), axis=0, tiled=True),
        lax.all_gather(q_gain, ("head", "blk"), axis=0, tiled=True),
        lax.all_gather(k_gain, ("head", "blk"), axis=0, tiled=True),
    )
    wqkv_all, wout_all, wgate_all, wup_all, wdown_all = gathered[:5]
    gain_attn = gathered[5].astype(jnp.float32)
    gain_ffn = gathered[6].astype(jnp.float32)
    gain_query = gathered[7].astype(jnp.float32).reshape(head_count, head_dim)
    gain_key = gathered[8].astype(jnp.float32).reshape(head_count, head_dim)
    local_bias = lax.dynamic_slice_in_dim(var_bias, head_rank * local_heads, local_heads, 0)
    bias_same = local_bias[:, 0]
    bias_other = local_bias[:, 1]
    query_index = jnp.arange(query_rows, dtype=jnp.int32)
    query_pos = (query_index // row_count * blk_n + blk_rank) * row_count + query_index % row_count
    ends_all = jnp.cumsum(doc_lengths, axis=1)
    outputs_list = []
    inputs_list = []
    totals = None
    bias_accum = jnp.zeros((local_heads, 2), jnp.float32)
    for batch_id in range(batch_count):
        doc_ends = ends_all[batch_id]
        time_row = times[batch_id]
        inputs_f = tokens[batch_id].astype(jnp.float32)
        scale_one = inverse_rms(inputs_f)
        normed_one = (inputs_f * scale_one * gain_attn).astype(jnp.bfloat16)
        qkv_all = jnp.dot(normed_one, wqkv_all, preferred_element_type=jnp.float32).reshape(
            row_count, head_count, 3 * head_dim
        )
        query_raw = qkv_all[..., :head_dim]
        key_raw = qkv_all[..., head_dim : 2 * head_dim]
        value_raw = qkv_all[..., 2 * head_dim :]
        query_scale = inverse_rms(query_raw)
        key_scale = inverse_rms(key_raw)
        query_rot = rotate(query_raw * query_scale * gain_query, time_row, 1.0)
        key_rot = rotate(key_raw * key_scale * gain_key, time_row, 1.0)
        packed = jnp.concatenate([query_rot, key_rot, value_raw], axis=-1).astype(jnp.bfloat16)
        variate_rep = jnp.broadcast_to(
            variate[batch_id].astype(jnp.bfloat16)[:, None], (row_count, head_count)
        )
        packed_heads, variate_heads = (
            lax.all_to_all(packed, "head", split_axis=1, concat_axis=0, tiled=True),
            lax.all_to_all(variate_rep, "head", split_axis=1, concat_axis=0, tiled=True),
        )
        queries = packed_heads[..., :head_dim]
        key_values = packed_heads[..., head_dim:]
        query_var = variate_heads[:, 0]
        query_doc = document_of(query_pos, doc_ends)
        initial = (
            jnp.full((query_rows, local_heads), NEGATIVE, jnp.float32),
            jnp.zeros((query_rows, local_heads), jnp.float32),
            jnp.zeros((query_rows, local_heads, head_dim), jnp.float32),
        )
        kv_piece = lax.all_gather(key_values, "blk", axis=0, tiled=True)
        var_piece = lax.all_gather(query_var, "blk", axis=0, tiled=True)
        piece_rows = kv_piece.shape[0]

        def one_block(state_blk, kv_block, var_block, block_start):
            key_doc = document_of(
                key_positions(block_start, kv_block.shape[0], query_rows, row_count, blk_n),
                doc_ends,
            )
            same_doc = query_doc[:, None] == key_doc[None, :]
            same_var = query_var[:, None] == var_block[None, :]
            return forward_block(
                state_blk,
                queries,
                kv_block[..., :head_dim],
                kv_block[..., head_dim:],
                same_var,
                same_doc,
                bias_same,
                bias_other,
                att_scale,
            )

        def loop_step(turn_index, state_loop):
            kv_block = lax.dynamic_slice_in_dim(kv_piece, turn_index * key_block, key_block, 0)
            var_block = lax.dynamic_slice_in_dim(var_piece, turn_index * key_block, key_block, 0)
            return one_block(state_loop, kv_block, var_block, turn_index * key_block)

        attn_state = lax.fori_loop(0, piece_rows // key_block, loop_step, initial)
        best_score, total_weight, accum = attn_state
        attn_heads = accum / total_weight[..., None]
        log_total = best_score + jnp.log(total_weight)
        attn_tok = lax.all_to_all(
            attn_heads.astype(jnp.bfloat16), "head", split_axis=0, concat_axis=1, tiled=True
        ).reshape(row_count, model_width)
        resid_one = inputs_f + jnp.dot(attn_tok, wout_all, preferred_element_type=jnp.float32)
        scale_two = inverse_rms(resid_one)
        normed_two = (resid_one * scale_two * gain_ffn).astype(jnp.bfloat16)
        gate_pre = jnp.dot(normed_two, wgate_all, preferred_element_type=jnp.float32)
        up_pre = jnp.dot(normed_two, wup_all, preferred_element_type=jnp.float32)
        sigmoid_gate = jax.nn.sigmoid(gate_pre)
        silu_gate = gate_pre * sigmoid_gate
        hidden_act = (silu_gate * up_pre).astype(jnp.bfloat16)
        result = resid_one + jnp.dot(hidden_act, wdown_all, preferred_element_type=jnp.float32)
        outputs_list.append(result.astype(jnp.bfloat16))
        grad_out = cotangent[batch_id].astype(jnp.float32)
        grad_ffn = grad_out.astype(jnp.bfloat16)
        grad_down = row_contract(hidden_act, grad_ffn)
        grad_hidden = col_contract(grad_ffn, wdown_all)
        grad_gate = (
            grad_hidden * up_pre * sigmoid_gate * (1.0 + gate_pre * (1.0 - sigmoid_gate))
        ).astype(jnp.bfloat16)
        grad_up = (grad_hidden * silu_gate).astype(jnp.bfloat16)
        grad_wgate = row_contract(normed_two, grad_gate)
        grad_wup = row_contract(normed_two, grad_up)
        grad_normed = col_contract(grad_gate, wgate_all) + col_contract(grad_up, wup_all)
        grad_gffn = jnp.sum(grad_normed * resid_one * scale_two, axis=0)
        grad_resid = grad_out + norm_back(grad_normed, resid_one, scale_two, gain_ffn)
        grad_branch = grad_resid.astype(jnp.bfloat16)
        grad_wout = row_contract(attn_tok, grad_branch)
        grad_attn = (
            col_contract(grad_branch, wout_all)
            .astype(jnp.bfloat16)
            .reshape(row_count, head_count, head_dim)
        )
        grad_heads = lax.all_to_all(grad_attn, "head", split_axis=1, concat_axis=0, tiled=True)
        delta_row = jnp.sum(grad_heads.astype(jnp.float32) * attn_heads, axis=-1)
        keys_all, key_var_all = (
            lax.all_gather(key_values, "blk", axis=0, tiled=True),
            lax.all_gather(query_var, "blk", axis=0, tiled=True),
        )
        keys_blocks = keys_all.reshape(block_count, key_block, local_heads, 2 * head_dim)
        var_blocks = key_var_all.reshape(block_count, key_block)
        block_starts = jnp.arange(block_count, dtype=jnp.int32) * key_block

        def back_step(carry_back, block_in):
            grad_query, bias_grad = carry_back
            kv_block, var_block, block_start = block_in
            key_doc = document_of(
                key_positions(block_start, key_block, query_rows, row_count, blk_n), doc_ends
            )
            same_doc = query_doc[:, None] == key_doc[None, :]
            same_var = query_var[:, None] == var_block[None, :]
            key_part = kv_block[..., :head_dim]
            value_part = kv_block[..., head_dim:]
            scores = block_scores(
                queries, key_part, same_var, same_doc, bias_same, bias_other, att_scale
            )
            probs = jnp.where(same_doc[:, None, :], jnp.exp(scores - log_total[..., None]), 0.0)
            grad_probs = jnp.einsum(
                "qhd,khd->qhk", grad_heads, value_part, preferred_element_type=jnp.float32
            )
            grad_scores = (probs * (grad_probs - delta_row[..., None])).astype(jnp.bfloat16)
            grad_scores_f = grad_scores.astype(jnp.float32)
            same_sum = jnp.sum(jnp.where(same_var[:, None, :], grad_scores_f, 0.0), axis=(0, 2))
            other_sum = jnp.sum(jnp.where(same_var[:, None, :], 0.0, grad_scores_f), axis=(0, 2))
            bias_grad = bias_grad + jnp.stack([same_sum, other_sum], axis=-1)
            grad_query = grad_query + att_scale * jnp.einsum(
                "qhk,khd->qhd", grad_scores, key_part, preferred_element_type=jnp.float32
            )
            grad_key = att_scale * jnp.einsum(
                "qhk,qhd->khd", grad_scores, queries, preferred_element_type=jnp.float32
            )
            grad_value = jnp.einsum(
                "qhk,qhd->khd",
                probs.astype(jnp.bfloat16),
                grad_heads,
                preferred_element_type=jnp.float32,
            )
            return ((grad_query, bias_grad), jnp.concatenate([grad_key, grad_value], axis=-1))

        carry_start = (
            jnp.zeros((query_rows, local_heads, head_dim), jnp.float32),
            jnp.zeros((local_heads, 2), jnp.float32),
        )
        (grad_query, bias_part), grad_kv_parts = lax.scan(
            back_step, carry_start, (keys_blocks, var_blocks, block_starts)
        )
        bias_accum = bias_accum + bias_part
        grad_kv_own = lax.psum_scatter(
            grad_kv_parts.reshape(key_rows, local_heads, 2 * head_dim).astype(jnp.bfloat16),
            "blk",
            scatter_dimension=0,
            tiled=True,
        )
        grad_packed = jnp.concatenate([grad_query.astype(jnp.bfloat16), grad_kv_own], axis=-1)
        grad_tok = lax.all_to_all(
            grad_packed, "head", split_axis=0, concat_axis=1, tiled=True
        ).astype(jnp.float32)
        grad_qrot = rotate(grad_tok[..., :head_dim], time_row, -1.0)
        grad_krot = rotate(grad_tok[..., head_dim : 2 * head_dim], time_row, -1.0)
        grad_gquery = jnp.sum(grad_qrot * query_raw * query_scale, axis=0)
        grad_gkey = jnp.sum(grad_krot * key_raw * key_scale, axis=0)
        grad_qraw = norm_back(grad_qrot, query_raw, query_scale, gain_query)
        grad_kraw = norm_back(grad_krot, key_raw, key_scale, gain_key)
        grad_qkv = (
            jnp.concatenate([grad_qraw, grad_kraw, grad_tok[..., 2 * head_dim :]], axis=-1)
            .reshape(row_count, 3 * model_width)
            .astype(jnp.bfloat16)
        )
        grad_wqkv = row_contract(normed_one, grad_qkv)
        grad_normed_one = col_contract(grad_qkv, wqkv_all)
        grad_gattn = jnp.sum(grad_normed_one * inputs_f * scale_one, axis=0)
        grad_in = grad_resid + norm_back(grad_normed_one, inputs_f, scale_one, gain_attn)
        inputs_list.append(grad_in.astype(jnp.bfloat16))
        batch_grads = (
            grad_wqkv,
            grad_wout,
            grad_wgate,
            grad_wup,
            grad_down,
            grad_gattn,
            grad_gffn,
            grad_gquery.reshape(model_width),
            grad_gkey.reshape(model_width),
        )
        if totals is None:
            totals = batch_grads
        else:
            totals = tuple(
                (first_term + second_term for first_term, second_term in zip(totals, batch_grads))
            )
    flat_totals = flatten_all(totals)
    summed_flat = (
        lax.psum_scatter(flat_totals[0], ("head", "blk"), scatter_dimension=0, tiled=True),
        lax.psum_scatter(flat_totals[1], ("head", "blk"), scatter_dimension=0, tiled=True),
        lax.psum_scatter(flat_totals[2], ("head", "blk"), scatter_dimension=0, tiled=True),
        lax.psum_scatter(flat_totals[3], ("head", "blk"), scatter_dimension=0, tiled=True),
        lax.psum_scatter(flat_totals[4], ("head", "blk"), scatter_dimension=0, tiled=True),
        lax.psum_scatter(flat_totals[5], ("head", "blk"), scatter_dimension=0, tiled=True),
        lax.psum_scatter(flat_totals[6], ("head", "blk"), scatter_dimension=0, tiled=True),
        lax.psum_scatter(flat_totals[7], ("head", "blk"), scatter_dimension=0, tiled=True),
        lax.psum_scatter(flat_totals[8], ("head", "blk"), scatter_dimension=0, tiled=True),
    )
    totals = unflatten_all(summed_flat, totals)
    bias_full = lax.dynamic_update_slice_in_dim(
        jnp.zeros((head_count, 2), jnp.float32), bias_accum, head_rank * local_heads, 0
    )
    grad_bias = lax.psum(bias_full, ("head", "blk"))
    return (
        jnp.stack(outputs_list),
        jnp.stack(inputs_list),
        totals[0],
        totals[1],
        totals[2],
        totals[3],
        totals[4],
        totals[5],
        totals[6],
        totals[7],
        totals[8],
        grad_bias,
    )


AXES = ("zh", "zl", "x", "y", "c")
CHIPS = ("zl", "x", "y")
VMEM_BYTES = 62 * 2**20
ROW_BLOCK = 256
SPAN = 512
LAST = (((1,), (1,)), ((), ()))
FIRST = (((0,), (0,)), ((), ()))
CHIP_FLIPS = [
    tuple(a for a, bit in zip(CHIPS, ((m >> 2) & 1, (m >> 1) & 1, m & 1)) if bit)
    for m in range(1, 8)
]
GROUP_FLIPS = [("zl",), ("x",), ("zl", "x")]


class Net:
    def __init__(self, send_sems, recv_sems, local_sems):
        self.me = {name: lax.axis_index(name) for name in AXES}
        self.send_sems, self.recv_sems, self.local_sems = send_sems, recv_sems, local_sems
        self.used = 0
        self.local_used = 0
        self.open = []

    def target(self, flips):
        return tuple(1 - self.me[a] if a in flips else self.me[a] for a in AXES)

    def index(self, names, flips=()):
        total = 0
        for a in names:
            total = total * 2 + (1 - self.me[a] if a in flips else self.me[a])
        return total

    def barrier(self, partners):
        sem = pltpu.get_barrier_semaphore()
        for flips in partners:
            pl.semaphore_signal(
                sem, inc=1, device_id=self.target(flips), device_id_type=pl.DeviceIdType.MESH
            )
        pl.semaphore_wait(sem, len(partners))

    def send(self, source, dest, flips):
        copy = pltpu.make_async_remote_copy(
            src_ref=source,
            dst_ref=dest,
            send_sem=self.send_sems.at[self.used],
            recv_sem=self.recv_sems.at[self.used],
            device_id=self.target(flips),
            device_id_type=pl.DeviceIdType.MESH,
        )
        self.used += 1
        copy.start()
        self.open.append(copy)
        return copy

    def local(self, source, dest):
        copy = pltpu.make_async_copy(source, dest, self.local_sems.at[self.local_used])
        self.local_used += 1
        copy.start()
        return copy

    def settle(self, copies):
        for copy in copies:
            copy.wait_send()
        gone = [id(copy) for copy in copies]
        self.open = [copy for copy in self.open if id(copy) not in gone]

    def drain(self):
        for copy in self.open:
            copy.wait_send()
        self.open = []


class Gather:
    def __init__(self, net, region, dims):
        self.net, self.region, self.dims = net, region, dims
        self.arrive = {}
        self.sibling = {}

    def key(self, flips):
        return tuple(sorted(flips))

    def push(self, flips, source=None):
        source = self.region(flips) if source is None else source
        level = max([self.dims.index(a) for a in flips], default=-1)
        for d in self.dims[level + 1 :]:
            copy = self.net.send(source, self.region(flips), (d,))
            self.arrive[self.key(flips + (d,))] = copy
        self.sibling[self.key(flips)] = self.net.send(source, self.region(flips), ("c",))

    def take(self, *flips):
        self.arrive[self.key(flips)].wait_recv()
        self.push(flips)

    def ready(self, *flips):
        self.sibling[self.key(flips)].wait_recv()


class Reduce:
    def __init__(self, net, dims, part, land, send, arrive):
        self.net, self.dims = net, dims
        self.part, self.land, self.send_slot, self.arrive = part, land, send, arrive
        self.from_sibling, self.incoming = {}, {}
        a, b, d = dims
        self.masks = [(a, b, d), (a, b), (a, d), (a,), (b, d), (b,), (d,), ()]
        self.slots = {}
        for rest in [(b, d), (b,), (d,), ()]:
            self.slots[rest, a] = len(self.slots)
        for rest in [(d,), ()]:
            self.slots[rest, b] = len(self.slots)
        self.slots[(), d] = len(self.slots)

    def ordered(self, flips):
        return tuple(a for a in self.dims if a in flips)

    def begin(self, flips):
        mask = self.ordered(flips)
        self.from_sibling[mask] = self.net.send(
            self.part(mask, 1 - self.net.me["c"]), self.land(self.masks.index(mask)), ("c",)
        )

    def total(self, mask, before):
        value = self.part(mask, self.net.me["c"])[...].astype(jnp.float32)
        value = value + self.land(self.masks.index(mask))[...].astype(jnp.float32)
        for stage in before:
            value = value + self.arrive(self.slots[mask, stage])[...].astype(jnp.float32)
        return value

    def settle(self, mask, before):
        self.from_sibling[mask].wait_recv()
        for stage in before:
            self.incoming[mask, stage].wait_recv()
        return self.total(mask, before)

    def forward(self, flips):
        mask = self.ordered(flips)
        stage, rest = mask[0], mask[1:]
        value = self.settle(mask, self.dims[: self.dims.index(stage)])
        slot = self.slots[rest, stage]
        self.send_slot(slot)[...] = value.astype(jnp.bfloat16)
        self.incoming[rest, stage] = self.net.send(
            self.send_slot(slot), self.arrive(slot), (stage,)
        )

    def result(self):
        return self.settle((), self.dims)


def lane_iota(rows, lanes=128):
    return lax.broadcasted_iota(jnp.int32, (rows, lanes), 1)


def pieces(value):
    first = value.astype(jnp.bfloat16).astype(jnp.float32)
    second = (value - first).astype(jnp.bfloat16).astype(jnp.float32)
    return first, second, value - first - second


def swap_halves(values):
    lane = lane_iota(values.shape[0])
    return jnp.where(lane % 64 < 32, pltpu.roll(values, 96, 1), pltpu.roll(values, 32, 1))


def pair_mean(values):
    lane = lane_iota(values.shape[0])
    low = jnp.sum(jnp.where(lane < 64, values, 0.0), axis=1, keepdims=True)
    high = jnp.sum(jnp.where(lane < 64, 0.0, values), axis=1, keepdims=True)
    return jnp.where(lane < 64, low, high) * (1.0 / 64.0)


def angles_of(packed):
    lane = lane_iota(packed.shape[0])
    turned = pltpu.roll(packed, 64, 1)
    return jnp.where(lane < 64, packed, turned), jnp.where(lane < 64, turned, packed)


def row_scale(value):
    return lax.rsqrt(jnp.mean(value * value, axis=1, keepdims=True) + EPS)


def layer_inputs():
    return ["lengths", "bias", "tok", "cot", "wqkv", "wout", "wgate", "wup", "wdown"] + [
        "norm_attn", "norm_ffn", "q_gain", "k_gain", "variate", "times", "freq",
    ]


def layer_outputs():
    bf, f32 = jnp.bfloat16, jnp.float32
    return {
        "out": ((128, 1024), bf),
        "gtok": ((2, 64, 1024), bf),
        "gwqkv": ((32, 3072), f32),
        "gwout": ((32, 1024), f32),
        "gwgate": ((32, 4096), f32),
        "gwup": ((32, 4096), f32),
        "gwdown": ((128, 1024), f32),
        "gsmall": ((8, 8, 128), f32),
    }


def layer_scratch():
    bf, f32 = jnp.bfloat16, jnp.float32
    return {
        "x": ((32, 64, 1024), bf),
        "wp": ((8, 2, 32, 192), bf),
        "wl": ((8, 2, 32, 192), bf),
        "wh": ((2, 8, 2, 32, 192), bf),
        "gp": ((4, 2, 2, 32, 512), bf),
        "gl": ((4, 2, 2, 32, 512), bf),
        "wgu": ((2, 2, 4, 2, 2, 32, 512), bf),
        "wd": ((2, 2, 128, 1024), bf),
        "wo": ((2, 16, 32, 1024), bf),
        "gf": ((8, 2, 64, 1024), bf),
        "tile": ((8, 128), f32),
        "sm": ((2, 2, 2, 2, 2, 8, 128), f32),
        "gain_s": ((4, 8, 128), f32),
        "feat": ((2048, 128), f32),
        "cs": ((2048, 128), f32),
        "raw": ((2048, 128), f32),
        "kept_o": ((2048, 128), f32),
        "qf": ((2048, 128), bf),
        "kf": ((2048, 128), bf),
        "vf": ((2048, 128), bf),
        "att": ((16, 2, 64, 64), bf),
        "lb": ((16, 64, 64), bf),
        "ap": ((2, 8, 64, 128), bf),
        "at2": ((2, 8, 64, 128), bf),
        "att_s": ((128, 1024), bf),
        "resid": ((128, 1024), f32),
        "n2": ((8, 2, 64, 1024), bf),
        "gate": ((4, 256, 512), f32),
        "up": ((4, 256, 512), f32),
        "hid": ((4, 256, 512), bf),
        "ggu": ((2, 4, 256, 512), bf),
        "kept": ((8, 128, 1024), f32),
        "sent": ((8, 2, 64, 1024), bf),
        "landed": ((8, 2, 64, 1024), bf),
        "red_send": ((2, 3, 128, 1024), bf),
        "red_land": ((2, 3, 128, 1024), bf),
        "branch": ((128, 1024), bf),
        "ga3": ((2, 8, 64, 128), bf),
        "ag1": ((2, 8, 64, 128), bf),
        "gatt": ((16, 2, 64, 64), bf),
        "gwgu": ((2, 2, 4, 2, 64, 512), bf),
        "gwd": ((2, 2, 128, 1024), bf),
        "gwo": ((2, 8, 2, 32, 1024), bf),
        "gb": ((2048, 128), bf),
        "gq": ((2048, 128), bf),
        "gw": ((2, 8, 2, 32, 192), bf),
        "bias_s": ((8, 128), f32),
        "sums": ((8, 1024), f32),
        "n_half": ((64, 1024), bf),
        "n_half_land": ((64, 1024), bf),
        "o_arr": ((7, 2, 32, 1024), bf),
        "o_half": ((32, 1024), bf),
        "o_half_land": ((32, 1024), bf),
        "y_wgu": ((2, 2, 4, 64, 512), bf),
        "y_wd": ((2, 128, 1024), bf),
        "h_wgu": ((2, 4, 64, 512), bf),
        "h_wd": ((128, 1024), bf),
        "h_wgu_land": ((2, 4, 64, 512), bf),
        "h_wd_land": ((128, 1024), bf),
        "f2": ((2, 4, 2, 32, 512), bf),
        "w_land": ((8, 2, 32, 192), bf),
        "w_t": ((8, 2, 32, 192), bf),
        "s_acc": ((3, 8, 8, 128), f32),
        "s_land": ((9, 8, 8, 128), f32),
    }


N_COPIES = 232


def layer_kernel(*refs):
    names = layer_inputs() + list(layer_outputs()) + list(layer_scratch())
    r = SimpleNamespace(**dict(zip(names, refs)))
    send_sems, recv_sems, local_sems = refs[len(names) :]
    bf, f32 = jnp.bfloat16, jnp.float32
    net = Net(send_sems, recv_sems, local_sems)
    zh, zl, x, y, c = (net.me[a] for a in AXES)
    mine, in_half = net.index(AXES), net.index(AXES[1:])
    my_chip, my_pair = net.index(CHIPS), net.index(("zl", "x"))
    head = in_half
    far_flips = [("zh",) + flips for flips in [()] + CHIP_FLIPS]
    net.barrier(CHIP_FLIPS + [("c",)] + far_flips)

    def x_region(part):
        def region(flips):
            return r.x.at[(zh if part == 0 else 1 - zh) * 16 + net.index(AXES[1:], flips)]

        return region

    x_own = Gather(net, x_region(0), ("zl", "y", "x"))
    x_far = Gather(net, x_region(1), ("zl", "x", "y"))
    wo_tree = Gather(net, lambda f: r.wo.at[:, net.index(AXES[1:], f)], ("zl", "y", "x"))
    gf_tree = Gather(net, lambda f: r.gf.at[net.index(("zl", "x", "c"), f)], ("zl", "x"))
    r.tile[...] = jnp.zeros_like(r.tile)
    r.tile[0:2, 0:64] = r.variate[...].astype(f32)
    r.tile[2:4, 0:64] = r.times[...].astype(f32)
    for k, gain in enumerate((r.norm_attn, r.norm_ffn, r.q_gain, r.k_gain)):
        r.tile[4 + k : 5 + k, 0:32] = gain[...].astype(f32)
    sm_step = net.send(r.tile, r.sm.at[zh, zl, x, y, c], ("zh",))
    swap = net.send(r.tok.at[1 - zh], r.x.at[mine], ("zh",))
    for h in range(16):
        r.wp[h // 2, h % 2] = r.wqkv[:, 192 * h : 192 * (h + 1)]
    w_arrive = []
    for flips in CHIP_FLIPS:
        w_arrive.append(net.send(r.wp.at[net.index(CHIPS, flips)], r.wl.at[my_chip], flips))
    x_own.push((), r.tok.at[zh])
    for pair in range(4):
        for cc in range(2):
            for part in range(4):
                idx = (part // 2) * 16 + pair * 4 + (part % 2) * 2 + cc
                col, lane = 128 * idx, 128 * part
                r.gp[pair, 0, cc, :, lane : lane + 128] = r.wgate[:, col : col + 128]
                r.gp[pair, 1, cc, :, lane : lane + 128] = r.wup[:, col : col + 128]

    def g_send(flips):
        return net.send(r.gp.at[net.index(("zl", "x"), flips)], r.gl.at[my_pair], flips)

    g_arrive = [g_send(("x",))]
    wd_y = net.send(r.wdown, r.wd.at[zh, y], ("y",))
    r.sm[zh, zl, x, y, c] = r.tile[...]
    r.wl[my_chip] = r.wp[my_chip]
    r.x[mine] = r.tok[zh]
    r.gl[my_pair] = r.gp[my_pair]
    r.gf[net.index(("zl", "x", "c"))] = r.cot[...]
    r.wd[zh, y] = r.wdown[...]
    r.wo[zh, in_half] = r.wout[...]

    sm_step.wait_recv()
    sm_step = net.send(r.sm.at[:, zl, x, y, c], r.sm.at[:, zl, x, y, c], ("x",))
    for copy in w_arrive:
        copy.wait_recv()
    w_c = net.send(r.wl.at[:, 1 - c], r.wh.at[zh, :, c], ("c",))
    r.wh[zh, :, c] = r.wl[:, c]
    sm_step.wait_recv()
    sm_step = net.send(r.sm.at[:, zl, :, y, c], r.sm.at[:, zl, :, y, c], ("y",))
    x_own.take("zl")
    x_own.take("y")
    w_c.wait_recv()
    swap.wait_recv()
    x_far.push(())
    w_zh = net.send(r.wh.at[zh], r.wh.at[zh], ("zh",))
    sm_step.wait_recv()
    sm_step = net.send(r.sm.at[:, zl, :, :, c], r.sm.at[:, zl, :, :, c], ("zl",))
    g_arrive += [g_send(("zl",)), g_send(("zl", "x"))]
    wo_zh = net.send(r.wout, r.wo.at[zh, in_half], ("zh",))
    x_own.take("zl", "y")
    x_own.take("x")
    x_far.take("zl")
    sm_step.wait_recv()
    sm_step = net.send(r.sm.at[:, :, :, :, c], r.sm.at[:, :, :, :, c], ("c",))

    def g_piece(k, half):
        return r.wgu.at[k // 2, half, pl.ds(2 * (k % 2), 2), y]

    g_c, g_zh, g_y, g_fwd = [], [], [], []

    x_far.take("x")
    x_own.take("zl", "x")
    x_own.take("y", "x")
    sm_step.wait_recv()

    lane8 = lane_iota(8)
    for group in range(8):
        for which in range(4):
            row = jnp.zeros((8, 128), f32)
            for j in range(4):
                block = 4 * group + j
                held = r.sm[
                    block // 16, (block // 8) % 2, (block // 4) % 2, (block // 2) % 2, block % 2
                ]
                moved = held if j == 0 else pltpu.roll(held, 32 * j, 1)
                row = jnp.where(lane8 // 32 == j, moved, row)
            r.gain_s[which, group : group + 1] = row[4 + which : 5 + which, :]
    gain_attn = jnp.concatenate([r.gain_s[0, k : k + 1] for k in range(8)], axis=1)
    gain_ffn = jnp.concatenate([r.gain_s[1, k : k + 1] for k in range(8)], axis=1)
    held_q = r.gain_s[2, pl.ds(my_chip, 1)]
    held_k = r.gain_s[3, pl.ds(my_chip, 1)]
    wide_q, wide_k = jnp.broadcast_to(held_q, (8, 128)), jnp.broadcast_to(held_k, (8, 128))
    wide_q = jnp.where(c == 0, wide_q, pltpu.roll(wide_q, 64, 1))
    wide_k = jnp.where(c == 0, pltpu.roll(wide_k, 64, 1), wide_k)
    qk_gain = jnp.where(lane8 < 64, wide_q, wide_k)[0:1, :]

    starts, ends, total = [], [], jnp.int32(0)
    for j in range(8):
        starts.append(total)
        total = total + r.lengths[zh, j]
        ends.append(total)
    sub = lax.broadcasted_iota(jnp.int32, (8, 128), 0)
    start_col = jnp.zeros((8, 128), jnp.int32)
    end_col = jnp.zeros((8, 128), jnp.int32)
    for j in range(8):
        start_col = jnp.where(sub == j, starts[j], start_col)
        end_col = jnp.where(sub == j, ends[j], end_col)
    same_bias = jnp.full((8, 128), r.bias[0, head], f32)
    other_bias = jnp.full((8, 128), r.bias[1, head], f32)
    diff_parts = pieces(same_bias - other_bias)
    zero = jnp.zeros((8, 128), f32)
    const_q = jnp.where(sub == 0, -256.0, 0.0)
    for i, part in enumerate(pieces(other_bias)):
        const_q = jnp.where(sub == i + 1, part, const_q)
    const_k = jnp.where(sub < 4, 1.0, 0.0)
    ones_k = jnp.where(sub < 3, 1.0, 0.0)

    @pl.loop(0, 16)
    def _(i):
        col = pl.ds(pl.multiple_of(i * 128, 128), 128)
        low = r.sm[i // 8, (i // 4) % 2, (i // 2) % 2, i % 2, 0]
        high = r.sm[i // 8, (i // 4) % 2, (i // 2) % 2, i % 2, 1]
        both = jnp.where(lane8 < 64, low, pltpu.roll(high, 64, 1))
        var_row = jnp.where(zh == 0, both[0:1, :], both[1:2, :])
        time_row = jnp.where(zh == 0, both[2:3, :], both[3:4, :])
        pos = lane8 + i * 128
        doc = jnp.where((pos >= start_col) & (pos < end_col), 1.0, 0.0)
        var = jnp.where(jnp.broadcast_to(var_row, (8, 128)) == sub.astype(f32), 1.0, 0.0)
        rows = [doc * 256.0, const_q] + [var * part for part in diff_parts] + [zero, zero, zero]
        rows += [doc, const_k, var, var, var, ones_k, zero, zero]
        r.feat[col, :] = jnp.concatenate(rows, axis=0).T
        angle = jnp.broadcast_to(time_row, (32, 128)) * jnp.broadcast_to(r.freq[...], (32, 128))
        cosine, sine = jnp.cos(angle), jnp.sin(angle)
        r.cs[col, :] = jnp.concatenate([cosine, cosine, -sine, sine], axis=0).T

    x_far.take("zl", "x")
    for copy in g_arrive:
        copy.wait_recv()
    for k in range(2):
        g_c.append(net.send(r.gl.at[:, k, 1 - c], r.wgu.at[k, zh, :, y, c], ("c",)))
        r.wgu[k, zh, :, y, c] = r.gl[:, k, c]
    wo_zh.wait_recv()
    wo_tree.push(())
    for k in range(4):
        if k % 2 == 0:
            g_c[k // 2].wait_recv()
        g_zh.append(net.send(g_piece(k, zh), g_piece(k, zh), ("zh",)))
    for k in range(4):
        g_y.append(net.send(g_piece(k, zh), g_piece(k, zh), ("y",)))
    gf_tree.push((), r.cot)

    lane = lane_iota(ROW_BLOCK)

    def arrived(part, *flips):
        tree = x_own if part == 0 else x_far
        tree.ready(*flips)
        tree.ready(*(flips + ("y",)))

    def project(j):
        part, far_x, far_zl = j // 4, (j // 2) % 2, j % 2
        at = ((zh + part - 2 * zh * part) * 2 + zl + far_zl - 2 * zl * far_zl) * 2
        at = (at + x + far_x - 2 * x * far_x) * ROW_BLOCK
        row = pl.ds(pl.multiple_of(at, ROW_BLOCK), ROW_BLOCK)
        blocks = pl.ds(at // 64, 4)
        value = r.x[blocks].reshape(ROW_BLOCK, 1024).astype(f32)
        normed = (value * row_scale(value) * gain_attn).astype(bf)
        qkv = jnp.dot(normed, r.wh[...].reshape(1024, 192), preferred_element_type=f32)
        raw = qkv[:, :128]
        r.raw[row, :] = raw
        scaled = raw * lax.rsqrt(pair_mean(raw * raw) + EPS) * qk_gain
        cosine, sine = angles_of(r.cs[row, :])
        turned = (scaled * cosine + swap_halves(scaled) * sine).astype(bf).astype(f32)
        marks = r.feat[row, :]
        r.qf[row, :] = jnp.where(lane < 64, turned * 0.125, pltpu.roll(marks, 64, 1)).astype(bf)
        r.kf[row, :] = jnp.where(lane < 64, pltpu.roll(turned, 64, 1), marks).astype(bf)
        third = jnp.concatenate([qkv[:, 128:192], jnp.zeros((ROW_BLOCK, 64), f32)], axis=1)
        r.vf[row, :] = jnp.where((lane >= 64) & (lane < 67), 1.0, third).astype(bf)

    w_zh.wait_recv()
    arrived(0)
    arrived(0, "zl")
    x_own.take("zl", "y", "x")
    x_far.take("y")
    x_far.take("zl", "y")
    arrived(0, "x")
    arrived(0, "zl", "x")
    pl.loop(0, 4)(project)
    x_far.take("x", "y")
    x_far.take("zl", "x", "y")
    arrived(1)
    arrived(1, "zl")
    arrived(1, "x")
    arrived(1, "zl", "x")
    pl.loop(4, 8)(project)
    wo_tree.take("zl")

    lane_span = lane_iota(SPAN)

    def attend(i):
        row = pl.ds(pl.multiple_of(i * SPAN, SPAN), SPAN)
        query = r.qf[row, :]

        def one_chunk(k, total):
            col = pl.ds(pl.multiple_of(k * SPAN, SPAN), SPAN)
            scores = lax.dot_general(query, r.kf[col, :], LAST, preferred_element_type=f32)
            weights = jnp.exp(scores).astype(bf)
            return total + jnp.dot(weights, r.vf[col, :], preferred_element_type=f32)

        total = lax.fori_loop(0, 2048 // SPAN, one_chunk, jnp.zeros((SPAN, 128), f32))
        weight = total[:, 64:65]
        result = total / weight
        r.kept_o[row, :] = jnp.where(lane_span < 64, result, jnp.log(weight))
        r.att[pl.ds(4 * i, 4)] = result[:, :64].astype(bf).reshape(4, 2, 64, 64)

    def g_pass(k):
        g_zh[k].wait_recv()
        g_fwd.append(net.send(g_piece(k, 1 - zh), g_piece(k, 1 - zh), ("y",)))

    pl.loop(0, 2)(attend)
    wo_tree.take("y")
    g_pass(0)
    pl.loop(2, 4)(attend)

    step = net.send(r.att.at[:, 1 - c], r.lb, ("c",))
    wo_tree.take("zl", "y")
    g_pass(1)
    step.wait_recv()
    lane64 = lane_iota(64)

    @pl.loop(0, 16)
    def _(i):
        own = jnp.concatenate([r.att[i, c]] * 2, axis=1)
        other = jnp.concatenate([r.lb[i]] * 2, axis=1)
        r.ap[i // 8, i % 8] = jnp.where((lane64 < 64) == (c == 0), own, other)

    arrive = []
    for flips in far_flips + CHIP_FLIPS:
        z_part = 1 - zh if "zh" in flips else zh
        arrive.append(
            net.send(r.ap.at[z_part, net.index(CHIPS, flips)], r.at2.at[zh, my_chip], flips)
        )
    r.at2[zh, my_chip] = r.ap[zh, my_chip]

    def w_down():
        return r.wd[...].reshape(512, 1024)

    def w_o():
        return r.wo[...].reshape(1024, 1024)

    def w_in(k):
        return r.wgu[k].reshape(1024, 512)

    for copy in arrive:
        copy.wait_recv()
    wd_zh = net.send(r.wdown, r.wd.at[zh, y], ("zh",))
    g_pass(2)
    gf_tree.take("zl")
    for b in range(2):
        for k in range(8):
            r.att_s[64 * b : 64 * (b + 1), 128 * k : 128 * (k + 1)] = r.at2[b, k]
    g_pass(3)
    wo_tree.take("x")
    wo_tree.take("y", "x")
    wo_tree.take("zl", "x")
    wo_tree.take("zl", "y", "x")
    for flips in [(), ("y",), ("zl",), ("zl", "y"), ("x",), ("y", "x"), ("zl", "x"), ("zl", "y", "x")]:
        wo_tree.ready(*flips)

    resid = r.tok[...].reshape(128, 1024).astype(f32)
    resid = resid + jnp.dot(r.att_s[...], w_o(), preferred_element_type=f32)
    scale = row_scale(resid)
    r.resid[...] = resid
    mine8 = 2 * my_pair + c
    r.n2[mine8] = (resid * scale * gain_ffn).astype(bf).reshape(2, 64, 1024)
    to_sibling = [net.send(r.n2.at[mine8], r.n2.at[mine8], ("c",))]
    from_chips = [net.send(r.n2.at[mine8], r.n2.at[mine8], flips) for flips in GROUP_FLIPS]
    def pair_rows(ref, pair):
        return ref[pl.ds(2 * pair, 2)].reshape(256, 1024)

    def feed(pair):
        rows = pair_rows(r.n2, pair)
        r.gate[pair] = jnp.dot(rows, w_in(0), preferred_element_type=f32)
        r.up[pair] = jnp.dot(rows, w_in(1), preferred_element_type=f32)

    def feed_back(pair):
        back = lax.dot_general(pair_rows(r.gf, pair), w_down(), LAST, preferred_element_type=f32)
        gate, up = r.gate[pair], r.up[pair]
        sig = 1.0 / (1.0 + jnp.exp(-gate))
        silu = gate * sig
        r.hid[pair] = (silu * up).astype(bf)
        r.ggu[0, pair] = (back * up * sig * (1.0 + gate * (1.0 - sig))).astype(bf)
        r.ggu[1, pair] = (back * silu).astype(bf)

    def back_product(pair):
        total = lax.dot_general(r.ggu[0, pair], w_in(0), LAST, preferred_element_type=f32)
        return total + lax.dot_general(r.ggu[1, pair], w_in(1), LAST, preferred_element_type=f32)

    def out_product(pair):
        return jnp.dot(r.hid[pair], w_down(), preferred_element_type=f32)

    halves, reduced = {}, {0: [], 1: []}

    def pair_at(slot):
        far_zl, far_x = slot % 2, slot // 2
        return (zl + far_zl - 2 * zl * far_zl) * 2 + x + far_x - 2 * x * far_x

    def keep_half(at, value):
        r.kept[at] = jnp.where(c == 0, value[:128], value[128:])
        r.sent[at] = jnp.where(c == 0, value[128:], value[:128]).astype(bf).reshape(2, 64, 1024)

    def share(kind, slot):
        at = 4 * kind + slot
        halves[at] = net.send(r.sent.at[at], r.landed.at[at], ("c",))

    def finish_half(kind, slot):
        at = 4 * kind + slot
        halves[at].wait_recv()
        total = r.kept[at] + r.landed[at].reshape(128, 1024).astype(f32)
        if slot == 0:
            r.kept[at] = total
        else:
            r.red_send[kind, slot - 1] = total.astype(bf)
            reduced[kind].append(
                net.send(
                    r.red_send.at[kind, slot - 1],
                    r.red_land.at[kind, slot - 1],
                    GROUP_FLIPS[slot - 1],
                )
            )

    pairs = [my_pair] + [net.index(("zl", "x"), flips) for flips in GROUP_FLIPS]
    for copy in g_y + g_fwd:
        copy.wait_recv()
    to_sibling[0].wait_recv()
    wd_zh.wait_recv()
    wd_fwd = net.send(r.wd.at[1 - zh, y], r.wd.at[1 - zh, y], ("y",))
    for k in range(3):
        from_chips[k].wait_recv()
        at = 2 * pairs[k + 1] + c
        to_sibling.append(net.send(r.n2.at[at], r.n2.at[at], ("c",)))
        if k == 0:
            to_sibling[1].wait_recv()
            pl.loop(0, 2)(lambda slot: feed(pair_at(slot)))
    gf_tree.take("x")
    gf_tree.take("zl", "x")
    to_sibling[2].wait_recv()
    to_sibling[3].wait_recv()
    pl.loop(2, 4)(lambda slot: feed(pair_at(slot)))
    gf_tree.ready()
    gf_tree.ready("zl")
    gf_tree.ready("x")
    gf_tree.ready("zl", "x")
    wd_y.wait_recv()
    wd_fwd.wait_recv()
    net.drain()

    def feed_both(slot):
        pair = pair_at(slot)
        feed_back(pair)
        keep_half(slot, back_product(pair))

    pl.loop(2, 4)(feed_both)
    share(0, 2)
    share(0, 3)
    pl.loop(0, 2)(feed_both)
    finish_half(0, 3)
    finish_half(0, 2)
    share(0, 1)
    share(0, 0)

    @pl.loop(0, 2)
    def _(k):
        r.gwgu[k] = (
            lax.dot_general(
                r.n2[...].reshape(1024, 1024),
                r.ggu[k].reshape(1024, 512),
                FIRST,
                preferred_element_type=f32,
            )
            .astype(bf)
            .reshape(2, 4, 2, 64, 512)
        )
    finish_half(0, 1)
    y_far = [net.send(r.gwgu.at[k, 1 - zh, :, 1 - y], r.y_wgu.at[k, 1], ("y",)) for k in range(2)]
    finish_half(0, 0)

    @pl.loop(0, 4)
    def _(slot):
        keep_half(4 + slot, out_product(pair_at(slot)))

    for k in range(4):
        share(1, k)
    for half in range(2):
        cols = slice(512 * half, 512 * (half + 1))
        r.gwd[:, :, :, cols] = (
            lax.dot_general(
                r.hid[...].reshape(1024, 512),
                r.gf[:, :, :, cols].reshape(1024, 512),
                FIRST,
                preferred_element_type=f32,
            )
            .astype(bf)
            .reshape(2, 2, 128, 512)
        )

    h_steps = []

    def half_gate_up(k):
        y_far[k].wait_recv()
        r.h_wgu[k] = (r.gwgu[k, 1 - zh, :, y].astype(f32) + r.y_wgu[k, 1].astype(f32)).astype(bf)
        h_steps.append(net.send(r.h_wgu.at[k], r.h_wgu_land.at[k], ("zh",)))

    def half_down():
        y_far[2].wait_recv()
        r.h_wd[...] = (r.gwd[1 - zh, y].astype(f32) + r.y_wd[1].astype(f32)).astype(bf)
        h_steps.append(net.send(r.h_wd, r.h_wd_land, ("zh",)))

    for copy in reduced[0]:
        copy.wait_recv()
    total = r.kept[0]
    for k in range(3):
        total = total + r.red_land[0, k].astype(f32)
    resid = r.resid[...]
    scale = row_scale(resid)
    r.sums[...] = jnp.zeros_like(r.sums)
    r.sums[1:2, :] = jnp.sum(total * resid * scale, axis=0, keepdims=True)
    weighted = total * gain_ffn
    mean = jnp.mean(weighted * resid, axis=1, keepdims=True)
    grad_resid = r.cot[...].reshape(128, 1024).astype(f32) + scale * weighted
    grad_resid = grad_resid - resid * (scale * scale * scale) * mean
    r.kept[0] = grad_resid
    r.branch[...] = grad_resid.astype(bf)
    grad_att = lax.dot_general(r.branch[...], w_o(), LAST, preferred_element_type=f32).astype(bf)
    for k in range(8):
        for b in range(2):
            r.ga3[b, k] = grad_att[64 * b : 64 * (b + 1), 128 * k : 128 * (k + 1)]
    arrive = []
    for flips in far_flips + CHIP_FLIPS:
        z_part = 1 - zh if "zh" in flips else zh
        arrive.append(
            net.send(r.ga3.at[z_part, net.index(CHIPS, flips)], r.ag1.at[zh, my_chip], flips)
        )
    r.ag1[zh, my_chip] = r.ga3[zh, my_chip]
    for j in range(8):
        cols = slice(128 * j, 128 * (j + 1))
        r.gwo[j // 4, 2 * (j % 4) : 2 * (j % 4) + 2] = (
            lax.dot_general(r.att_s[:, cols], r.branch[...], FIRST, preferred_element_type=f32)
            .astype(bf)
            .reshape(2, 2, 32, 1024)
        )
    for copy in arrive:
        copy.wait_recv()

    @pl.loop(0, 16)
    def _(i):
        both = r.ag1[i // 8, i % 8]
        low, high = both[:, :64].astype(f32), both[:, 64:].astype(f32)
        r.lb[i] = jnp.where(c == 0, high, low).astype(bf)
        r.gatt[i, c] = jnp.where(c == 0, low, high).astype(bf)

    for k in (3, 2, 1, 0):
        finish_half(1, k)
    step = net.send(r.lb, r.gatt.at[:, c], ("c",))
    half_gate_up(0)
    y_far.append(net.send(r.gwd.at[1 - zh, 1 - y], r.y_wd.at[1], ("y",)))
    r.feat[...] = jnp.zeros_like(r.feat)
    r.bias_s[...] = jnp.zeros_like(r.bias_s)
    r.gate[...] = jnp.zeros_like(r.gate)
    step.wait_recv()

    @pl.loop(0, 4)
    def _(i):
        row = pl.ds(pl.multiple_of(i * SPAN, SPAN), SPAN)
        kept = r.kept_o[row, :]
        grad = r.gatt[pl.ds(i * 4, 4)].reshape(SPAN, 64).astype(f32)
        grad = jnp.concatenate([grad, jnp.zeros((SPAN, 64), f32)], axis=1)
        delta = jnp.sum(jnp.where(lane_span < 64, grad * kept, 0.0), axis=1, keepdims=True)
        query = r.qf[row, :].astype(f32)
        for j, part in enumerate(pieces(kept[:, 64:65])):
            query = jnp.where(lane_span == 64 + 40 + j, -part, query)
        r.qf[row, :] = query.astype(bf)
        for j, part in enumerate(pieces(delta)):
            grad = jnp.where(lane_span == 64 + j, -part, grad)
        r.gb[row, :] = grad.astype(bf)

    grad_k, grad_v = r.feat, r.kept_o
    grad_v[...] = jnp.zeros_like(grad_v)
    tree_o = Reduce(
        net,
        ("x", "zl", "y"),
        lambda mask, core: r.gwo.at[:, net.index(CHIPS, mask), core],
        lambda slot: r.wo.at[0, pl.ds(2 * slot, 2)],
        lambda slot: r.wo.at[1, pl.ds(2 * slot, 2)],
        lambda slot: r.o_arr.at[slot],
    )
    for mask in tree_o.masks:
        tree_o.begin(mask)

    def attend_back(i):
        row = pl.ds(pl.multiple_of(i * SPAN, SPAN), SPAN)
        query, grad = r.qf[row, :], r.gb[row, :]

        def one_chunk(k, total):
            col = pl.ds(pl.multiple_of(k * SPAN, SPAN), SPAN)
            key = r.kf[col, :]
            scores = lax.dot_general(query, key, LAST, preferred_element_type=f32)
            probs = jnp.exp(scores)
            centred = lax.dot_general(grad, r.vf[col, :], LAST, preferred_element_type=f32)
            back = (probs * centred).astype(bf)
            grad_v[col, :] += lax.dot_general(
                probs.astype(bf), grad, FIRST, preferred_element_type=f32
            )
            grad_k[col, :] += lax.dot_general(back, query, FIRST, preferred_element_type=f32)
            return total + jnp.dot(back, key, preferred_element_type=f32)

        total = lax.fori_loop(0, 2048 // SPAN, one_chunk, jnp.zeros((SPAN, 128), f32))
        r.gq[row, :] = (total * 0.125).astype(bf)
        marks = r.kf[row, :].astype(f32)
        same = jnp.where((lane_span >= 80) & (lane_span < 88), total * marks, 0.0)
        every = jnp.where(lane_span == 72, total, 0.0)
        r.bias_s[0:1, :] += jnp.sum(same, axis=0, keepdims=True)
        r.bias_s[1:2, :] += jnp.sum(every, axis=0, keepdims=True)

    half_gate_up(1)
    pl.loop(0, 1)(attend_back)
    y_near = [net.send(r.gwgu.at[k, zh, :, 1 - y], r.y_wgu.at[k, 0], ("y",)) for k in range(2)]
    y_near.append(net.send(r.gwd.at[zh, 1 - y], r.y_wd.at[0], ("y",)))
    for mask in tree_o.masks[:4]:
        tree_o.forward(mask)
    half_down()
    pl.loop(1, 2)(attend_back)
    pl.loop(2, 4)(attend_back)

    def token_tree(part, dims):
        return Reduce(
            net,
            dims,
            lambda mask, core: r.x.at[part * 16 + 2 * net.index(CHIPS, mask) + core],
            lambda slot: r.landed.at[slot, part],
            lambda slot: r.sent.at[slot, part],
            lambda slot: r.n2.at[slot, part],
        )

    trees = [token_tree(0, ("x", "y", "zl")), token_tree(1, ("y", "x", "zl"))]

    def project_back(part, where):
        start = (part * 4 + where) * ROW_BLOCK
        row, blocks = pl.ds(pl.multiple_of(start, ROW_BLOCK), ROW_BLOCK), pl.ds(start // 64, 4)
        raw = r.raw[row, :]
        scale = lax.rsqrt(pair_mean(raw * raw) + EPS)
        cosine, sine = angles_of(r.cs[row, :])
        key_part = pltpu.roll(grad_k[row, :].astype(bf).astype(f32), 64, 1)
        grad = jnp.where(lane < 64, r.gq[row, :].astype(f32), key_part)
        turned = grad * cosine - swap_halves(grad) * sine
        r.bias_s[2:3, :] += jnp.sum(turned * raw * scale, axis=0, keepdims=True)
        weighted = turned * qk_gain
        back = scale * weighted - raw * (scale * scale * scale) * pair_mean(weighted * raw)
        grad_qkv = jnp.concatenate([back, grad_v[row, :][:, :64]], axis=1).astype(bf)
        grad_normed = lax.dot_general(
            grad_qkv, r.wh[...].reshape(1024, 192), LAST, preferred_element_type=f32
        )
        value = r.x[blocks].reshape(ROW_BLOCK, 1024).astype(f32)
        shaped = value * row_scale(value)
        r.sums[0:1, :] += jnp.sum(grad_normed * shaped, axis=0, keepdims=True)
        normed = (shaped * gain_attn).astype(bf)
        term = lax.dot_general(normed, grad_qkv, FIRST, preferred_element_type=f32)
        r.gate[:, :, :192] += term.reshape(4, 256, 192)
        r.x[blocks] = grad_normed.astype(bf).reshape(4, 64, 1024)

    f_steps, f_c = [], []

    def feed_sum(k):
        y_near[k].wait_recv()
        h_steps[k].wait_recv()
        for j in range(4):
            rows = r.gwgu[k, zh, j, y].astype(f32) + r.y_wgu[k, 0, j].astype(f32)
            rows = rows + r.h_wgu_land[k, j].astype(f32)
            r.gp[j, k, 0] = rows[:32].astype(bf)
            r.gp[j, k, 1] = rows[32:].astype(bf)
        for flips in GROUP_FLIPS:
            f_steps.append(
                net.send(r.gp.at[net.index(("zl", "x"), flips), k], r.gl.at[my_pair, k], flips)
            )
        r.gl[my_pair, k] = r.gp[my_pair, k]

    def feed_sibling(k):
        for j in range(3):
            f_steps[3 * k + j].wait_recv()
        f_c.append(net.send(r.gl.at[:, k, 1 - c], r.f2.at[k, :, c], ("c",)))
        r.f2[k, :, c] = r.gl[:, k, c]

    def two_back(*flips):
        where = net.index(("zl", "x"), flips)
        pl.loop(0, 2)(lambda part: project_back(part, where))
        for tree in trees:
            tree.begin(flips)
            tree.begin(flips + ("y",))

    net.settle(list(halves.values()))
    feed_sum(0)
    two_back("zl", "x")
    two_back("x")
    trees[0].forward(("zl", "x", "y"))
    trees[0].forward(("zl", "x"))
    trees[1].forward(("zl", "x", "y"))
    tree_o.forward(("zl", "y"))
    tree_o.forward(("zl",))
    two_back("zl")
    trees[0].forward(("x", "y"))
    trees[0].forward(("x",))
    trees[1].forward(("x", "y"))
    two_back()
    trees[1].forward(("zl", "y"))
    trees[1].forward(("y",))
    trees[0].forward(("zl", "y"))
    trees[1].forward(("zl", "x"))

    one = lane_iota(8)
    both = jnp.broadcast_to(r.bias_s[2:3, :], (8, 128))
    turned = pltpu.roll(both, 64, 1)
    wide = lane_iota(1, 1024)
    query_gain = jnp.concatenate([jnp.where(one < 64, both, turned)[0:1]] * 8, axis=1)
    key_gain = jnp.concatenate([jnp.where(one < 64, turned, both)[0:1]] * 8, axis=1)
    r.sums[2:3, :] = jnp.where(wide // 64 == head, query_gain, 0.0)
    r.sums[3:4, :] = jnp.where(wide // 64 == head, key_gain, 0.0)
    same = jnp.sum(r.bias_s[0:1, :], axis=1, keepdims=True)
    every = jnp.sum(r.bias_s[1:2, :], axis=1, keepdims=True)
    row_bias = jnp.where(wide == head, same, 0.0)
    r.sums[4:5, :] = jnp.where(wide == 16 + head, every - same, row_bias)
    for k in range(8):
        r.s_acc[0, k] = r.sums[:, 128 * k : 128 * (k + 1)]
    s_steps = [net.send(r.s_acc.at[0], r.s_land.at[k], f) for k, f in enumerate(CHIP_FLIPS)]

    r.gw[...] = r.gate[:, :, :192].astype(bf).reshape(2, 8, 2, 32, 192)
    w_zh = net.send(r.gw.at[1 - zh], r.w_land, ("zh",))
    trees[0].forward(("y",))
    trees[1].forward(("x",))
    tree_o.forward(("y",))
    for copy in reduced[1]:
        copy.wait_recv()
    total = r.kept[4] + r.resid[...]
    for k in range(3):
        total = total + r.red_land[1, k].astype(f32)
    r.out[...] = total.astype(bf)
    trees[0].forward(("zl",))
    trees[1].forward(("zl",))
    r.kept[1, :64] = trees[0].result()
    r.kept[2, :64] = trees[1].result()
    r.n_half[...] = r.kept[2 - zh, :64].astype(bf)
    n_step = net.send(r.n_half, r.n_half_land, ("zh",))
    total = tree_o.result()
    r.kept[3, :32] = total[0]
    r.kept[4, :32] = total[1]
    r.o_half[...] = r.kept[4 - zh, :32].astype(bf)
    o_step = net.send(r.o_half, r.o_half_land, ("zh",))
    total = r.s_acc[0]
    for k, copy in enumerate(s_steps):
        copy.wait_recv()
        total = total + r.s_land[k]
    r.s_acc[1] = total
    s_step = net.send(r.s_acc.at[1], r.s_land.at[7], ("zh",))
    w_zh.wait_recv()
    r.w_t[...] = (r.gw[zh].astype(f32) + r.w_land[...].astype(f32)).astype(bf)
    w_c = net.send(r.w_t.at[:, 1 - c], r.wp.at[:, c], ("c",))
    r.wp[:, c] = r.w_t[:, c]
    feed_sum(1)
    w_c.wait_recv()
    w_steps = []
    for flips in CHIP_FLIPS:
        w_steps.append(net.send(r.wp.at[net.index(CHIPS, flips)], r.wl.at[my_chip], flips))
    r.wl[my_chip] = r.wp[my_chip]
    s_step.wait_recv()
    r.s_acc[2] = r.s_acc[1] + r.s_land[7]
    s_step = net.send(r.s_acc.at[2], r.s_land.at[8], ("c",))
    y_near[2].wait_recv()
    h_steps[2].wait_recv()
    r.gwdown[...] = r.gwd[zh, y].astype(f32) + r.y_wd[0].astype(f32) + r.h_wd_land[...].astype(f32)
    feed_sibling(0)
    feed_sibling(1)
    n_step.wait_recv()
    r.kept[2 - zh, :64] = r.n_half_land[...].astype(f32)
    for b in range(2):
        value = r.tok[b].astype(f32)
        scale = row_scale(value)
        weighted = r.kept[1 + b, :64] * gain_attn
        mean = jnp.mean(weighted * value, axis=1, keepdims=True)
        back = scale * weighted - value * (scale * scale * scale) * mean
        r.gtok[b] = (r.kept[0, 64 * b : 64 * (b + 1), :] + back).astype(bf)
    for copy in w_steps:
        copy.wait_recv()
    for h in range(16):
        r.gwqkv[:, 192 * h : 192 * (h + 1)] = r.wl[h // 2, h % 2].astype(f32)
    o_step.wait_recv()
    r.gwout[...] = r.kept[3 + zh, :32] + r.o_half_land[...].astype(f32)
    for k, out in ((0, r.gwgate), (1, r.gwup)):
        f_c[k].wait_recv()
        for pair in range(4):
            for cc in range(2):
                for part in range(4):
                    idx = (part // 2) * 16 + pair * 4 + (part % 2) * 2 + cc
                    out[:, 128 * idx : 128 * (idx + 1)] = r.f2[
                        k, pair, cc, :, 128 * part : 128 * (part + 1)
                    ].astype(f32)
    s_step.wait_recv()
    r.gsmall[...] = r.s_acc[2] + r.s_land[8]
    net.drain()


def layer(*arrays):
    sm = pl.BlockSpec(memory_space=pltpu.SMEM)
    vm = pl.BlockSpec(memory_space=pltpu.VMEM)
    outs = layer_outputs()
    return pl.pallas_call(
        layer_kernel,
        out_shape=[jax.ShapeDtypeStruct(*spec) for spec in outs.values()],
        in_specs=[sm, sm] + [vm] * (len(layer_inputs()) - 2),
        out_specs=[vm] * len(outs),
        scratch_shapes=[pltpu.VMEM(*spec) for spec in layer_scratch().values()]
        + [
            pltpu.SemaphoreType.DMA((N_COPIES,)),
            pltpu.SemaphoreType.DMA((N_COPIES,)),
            pltpu.SemaphoreType.DMA((2,)),
        ],
        compiler_params=pltpu.CompilerParams(
            collective_id=1, has_side_effects=True, vmem_limit_bytes=VMEM_BYTES
        ),
        name="layer",
    )(*arrays)


def give_out_kernel(small, *refs):
    n = (len(refs) - 5) // 2
    gains, bias = refs[2 * n : 2 * n + 4], refs[-1]
    for source, dest in zip(refs[:n], refs[n : 2 * n]):
        dest[...] = source[...]
    rank = jnp.int32(0)
    for name in AXES:
        rank = rank * 2 + lax.axis_index(name)
    held = small[rank // 4]
    mine = held
    for k in range(1, 4):
        mine = jnp.where(rank % 4 == k, pltpu.roll(held, 128 - 32 * k, 1), mine)
    for k, gain in enumerate(gains):
        gain[...] = mine[k : k + 1, :32]
    first = small[0]
    bias[0:1, :] = first[4:5, :16]
    bias[1:2, :] = pltpu.roll(first, 112, 1)[4:5, :16]


def give_out(small, *large):
    f32 = jnp.float32
    vm = pl.BlockSpec(memory_space=pltpu.VMEM)
    n = len(large)
    return pl.pallas_call(
        give_out_kernel,
        out_shape=[jax.ShapeDtypeStruct(a.shape, a.dtype) for a in large]
        + [jax.ShapeDtypeStruct((1, 32), f32)] * 4
        + [jax.ShapeDtypeStruct((2, 16), f32)],
        in_specs=[vm] * (n + 1),
        out_specs=[vm] * (n + 5),
        name="give_out",
    )(small, *large)


def frequencies():
    index = np.arange(32, dtype=np.float32)
    return (THETA ** (-2.0 * index / 64.0)).astype(np.float32)[:, None]


def on_device_cube(
    tokens,
    cotangent,
    w_qkv,
    w_out,
    w_gate,
    w_up,
    w_down,
    norm_attn,
    norm_ffn,
    q_gain,
    k_gain,
    var_bias,
    doc_lengths,
    variate,
    times,
):
    results = layer(
        doc_lengths, var_bias.T, tokens, cotangent, w_qkv, w_out, w_gate, w_up, w_down,
        *(gain.reshape(1, 32) for gain in (norm_attn, norm_ffn, q_gain, k_gain)),
        variate, times, jnp.asarray(frequencies()),
    )
    *large, small = results
    out, gtok, gwqkv, gwout, gwgate, gwup, gwdown, *gains, bias = give_out(small, *large)
    return (
        out.reshape(2, 64, 1024),
        gtok,
        gwqkv,
        gwout,
        gwgate,
        gwup,
        gwdown,
        *(gain.reshape(32) for gain in gains),
        bias.T,
    )


def run_parts(mesh, body, split):
    rows, cut = P(split, None), P(split)
    part = P(None, split, None)
    return jax.shard_map(
        body,
        mesh=mesh,
        in_specs=(part, part) + (rows,) * 5 + (cut,) * 4 + (P(), P(), P(None, split), P(None, split)),
        out_specs=(part, part) + (rows,) * 5 + (cut,) * 4 + (P(),),
        check_vma=False,
    )


def solution(mesh):
    sizes = (mesh.shape["head"], mesh.shape["blk"])
    general = run_parts(mesh, on_device, ("head", "blk"))
    if sizes != (8, 4):
        return general
    cube = jax.sharding.Mesh(mesh.devices.reshape(2, 2, 2, 2, 2), AXES)
    special = run_parts(cube, on_device_cube, AXES)

    def chosen(*arrays):
        tokens, w_gate, var_bias, lengths = arrays[0], arrays[4], arrays[11], arrays[12]
        shapes = (tokens.shape, w_gate.shape, var_bias.shape, lengths.shape)
        if shapes == ((2, 2048, 1024), (1024, 4096), (16, 2), (2, 8)):
            return special(*arrays)
        return general(*arrays)

    return chosen
```

```python
import math
from types import SimpleNamespace

import jax
import jax.numpy as jnp
import numpy as np
from jax import lax
from jax.experimental import pallas as pl
from jax.experimental.pallas import tpu as pltpu
from jax.sharding import PartitionSpec as P

EPS = 1e-06
THETA = 10000.0
NEGATIVE = -1e30
KEY_BLOCK = 1024


def inverse_rms(values_in):
    return lax.rsqrt(jnp.mean(values_in * values_in, axis=-1, keepdims=True) + EPS)


def rotate(values_in, time_index, sign_value):
    half_dim = values_in.shape[-1] // 2
    frequency = THETA ** (-2.0 * jnp.arange(half_dim, dtype=jnp.float32) / values_in.shape[-1])
    angles = time_index.astype(jnp.float32)[:, None] * frequency[None, :]
    cosine = jnp.cos(angles)[:, None, :]
    sine_part = sign_value * jnp.sin(angles)[:, None, :]
    first_half = values_in[..., :half_dim]
    second_half = values_in[..., half_dim:]
    return jnp.concatenate(
        [
            first_half * cosine - second_half * sine_part,
            first_half * sine_part + second_half * cosine,
        ],
        axis=-1,
    )


def norm_back(grad_in, value_in, scale_in, gain_in):
    weighted = grad_in * gain_in
    scale_cube = scale_in * scale_in * scale_in
    return scale_in * weighted - value_in * scale_cube * jnp.mean(
        weighted * value_in, axis=-1, keepdims=True
    )


def row_contract(left_mat, right_mat):
    return lax.dot_general(
        left_mat, right_mat, (((0,), (0,)), ((), ())), preferred_element_type=jnp.float32
    )


def col_contract(left_mat, right_mat):
    return lax.dot_general(
        left_mat, right_mat, (((1,), (1,)), ((), ())), preferred_element_type=jnp.float32
    )


def document_of(positions, doc_ends):
    return jnp.sum((positions[:, None] >= doc_ends[None, :]).astype(jnp.int32), axis=1)


def key_positions(first_row, row_total, per_group, row_count, blk_n):
    row_index = first_row + jnp.arange(row_total, dtype=jnp.int32)
    source_blk = row_index // per_group
    within = row_index % per_group
    return (within // row_count * blk_n + source_blk) * row_count + within % row_count


def block_scores(queries, key_part, same_var, same_doc, bias_same, bias_other, att_scale):
    raw_scores = (
        jnp.einsum("qhd,khd->qhk", queries, key_part, preferred_element_type=jnp.float32)
        * att_scale
    )
    bias_terms = jnp.where(
        same_var[:, None, :], bias_same[None, :, None], bias_other[None, :, None]
    )
    return jnp.where(same_doc[:, None, :], raw_scores + bias_terms, NEGATIVE)


def forward_block(
    state_in, queries, key_part, value_part, same_var, same_doc, bias_same, bias_other, att_scale
):
    best_prev, total_prev, accum_prev = state_in
    scores = block_scores(queries, key_part, same_var, same_doc, bias_same, bias_other, att_scale)
    best_next = jnp.maximum(best_prev, jnp.max(scores, axis=-1))
    factor = jnp.exp(best_prev - best_next)
    weights = jnp.where(same_doc[:, None, :], jnp.exp(scores - best_next[..., None]), 0.0)
    total_next = total_prev * factor + jnp.sum(weights, axis=-1)
    accum_next = accum_prev * factor[..., None] + jnp.einsum(
        "qhk,khd->qhd", weights.astype(jnp.bfloat16), value_part, preferred_element_type=jnp.float32
    )
    return (best_next, total_next, accum_next)


def flatten_all(grads_in):
    return tuple((member.reshape(-1) for member in grads_in))


def unflatten_all(flat_in, grads_like):
    return tuple(
        (flat.reshape((-1,) + member.shape[1:]) for flat, member in zip(flat_in, grads_like))
    )


def on_device(
    tokens,
    cotangent,
    w_qkv,
    w_out,
    w_gate,
    w_up,
    w_down,
    norm_attn,
    norm_ffn,
    q_gain,
    k_gain,
    var_bias,
    doc_lengths,
    variate,
    times,
):
    heads_n = lax.axis_size("head")
    blk_n = lax.axis_size("blk")
    head_rank = lax.axis_index("head")
    blk_rank = lax.axis_index("blk")
    batch_count, row_count, model_width = tokens.shape
    head_count = var_bias.shape[0]
    head_dim = model_width // head_count
    local_heads = head_count // heads_n
    query_rows = heads_n * row_count
    key_rows = blk_n * query_rows
    key_block = min(KEY_BLOCK, key_rows)
    block_count = key_rows // key_block
    att_scale = 1.0 / math.sqrt(head_dim)
    gathered = (
        lax.all_gather(w_qkv, ("head", "blk"), axis=0, tiled=True),
        lax.all_gather(w_out, ("head", "blk"), axis=0, tiled=True),
        lax.all_gather(w_gate, ("head", "blk"), axis=0, tiled=True),
        lax.all_gather(w_up, ("head", "blk"), axis=0, tiled=True),
        lax.all_gather(w_down, ("head", "blk"), axis=0, tiled=True),
        lax.all_gather(norm_attn, ("head", "blk"), axis=0, tiled=True),
        lax.all_gather(norm_ffn, ("head", "blk"), axis=0, tiled=True),
        lax.all_gather(q_gain, ("head", "blk"), axis=0, tiled=True),
        lax.all_gather(k_gain, ("head", "blk"), axis=0, tiled=True),
    )
    wqkv_all, wout_all, wgate_all, wup_all, wdown_all = gathered[:5]
    gain_attn = gathered[5].astype(jnp.float32)
    gain_ffn = gathered[6].astype(jnp.float32)
    gain_query = gathered[7].astype(jnp.float32).reshape(head_count, head_dim)
    gain_key = gathered[8].astype(jnp.float32).reshape(head_count, head_dim)
    local_bias = lax.dynamic_slice_in_dim(var_bias, head_rank * local_heads, local_heads, 0)
    bias_same = local_bias[:, 0]
    bias_other = local_bias[:, 1]
    query_index = jnp.arange(query_rows, dtype=jnp.int32)
    query_pos = (query_index // row_count * blk_n + blk_rank) * row_count + query_index % row_count
    ends_all = jnp.cumsum(doc_lengths, axis=1)
    outputs_list = []
    inputs_list = []
    totals = None
    bias_accum = jnp.zeros((local_heads, 2), jnp.float32)
    for batch_id in range(batch_count):
        doc_ends = ends_all[batch_id]
        time_row = times[batch_id]
        inputs_f = tokens[batch_id].astype(jnp.float32)
        scale_one = inverse_rms(inputs_f)
        normed_one = (inputs_f * scale_one * gain_attn).astype(jnp.bfloat16)
        qkv_all = jnp.dot(normed_one, wqkv_all, preferred_element_type=jnp.float32).reshape(
            row_count, head_count, 3 * head_dim
        )
        query_raw = qkv_all[..., :head_dim]
        key_raw = qkv_all[..., head_dim : 2 * head_dim]
        value_raw = qkv_all[..., 2 * head_dim :]
        query_scale = inverse_rms(query_raw)
        key_scale = inverse_rms(key_raw)
        query_rot = rotate(query_raw * query_scale * gain_query, time_row, 1.0)
        key_rot = rotate(key_raw * key_scale * gain_key, time_row, 1.0)
        packed = jnp.concatenate([query_rot, key_rot, value_raw], axis=-1).astype(jnp.bfloat16)
        variate_rep = jnp.broadcast_to(
            variate[batch_id].astype(jnp.bfloat16)[:, None], (row_count, head_count)
        )
        packed_heads, variate_heads = (
            lax.all_to_all(packed, "head", split_axis=1, concat_axis=0, tiled=True),
            lax.all_to_all(variate_rep, "head", split_axis=1, concat_axis=0, tiled=True),
        )
        queries = packed_heads[..., :head_dim]
        key_values = packed_heads[..., head_dim:]
        query_var = variate_heads[:, 0]
        query_doc = document_of(query_pos, doc_ends)
        initial = (
            jnp.full((query_rows, local_heads), NEGATIVE, jnp.float32),
            jnp.zeros((query_rows, local_heads), jnp.float32),
            jnp.zeros((query_rows, local_heads, head_dim), jnp.float32),
        )
        kv_piece = lax.all_gather(key_values, "blk", axis=0, tiled=True)
        var_piece = lax.all_gather(query_var, "blk", axis=0, tiled=True)
        piece_rows = kv_piece.shape[0]

        def one_block(state_blk, kv_block, var_block, block_start):
            key_doc = document_of(
                key_positions(block_start, kv_block.shape[0], query_rows, row_count, blk_n),
                doc_ends,
            )
            same_doc = query_doc[:, None] == key_doc[None, :]
            same_var = query_var[:, None] == var_block[None, :]
            return forward_block(
                state_blk,
                queries,
                kv_block[..., :head_dim],
                kv_block[..., head_dim:],
                same_var,
                same_doc,
                bias_same,
                bias_other,
                att_scale,
            )

        def loop_step(turn_index, state_loop):
            kv_block = lax.dynamic_slice_in_dim(kv_piece, turn_index * key_block, key_block, 0)
            var_block = lax.dynamic_slice_in_dim(var_piece, turn_index * key_block, key_block, 0)
            return one_block(state_loop, kv_block, var_block, turn_index * key_block)

        attn_state = lax.fori_loop(0, piece_rows // key_block, loop_step, initial)
        best_score, total_weight, accum = attn_state
        attn_heads = accum / total_weight[..., None]
        log_total = best_score + jnp.log(total_weight)
        attn_tok = lax.all_to_all(
            attn_heads.astype(jnp.bfloat16), "head", split_axis=0, concat_axis=1, tiled=True
        ).reshape(row_count, model_width)
        resid_one = inputs_f + jnp.dot(attn_tok, wout_all, preferred_element_type=jnp.float32)
        scale_two = inverse_rms(resid_one)
        normed_two = (resid_one * scale_two * gain_ffn).astype(jnp.bfloat16)
        gate_pre = jnp.dot(normed_two, wgate_all, preferred_element_type=jnp.float32)
        up_pre = jnp.dot(normed_two, wup_all, preferred_element_type=jnp.float32)
        sigmoid_gate = jax.nn.sigmoid(gate_pre)
        silu_gate = gate_pre * sigmoid_gate
        hidden_act = (silu_gate * up_pre).astype(jnp.bfloat16)
        result = resid_one + jnp.dot(hidden_act, wdown_all, preferred_element_type=jnp.float32)
        outputs_list.append(result.astype(jnp.bfloat16))
        grad_out = cotangent[batch_id].astype(jnp.float32)
        grad_ffn = grad_out.astype(jnp.bfloat16)
        grad_down = row_contract(hidden_act, grad_ffn)
        grad_hidden = col_contract(grad_ffn, wdown_all)
        grad_gate = (
            grad_hidden * up_pre * sigmoid_gate * (1.0 + gate_pre * (1.0 - sigmoid_gate))
        ).astype(jnp.bfloat16)
        grad_up = (grad_hidden * silu_gate).astype(jnp.bfloat16)
        grad_wgate = row_contract(normed_two, grad_gate)
        grad_wup = row_contract(normed_two, grad_up)
        grad_normed = col_contract(grad_gate, wgate_all) + col_contract(grad_up, wup_all)
        grad_gffn = jnp.sum(grad_normed * resid_one * scale_two, axis=0)
        grad_resid = grad_out + norm_back(grad_normed, resid_one, scale_two, gain_ffn)
        grad_branch = grad_resid.astype(jnp.bfloat16)
        grad_wout = row_contract(attn_tok, grad_branch)
        grad_attn = (
            col_contract(grad_branch, wout_all)
            .astype(jnp.bfloat16)
            .reshape(row_count, head_count, head_dim)
        )
        grad_heads = lax.all_to_all(grad_attn, "head", split_axis=1, concat_axis=0, tiled=True)
        delta_row = jnp.sum(grad_heads.astype(jnp.float32) * attn_heads, axis=-1)
        keys_all, key_var_all = (
            lax.all_gather(key_values, "blk", axis=0, tiled=True),
            lax.all_gather(query_var, "blk", axis=0, tiled=True),
        )
        keys_blocks = keys_all.reshape(block_count, key_block, local_heads, 2 * head_dim)
        var_blocks = key_var_all.reshape(block_count, key_block)
        block_starts = jnp.arange(block_count, dtype=jnp.int32) * key_block

        def back_step(carry_back, block_in):
            grad_query, bias_grad = carry_back
            kv_block, var_block, block_start = block_in
            key_doc = document_of(
                key_positions(block_start, key_block, query_rows, row_count, blk_n), doc_ends
            )
            same_doc = query_doc[:, None] == key_doc[None, :]
            same_var = query_var[:, None] == var_block[None, :]
            key_part = kv_block[..., :head_dim]
            value_part = kv_block[..., head_dim:]
            scores = block_scores(
                queries, key_part, same_var, same_doc, bias_same, bias_other, att_scale
            )
            probs = jnp.where(same_doc[:, None, :], jnp.exp(scores - log_total[..., None]), 0.0)
            grad_probs = jnp.einsum(
                "qhd,khd->qhk", grad_heads, value_part, preferred_element_type=jnp.float32
            )
            grad_scores = (probs * (grad_probs - delta_row[..., None])).astype(jnp.bfloat16)
            grad_scores_f = grad_scores.astype(jnp.float32)
            same_sum = jnp.sum(jnp.where(same_var[:, None, :], grad_scores_f, 0.0), axis=(0, 2))
            other_sum = jnp.sum(jnp.where(same_var[:, None, :], 0.0, grad_scores_f), axis=(0, 2))
            bias_grad = bias_grad + jnp.stack([same_sum, other_sum], axis=-1)
            grad_query = grad_query + att_scale * jnp.einsum(
                "qhk,khd->qhd", grad_scores, key_part, preferred_element_type=jnp.float32
            )
            grad_key = att_scale * jnp.einsum(
                "qhk,qhd->khd", grad_scores, queries, preferred_element_type=jnp.float32
            )
            grad_value = jnp.einsum(
                "qhk,qhd->khd",
                probs.astype(jnp.bfloat16),
                grad_heads,
                preferred_element_type=jnp.float32,
            )
            return ((grad_query, bias_grad), jnp.concatenate([grad_key, grad_value], axis=-1))

        carry_start = (
            jnp.zeros((query_rows, local_heads, head_dim), jnp.float32),
            jnp.zeros((local_heads, 2), jnp.float32),
        )
        (grad_query, bias_part), grad_kv_parts = lax.scan(
            back_step, carry_start, (keys_blocks, var_blocks, block_starts)
        )
        bias_accum = bias_accum + bias_part
        grad_kv_own = lax.psum_scatter(
            grad_kv_parts.reshape(key_rows, local_heads, 2 * head_dim).astype(jnp.bfloat16),
            "blk",
            scatter_dimension=0,
            tiled=True,
        )
        grad_packed = jnp.concatenate([grad_query.astype(jnp.bfloat16), grad_kv_own], axis=-1)
        grad_tok = lax.all_to_all(
            grad_packed, "head", split_axis=0, concat_axis=1, tiled=True
        ).astype(jnp.float32)
        grad_qrot = rotate(grad_tok[..., :head_dim], time_row, -1.0)
        grad_krot = rotate(grad_tok[..., head_dim : 2 * head_dim], time_row, -1.0)
        grad_gquery = jnp.sum(grad_qrot * query_raw * query_scale, axis=0)
        grad_gkey = jnp.sum(grad_krot * key_raw * key_scale, axis=0)
        grad_qraw = norm_back(grad_qrot, query_raw, query_scale, gain_query)
        grad_kraw = norm_back(grad_krot, key_raw, key_scale, gain_key)
        grad_qkv = (
            jnp.concatenate([grad_qraw, grad_kraw, grad_tok[..., 2 * head_dim :]], axis=-1)
            .reshape(row_count, 3 * model_width)
            .astype(jnp.bfloat16)
        )
        grad_wqkv = row_contract(normed_one, grad_qkv)
        grad_normed_one = col_contract(grad_qkv, wqkv_all)
        grad_gattn = jnp.sum(grad_normed_one * inputs_f * scale_one, axis=0)
        grad_in = grad_resid + norm_back(grad_normed_one, inputs_f, scale_one, gain_attn)
        inputs_list.append(grad_in.astype(jnp.bfloat16))
        batch_grads = (
            grad_wqkv,
            grad_wout,
            grad_wgate,
            grad_wup,
            grad_down,
            grad_gattn,
            grad_gffn,
            grad_gquery.reshape(model_width),
            grad_gkey.reshape(model_width),
        )
        if totals is None:
            totals = batch_grads
        else:
            totals = tuple(
                (first_term + second_term for first_term, second_term in zip(totals, batch_grads))
            )
    flat_totals = flatten_all(totals)
    summed_flat = (
        lax.psum_scatter(flat_totals[0], ("head", "blk"), scatter_dimension=0, tiled=True),
        lax.psum_scatter(flat_totals[1], ("head", "blk"), scatter_dimension=0, tiled=True),
        lax.psum_scatter(flat_totals[2], ("head", "blk"), scatter_dimension=0, tiled=True),
        lax.psum_scatter(flat_totals[3], ("head", "blk"), scatter_dimension=0, tiled=True),
        lax.psum_scatter(flat_totals[4], ("head", "blk"), scatter_dimension=0, tiled=True),
        lax.psum_scatter(flat_totals[5], ("head", "blk"), scatter_dimension=0, tiled=True),
        lax.psum_scatter(flat_totals[6], ("head", "blk"), scatter_dimension=0, tiled=True),
        lax.psum_scatter(flat_totals[7], ("head", "blk"), scatter_dimension=0, tiled=True),
        lax.psum_scatter(flat_totals[8], ("head", "blk"), scatter_dimension=0, tiled=True),
    )
    totals = unflatten_all(summed_flat, totals)
    bias_full = lax.dynamic_update_slice_in_dim(
        jnp.zeros((head_count, 2), jnp.float32), bias_accum, head_rank * local_heads, 0
    )
    grad_bias = lax.psum(bias_full, ("head", "blk"))
    return (
        jnp.stack(outputs_list),
        jnp.stack(inputs_list),
        totals[0],
        totals[1],
        totals[2],
        totals[3],
        totals[4],
        totals[5],
        totals[6],
        totals[7],
        totals[8],
        grad_bias,
    )


AXES = ("zh", "zl", "x", "y", "c")
CHIPS = ("zl", "x", "y")
VMEM_BYTES = 63 * 2**20
ROW_BLOCK = 256
SPAN = 512
LAST = (((1,), (1,)), ((), ()))
FIRST = (((0,), (0,)), ((), ()))
CHIP_FLIPS = [
    tuple(a for a, bit in zip(CHIPS, ((m >> 2) & 1, (m >> 1) & 1, m & 1)) if bit)
    for m in range(1, 8)
]
GROUP_FLIPS = [("zl",), ("x",), ("zl", "x")]


class Net:
    def __init__(self, send_sems, recv_sems, local_sems):
        self.me = {name: lax.axis_index(name) for name in AXES}
        self.send_sems, self.recv_sems, self.local_sems = send_sems, recv_sems, local_sems
        self.used = 0
        self.local_used = 0
        self.open = []

    def target(self, flips):
        return tuple(1 - self.me[a] if a in flips else self.me[a] for a in AXES)

    def index(self, names, flips=()):
        total = 0
        for a in names:
            total = total * 2 + (1 - self.me[a] if a in flips else self.me[a])
        return total

    def barrier(self, partners):
        sem = pltpu.get_barrier_semaphore()
        for flips in partners:
            pl.semaphore_signal(
                sem, inc=1, device_id=self.target(flips), device_id_type=pl.DeviceIdType.MESH
            )
        pl.semaphore_wait(sem, len(partners))

    def send(self, source, dest, flips):
        copy = pltpu.make_async_remote_copy(
            src_ref=source,
            dst_ref=dest,
            send_sem=self.send_sems.at[self.used],
            recv_sem=self.recv_sems.at[self.used],
            device_id=self.target(flips),
            device_id_type=pl.DeviceIdType.MESH,
        )
        self.used += 1
        copy.start()
        self.open.append(copy)
        return copy

    def local(self, source, dest):
        copy = pltpu.make_async_copy(source, dest, self.local_sems.at[self.local_used])
        self.local_used += 1
        copy.start()
        return copy

    def settle(self, copies):
        for copy in copies:
            copy.wait_send()
        gone = [id(copy) for copy in copies]
        self.open = [copy for copy in self.open if id(copy) not in gone]

    def drain(self):
        for copy in self.open:
            copy.wait_send()
        self.open = []


class Gather:
    def __init__(self, net, region, dims):
        self.net, self.region, self.dims = net, region, dims
        self.arrive = {}
        self.sibling = {}

    def key(self, flips):
        return tuple(sorted(flips))

    def push(self, flips, source=None):
        source = self.region(flips) if source is None else source
        level = max([self.dims.index(a) for a in flips], default=-1)
        for d in self.dims[level + 1 :]:
            copy = self.net.send(source, self.region(flips), (d,))
            self.arrive[self.key(flips + (d,))] = copy
        self.sibling[self.key(flips)] = self.net.send(source, self.region(flips), ("c",))

    def take(self, *flips):
        self.arrive[self.key(flips)].wait_recv()
        self.push(flips)

    def ready(self, *flips):
        self.sibling[self.key(flips)].wait_recv()


class Reduce:
    def __init__(self, net, dims, part, land, send, arrive):
        self.net, self.dims = net, dims
        self.part, self.land, self.send_slot, self.arrive = part, land, send, arrive
        self.from_sibling, self.incoming = {}, {}
        a, b, d = dims
        self.masks = [(a, b, d), (a, b), (a, d), (a,), (b, d), (b,), (d,), ()]
        self.slots = {}
        for rest in [(b, d), (b,), (d,), ()]:
            self.slots[rest, a] = len(self.slots)
        for rest in [(d,), ()]:
            self.slots[rest, b] = len(self.slots)
        self.slots[(), d] = len(self.slots)

    def ordered(self, flips):
        return tuple(a for a in self.dims if a in flips)

    def begin(self, flips):
        mask = self.ordered(flips)
        self.from_sibling[mask] = self.net.send(
            self.part(mask, 1 - self.net.me["c"]), self.land(self.masks.index(mask)), ("c",)
        )

    def total(self, mask, before):
        value = self.part(mask, self.net.me["c"])[...].astype(jnp.float32)
        value = value + self.land(self.masks.index(mask))[...].astype(jnp.float32)
        for stage in before:
            value = value + self.arrive(self.slots[mask, stage])[...].astype(jnp.float32)
        return value

    def settle(self, mask, before):
        self.from_sibling[mask].wait_recv()
        for stage in before:
            self.incoming[mask, stage].wait_recv()
        return self.total(mask, before)

    def forward(self, flips):
        mask = self.ordered(flips)
        stage, rest = mask[0], mask[1:]
        value = self.settle(mask, self.dims[: self.dims.index(stage)])
        slot = self.slots[rest, stage]
        self.send_slot(slot)[...] = value.astype(jnp.bfloat16)
        self.incoming[rest, stage] = self.net.send(
            self.send_slot(slot), self.arrive(slot), (stage,)
        )

    def result(self):
        return self.settle((), self.dims)


def lane_iota(rows, lanes=128):
    return lax.broadcasted_iota(jnp.int32, (rows, lanes), 1)


def pieces(value):
    first = value.astype(jnp.bfloat16).astype(jnp.float32)
    second = (value - first).astype(jnp.bfloat16).astype(jnp.float32)
    return first, second, value - first - second


def swap_halves(values):
    lane = lane_iota(values.shape[0])
    return jnp.where(lane % 64 < 32, pltpu.roll(values, 96, 1), pltpu.roll(values, 32, 1))


def pair_mean(values):
    lane = lane_iota(values.shape[0])
    low = jnp.sum(jnp.where(lane < 64, values, 0.0), axis=1, keepdims=True)
    high = jnp.sum(jnp.where(lane < 64, 0.0, values), axis=1, keepdims=True)
    return jnp.where(lane < 64, low, high) * (1.0 / 64.0)


def angles_of(packed):
    lane = lane_iota(packed.shape[0])
    turned = pltpu.roll(packed, 64, 1)
    return jnp.where(lane < 64, packed, turned), jnp.where(lane < 64, turned, packed)


def row_scale(value):
    return lax.rsqrt(jnp.mean(value * value, axis=1, keepdims=True) + EPS)


def layer_inputs():
    return ["lengths", "bias", "tok", "cot", "wqkv", "wout", "wgate", "wup", "wdown"] + [
        "norm_attn", "norm_ffn", "q_gain", "k_gain", "variate", "times", "freq",
    ]


def layer_outputs():
    bf, f32 = jnp.bfloat16, jnp.float32
    return {
        "out": ((128, 1024), bf),
        "gtok": ((2, 64, 1024), bf),
        "gwqkv": ((32, 3072), f32),
        "gwout": ((32, 1024), f32),
        "gwgate": ((32, 4096), f32),
        "gwup": ((32, 4096), f32),
        "gwdown": ((128, 1024), f32),
        "gsmall": ((8, 8, 128), f32),
    }


def layer_scratch():
    bf, f32 = jnp.bfloat16, jnp.float32
    return {
        "x": ((32, 64, 1024), bf),
        "wp": ((8, 2, 32, 192), bf),
        "wl": ((8, 2, 32, 192), bf),
        "wh": ((2, 8, 2, 32, 192), bf),
        "gp": ((4, 2, 2, 32, 512), bf),
        "gl": ((4, 2, 2, 32, 512), bf),
        "wgu": ((2, 2, 4, 2, 2, 32, 512), bf),
        "wd": ((2, 2, 128, 1024), bf),
        "wo": ((2, 16, 32, 1024), bf),
        "gf": ((8, 2, 64, 1024), bf),
        "tile": ((8, 128), f32),
        "sm": ((2, 2, 2, 2, 2, 8, 128), f32),
        "gain_s": ((4, 8, 128), f32),
        "feat": ((2048, 128), f32),
        "cs": ((2048, 128), f32),
        "raw": ((2048, 128), f32),
        "kept_o": ((2048, 128), f32),
        "qf": ((2048, 128), bf),
        "kf": ((2048, 128), bf),
        "vf": ((2048, 128), bf),
        "att": ((16, 2, 64, 64), bf),
        "lb": ((16, 64, 64), bf),
        "ap": ((2, 8, 64, 128), bf),
        "at2": ((2, 8, 64, 128), bf),
        "att_s": ((128, 1024), bf),
        "resid": ((128, 1024), f32),
        "n2": ((8, 2, 64, 1024), bf),
        "gate": ((4, 256, 512), f32),
        "up": ((4, 256, 512), f32),
        "hid": ((4, 256, 512), bf),
        "ggu": ((2, 4, 256, 512), bf),
        "kept": ((8, 128, 1024), f32),
        "sent": ((8, 2, 64, 1024), bf),
        "landed": ((8, 2, 64, 1024), bf),
        "red_send": ((2, 3, 128, 1024), bf),
        "red_land": ((2, 3, 128, 1024), bf),
        "branch": ((128, 1024), bf),
        "ga3": ((2, 8, 64, 128), bf),
        "ag1": ((2, 8, 64, 128), bf),
        "gatt": ((16, 2, 64, 64), bf),
        "gwgu": ((2, 2, 4, 2, 64, 512), bf),
        "gwd": ((2, 2, 128, 1024), bf),
        "gwo": ((2, 8, 2, 32, 1024), bf),
        "gb": ((2048, 128), bf),
        "gq": ((2048, 128), bf),
        "gw": ((2, 8, 2, 32, 192), bf),
        "bias_s": ((8, 128), f32),
        "sums": ((8, 1024), f32),
        "n_half": ((64, 1024), bf),
        "n_half_land": ((64, 1024), bf),
        "o_arr": ((7, 2, 32, 1024), bf),
        "o_half": ((32, 1024), bf),
        "o_half_land": ((32, 1024), bf),
        "y_wgu": ((2, 2, 4, 64, 512), bf),
        "y_wd": ((2, 128, 1024), bf),
        "h_wgu": ((2, 4, 64, 512), bf),
        "h_wd": ((128, 1024), bf),
        "h_wgu_land": ((2, 4, 64, 512), bf),
        "h_wd_land": ((128, 1024), bf),
        "f2": ((2, 4, 2, 32, 512), bf),
        "w_land": ((8, 2, 32, 192), bf),
        "w_t": ((8, 2, 32, 192), bf),
        "s_acc": ((3, 8, 8, 128), f32),
        "s_land": ((9, 8, 8, 128), f32),
    }


N_COPIES = 232


def layer_kernel(*refs):
    names = layer_inputs() + list(layer_outputs()) + list(layer_scratch())
    r = SimpleNamespace(**dict(zip(names, refs)))
    send_sems, recv_sems, local_sems = refs[len(names) :]
    bf, f32 = jnp.bfloat16, jnp.float32
    net = Net(send_sems, recv_sems, local_sems)
    zh, zl, x, y, c = (net.me[a] for a in AXES)
    mine, in_half = net.index(AXES), net.index(AXES[1:])
    my_chip, my_pair = net.index(CHIPS), net.index(("zl", "x"))
    head = in_half
    far_flips = [("zh",) + flips for flips in [()] + CHIP_FLIPS]
    net.barrier(CHIP_FLIPS + [("c",)] + far_flips)

    def x_region(part):
        def region(flips):
            return r.x.at[(zh if part == 0 else 1 - zh) * 16 + net.index(AXES[1:], flips)]

        return region

    x_own = Gather(net, x_region(0), ("zl", "y", "x"))
    x_far = Gather(net, x_region(1), ("zl", "x", "y"))
    wo_tree = Gather(net, lambda f: r.wo.at[:, net.index(AXES[1:], f)], ("zl", "y", "x"))
    gf_tree = Gather(net, lambda f: r.gf.at[net.index(("zl", "x", "c"), f)], ("zl", "x"))
    r.tile[...] = jnp.zeros_like(r.tile)
    r.tile[0:2, 0:64] = r.variate[...].astype(f32)
    r.tile[2:4, 0:64] = r.times[...].astype(f32)
    for k, gain in enumerate((r.norm_attn, r.norm_ffn, r.q_gain, r.k_gain)):
        r.tile[4 + k : 5 + k, 0:32] = gain[...].astype(f32)
    sm_step = net.send(r.tile, r.sm.at[zh, zl, x, y, c], ("zh",))
    swap = net.send(r.tok.at[1 - zh], r.x.at[mine], ("zh",))
    for h in range(16):
        r.wp[h // 2, h % 2] = r.wqkv[:, 192 * h : 192 * (h + 1)]
    w_arrive = []
    for flips in CHIP_FLIPS:
        w_arrive.append(net.send(r.wp.at[net.index(CHIPS, flips)], r.wl.at[my_chip], flips))
    x_own.push((), r.tok.at[zh])
    for pair in range(4):
        for cc in range(2):
            for part in range(4):
                idx = (part // 2) * 16 + pair * 4 + (part % 2) * 2 + cc
                col, lane = 128 * idx, 128 * part
                r.gp[pair, 0, cc, :, lane : lane + 128] = r.wgate[:, col : col + 128]
                r.gp[pair, 1, cc, :, lane : lane + 128] = r.wup[:, col : col + 128]

    def g_send(flips):
        return net.send(r.gp.at[net.index(("zl", "x"), flips)], r.gl.at[my_pair], flips)

    g_arrive = [g_send(("x",))]
    wd_y = net.send(r.wdown, r.wd.at[zh, y], ("y",))
    r.sm[zh, zl, x, y, c] = r.tile[...]
    r.wl[my_chip] = r.wp[my_chip]
    r.x[mine] = r.tok[zh]
    r.gl[my_pair] = r.gp[my_pair]
    r.gf[net.index(("zl", "x", "c"))] = r.cot[...]
    r.wd[zh, y] = r.wdown[...]
    r.wo[zh, in_half] = r.wout[...]

    sm_step.wait_recv()
    sm_step = net.send(r.sm.at[:, zl, x, y, c], r.sm.at[:, zl, x, y, c], ("x",))
    for copy in w_arrive:
        copy.wait_recv()
    w_c = net.send(r.wl.at[:, 1 - c], r.wh.at[zh, :, c], ("c",))
    r.wh[zh, :, c] = r.wl[:, c]
    sm_step.wait_recv()
    sm_step = net.send(r.sm.at[:, zl, :, y, c], r.sm.at[:, zl, :, y, c], ("y",))
    x_own.take("zl")
    x_own.take("y")
    w_c.wait_recv()
    swap.wait_recv()
    x_far.push(())
    w_zh = net.send(r.wh.at[zh], r.wh.at[zh], ("zh",))
    sm_step.wait_recv()
    sm_step = net.send(r.sm.at[:, zl, :, :, c], r.sm.at[:, zl, :, :, c], ("zl",))
    g_arrive += [g_send(("zl",)), g_send(("zl", "x"))]
    wo_zh = net.send(r.wout, r.wo.at[zh, in_half], ("zh",))
    x_own.take("zl", "y")
    x_own.take("x")
    x_far.take("zl")
    sm_step.wait_recv()
    sm_step = net.send(r.sm.at[:, :, :, :, c], r.sm.at[:, :, :, :, c], ("c",))

    def g_piece(k, half):
        return r.wgu.at[k // 2, half, pl.ds(2 * (k % 2), 2), y]

    g_c, g_zh, g_y, g_fwd = [], [], [], []

    x_far.take("x")
    x_own.take("zl", "x")
    x_own.take("y", "x")
    x_far.take("y")
    sm_step.wait_recv()

    lane8 = lane_iota(8)
    for group in range(8):
        for which in range(4):
            row = jnp.zeros((8, 128), f32)
            for j in range(4):
                block = 4 * group + j
                held = r.sm[
                    block // 16, (block // 8) % 2, (block // 4) % 2, (block // 2) % 2, block % 2
                ]
                moved = held if j == 0 else pltpu.roll(held, 32 * j, 1)
                row = jnp.where(lane8 // 32 == j, moved, row)
            r.gain_s[which, group : group + 1] = row[4 + which : 5 + which, :]
    gain_attn = jnp.concatenate([r.gain_s[0, k : k + 1] for k in range(8)], axis=1)
    gain_ffn = jnp.concatenate([r.gain_s[1, k : k + 1] for k in range(8)], axis=1)
    held_q = r.gain_s[2, pl.ds(my_chip, 1)]
    held_k = r.gain_s[3, pl.ds(my_chip, 1)]
    wide_q, wide_k = jnp.broadcast_to(held_q, (8, 128)), jnp.broadcast_to(held_k, (8, 128))
    wide_q = jnp.where(c == 0, wide_q, pltpu.roll(wide_q, 64, 1))
    wide_k = jnp.where(c == 0, pltpu.roll(wide_k, 64, 1), wide_k)
    qk_gain = jnp.where(lane8 < 64, wide_q, wide_k)[0:1, :]

    starts, ends, total = [], [], jnp.int32(0)
    for j in range(8):
        starts.append(total)
        total = total + r.lengths[zh, j]
        ends.append(total)
    sub = lax.broadcasted_iota(jnp.int32, (8, 128), 0)
    start_col = jnp.zeros((8, 128), jnp.int32)
    end_col = jnp.zeros((8, 128), jnp.int32)
    for j in range(8):
        start_col = jnp.where(sub == j, starts[j], start_col)
        end_col = jnp.where(sub == j, ends[j], end_col)
    same_bias = jnp.full((8, 128), r.bias[0, head], f32)
    other_bias = jnp.full((8, 128), r.bias[1, head], f32)
    diff_parts = pieces(same_bias - other_bias)
    zero = jnp.zeros((8, 128), f32)
    const_q = jnp.where(sub == 0, -256.0, 0.0)
    for i, part in enumerate(pieces(other_bias)):
        const_q = jnp.where(sub == i + 1, part, const_q)
    const_k = jnp.where(sub < 4, 1.0, 0.0)
    ones_k = jnp.where(sub < 3, 1.0, 0.0)

    @pl.loop(0, 16)
    def _(i):
        col = pl.ds(pl.multiple_of(i * 128, 128), 128)
        low = r.sm[i // 8, (i // 4) % 2, (i // 2) % 2, i % 2, 0]
        high = r.sm[i // 8, (i // 4) % 2, (i // 2) % 2, i % 2, 1]
        both = jnp.where(lane8 < 64, low, pltpu.roll(high, 64, 1))
        var_row = jnp.where(zh == 0, both[0:1, :], both[1:2, :])
        time_row = jnp.where(zh == 0, both[2:3, :], both[3:4, :])
        pos = lane8 + i * 128
        doc = jnp.where((pos >= start_col) & (pos < end_col), 1.0, 0.0)
        var = jnp.where(jnp.broadcast_to(var_row, (8, 128)) == sub.astype(f32), 1.0, 0.0)
        rows = [doc * 256.0, const_q] + [var * part for part in diff_parts] + [zero, zero, zero]
        rows += [doc, const_k, var, var, var, ones_k, zero, zero]
        r.feat[col, :] = jnp.concatenate(rows, axis=0).T
        angle = jnp.broadcast_to(time_row, (32, 128)) * jnp.broadcast_to(r.freq[...], (32, 128))
        cosine, sine = jnp.cos(angle), jnp.sin(angle)
        r.cs[col, :] = jnp.concatenate([cosine, cosine, -sine, sine], axis=0).T

    x_own.take("zl", "y", "x")
    x_far.take("zl", "y")
    x_far.take("zl", "x")
    for copy in g_arrive:
        copy.wait_recv()
    for k in range(2):
        g_c.append(net.send(r.gl.at[:, k, 1 - c], r.wgu.at[k, zh, :, y, c], ("c",)))
        r.wgu[k, zh, :, y, c] = r.gl[:, k, c]
    wo_zh.wait_recv()
    wo_tree.push(())
    for k in range(4):
        if k % 2 == 0:
            g_c[k // 2].wait_recv()
        g_zh.append(net.send(g_piece(k, zh), g_piece(k, zh), ("zh",)))
    for k in range(4):
        g_y.append(net.send(g_piece(k, zh), g_piece(k, zh), ("y",)))
    gf_tree.push((), r.cot)

    lane = lane_iota(ROW_BLOCK)

    def arrived(part, *flips):
        tree = x_own if part == 0 else x_far
        tree.ready(*flips)
        tree.ready(*(flips + ("y",)))

    def project(j):
        part, far_x, far_zl = j // 4, (j // 2) % 2, j % 2
        at = ((zh + part - 2 * zh * part) * 2 + zl + far_zl - 2 * zl * far_zl) * 2
        at = (at + x + far_x - 2 * x * far_x) * ROW_BLOCK
        row = pl.ds(pl.multiple_of(at, ROW_BLOCK), ROW_BLOCK)
        blocks = pl.ds(at // 64, 4)
        value = r.x[blocks].reshape(ROW_BLOCK, 1024).astype(f32)
        normed = (value * row_scale(value) * gain_attn).astype(bf)
        qkv = jnp.dot(normed, r.wh[...].reshape(1024, 192), preferred_element_type=f32)
        raw = qkv[:, :128]
        r.raw[row, :] = raw
        scaled = raw * lax.rsqrt(pair_mean(raw * raw) + EPS) * qk_gain
        cosine, sine = angles_of(r.cs[row, :])
        turned = (scaled * cosine + swap_halves(scaled) * sine).astype(bf).astype(f32)
        marks = r.feat[row, :]
        r.qf[row, :] = jnp.where(lane < 64, turned * 0.125, pltpu.roll(marks, 64, 1)).astype(bf)
        r.kf[row, :] = jnp.where(lane < 64, pltpu.roll(turned, 64, 1), marks).astype(bf)
        third = jnp.concatenate([qkv[:, 128:192], jnp.zeros((ROW_BLOCK, 64), f32)], axis=1)
        r.vf[row, :] = jnp.where((lane >= 64) & (lane < 67), 1.0, third).astype(bf)

    w_zh.wait_recv()
    arrived(0)
    arrived(0, "zl")
    arrived(0, "x")
    arrived(0, "zl", "x")
    pl.loop(0, 4)(project)
    x_far.take("x", "y")
    x_far.take("zl", "x", "y")
    arrived(1)
    arrived(1, "zl")
    arrived(1, "x")
    arrived(1, "zl", "x")
    pl.loop(4, 8)(project)
    wo_tree.take("zl")

    lane_span = lane_iota(SPAN)

    def attend(i):
        row = pl.ds(pl.multiple_of(i * SPAN, SPAN), SPAN)
        query = r.qf[row, :]

        def one_chunk(k, total):
            col = pl.ds(pl.multiple_of(k * SPAN, SPAN), SPAN)
            scores = lax.dot_general(query, r.kf[col, :], LAST, preferred_element_type=f32)
            weights = jnp.exp(scores).astype(bf)
            return total + jnp.dot(weights, r.vf[col, :], preferred_element_type=f32)

        total = lax.fori_loop(0, 2048 // SPAN, one_chunk, jnp.zeros((SPAN, 128), f32))
        weight = total[:, 64:65]
        result = total / weight
        r.kept_o[row, :] = jnp.where(lane_span < 64, result, jnp.log(weight))
        r.att[pl.ds(4 * i, 4)] = result[:, :64].astype(bf).reshape(4, 2, 64, 64)

    def g_pass(k):
        g_zh[k].wait_recv()
        g_fwd.append(net.send(g_piece(k, 1 - zh), g_piece(k, 1 - zh), ("y",)))

    pl.loop(0, 2)(attend)
    wo_tree.take("y")
    pl.loop(2, 4)(attend)

    step = net.send(r.att.at[:, 1 - c], r.lb, ("c",))
    wo_tree.take("zl", "y")
    g_pass(0)
    g_pass(1)
    step.wait_recv()
    lane64 = lane_iota(64)

    @pl.loop(0, 16)
    def _(i):
        own = jnp.concatenate([r.att[i, c]] * 2, axis=1)
        other = jnp.concatenate([r.lb[i]] * 2, axis=1)
        r.ap[i // 8, i % 8] = jnp.where((lane64 < 64) == (c == 0), own, other)

    arrive = []
    for flips in far_flips + CHIP_FLIPS:
        z_part = 1 - zh if "zh" in flips else zh
        arrive.append(
            net.send(r.ap.at[z_part, net.index(CHIPS, flips)], r.at2.at[zh, my_chip], flips)
        )
    r.at2[zh, my_chip] = r.ap[zh, my_chip]

    def w_down():
        return r.wd[...].reshape(512, 1024)

    def w_o():
        return r.wo[...].reshape(1024, 1024)

    def w_in(k):
        return r.wgu[k].reshape(1024, 512)

    for copy in arrive:
        copy.wait_recv()
    wd_zh = net.send(r.wdown, r.wd.at[zh, y], ("zh",))
    g_pass(2)
    gf_tree.take("zl")
    for b in range(2):
        for k in range(8):
            r.att_s[64 * b : 64 * (b + 1), 128 * k : 128 * (k + 1)] = r.at2[b, k]
    g_pass(3)
    wo_tree.take("x")
    wo_tree.take("y", "x")
    wo_tree.take("zl", "x")
    wo_tree.take("zl", "y", "x")
    for flips in [(), ("y",), ("zl",), ("zl", "y"), ("x",), ("y", "x"), ("zl", "x"), ("zl", "y", "x")]:
        wo_tree.ready(*flips)

    resid = r.tok[...].reshape(128, 1024).astype(f32)
    resid = resid + jnp.dot(r.att_s[...], w_o(), preferred_element_type=f32)
    scale = row_scale(resid)
    r.resid[...] = resid
    mine8 = 2 * my_pair + c
    r.n2[mine8] = (resid * scale * gain_ffn).astype(bf).reshape(2, 64, 1024)
    to_sibling = [net.send(r.n2.at[mine8], r.n2.at[mine8], ("c",))]
    from_chips = [net.send(r.n2.at[mine8], r.n2.at[mine8], flips) for flips in GROUP_FLIPS]
    def pair_rows(ref, pair):
        return ref[pl.ds(2 * pair, 2)].reshape(256, 1024)

    def feed(pair):
        rows = pair_rows(r.n2, pair)
        r.gate[pair] = jnp.dot(rows, w_in(0), preferred_element_type=f32)
        r.up[pair] = jnp.dot(rows, w_in(1), preferred_element_type=f32)

    def feed_back(pair):
        back = lax.dot_general(pair_rows(r.gf, pair), w_down(), LAST, preferred_element_type=f32)
        gate, up = r.gate[pair], r.up[pair]
        sig = 1.0 / (1.0 + jnp.exp(-gate))
        silu = gate * sig
        r.hid[pair] = (silu * up).astype(bf)
        r.ggu[0, pair] = (back * up * sig * (1.0 + gate * (1.0 - sig))).astype(bf)
        r.ggu[1, pair] = (back * silu).astype(bf)

    def back_product(pair):
        total = lax.dot_general(r.ggu[0, pair], w_in(0), LAST, preferred_element_type=f32)
        return total + lax.dot_general(r.ggu[1, pair], w_in(1), LAST, preferred_element_type=f32)

    def out_product(pair):
        return jnp.dot(r.hid[pair], w_down(), preferred_element_type=f32)

    halves, reduced = {}, {0: [], 1: []}

    def pair_at(slot):
        far_zl, far_x = slot % 2, slot // 2
        return (zl + far_zl - 2 * zl * far_zl) * 2 + x + far_x - 2 * x * far_x

    def keep_half(at, value):
        r.kept[at] = jnp.where(c == 0, value[:128], value[128:])
        r.sent[at] = jnp.where(c == 0, value[128:], value[:128]).astype(bf).reshape(2, 64, 1024)

    def share(kind, slot):
        at = 4 * kind + slot
        halves[at] = net.send(r.sent.at[at], r.landed.at[at], ("c",))

    def finish_half(kind, slot):
        at = 4 * kind + slot
        halves[at].wait_recv()
        total = r.kept[at] + r.landed[at].reshape(128, 1024).astype(f32)
        if slot == 0:
            r.kept[at] = total
        else:
            r.red_send[kind, slot - 1] = total.astype(bf)
            reduced[kind].append(
                net.send(
                    r.red_send.at[kind, slot - 1],
                    r.red_land.at[kind, slot - 1],
                    GROUP_FLIPS[slot - 1],
                )
            )

    pairs = [my_pair] + [net.index(("zl", "x"), flips) for flips in GROUP_FLIPS]
    for copy in g_y + g_fwd:
        copy.wait_recv()
    to_sibling[0].wait_recv()
    for k in range(3):
        from_chips[k].wait_recv()
        at = 2 * pairs[k + 1] + c
        to_sibling.append(net.send(r.n2.at[at], r.n2.at[at], ("c",)))
        if k == 0:
            to_sibling[1].wait_recv()
            wd_zh.wait_recv()
            wd_fwd = net.send(r.wd.at[1 - zh, y], r.wd.at[1 - zh, y], ("y",))
            pl.loop(0, 2)(lambda slot: feed(pair_at(slot)))
    gf_tree.take("x")
    gf_tree.take("zl", "x")
    to_sibling[2].wait_recv()
    to_sibling[3].wait_recv()
    pl.loop(2, 4)(lambda slot: feed(pair_at(slot)))
    gf_tree.ready()
    gf_tree.ready("zl")
    gf_tree.ready("x")
    gf_tree.ready("zl", "x")
    wd_y.wait_recv()
    wd_fwd.wait_recv()
    net.drain()

    def feed_both(slot):
        pair = pair_at(slot)
        feed_back(pair)
        keep_half(slot, back_product(pair))

    pl.loop(3, 4)(feed_both)
    share(0, 3)
    pl.loop(2, 3)(feed_both)
    share(0, 2)
    finish_half(0, 3)
    pl.loop(1, 2)(feed_both)
    share(0, 1)
    finish_half(0, 2)
    pl.loop(0, 1)(feed_both)
    share(0, 0)
    finish_half(0, 1)

    @pl.loop(0, 2)
    def _(k):
        r.gwgu[k] = (
            lax.dot_general(
                r.n2[...].reshape(1024, 1024),
                r.ggu[k].reshape(1024, 512),
                FIRST,
                preferred_element_type=f32,
            )
            .astype(bf)
            .reshape(2, 4, 2, 64, 512)
        )
    y_far = [net.send(r.gwgu.at[k, 1 - zh, :, 1 - y], r.y_wgu.at[k, 1], ("y",)) for k in range(2)]
    finish_half(0, 0)

    @pl.loop(0, 4)
    def _(slot):
        keep_half(4 + slot, out_product(pair_at(slot)))

    for k in range(4):
        share(1, k)
    for half in range(2):
        cols = slice(512 * half, 512 * (half + 1))
        r.gwd[:, :, :, cols] = (
            lax.dot_general(
                r.hid[...].reshape(1024, 512),
                r.gf[:, :, :, cols].reshape(1024, 512),
                FIRST,
                preferred_element_type=f32,
            )
            .astype(bf)
            .reshape(2, 2, 128, 512)
        )

    h_steps = []

    def half_gate_up(k):
        y_far[k].wait_recv()
        r.h_wgu[k] = (r.gwgu[k, 1 - zh, :, y].astype(f32) + r.y_wgu[k, 1].astype(f32)).astype(bf)
        h_steps.append(net.send(r.h_wgu.at[k], r.h_wgu_land.at[k], ("zh",)))

    def half_down():
        y_far[2].wait_recv()
        r.h_wd[...] = (r.gwd[1 - zh, y].astype(f32) + r.y_wd[1].astype(f32)).astype(bf)
        h_steps.append(net.send(r.h_wd, r.h_wd_land, ("zh",)))

    for copy in reduced[0]:
        copy.wait_recv()
    total = r.kept[0]
    for k in range(3):
        total = total + r.red_land[0, k].astype(f32)
    resid = r.resid[...]
    scale = row_scale(resid)
    r.sums[...] = jnp.zeros_like(r.sums)
    r.sums[1:2, :] = jnp.sum(total * resid * scale, axis=0, keepdims=True)
    weighted = total * gain_ffn
    mean = jnp.mean(weighted * resid, axis=1, keepdims=True)
    grad_resid = r.cot[...].reshape(128, 1024).astype(f32) + scale * weighted
    grad_resid = grad_resid - resid * (scale * scale * scale) * mean
    r.kept[0] = grad_resid
    r.branch[...] = grad_resid.astype(bf)
    grad_att = lax.dot_general(r.branch[...], w_o(), LAST, preferred_element_type=f32).astype(bf)
    for k in range(8):
        for b in range(2):
            r.ga3[b, k] = grad_att[64 * b : 64 * (b + 1), 128 * k : 128 * (k + 1)]
    arrive = []
    for flips in far_flips + CHIP_FLIPS:
        z_part = 1 - zh if "zh" in flips else zh
        arrive.append(
            net.send(r.ga3.at[z_part, net.index(CHIPS, flips)], r.ag1.at[zh, my_chip], flips)
        )
    r.ag1[zh, my_chip] = r.ga3[zh, my_chip]
    for j in range(8):
        cols = slice(128 * j, 128 * (j + 1))
        r.gwo[j // 4, 2 * (j % 4) : 2 * (j % 4) + 2] = (
            lax.dot_general(r.att_s[:, cols], r.branch[...], FIRST, preferred_element_type=f32)
            .astype(bf)
            .reshape(2, 2, 32, 1024)
        )
    for copy in arrive:
        copy.wait_recv()

    @pl.loop(0, 16)
    def _(i):
        both = r.ag1[i // 8, i % 8]
        low, high = both[:, :64].astype(f32), both[:, 64:].astype(f32)
        r.lb[i] = jnp.where(c == 0, high, low).astype(bf)
        r.gatt[i, c] = jnp.where(c == 0, low, high).astype(bf)

    for k in (3, 2, 1, 0):
        finish_half(1, k)
    step = net.send(r.lb, r.gatt.at[:, c], ("c",))
    half_gate_up(0)
    y_far.append(net.send(r.gwd.at[1 - zh, 1 - y], r.y_wd.at[1], ("y",)))
    r.feat[...] = jnp.zeros_like(r.feat)
    r.bias_s[...] = jnp.zeros_like(r.bias_s)
    r.gate[...] = jnp.zeros_like(r.gate)
    step.wait_recv()

    @pl.loop(0, 4)
    def _(i):
        row = pl.ds(pl.multiple_of(i * SPAN, SPAN), SPAN)
        kept = r.kept_o[row, :]
        grad = r.gatt[pl.ds(i * 4, 4)].reshape(SPAN, 64).astype(f32)
        grad = jnp.concatenate([grad, jnp.zeros((SPAN, 64), f32)], axis=1)
        delta = jnp.sum(jnp.where(lane_span < 64, grad * kept, 0.0), axis=1, keepdims=True)
        query = r.qf[row, :].astype(f32)
        for j, part in enumerate(pieces(kept[:, 64:65])):
            query = jnp.where(lane_span == 64 + 40 + j, -part, query)
        r.qf[row, :] = query.astype(bf)
        for j, part in enumerate(pieces(delta)):
            grad = jnp.where(lane_span == 64 + j, -part, grad)
        r.gb[row, :] = grad.astype(bf)

    grad_k, grad_v = r.feat, r.kept_o
    grad_v[...] = jnp.zeros_like(grad_v)
    tree_o = Reduce(
        net,
        ("x", "zl", "y"),
        lambda mask, core: r.gwo.at[:, net.index(CHIPS, mask), core],
        lambda slot: r.wo.at[0, pl.ds(2 * slot, 2)],
        lambda slot: r.wo.at[1, pl.ds(2 * slot, 2)],
        lambda slot: r.o_arr.at[slot],
    )
    for mask in tree_o.masks:
        tree_o.begin(mask)

    def attend_back(i):
        row = pl.ds(pl.multiple_of(i * SPAN, SPAN), SPAN)
        query, grad = r.qf[row, :], r.gb[row, :]

        def one_chunk(k, total):
            col = pl.ds(pl.multiple_of(k * SPAN, SPAN), SPAN)
            key = r.kf[col, :]
            scores = lax.dot_general(key, query, LAST, preferred_element_type=f32)
            probs = jnp.exp(scores)
            centred = lax.dot_general(r.vf[col, :], grad, LAST, preferred_element_type=f32)
            back = (probs * centred).astype(bf)
            grad_v[col, :] += jnp.dot(probs.astype(bf), grad, preferred_element_type=f32)
            grad_k[col, :] += jnp.dot(back, query, preferred_element_type=f32)
            return total + lax.dot_general(back, key, FIRST, preferred_element_type=f32)

        total = lax.fori_loop(0, 2048 // SPAN, one_chunk, jnp.zeros((SPAN, 128), f32))
        r.gq[row, :] = (total * 0.125).astype(bf)
        marks = r.kf[row, :].astype(f32)
        same = jnp.where((lane_span >= 80) & (lane_span < 88), total * marks, 0.0)
        every = jnp.where(lane_span == 72, total, 0.0)
        r.bias_s[0:1, :] += jnp.sum(same, axis=0, keepdims=True)
        r.bias_s[1:2, :] += jnp.sum(every, axis=0, keepdims=True)

    half_gate_up(1)
    pl.loop(0, 1)(attend_back)
    y_near = [net.send(r.gwgu.at[k, zh, :, 1 - y], r.y_wgu.at[k, 0], ("y",)) for k in range(2)]
    y_near.append(net.send(r.gwd.at[zh, 1 - y], r.y_wd.at[0], ("y",)))
    for mask in tree_o.masks[:4]:
        tree_o.forward(mask)
    half_down()
    pl.loop(1, 2)(attend_back)
    pl.loop(2, 4)(attend_back)

    def token_tree(part, half, dims):
        return Reduce(
            net,
            dims,
            lambda mask, core: r.x.at[half * 16 + 2 * net.index(CHIPS, mask) + core],
            lambda slot: r.landed.at[slot, part],
            lambda slot: r.sent.at[slot, part],
            lambda slot: r.n2.at[slot, part],
        )

    trees = [token_tree(0, 1 - zh, ("x", "y", "zl")), token_tree(1, zh, ("y", "x", "zl"))]

    def project_back(part, where):
        start = (part * 4 + where) * ROW_BLOCK
        row, blocks = pl.ds(pl.multiple_of(start, ROW_BLOCK), ROW_BLOCK), pl.ds(start // 64, 4)
        raw = r.raw[row, :]
        scale = lax.rsqrt(pair_mean(raw * raw) + EPS)
        cosine, sine = angles_of(r.cs[row, :])
        key_part = pltpu.roll(grad_k[row, :].astype(bf).astype(f32), 64, 1)
        grad = jnp.where(lane < 64, r.gq[row, :].astype(f32), key_part)
        turned = grad * cosine - swap_halves(grad) * sine
        r.bias_s[2:3, :] += jnp.sum(turned * raw * scale, axis=0, keepdims=True)
        weighted = turned * qk_gain
        back = scale * weighted - raw * (scale * scale * scale) * pair_mean(weighted * raw)
        grad_qkv = jnp.concatenate([back, grad_v[row, :][:, :64]], axis=1).astype(bf)
        grad_normed = lax.dot_general(
            grad_qkv, r.wh[...].reshape(1024, 192), LAST, preferred_element_type=f32
        )
        value = r.x[blocks].reshape(ROW_BLOCK, 1024).astype(f32)
        shaped = value * row_scale(value)
        r.sums[0:1, :] += jnp.sum(grad_normed * shaped, axis=0, keepdims=True)
        normed = (shaped * gain_attn).astype(bf)
        term = lax.dot_general(normed, grad_qkv, FIRST, preferred_element_type=f32)
        r.gate[:, :, :192] += term.reshape(4, 256, 192)
        r.x[blocks] = grad_normed.astype(bf).reshape(4, 64, 1024)

    f_steps, f_c = [], []

    def feed_sum(k):
        y_near[k].wait_recv()
        h_steps[k].wait_recv()
        for j in range(4):
            rows = r.gwgu[k, zh, j, y].astype(f32) + r.y_wgu[k, 0, j].astype(f32)
            rows = rows + r.h_wgu_land[k, j].astype(f32)
            r.gp[j, k, 0] = rows[:32].astype(bf)
            r.gp[j, k, 1] = rows[32:].astype(bf)
        for flips in GROUP_FLIPS:
            f_steps.append(
                net.send(r.gp.at[net.index(("zl", "x"), flips), k], r.gl.at[my_pair, k], flips)
            )
        r.gl[my_pair, k] = r.gp[my_pair, k]

    def feed_sibling(k):
        for j in range(3):
            f_steps[3 * k + j].wait_recv()
        f_c.append(net.send(r.gl.at[:, k, 1 - c], r.f2.at[k, :, c], ("c",)))
        r.f2[k, :, c] = r.gl[:, k, c]

    def two_back(*flips):
        where = net.index(("zl", "x"), flips)
        pl.loop(0, 2)(lambda part: project_back(part, where))
        for tree in trees:
            tree.begin(flips)
            tree.begin(flips + ("y",))

    net.settle(list(halves.values()))
    two_back("zl", "x")
    feed_sum(0)
    two_back("x")
    trees[0].forward(("zl", "x", "y"))
    trees[0].forward(("zl", "x"))
    trees[1].forward(("zl", "x", "y"))
    tree_o.forward(("zl", "y"))
    tree_o.forward(("zl",))
    two_back("zl")
    trees[0].forward(("x", "y"))
    trees[0].forward(("x",))
    trees[1].forward(("x", "y"))
    two_back()
    trees[0].forward(("zl", "y"))
    trees[1].forward(("zl", "y"))
    trees[1].forward(("y",))
    trees[1].forward(("zl", "x"))

    one = lane_iota(8)
    both = jnp.broadcast_to(r.bias_s[2:3, :], (8, 128))
    turned = pltpu.roll(both, 64, 1)
    wide = lane_iota(1, 1024)
    query_gain = jnp.concatenate([jnp.where(one < 64, both, turned)[0:1]] * 8, axis=1)
    key_gain = jnp.concatenate([jnp.where(one < 64, turned, both)[0:1]] * 8, axis=1)
    r.sums[2:3, :] = jnp.where(wide // 64 == head, query_gain, 0.0)
    r.sums[3:4, :] = jnp.where(wide // 64 == head, key_gain, 0.0)
    same = jnp.sum(r.bias_s[0:1, :], axis=1, keepdims=True)
    every = jnp.sum(r.bias_s[1:2, :], axis=1, keepdims=True)
    row_bias = jnp.where(wide == head, same, 0.0)
    r.sums[4:5, :] = jnp.where(wide == 16 + head, every - same, row_bias)
    for k in range(8):
        r.s_acc[0, k] = r.sums[:, 128 * k : 128 * (k + 1)]
    s_steps = [net.send(r.s_acc.at[0], r.s_land.at[k], f) for k, f in enumerate(CHIP_FLIPS)]

    r.gw[...] = r.gate[:, :, :192].astype(bf).reshape(2, 8, 2, 32, 192)
    w_zh = net.send(r.gw.at[1 - zh], r.w_land, ("zh",))
    trees[0].forward(("y",))
    trees[0].forward(("zl",))
    trees[1].forward(("x",))
    tree_o.forward(("y",))
    for copy in reduced[1]:
        copy.wait_recv()
    total = r.kept[4] + r.resid[...]
    for k in range(3):
        total = total + r.red_land[1, k].astype(f32)
    r.out[...] = total.astype(bf)
    trees[1].forward(("zl",))
    w_zh.wait_recv()
    r.w_t[...] = (r.gw[zh].astype(f32) + r.w_land[...].astype(f32)).astype(bf)
    w_c = net.send(r.w_t.at[:, 1 - c], r.wp.at[:, c], ("c",))
    r.wp[:, c] = r.w_t[:, c]
    r.n_half[...] = trees[0].result().astype(bf)
    n_step = net.send(r.n_half, r.n_half_land, ("zh",))
    feed_sum(1)
    total = r.s_acc[0]
    for k, copy in enumerate(s_steps):
        copy.wait_recv()
        total = total + r.s_land[k]
    r.s_acc[1] = total
    s_step = net.send(r.s_acc.at[1], r.s_land.at[7], ("zh",))
    w_c.wait_recv()
    w_steps = []
    for flips in CHIP_FLIPS:
        w_steps.append(net.send(r.wp.at[net.index(CHIPS, flips)], r.wl.at[my_chip], flips))
    r.wl[my_chip] = r.wp[my_chip]
    total = tree_o.result()
    r.kept[3, :32] = total[0]
    r.kept[4, :32] = total[1]
    r.o_half[...] = r.kept[4 - zh, :32].astype(bf)
    o_step = net.send(r.o_half, r.o_half_land, ("zh",))
    r.kept[1 + zh, :64] = trees[1].result()
    s_step.wait_recv()
    r.s_acc[2] = r.s_acc[1] + r.s_land[7]
    s_step = net.send(r.s_acc.at[2], r.s_land.at[8], ("c",))
    y_near[2].wait_recv()
    h_steps[2].wait_recv()
    r.gwdown[...] = r.gwd[zh, y].astype(f32) + r.y_wd[0].astype(f32) + r.h_wd_land[...].astype(f32)
    feed_sibling(0)
    feed_sibling(1)
    n_step.wait_recv()
    r.kept[2 - zh, :64] = r.n_half_land[...].astype(f32)
    for b in range(2):
        value = r.tok[b].astype(f32)
        scale = row_scale(value)
        weighted = r.kept[1 + b, :64] * gain_attn
        mean = jnp.mean(weighted * value, axis=1, keepdims=True)
        back = scale * weighted - value * (scale * scale * scale) * mean
        r.gtok[b] = (r.kept[0, 64 * b : 64 * (b + 1), :] + back).astype(bf)
    for copy in w_steps:
        copy.wait_recv()
    for h in range(16):
        r.gwqkv[:, 192 * h : 192 * (h + 1)] = r.wl[h // 2, h % 2].astype(f32)
    o_step.wait_recv()
    r.gwout[...] = r.kept[3 + zh, :32] + r.o_half_land[...].astype(f32)
    for k, out in ((0, r.gwgate), (1, r.gwup)):
        f_c[k].wait_recv()
        for pair in range(4):
            for cc in range(2):
                for part in range(4):
                    idx = (part // 2) * 16 + pair * 4 + (part % 2) * 2 + cc
                    out[:, 128 * idx : 128 * (idx + 1)] = r.f2[
                        k, pair, cc, :, 128 * part : 128 * (part + 1)
                    ].astype(f32)
    s_step.wait_recv()
    r.gsmall[...] = r.s_acc[2] + r.s_land[8]
    net.drain()


def layer(*arrays):
    sm = pl.BlockSpec(memory_space=pltpu.SMEM)
    vm = pl.BlockSpec(memory_space=pltpu.VMEM)
    outs = layer_outputs()
    return pl.pallas_call(
        layer_kernel,
        out_shape=[jax.ShapeDtypeStruct(*spec) for spec in outs.values()],
        in_specs=[sm, sm] + [vm] * (len(layer_inputs()) - 2),
        out_specs=[vm] * len(outs),
        scratch_shapes=[pltpu.VMEM(*spec) for spec in layer_scratch().values()]
        + [
            pltpu.SemaphoreType.DMA((N_COPIES,)),
            pltpu.SemaphoreType.DMA((N_COPIES,)),
            pltpu.SemaphoreType.DMA((2,)),
        ],
        compiler_params=pltpu.CompilerParams(
            collective_id=1, has_side_effects=True, vmem_limit_bytes=VMEM_BYTES
        ),
        name="layer",
    )(*arrays)


def give_out_kernel(small, *refs):
    n = (len(refs) - 5) // 2
    gains, bias = refs[2 * n : 2 * n + 4], refs[-1]
    for source, dest in zip(refs[:n], refs[n : 2 * n]):
        dest[...] = source[...]
    rank = jnp.int32(0)
    for name in AXES:
        rank = rank * 2 + lax.axis_index(name)
    held = small[rank // 4]
    mine = held
    for k in range(1, 4):
        mine = jnp.where(rank % 4 == k, pltpu.roll(held, 128 - 32 * k, 1), mine)
    for k, gain in enumerate(gains):
        gain[...] = mine[k : k + 1, :32]
    first = small[0]
    bias[0:1, :] = first[4:5, :16]
    bias[1:2, :] = pltpu.roll(first, 112, 1)[4:5, :16]


def give_out(small, *large):
    f32 = jnp.float32
    vm = pl.BlockSpec(memory_space=pltpu.VMEM)
    n = len(large)
    return pl.pallas_call(
        give_out_kernel,
        out_shape=[jax.ShapeDtypeStruct(a.shape, a.dtype) for a in large]
        + [jax.ShapeDtypeStruct((1, 32), f32)] * 4
        + [jax.ShapeDtypeStruct((2, 16), f32)],
        in_specs=[vm] * (n + 1),
        out_specs=[vm] * (n + 5),
        name="give_out",
    )(small, *large)


def frequencies():
    index = np.arange(32, dtype=np.float32)
    return (THETA ** (-2.0 * index / 64.0)).astype(np.float32)[:, None]


def on_device_cube(
    tokens,
    cotangent,
    w_qkv,
    w_out,
    w_gate,
    w_up,
    w_down,
    norm_attn,
    norm_ffn,
    q_gain,
    k_gain,
    var_bias,
    doc_lengths,
    variate,
    times,
):
    results = layer(
        doc_lengths, var_bias.T, tokens, cotangent, w_qkv, w_out, w_gate, w_up, w_down,
        *(gain.reshape(1, 32) for gain in (norm_attn, norm_ffn, q_gain, k_gain)),
        variate, times, jnp.asarray(frequencies()),
    )
    *large, small = results
    out, gtok, gwqkv, gwout, gwgate, gwup, gwdown, *gains, bias = give_out(small, *large)
    return (
        out.reshape(2, 64, 1024),
        gtok,
        gwqkv,
        gwout,
        gwgate,
        gwup,
        gwdown,
        *(gain.reshape(32) for gain in gains),
        bias.T,
    )


def run_parts(mesh, body, split):
    rows, cut = P(split, None), P(split)
    part = P(None, split, None)
    return jax.shard_map(
        body,
        mesh=mesh,
        in_specs=(part, part) + (rows,) * 5 + (cut,) * 4 + (P(), P(), P(None, split), P(None, split)),
        out_specs=(part, part) + (rows,) * 5 + (cut,) * 4 + (P(),),
        check_vma=False,
    )


def solution(mesh):
    sizes = (mesh.shape["head"], mesh.shape["blk"])
    general = run_parts(mesh, on_device, ("head", "blk"))
    if sizes != (8, 4):
        return general
    cube = jax.sharding.Mesh(mesh.devices.reshape(2, 2, 2, 2, 2), AXES)
    special = run_parts(cube, on_device_cube, AXES)

    def chosen(*arrays):
        tokens, w_gate, var_bias, lengths = arrays[0], arrays[4], arrays[11], arrays[12]
        shapes = (tokens.shape, w_gate.shape, var_bias.shape, lengths.shape)
        if shapes == ((2, 2048, 1024), (1024, 4096), (16, 2), (2, 8)):
            return special(*arrays)
        return general(*arrays)

    return chosen
```

```python
import math
from types import SimpleNamespace

import jax
import jax.numpy as jnp
import numpy as np
from jax import lax
from jax.experimental import pallas as pl
from jax.experimental.pallas import tpu as pltpu
from jax.sharding import PartitionSpec as P

EPS = 1e-06
THETA = 10000.0
NEGATIVE = -1e30
KEY_BLOCK = 1024


def inverse_rms(values_in):
    return lax.rsqrt(jnp.mean(values_in * values_in, axis=-1, keepdims=True) + EPS)


def rotate(values_in, time_index, sign_value):
    half_dim = values_in.shape[-1] // 2
    frequency = THETA ** (-2.0 * jnp.arange(half_dim, dtype=jnp.float32) / values_in.shape[-1])
    angles = time_index.astype(jnp.float32)[:, None] * frequency[None, :]
    cosine = jnp.cos(angles)[:, None, :]
    sine_part = sign_value * jnp.sin(angles)[:, None, :]
    first_half = values_in[..., :half_dim]
    second_half = values_in[..., half_dim:]
    return jnp.concatenate(
        [
            first_half * cosine - second_half * sine_part,
            first_half * sine_part + second_half * cosine,
        ],
        axis=-1,
    )


def norm_back(grad_in, value_in, scale_in, gain_in):
    weighted = grad_in * gain_in
    scale_cube = scale_in * scale_in * scale_in
    return scale_in * weighted - value_in * scale_cube * jnp.mean(
        weighted * value_in, axis=-1, keepdims=True
    )


def row_contract(left_mat, right_mat):
    return lax.dot_general(
        left_mat, right_mat, (((0,), (0,)), ((), ())), preferred_element_type=jnp.float32
    )


def col_contract(left_mat, right_mat):
    return lax.dot_general(
        left_mat, right_mat, (((1,), (1,)), ((), ())), preferred_element_type=jnp.float32
    )


def document_of(positions, doc_ends):
    return jnp.sum((positions[:, None] >= doc_ends[None, :]).astype(jnp.int32), axis=1)


def key_positions(first_row, row_total, per_group, row_count, blk_n):
    row_index = first_row + jnp.arange(row_total, dtype=jnp.int32)
    source_blk = row_index // per_group
    within = row_index % per_group
    return (within // row_count * blk_n + source_blk) * row_count + within % row_count


def block_scores(queries, key_part, same_var, same_doc, bias_same, bias_other, att_scale):
    raw_scores = (
        jnp.einsum("qhd,khd->qhk", queries, key_part, preferred_element_type=jnp.float32)
        * att_scale
    )
    bias_terms = jnp.where(
        same_var[:, None, :], bias_same[None, :, None], bias_other[None, :, None]
    )
    return jnp.where(same_doc[:, None, :], raw_scores + bias_terms, NEGATIVE)


def forward_block(
    state_in, queries, key_part, value_part, same_var, same_doc, bias_same, bias_other, att_scale
):
    best_prev, total_prev, accum_prev = state_in
    scores = block_scores(queries, key_part, same_var, same_doc, bias_same, bias_other, att_scale)
    best_next = jnp.maximum(best_prev, jnp.max(scores, axis=-1))
    factor = jnp.exp(best_prev - best_next)
    weights = jnp.where(same_doc[:, None, :], jnp.exp(scores - best_next[..., None]), 0.0)
    total_next = total_prev * factor + jnp.sum(weights, axis=-1)
    accum_next = accum_prev * factor[..., None] + jnp.einsum(
        "qhk,khd->qhd", weights.astype(jnp.bfloat16), value_part, preferred_element_type=jnp.float32
    )
    return (best_next, total_next, accum_next)


def flatten_all(grads_in):
    return tuple((member.reshape(-1) for member in grads_in))


def unflatten_all(flat_in, grads_like):
    return tuple(
        (flat.reshape((-1,) + member.shape[1:]) for flat, member in zip(flat_in, grads_like))
    )


def on_device(
    tokens,
    cotangent,
    w_qkv,
    w_out,
    w_gate,
    w_up,
    w_down,
    norm_attn,
    norm_ffn,
    q_gain,
    k_gain,
    var_bias,
    doc_lengths,
    variate,
    times,
):
    heads_n = lax.axis_size("head")
    blk_n = lax.axis_size("blk")
    head_rank = lax.axis_index("head")
    blk_rank = lax.axis_index("blk")
    batch_count, row_count, model_width = tokens.shape
    head_count = var_bias.shape[0]
    head_dim = model_width // head_count
    local_heads = head_count // heads_n
    query_rows = heads_n * row_count
    key_rows = blk_n * query_rows
    key_block = min(KEY_BLOCK, key_rows)
    block_count = key_rows // key_block
    att_scale = 1.0 / math.sqrt(head_dim)
    gathered = (
        lax.all_gather(w_qkv, ("head", "blk"), axis=0, tiled=True),
        lax.all_gather(w_out, ("head", "blk"), axis=0, tiled=True),
        lax.all_gather(w_gate, ("head", "blk"), axis=0, tiled=True),
        lax.all_gather(w_up, ("head", "blk"), axis=0, tiled=True),
        lax.all_gather(w_down, ("head", "blk"), axis=0, tiled=True),
        lax.all_gather(norm_attn, ("head", "blk"), axis=0, tiled=True),
        lax.all_gather(norm_ffn, ("head", "blk"), axis=0, tiled=True),
        lax.all_gather(q_gain, ("head", "blk"), axis=0, tiled=True),
        lax.all_gather(k_gain, ("head", "blk"), axis=0, tiled=True),
    )
    wqkv_all, wout_all, wgate_all, wup_all, wdown_all = gathered[:5]
    gain_attn = gathered[5].astype(jnp.float32)
    gain_ffn = gathered[6].astype(jnp.float32)
    gain_query = gathered[7].astype(jnp.float32).reshape(head_count, head_dim)
    gain_key = gathered[8].astype(jnp.float32).reshape(head_count, head_dim)
    local_bias = lax.dynamic_slice_in_dim(var_bias, head_rank * local_heads, local_heads, 0)
    bias_same = local_bias[:, 0]
    bias_other = local_bias[:, 1]
    query_index = jnp.arange(query_rows, dtype=jnp.int32)
    query_pos = (query_index // row_count * blk_n + blk_rank) * row_count + query_index % row_count
    ends_all = jnp.cumsum(doc_lengths, axis=1)
    outputs_list = []
    inputs_list = []
    totals = None
    bias_accum = jnp.zeros((local_heads, 2), jnp.float32)
    for batch_id in range(batch_count):
        doc_ends = ends_all[batch_id]
        time_row = times[batch_id]
        inputs_f = tokens[batch_id].astype(jnp.float32)
        scale_one = inverse_rms(inputs_f)
        normed_one = (inputs_f * scale_one * gain_attn).astype(jnp.bfloat16)
        qkv_all = jnp.dot(normed_one, wqkv_all, preferred_element_type=jnp.float32).reshape(
            row_count, head_count, 3 * head_dim
        )
        query_raw = qkv_all[..., :head_dim]
        key_raw = qkv_all[..., head_dim : 2 * head_dim]
        value_raw = qkv_all[..., 2 * head_dim :]
        query_scale = inverse_rms(query_raw)
        key_scale = inverse_rms(key_raw)
        query_rot = rotate(query_raw * query_scale * gain_query, time_row, 1.0)
        key_rot = rotate(key_raw * key_scale * gain_key, time_row, 1.0)
        packed = jnp.concatenate([query_rot, key_rot, value_raw], axis=-1).astype(jnp.bfloat16)
        variate_rep = jnp.broadcast_to(
            variate[batch_id].astype(jnp.bfloat16)[:, None], (row_count, head_count)
        )
        packed_heads, variate_heads = (
            lax.all_to_all(packed, "head", split_axis=1, concat_axis=0, tiled=True),
            lax.all_to_all(variate_rep, "head", split_axis=1, concat_axis=0, tiled=True),
        )
        queries = packed_heads[..., :head_dim]
        key_values = packed_heads[..., head_dim:]
        query_var = variate_heads[:, 0]
        query_doc = document_of(query_pos, doc_ends)
        initial = (
            jnp.full((query_rows, local_heads), NEGATIVE, jnp.float32),
            jnp.zeros((query_rows, local_heads), jnp.float32),
            jnp.zeros((query_rows, local_heads, head_dim), jnp.float32),
        )
        kv_piece = lax.all_gather(key_values, "blk", axis=0, tiled=True)
        var_piece = lax.all_gather(query_var, "blk", axis=0, tiled=True)
        piece_rows = kv_piece.shape[0]

        def one_block(state_blk, kv_block, var_block, block_start):
            key_doc = document_of(
                key_positions(block_start, kv_block.shape[0], query_rows, row_count, blk_n),
                doc_ends,
            )
            same_doc = query_doc[:, None] == key_doc[None, :]
            same_var = query_var[:, None] == var_block[None, :]
            return forward_block(
                state_blk,
                queries,
                kv_block[..., :head_dim],
                kv_block[..., head_dim:],
                same_var,
                same_doc,
                bias_same,
                bias_other,
                att_scale,
            )

        def loop_step(turn_index, state_loop):
            kv_block = lax.dynamic_slice_in_dim(kv_piece, turn_index * key_block, key_block, 0)
            var_block = lax.dynamic_slice_in_dim(var_piece, turn_index * key_block, key_block, 0)
            return one_block(state_loop, kv_block, var_block, turn_index * key_block)

        attn_state = lax.fori_loop(0, piece_rows // key_block, loop_step, initial)
        best_score, total_weight, accum = attn_state
        attn_heads = accum / total_weight[..., None]
        log_total = best_score + jnp.log(total_weight)
        attn_tok = lax.all_to_all(
            attn_heads.astype(jnp.bfloat16), "head", split_axis=0, concat_axis=1, tiled=True
        ).reshape(row_count, model_width)
        resid_one = inputs_f + jnp.dot(attn_tok, wout_all, preferred_element_type=jnp.float32)
        scale_two = inverse_rms(resid_one)
        normed_two = (resid_one * scale_two * gain_ffn).astype(jnp.bfloat16)
        gate_pre = jnp.dot(normed_two, wgate_all, preferred_element_type=jnp.float32)
        up_pre = jnp.dot(normed_two, wup_all, preferred_element_type=jnp.float32)
        sigmoid_gate = jax.nn.sigmoid(gate_pre)
        silu_gate = gate_pre * sigmoid_gate
        hidden_act = (silu_gate * up_pre).astype(jnp.bfloat16)
        result = resid_one + jnp.dot(hidden_act, wdown_all, preferred_element_type=jnp.float32)
        outputs_list.append(result.astype(jnp.bfloat16))
        grad_out = cotangent[batch_id].astype(jnp.float32)
        grad_ffn = grad_out.astype(jnp.bfloat16)
        grad_down = row_contract(hidden_act, grad_ffn)
        grad_hidden = col_contract(grad_ffn, wdown_all)
        grad_gate = (
            grad_hidden * up_pre * sigmoid_gate * (1.0 + gate_pre * (1.0 - sigmoid_gate))
        ).astype(jnp.bfloat16)
        grad_up = (grad_hidden * silu_gate).astype(jnp.bfloat16)
        grad_wgate = row_contract(normed_two, grad_gate)
        grad_wup = row_contract(normed_two, grad_up)
        grad_normed = col_contract(grad_gate, wgate_all) + col_contract(grad_up, wup_all)
        grad_gffn = jnp.sum(grad_normed * resid_one * scale_two, axis=0)
        grad_resid = grad_out + norm_back(grad_normed, resid_one, scale_two, gain_ffn)
        grad_branch = grad_resid.astype(jnp.bfloat16)
        grad_wout = row_contract(attn_tok, grad_branch)
        grad_attn = (
            col_contract(grad_branch, wout_all)
            .astype(jnp.bfloat16)
            .reshape(row_count, head_count, head_dim)
        )
        grad_heads = lax.all_to_all(grad_attn, "head", split_axis=1, concat_axis=0, tiled=True)
        delta_row = jnp.sum(grad_heads.astype(jnp.float32) * attn_heads, axis=-1)
        keys_all, key_var_all = (
            lax.all_gather(key_values, "blk", axis=0, tiled=True),
            lax.all_gather(query_var, "blk", axis=0, tiled=True),
        )
        keys_blocks = keys_all.reshape(block_count, key_block, local_heads, 2 * head_dim)
        var_blocks = key_var_all.reshape(block_count, key_block)
        block_starts = jnp.arange(block_count, dtype=jnp.int32) * key_block

        def back_step(carry_back, block_in):
            grad_query, bias_grad = carry_back
            kv_block, var_block, block_start = block_in
            key_doc = document_of(
                key_positions(block_start, key_block, query_rows, row_count, blk_n), doc_ends
            )
            same_doc = query_doc[:, None] == key_doc[None, :]
            same_var = query_var[:, None] == var_block[None, :]
            key_part = kv_block[..., :head_dim]
            value_part = kv_block[..., head_dim:]
            scores = block_scores(
                queries, key_part, same_var, same_doc, bias_same, bias_other, att_scale
            )
            probs = jnp.where(same_doc[:, None, :], jnp.exp(scores - log_total[..., None]), 0.0)
            grad_probs = jnp.einsum(
                "qhd,khd->qhk", grad_heads, value_part, preferred_element_type=jnp.float32
            )
            grad_scores = (probs * (grad_probs - delta_row[..., None])).astype(jnp.bfloat16)
            grad_scores_f = grad_scores.astype(jnp.float32)
            same_sum = jnp.sum(jnp.where(same_var[:, None, :], grad_scores_f, 0.0), axis=(0, 2))
            other_sum = jnp.sum(jnp.where(same_var[:, None, :], 0.0, grad_scores_f), axis=(0, 2))
            bias_grad = bias_grad + jnp.stack([same_sum, other_sum], axis=-1)
            grad_query = grad_query + att_scale * jnp.einsum(
                "qhk,khd->qhd", grad_scores, key_part, preferred_element_type=jnp.float32
            )
            grad_key = att_scale * jnp.einsum(
                "qhk,qhd->khd", grad_scores, queries, preferred_element_type=jnp.float32
            )
            grad_value = jnp.einsum(
                "qhk,qhd->khd",
                probs.astype(jnp.bfloat16),
                grad_heads,
                preferred_element_type=jnp.float32,
            )
            return ((grad_query, bias_grad), jnp.concatenate([grad_key, grad_value], axis=-1))

        carry_start = (
            jnp.zeros((query_rows, local_heads, head_dim), jnp.float32),
            jnp.zeros((local_heads, 2), jnp.float32),
        )
        (grad_query, bias_part), grad_kv_parts = lax.scan(
            back_step, carry_start, (keys_blocks, var_blocks, block_starts)
        )
        bias_accum = bias_accum + bias_part
        grad_kv_own = lax.psum_scatter(
            grad_kv_parts.reshape(key_rows, local_heads, 2 * head_dim).astype(jnp.bfloat16),
            "blk",
            scatter_dimension=0,
            tiled=True,
        )
        grad_packed = jnp.concatenate([grad_query.astype(jnp.bfloat16), grad_kv_own], axis=-1)
        grad_tok = lax.all_to_all(
            grad_packed, "head", split_axis=0, concat_axis=1, tiled=True
        ).astype(jnp.float32)
        grad_qrot = rotate(grad_tok[..., :head_dim], time_row, -1.0)
        grad_krot = rotate(grad_tok[..., head_dim : 2 * head_dim], time_row, -1.0)
        grad_gquery = jnp.sum(grad_qrot * query_raw * query_scale, axis=0)
        grad_gkey = jnp.sum(grad_krot * key_raw * key_scale, axis=0)
        grad_qraw = norm_back(grad_qrot, query_raw, query_scale, gain_query)
        grad_kraw = norm_back(grad_krot, key_raw, key_scale, gain_key)
        grad_qkv = (
            jnp.concatenate([grad_qraw, grad_kraw, grad_tok[..., 2 * head_dim :]], axis=-1)
            .reshape(row_count, 3 * model_width)
            .astype(jnp.bfloat16)
        )
        grad_wqkv = row_contract(normed_one, grad_qkv)
        grad_normed_one = col_contract(grad_qkv, wqkv_all)
        grad_gattn = jnp.sum(grad_normed_one * inputs_f * scale_one, axis=0)
        grad_in = grad_resid + norm_back(grad_normed_one, inputs_f, scale_one, gain_attn)
        inputs_list.append(grad_in.astype(jnp.bfloat16))
        batch_grads = (
            grad_wqkv,
            grad_wout,
            grad_wgate,
            grad_wup,
            grad_down,
            grad_gattn,
            grad_gffn,
            grad_gquery.reshape(model_width),
            grad_gkey.reshape(model_width),
        )
        if totals is None:
            totals = batch_grads
        else:
            totals = tuple(
                (first_term + second_term for first_term, second_term in zip(totals, batch_grads))
            )
    flat_totals = flatten_all(totals)
    summed_flat = (
        lax.psum_scatter(flat_totals[0], ("head", "blk"), scatter_dimension=0, tiled=True),
        lax.psum_scatter(flat_totals[1], ("head", "blk"), scatter_dimension=0, tiled=True),
        lax.psum_scatter(flat_totals[2], ("head", "blk"), scatter_dimension=0, tiled=True),
        lax.psum_scatter(flat_totals[3], ("head", "blk"), scatter_dimension=0, tiled=True),
        lax.psum_scatter(flat_totals[4], ("head", "blk"), scatter_dimension=0, tiled=True),
        lax.psum_scatter(flat_totals[5], ("head", "blk"), scatter_dimension=0, tiled=True),
        lax.psum_scatter(flat_totals[6], ("head", "blk"), scatter_dimension=0, tiled=True),
        lax.psum_scatter(flat_totals[7], ("head", "blk"), scatter_dimension=0, tiled=True),
        lax.psum_scatter(flat_totals[8], ("head", "blk"), scatter_dimension=0, tiled=True),
    )
    totals = unflatten_all(summed_flat, totals)
    bias_full = lax.dynamic_update_slice_in_dim(
        jnp.zeros((head_count, 2), jnp.float32), bias_accum, head_rank * local_heads, 0
    )
    grad_bias = lax.psum(bias_full, ("head", "blk"))
    return (
        jnp.stack(outputs_list),
        jnp.stack(inputs_list),
        totals[0],
        totals[1],
        totals[2],
        totals[3],
        totals[4],
        totals[5],
        totals[6],
        totals[7],
        totals[8],
        grad_bias,
    )


AXES = ("zh", "zl", "x", "y", "c")
CHIPS = ("zl", "x", "y")
VMEM_BYTES = 63 * 2**20
ROW_BLOCK = 256
SPAN = 512
LAST = (((1,), (1,)), ((), ()))
FIRST = (((0,), (0,)), ((), ()))
CHIP_FLIPS = [
    tuple(a for a, bit in zip(CHIPS, ((m >> 2) & 1, (m >> 1) & 1, m & 1)) if bit)
    for m in range(1, 8)
]
GROUP_FLIPS = [("zl",), ("x",), ("zl", "x")]


class Net:
    def __init__(self, send_sems, recv_sems, local_sems):
        self.me = {name: lax.axis_index(name) for name in AXES}
        self.send_sems, self.recv_sems, self.local_sems = send_sems, recv_sems, local_sems
        self.used = 0
        self.local_used = 0
        self.open = []

    def target(self, flips):
        return tuple(1 - self.me[a] if a in flips else self.me[a] for a in AXES)

    def index(self, names, flips=()):
        total = 0
        for a in names:
            total = total * 2 + (1 - self.me[a] if a in flips else self.me[a])
        return total

    def barrier(self, partners):
        sem = pltpu.get_barrier_semaphore()
        for flips in partners:
            pl.semaphore_signal(
                sem, inc=1, device_id=self.target(flips), device_id_type=pl.DeviceIdType.MESH
            )
        pl.semaphore_wait(sem, len(partners))

    def send(self, source, dest, flips):
        copy = pltpu.make_async_remote_copy(
            src_ref=source,
            dst_ref=dest,
            send_sem=self.send_sems.at[self.used],
            recv_sem=self.recv_sems.at[self.used],
            device_id=self.target(flips),
            device_id_type=pl.DeviceIdType.MESH,
        )
        self.used += 1
        copy.start()
        self.open.append(copy)
        return copy

    def local(self, source, dest):
        copy = pltpu.make_async_copy(source, dest, self.local_sems.at[self.local_used])
        self.local_used += 1
        copy.start()
        return copy

    def settle(self, copies):
        for copy in copies:
            copy.wait_send()
        gone = [id(copy) for copy in copies]
        self.open = [copy for copy in self.open if id(copy) not in gone]

    def drain(self):
        for copy in self.open:
            copy.wait_send()
        self.open = []


class Gather:
    def __init__(self, net, region, dims):
        self.net, self.region, self.dims = net, region, dims
        self.arrive = {}
        self.sibling = {}

    def key(self, flips):
        return tuple(sorted(flips))

    def push(self, flips, source=None):
        source = self.region(flips) if source is None else source
        level = max([self.dims.index(a) for a in flips], default=-1)
        for d in self.dims[level + 1 :]:
            copy = self.net.send(source, self.region(flips), (d,))
            self.arrive[self.key(flips + (d,))] = copy
        self.sibling[self.key(flips)] = self.net.send(source, self.region(flips), ("c",))

    def take(self, *flips):
        self.arrive[self.key(flips)].wait_recv()
        self.push(flips)

    def ready(self, *flips):
        self.sibling[self.key(flips)].wait_recv()


class Reduce:
    def __init__(self, net, dims, part, land, send, arrive):
        self.net, self.dims = net, dims
        self.part, self.land, self.send_slot, self.arrive = part, land, send, arrive
        self.from_sibling, self.incoming = {}, {}
        a, b, d = dims
        self.masks = [(a, b, d), (a, b), (a, d), (a,), (b, d), (b,), (d,), ()]
        self.slots = {}
        for rest in [(b, d), (b,), (d,), ()]:
            self.slots[rest, a] = len(self.slots)
        for rest in [(d,), ()]:
            self.slots[rest, b] = len(self.slots)
        self.slots[(), d] = len(self.slots)

    def ordered(self, flips):
        return tuple(a for a in self.dims if a in flips)

    def begin(self, flips):
        mask = self.ordered(flips)
        self.from_sibling[mask] = self.net.send(
            self.part(mask, 1 - self.net.me["c"]), self.land(self.masks.index(mask)), ("c",)
        )

    def total(self, mask, before):
        value = self.part(mask, self.net.me["c"])[...].astype(jnp.float32)
        value = value + self.land(self.masks.index(mask))[...].astype(jnp.float32)
        for stage in before:
            value = value + self.arrive(self.slots[mask, stage])[...].astype(jnp.float32)
        return value

    def settle(self, mask, before):
        self.from_sibling[mask].wait_recv()
        for stage in before:
            self.incoming[mask, stage].wait_recv()
        return self.total(mask, before)

    def forward(self, flips):
        mask = self.ordered(flips)
        stage, rest = mask[0], mask[1:]
        value = self.settle(mask, self.dims[: self.dims.index(stage)])
        slot = self.slots[rest, stage]
        self.send_slot(slot)[...] = value.astype(jnp.bfloat16)
        self.incoming[rest, stage] = self.net.send(
            self.send_slot(slot), self.arrive(slot), (stage,)
        )

    def result(self):
        return self.settle((), self.dims)


def lane_iota(rows, lanes=128):
    return lax.broadcasted_iota(jnp.int32, (rows, lanes), 1)


def pieces(value):
    first = value.astype(jnp.bfloat16).astype(jnp.float32)
    second = (value - first).astype(jnp.bfloat16).astype(jnp.float32)
    return first, second, value - first - second


def swap_halves(values):
    lane = lane_iota(values.shape[0])
    return jnp.where(lane % 64 < 32, pltpu.roll(values, 96, 1), pltpu.roll(values, 32, 1))


def pair_mean(values):
    lane = lane_iota(values.shape[0])
    low = jnp.sum(jnp.where(lane < 64, values, 0.0), axis=1, keepdims=True)
    high = jnp.sum(jnp.where(lane < 64, 0.0, values), axis=1, keepdims=True)
    return jnp.where(lane < 64, low, high) * (1.0 / 64.0)


def angles_of(packed):
    lane = lane_iota(packed.shape[0])
    turned = pltpu.roll(packed, 64, 1)
    return jnp.where(lane < 64, packed, turned), jnp.where(lane < 64, turned, packed)


def row_scale(value):
    return lax.rsqrt(jnp.mean(value * value, axis=1, keepdims=True) + EPS)


def layer_inputs():
    return ["lengths", "bias", "tok", "cot", "wqkv", "wout", "wgate", "wup", "wdown"] + [
        "norm_attn", "norm_ffn", "q_gain", "k_gain", "variate", "times", "freq",
    ]


def layer_outputs():
    bf, f32 = jnp.bfloat16, jnp.float32
    return {
        "out": ((128, 1024), bf),
        "gtok": ((2, 64, 1024), bf),
        "gwqkv": ((32, 3072), f32),
        "gwout": ((32, 1024), f32),
        "gwgate": ((32, 4096), f32),
        "gwup": ((32, 4096), f32),
        "gwdown": ((128, 1024), f32),
        "gsmall": ((8, 8, 128), f32),
    }


def layer_scratch():
    bf, f32 = jnp.bfloat16, jnp.float32
    return {
        "x": ((32, 64, 1024), bf),
        "wp": ((8, 2, 32, 192), bf),
        "wl": ((8, 2, 32, 192), bf),
        "wh": ((2, 8, 2, 32, 192), bf),
        "gp": ((4, 2, 2, 32, 512), bf),
        "gl": ((4, 2, 2, 32, 512), bf),
        "wgu": ((2, 2, 4, 2, 2, 32, 512), bf),
        "wd": ((2, 2, 128, 1024), bf),
        "wo": ((2, 16, 32, 1024), bf),
        "gf": ((8, 2, 64, 1024), bf),
        "tile": ((8, 128), f32),
        "sm": ((2, 2, 2, 2, 2, 8, 128), f32),
        "gain_s": ((4, 8, 128), f32),
        "feat": ((2048, 128), f32),
        "cs": ((2048, 128), f32),
        "raw": ((2048, 128), f32),
        "kept_o": ((2048, 128), f32),
        "qf": ((2048, 128), bf),
        "kf": ((2048, 128), bf),
        "vf": ((2048, 128), bf),
        "att": ((16, 2, 64, 64), bf),
        "lb": ((16, 64, 64), bf),
        "ap": ((2, 8, 64, 128), bf),
        "at2": ((2, 8, 64, 128), bf),
        "att_s": ((128, 1024), bf),
        "resid": ((128, 1024), f32),
        "n2": ((8, 2, 64, 1024), bf),
        "gate": ((4, 256, 512), f32),
        "up": ((4, 256, 512), f32),
        "hid": ((4, 256, 512), bf),
        "ggu": ((2, 4, 256, 512), bf),
        "kept": ((8, 128, 1024), f32),
        "sent": ((8, 2, 64, 1024), bf),
        "landed": ((8, 2, 64, 1024), bf),
        "red_send": ((2, 3, 128, 1024), bf),
        "red_land": ((2, 3, 128, 1024), bf),
        "branch": ((128, 1024), bf),
        "ga3": ((2, 8, 64, 128), bf),
        "ag1": ((2, 8, 64, 128), bf),
        "gatt": ((16, 2, 64, 64), bf),
        "gwgu": ((2, 2, 4, 2, 64, 512), bf),
        "gwd": ((2, 2, 128, 1024), bf),
        "gwo": ((2, 8, 2, 32, 1024), bf),
        "gb": ((2048, 128), bf),
        "gq": ((2048, 128), bf),
        "gw": ((2, 8, 2, 32, 192), bf),
        "bias_s": ((8, 128), f32),
        "sums": ((8, 1024), f32),
        "n_half": ((64, 1024), bf),
        "n_half_land": ((64, 1024), bf),
        "o_arr": ((7, 2, 32, 1024), bf),
        "o_half": ((32, 1024), bf),
        "o_half_land": ((32, 1024), bf),
        "y_wgu": ((2, 2, 4, 64, 512), bf),
        "y_wd": ((2, 128, 1024), bf),
        "h_wgu": ((2, 4, 64, 512), bf),
        "h_wd": ((128, 1024), bf),
        "h_wgu_land": ((2, 4, 64, 512), bf),
        "h_wd_land": ((128, 1024), bf),
        "f2": ((2, 4, 2, 32, 512), bf),
        "w_land": ((8, 2, 32, 192), bf),
        "w_t": ((8, 2, 32, 192), bf),
        "s_acc": ((3, 8, 8, 128), f32),
        "s_land": ((9, 8, 8, 128), f32),
    }


N_COPIES = 232


def layer_kernel(*refs):
    names = layer_inputs() + list(layer_outputs()) + list(layer_scratch())
    r = SimpleNamespace(**dict(zip(names, refs)))
    send_sems, recv_sems, local_sems = refs[len(names) :]
    bf, f32 = jnp.bfloat16, jnp.float32
    net = Net(send_sems, recv_sems, local_sems)
    zh, zl, x, y, c = (net.me[a] for a in AXES)
    mine, in_half = net.index(AXES), net.index(AXES[1:])
    my_chip, my_pair = net.index(CHIPS), net.index(("zl", "x"))
    head = in_half
    far_flips = [("zh",) + flips for flips in [()] + CHIP_FLIPS]
    net.barrier(CHIP_FLIPS + [("c",)] + far_flips)

    def x_region(part):
        def region(flips):
            return r.x.at[(zh if part == 0 else 1 - zh) * 16 + net.index(AXES[1:], flips)]

        return region

    x_own = Gather(net, x_region(0), ("zl", "y", "x"))
    x_far = Gather(net, x_region(1), ("zl", "x", "y"))
    wo_tree = Gather(net, lambda f: r.wo.at[:, net.index(AXES[1:], f)], ("zl", "y", "x"))
    gf_tree = Gather(net, lambda f: r.gf.at[net.index(("zl", "x", "c"), f)], ("zl", "x"))
    r.tile[...] = jnp.zeros_like(r.tile)
    r.tile[0:2, 0:64] = r.variate[...].astype(f32)
    r.tile[2:4, 0:64] = r.times[...].astype(f32)
    for k, gain in enumerate((r.norm_attn, r.norm_ffn, r.q_gain, r.k_gain)):
        r.tile[4 + k : 5 + k, 0:32] = gain[...].astype(f32)
    sm_step = net.send(r.tile, r.sm.at[zh, zl, x, y, c], ("zh",))
    swap = net.send(r.tok.at[1 - zh], r.x.at[mine], ("zh",))
    for h in range(16):
        r.wp[h // 2, h % 2] = r.wqkv[:, 192 * h : 192 * (h + 1)]
    w_arrive = []
    for flips in CHIP_FLIPS:
        w_arrive.append(net.send(r.wp.at[net.index(CHIPS, flips)], r.wl.at[my_chip], flips))
    x_own.push((), r.tok.at[zh])
    for pair in range(4):
        for cc in range(2):
            for part in range(4):
                idx = (part // 2) * 16 + pair * 4 + (part % 2) * 2 + cc
                col, lane = 128 * idx, 128 * part
                r.gp[pair, 0, cc, :, lane : lane + 128] = r.wgate[:, col : col + 128]
                r.gp[pair, 1, cc, :, lane : lane + 128] = r.wup[:, col : col + 128]

    def g_send(flips):
        return net.send(r.gp.at[net.index(("zl", "x"), flips)], r.gl.at[my_pair], flips)

    g_arrive = [g_send(("x",))]
    wd_y = net.send(r.wdown, r.wd.at[zh, y], ("y",))
    r.sm[zh, zl, x, y, c] = r.tile[...]
    r.wl[my_chip] = r.wp[my_chip]
    r.x[mine] = r.tok[zh]
    r.gl[my_pair] = r.gp[my_pair]
    r.gf[net.index(("zl", "x", "c"))] = r.cot[...]
    r.wd[zh, y] = r.wdown[...]
    r.wo[zh, in_half] = r.wout[...]

    sm_step.wait_recv()
    sm_step = net.send(r.sm.at[:, zl, x, y, c], r.sm.at[:, zl, x, y, c], ("x",))
    for copy in w_arrive:
        copy.wait_recv()
    w_c = net.send(r.wl.at[:, 1 - c], r.wh.at[zh, :, c], ("c",))
    r.wh[zh, :, c] = r.wl[:, c]
    sm_step.wait_recv()
    sm_step = net.send(r.sm.at[:, zl, :, y, c], r.sm.at[:, zl, :, y, c], ("y",))
    x_own.take("zl")
    x_own.take("y")
    w_c.wait_recv()
    swap.wait_recv()
    x_far.push(())
    w_zh = net.send(r.wh.at[zh], r.wh.at[zh], ("zh",))
    sm_step.wait_recv()
    sm_step = net.send(r.sm.at[:, zl, :, :, c], r.sm.at[:, zl, :, :, c], ("zl",))
    g_arrive += [g_send(("zl",)), g_send(("zl", "x"))]
    wo_zh = net.send(r.wout, r.wo.at[zh, in_half], ("zh",))
    x_own.take("zl", "y")
    x_own.take("x")
    x_far.take("zl")
    sm_step.wait_recv()
    sm_step = net.send(r.sm.at[:, :, :, :, c], r.sm.at[:, :, :, :, c], ("c",))

    def g_piece(k, half):
        return r.wgu.at[k // 2, half, pl.ds(2 * (k % 2), 2), y]

    g_c, g_zh, g_y, g_fwd = [], [], [], []

    x_far.take("x")
    x_own.take("zl", "x")
    x_own.take("y", "x")
    x_far.take("y")
    sm_step.wait_recv()

    lane8 = lane_iota(8)
    for group in range(8):
        for which in range(4):
            row = jnp.zeros((8, 128), f32)
            for j in range(4):
                block = 4 * group + j
                held = r.sm[
                    block // 16, (block // 8) % 2, (block // 4) % 2, (block // 2) % 2, block % 2
                ]
                moved = held if j == 0 else pltpu.roll(held, 32 * j, 1)
                row = jnp.where(lane8 // 32 == j, moved, row)
            r.gain_s[which, group : group + 1] = row[4 + which : 5 + which, :]
    gain_attn = jnp.concatenate([r.gain_s[0, k : k + 1] for k in range(8)], axis=1)
    gain_ffn = jnp.concatenate([r.gain_s[1, k : k + 1] for k in range(8)], axis=1)
    held_q = r.gain_s[2, pl.ds(my_chip, 1)]
    held_k = r.gain_s[3, pl.ds(my_chip, 1)]
    wide_q, wide_k = jnp.broadcast_to(held_q, (8, 128)), jnp.broadcast_to(held_k, (8, 128))
    wide_q = jnp.where(c == 0, wide_q, pltpu.roll(wide_q, 64, 1))
    wide_k = jnp.where(c == 0, pltpu.roll(wide_k, 64, 1), wide_k)
    qk_gain = jnp.where(lane8 < 64, wide_q, wide_k)[0:1, :]

    starts, ends, total = [], [], jnp.int32(0)
    for j in range(8):
        starts.append(total)
        total = total + r.lengths[zh, j]
        ends.append(total)
    sub = lax.broadcasted_iota(jnp.int32, (8, 128), 0)
    start_col = jnp.zeros((8, 128), jnp.int32)
    end_col = jnp.zeros((8, 128), jnp.int32)
    for j in range(8):
        start_col = jnp.where(sub == j, starts[j], start_col)
        end_col = jnp.where(sub == j, ends[j], end_col)
    same_bias = jnp.full((8, 128), r.bias[0, head], f32)
    other_bias = jnp.full((8, 128), r.bias[1, head], f32)
    diff_parts = pieces(same_bias - other_bias)
    zero = jnp.zeros((8, 128), f32)
    const_q = jnp.where(sub == 0, -256.0, 0.0)
    for i, part in enumerate(pieces(other_bias)):
        const_q = jnp.where(sub == i + 1, part, const_q)
    const_k = jnp.where(sub < 4, 1.0, 0.0)
    ones_k = jnp.where(sub < 3, 1.0, 0.0)

    @pl.loop(0, 16)
    def _(i):
        col = pl.ds(pl.multiple_of(i * 128, 128), 128)
        low = r.sm[i // 8, (i // 4) % 2, (i // 2) % 2, i % 2, 0]
        high = r.sm[i // 8, (i // 4) % 2, (i // 2) % 2, i % 2, 1]
        both = jnp.where(lane8 < 64, low, pltpu.roll(high, 64, 1))
        var_row = jnp.where(zh == 0, both[0:1, :], both[1:2, :])
        time_row = jnp.where(zh == 0, both[2:3, :], both[3:4, :])
        pos = lane8 + i * 128
        doc = jnp.where((pos >= start_col) & (pos < end_col), 1.0, 0.0)
        var = jnp.where(jnp.broadcast_to(var_row, (8, 128)) == sub.astype(f32), 1.0, 0.0)
        rows = [doc * 256.0, const_q] + [var * part for part in diff_parts] + [zero, zero, zero]
        rows += [doc, const_k, var, var, var, ones_k, zero, zero]
        r.feat[col, :] = jnp.concatenate(rows, axis=0).T
        angle = jnp.broadcast_to(time_row, (32, 128)) * jnp.broadcast_to(r.freq[...], (32, 128))
        cosine, sine = jnp.cos(angle), jnp.sin(angle)
        r.cs[col, :] = jnp.concatenate([cosine, cosine, -sine, sine], axis=0).T

    x_own.take("zl", "y", "x")
    x_far.take("zl", "y")
    x_far.take("zl", "x")
    for copy in g_arrive:
        copy.wait_recv()
    for k in range(2):
        g_c.append(net.send(r.gl.at[:, k, 1 - c], r.wgu.at[k, zh, :, y, c], ("c",)))
        r.wgu[k, zh, :, y, c] = r.gl[:, k, c]
    wo_zh.wait_recv()
    wo_tree.push(())
    for k in range(4):
        if k % 2 == 0:
            g_c[k // 2].wait_recv()
        g_zh.append(net.send(g_piece(k, zh), g_piece(k, zh), ("zh",)))
    for k in range(4):
        g_y.append(net.send(g_piece(k, zh), g_piece(k, zh), ("y",)))
    gf_tree.push((), r.cot)

    lane = lane_iota(ROW_BLOCK)

    def arrived(part, *flips):
        tree = x_own if part == 0 else x_far
        tree.ready(*flips)
        tree.ready(*(flips + ("y",)))

    def project(j):
        part, far_x, far_zl = j // 4, (j // 2) % 2, j % 2
        at = ((zh + part - 2 * zh * part) * 2 + zl + far_zl - 2 * zl * far_zl) * 2
        at = (at + x + far_x - 2 * x * far_x) * ROW_BLOCK
        row = pl.ds(pl.multiple_of(at, ROW_BLOCK), ROW_BLOCK)
        blocks = pl.ds(at // 64, 4)
        value = r.x[blocks].reshape(ROW_BLOCK, 1024).astype(f32)
        normed = (value * row_scale(value) * gain_attn).astype(bf)
        qkv = jnp.dot(normed, r.wh[...].reshape(1024, 192), preferred_element_type=f32)
        raw = qkv[:, :128]
        r.raw[row, :] = raw
        scaled = raw * lax.rsqrt(pair_mean(raw * raw) + EPS) * qk_gain
        cosine, sine = angles_of(r.cs[row, :])
        turned = (scaled * cosine + swap_halves(scaled) * sine).astype(bf).astype(f32)
        marks = r.feat[row, :]
        r.qf[row, :] = jnp.where(lane < 64, turned * 0.125, pltpu.roll(marks, 64, 1)).astype(bf)
        r.kf[row, :] = jnp.where(lane < 64, pltpu.roll(turned, 64, 1), marks).astype(bf)
        third = jnp.concatenate([qkv[:, 128:192], jnp.zeros((ROW_BLOCK, 64), f32)], axis=1)
        r.vf[row, :] = jnp.where((lane >= 64) & (lane < 67), 1.0, third).astype(bf)

    w_zh.wait_recv()
    arrived(0)
    arrived(0, "zl")
    arrived(0, "x")
    arrived(0, "zl", "x")
    pl.loop(0, 4)(project)
    x_far.take("x", "y")
    x_far.take("zl", "x", "y")
    arrived(1)
    arrived(1, "zl")
    arrived(1, "x")
    arrived(1, "zl", "x")
    pl.loop(4, 8)(project)
    wo_tree.take("zl")

    lane_span = lane_iota(SPAN)

    def attend(i):
        row = pl.ds(pl.multiple_of(i * SPAN, SPAN), SPAN)
        query = r.qf[row, :]

        def one_chunk(k, total):
            col = pl.ds(pl.multiple_of(k * SPAN, SPAN), SPAN)
            scores = lax.dot_general(query, r.kf[col, :], LAST, preferred_element_type=f32)
            weights = jnp.exp(scores).astype(bf)
            return total + jnp.dot(weights, r.vf[col, :], preferred_element_type=f32)

        total = lax.fori_loop(0, 2048 // SPAN, one_chunk, jnp.zeros((SPAN, 128), f32), unroll=2)
        weight = total[:, 64:65]
        result = total / weight
        r.kept_o[row, :] = jnp.where(lane_span < 64, result, jnp.log(weight))
        r.att[pl.ds(4 * i, 4)] = result[:, :64].astype(bf).reshape(4, 2, 64, 64)

    def g_pass(k):
        g_zh[k].wait_recv()
        g_fwd.append(net.send(g_piece(k, 1 - zh), g_piece(k, 1 - zh), ("y",)))

    pl.loop(0, 2)(attend)
    wo_tree.take("y")
    pl.loop(2, 4)(attend)

    step = net.send(r.att.at[:, 1 - c], r.lb, ("c",))
    wo_tree.take("zl", "y")
    g_pass(0)
    g_pass(1)
    step.wait_recv()
    lane64 = lane_iota(64)

    @pl.loop(0, 16, unroll=4)
    def _(i):
        own = jnp.concatenate([r.att[i, c]] * 2, axis=1)
        other = jnp.concatenate([r.lb[i]] * 2, axis=1)
        r.ap[i // 8, i % 8] = jnp.where((lane64 < 64) == (c == 0), own, other)

    arrive = []
    for flips in far_flips + CHIP_FLIPS:
        z_part = 1 - zh if "zh" in flips else zh
        arrive.append(
            net.send(r.ap.at[z_part, net.index(CHIPS, flips)], r.at2.at[zh, my_chip], flips)
        )
    r.at2[zh, my_chip] = r.ap[zh, my_chip]

    def w_down():
        return r.wd[...].reshape(512, 1024)

    def w_o():
        return r.wo[...].reshape(1024, 1024)

    def w_in(k):
        return r.wgu[k].reshape(1024, 512)

    for copy in arrive:
        copy.wait_recv()
    wd_zh = net.send(r.wdown, r.wd.at[zh, y], ("zh",))
    g_pass(2)
    gf_tree.take("zl")
    for b in range(2):
        for k in range(8):
            r.att_s[64 * b : 64 * (b + 1), 128 * k : 128 * (k + 1)] = r.at2[b, k]
    g_pass(3)
    wo_tree.take("x")
    wo_tree.take("y", "x")
    wo_tree.take("zl", "x")
    wo_tree.take("zl", "y", "x")
    for flips in [(), ("y",), ("zl",), ("zl", "y"), ("x",), ("y", "x"), ("zl", "x"), ("zl", "y", "x")]:
        wo_tree.ready(*flips)

    resid = r.tok[...].reshape(128, 1024).astype(f32)
    resid = resid + jnp.dot(r.att_s[...], w_o(), preferred_element_type=f32)
    scale = row_scale(resid)
    r.resid[...] = resid
    mine8 = 2 * my_pair + c
    r.n2[mine8] = (resid * scale * gain_ffn).astype(bf).reshape(2, 64, 1024)
    to_sibling = [net.send(r.n2.at[mine8], r.n2.at[mine8], ("c",))]
    from_chips = [net.send(r.n2.at[mine8], r.n2.at[mine8], flips) for flips in GROUP_FLIPS]
    def pair_rows(ref, pair):
        return ref[pl.ds(2 * pair, 2)].reshape(256, 1024)

    def feed(pair):
        rows = pair_rows(r.n2, pair)
        r.gate[pair] = jnp.dot(rows, w_in(0), preferred_element_type=f32)
        r.up[pair] = jnp.dot(rows, w_in(1), preferred_element_type=f32)

    def feed_back(pair):
        back = lax.dot_general(pair_rows(r.gf, pair), w_down(), LAST, preferred_element_type=f32)
        gate, up = r.gate[pair], r.up[pair]
        sig = 1.0 / (1.0 + jnp.exp(-gate))
        silu = gate * sig
        r.hid[pair] = (silu * up).astype(bf)
        r.ggu[0, pair] = (back * up * sig * (1.0 + gate * (1.0 - sig))).astype(bf)
        r.ggu[1, pair] = (back * silu).astype(bf)

    def back_product(pair):
        total = lax.dot_general(r.ggu[0, pair], w_in(0), LAST, preferred_element_type=f32)
        return total + lax.dot_general(r.ggu[1, pair], w_in(1), LAST, preferred_element_type=f32)

    def out_product(pair):
        return jnp.dot(r.hid[pair], w_down(), preferred_element_type=f32)

    halves, reduced = {}, {0: [], 1: []}

    def pair_at(slot):
        far_zl, far_x = slot % 2, slot // 2
        return (zl + far_zl - 2 * zl * far_zl) * 2 + x + far_x - 2 * x * far_x

    def keep_half(at, value):
        r.kept[at] = jnp.where(c == 0, value[:128], value[128:])
        r.sent[at] = jnp.where(c == 0, value[128:], value[:128]).astype(bf).reshape(2, 64, 1024)

    def share(kind, slot):
        at = 4 * kind + slot
        halves[at] = net.send(r.sent.at[at], r.landed.at[at], ("c",))

    def finish_half(kind, slot):
        at = 4 * kind + slot
        halves[at].wait_recv()
        total = r.kept[at] + r.landed[at].reshape(128, 1024).astype(f32)
        if slot == 0:
            r.kept[at] = total
        else:
            r.red_send[kind, slot - 1] = total.astype(bf)
            reduced[kind].append(
                net.send(
                    r.red_send.at[kind, slot - 1],
                    r.red_land.at[kind, slot - 1],
                    GROUP_FLIPS[slot - 1],
                )
            )

    pairs = [my_pair] + [net.index(("zl", "x"), flips) for flips in GROUP_FLIPS]
    for copy in g_y + g_fwd:
        copy.wait_recv()
    to_sibling[0].wait_recv()
    for k in range(3):
        from_chips[k].wait_recv()
        at = 2 * pairs[k + 1] + c
        to_sibling.append(net.send(r.n2.at[at], r.n2.at[at], ("c",)))
        if k == 0:
            to_sibling[1].wait_recv()
            wd_zh.wait_recv()
            wd_fwd = net.send(r.wd.at[1 - zh, y], r.wd.at[1 - zh, y], ("y",))
            pl.loop(0, 2)(lambda slot: feed(pair_at(slot)))
    gf_tree.take("x")
    gf_tree.take("zl", "x")
    to_sibling[2].wait_recv()
    to_sibling[3].wait_recv()
    pl.loop(2, 4)(lambda slot: feed(pair_at(slot)))
    gf_tree.ready()
    gf_tree.ready("zl")
    gf_tree.ready("x")
    gf_tree.ready("zl", "x")
    wd_y.wait_recv()
    wd_fwd.wait_recv()
    net.drain()

    def feed_both(slot):
        pair = pair_at(slot)
        feed_back(pair)
        keep_half(slot, back_product(pair))

    pl.loop(3, 4)(feed_both)
    share(0, 3)
    pl.loop(2, 3)(feed_both)
    share(0, 2)
    finish_half(0, 3)
    pl.loop(1, 2)(feed_both)
    share(0, 1)
    finish_half(0, 2)
    pl.loop(0, 1)(feed_both)
    share(0, 0)
    finish_half(0, 1)

    @pl.loop(0, 2)
    def _(k):
        r.gwgu[k] = (
            lax.dot_general(
                r.n2[...].reshape(1024, 1024),
                r.ggu[k].reshape(1024, 512),
                FIRST,
                preferred_element_type=f32,
            )
            .astype(bf)
            .reshape(2, 4, 2, 64, 512)
        )
    y_far = [net.send(r.gwgu.at[k, 1 - zh, :, 1 - y], r.y_wgu.at[k, 1], ("y",)) for k in range(2)]
    finish_half(0, 0)

    @pl.loop(0, 4)
    def _(slot):
        keep_half(4 + slot, out_product(pair_at(slot)))

    for k in range(4):
        share(1, k)
    for half in range(2):
        cols = slice(512 * half, 512 * (half + 1))
        r.gwd[:, :, :, cols] = (
            lax.dot_general(
                r.hid[...].reshape(1024, 512),
                r.gf[:, :, :, cols].reshape(1024, 512),
                FIRST,
                preferred_element_type=f32,
            )
            .astype(bf)
            .reshape(2, 2, 128, 512)
        )

    h_steps = []

    def half_gate_up(k):
        y_far[k].wait_recv()
        r.h_wgu[k] = (r.gwgu[k, 1 - zh, :, y].astype(f32) + r.y_wgu[k, 1].astype(f32)).astype(bf)
        h_steps.append(net.send(r.h_wgu.at[k], r.h_wgu_land.at[k], ("zh",)))

    def half_down():
        y_far[2].wait_recv()
        r.h_wd[...] = (r.gwd[1 - zh, y].astype(f32) + r.y_wd[1].astype(f32)).astype(bf)
        h_steps.append(net.send(r.h_wd, r.h_wd_land, ("zh",)))

    for copy in reduced[0]:
        copy.wait_recv()
    total = r.kept[0]
    for k in range(3):
        total = total + r.red_land[0, k].astype(f32)
    resid = r.resid[...]
    scale = row_scale(resid)
    r.sums[...] = jnp.zeros_like(r.sums)
    r.sums[1:2, :] = jnp.sum(total * resid * scale, axis=0, keepdims=True)
    weighted = total * gain_ffn
    mean = jnp.mean(weighted * resid, axis=1, keepdims=True)
    grad_resid = r.cot[...].reshape(128, 1024).astype(f32) + scale * weighted
    grad_resid = grad_resid - resid * (scale * scale * scale) * mean
    r.kept[0] = grad_resid
    r.branch[...] = grad_resid.astype(bf)
    grad_att = lax.dot_general(r.branch[...], w_o(), LAST, preferred_element_type=f32).astype(bf)
    for k in range(8):
        for b in range(2):
            r.ga3[b, k] = grad_att[64 * b : 64 * (b + 1), 128 * k : 128 * (k + 1)]
    arrive = []
    for flips in far_flips + CHIP_FLIPS:
        z_part = 1 - zh if "zh" in flips else zh
        arrive.append(
            net.send(r.ga3.at[z_part, net.index(CHIPS, flips)], r.ag1.at[zh, my_chip], flips)
        )
    r.ag1[zh, my_chip] = r.ga3[zh, my_chip]
    for j in range(8):
        cols = slice(128 * j, 128 * (j + 1))
        r.gwo[j // 4, 2 * (j % 4) : 2 * (j % 4) + 2] = (
            lax.dot_general(r.att_s[:, cols], r.branch[...], FIRST, preferred_element_type=f32)
            .astype(bf)
            .reshape(2, 2, 32, 1024)
        )
    for copy in arrive:
        copy.wait_recv()

    @pl.loop(0, 16)
    def _(i):
        both = r.ag1[i // 8, i % 8]
        low, high = both[:, :64].astype(f32), both[:, 64:].astype(f32)
        r.lb[i] = jnp.where(c == 0, high, low).astype(bf)
        r.gatt[i, c] = jnp.where(c == 0, low, high).astype(bf)

    for k in (3, 2, 1, 0):
        finish_half(1, k)
    step = net.send(r.lb, r.gatt.at[:, c], ("c",))
    half_gate_up(0)
    y_far.append(net.send(r.gwd.at[1 - zh, 1 - y], r.y_wd.at[1], ("y",)))
    r.feat[...] = jnp.zeros_like(r.feat)
    r.bias_s[...] = jnp.zeros_like(r.bias_s)
    r.gate[...] = jnp.zeros_like(r.gate)
    step.wait_recv()

    @pl.loop(0, 4)
    def _(i):
        row = pl.ds(pl.multiple_of(i * SPAN, SPAN), SPAN)
        kept = r.kept_o[row, :]
        grad = r.gatt[pl.ds(i * 4, 4)].reshape(SPAN, 64).astype(f32)
        grad = jnp.concatenate([grad, jnp.zeros((SPAN, 64), f32)], axis=1)
        delta = jnp.sum(jnp.where(lane_span < 64, grad * kept, 0.0), axis=1, keepdims=True)
        query = r.qf[row, :].astype(f32)
        for j, part in enumerate(pieces(kept[:, 64:65])):
            query = jnp.where(lane_span == 64 + 40 + j, -part, query)
        r.qf[row, :] = query.astype(bf)
        for j, part in enumerate(pieces(delta)):
            grad = jnp.where(lane_span == 64 + j, -part, grad)
        r.gb[row, :] = grad.astype(bf)

    grad_k, grad_v = r.feat, r.kept_o
    grad_v[...] = jnp.zeros_like(grad_v)
    tree_o = Reduce(
        net,
        ("x", "zl", "y"),
        lambda mask, core: r.gwo.at[:, net.index(CHIPS, mask), core],
        lambda slot: r.wo.at[0, pl.ds(2 * slot, 2)],
        lambda slot: r.wo.at[1, pl.ds(2 * slot, 2)],
        lambda slot: r.o_arr.at[slot],
    )
    for mask in tree_o.masks:
        tree_o.begin(mask)

    def attend_back(i):
        row = pl.ds(pl.multiple_of(i * SPAN, SPAN), SPAN)
        query, grad = r.qf[row, :], r.gb[row, :]

        def one_chunk(k, total):
            col = pl.ds(pl.multiple_of(k * SPAN, SPAN), SPAN)
            key = r.kf[col, :]
            scores = lax.dot_general(key, query, LAST, preferred_element_type=f32)
            probs = jnp.exp(scores)
            centred = lax.dot_general(r.vf[col, :], grad, LAST, preferred_element_type=f32)
            back = (probs * centred).astype(bf)
            grad_v[col, :] += jnp.dot(probs.astype(bf), grad, preferred_element_type=f32)
            grad_k[col, :] += jnp.dot(back, query, preferred_element_type=f32)
            return total + lax.dot_general(back, key, FIRST, preferred_element_type=f32)

        total = lax.fori_loop(0, 2048 // SPAN, one_chunk, jnp.zeros((SPAN, 128), f32), unroll=2)
        r.gq[row, :] = (total * 0.125).astype(bf)
        marks = r.kf[row, :].astype(f32)
        same = jnp.where((lane_span >= 80) & (lane_span < 88), total * marks, 0.0)
        every = jnp.where(lane_span == 72, total, 0.0)
        r.bias_s[0:1, :] += jnp.sum(same, axis=0, keepdims=True)
        r.bias_s[1:2, :] += jnp.sum(every, axis=0, keepdims=True)

    half_gate_up(1)
    pl.loop(0, 1)(attend_back)
    y_near = [net.send(r.gwgu.at[k, zh, :, 1 - y], r.y_wgu.at[k, 0], ("y",)) for k in range(2)]
    y_near.append(net.send(r.gwd.at[zh, 1 - y], r.y_wd.at[0], ("y",)))
    for mask in tree_o.masks[:4]:
        tree_o.forward(mask)
    half_down()
    pl.loop(1, 2)(attend_back)
    pl.loop(2, 4)(attend_back)

    def token_tree(part, half, dims):
        return Reduce(
            net,
            dims,
            lambda mask, core: r.x.at[half * 16 + 2 * net.index(CHIPS, mask) + core],
            lambda slot: r.landed.at[slot, part],
            lambda slot: r.sent.at[slot, part],
            lambda slot: r.n2.at[slot, part],
        )

    trees = [token_tree(0, 1 - zh, ("x", "y", "zl")), token_tree(1, zh, ("y", "x", "zl"))]

    def project_back(part, where):
        start = (part * 4 + where) * ROW_BLOCK
        row, blocks = pl.ds(pl.multiple_of(start, ROW_BLOCK), ROW_BLOCK), pl.ds(start // 64, 4)
        raw = r.raw[row, :]
        scale = lax.rsqrt(pair_mean(raw * raw) + EPS)
        cosine, sine = angles_of(r.cs[row, :])
        key_part = pltpu.roll(grad_k[row, :].astype(bf).astype(f32), 64, 1)
        grad = jnp.where(lane < 64, r.gq[row, :].astype(f32), key_part)
        turned = grad * cosine - swap_halves(grad) * sine
        r.bias_s[2:3, :] += jnp.sum(turned * raw * scale, axis=0, keepdims=True)
        weighted = turned * qk_gain
        back = scale * weighted - raw * (scale * scale * scale) * pair_mean(weighted * raw)
        grad_qkv = jnp.concatenate([back, grad_v[row, :][:, :64]], axis=1).astype(bf)
        grad_normed = lax.dot_general(
            grad_qkv, r.wh[...].reshape(1024, 192), LAST, preferred_element_type=f32
        )
        value = r.x[blocks].reshape(ROW_BLOCK, 1024).astype(f32)
        shaped = value * row_scale(value)
        r.sums[0:1, :] += jnp.sum(grad_normed * shaped, axis=0, keepdims=True)
        normed = (shaped * gain_attn).astype(bf)
        term = lax.dot_general(normed, grad_qkv, FIRST, preferred_element_type=f32)
        r.gate[:, :, :192] += term.reshape(4, 256, 192)
        r.x[blocks] = grad_normed.astype(bf).reshape(4, 64, 1024)

    f_steps, f_c = [], []

    def feed_sum(k):
        y_near[k].wait_recv()
        h_steps[k].wait_recv()
        for j in range(4):
            rows = r.gwgu[k, zh, j, y].astype(f32) + r.y_wgu[k, 0, j].astype(f32)
            rows = rows + r.h_wgu_land[k, j].astype(f32)
            r.gp[j, k, 0] = rows[:32].astype(bf)
            r.gp[j, k, 1] = rows[32:].astype(bf)
        for flips in GROUP_FLIPS:
            f_steps.append(
                net.send(r.gp.at[net.index(("zl", "x"), flips), k], r.gl.at[my_pair, k], flips)
            )
        r.gl[my_pair, k] = r.gp[my_pair, k]

    def feed_sibling(k):
        for j in range(3):
            f_steps[3 * k + j].wait_recv()
        f_c.append(net.send(r.gl.at[:, k, 1 - c], r.f2.at[k, :, c], ("c",)))
        r.f2[k, :, c] = r.gl[:, k, c]

    def two_back(*flips):
        where = net.index(("zl", "x"), flips)
        pl.loop(0, 2)(lambda part: project_back(part, where))
        for tree in trees:
            tree.begin(flips)
            tree.begin(flips + ("y",))

    net.settle(list(halves.values()))
    two_back("zl", "x")
    two_back("x")
    trees[0].forward(("zl", "x", "y"))
    trees[0].forward(("zl", "x"))
    trees[1].forward(("zl", "x", "y"))
    feed_sum(0)
    tree_o.forward(("zl", "y"))
    tree_o.forward(("zl",))
    two_back("zl")
    trees[0].forward(("x", "y"))
    trees[0].forward(("x",))
    trees[1].forward(("x", "y"))
    two_back()
    trees[0].forward(("zl", "y"))
    trees[1].forward(("zl", "y"))
    trees[1].forward(("y",))
    trees[1].forward(("zl", "x"))

    one = lane_iota(8)
    both = jnp.broadcast_to(r.bias_s[2:3, :], (8, 128))
    turned = pltpu.roll(both, 64, 1)
    wide = lane_iota(1, 1024)
    query_gain = jnp.concatenate([jnp.where(one < 64, both, turned)[0:1]] * 8, axis=1)
    key_gain = jnp.concatenate([jnp.where(one < 64, turned, both)[0:1]] * 8, axis=1)
    r.sums[2:3, :] = jnp.where(wide // 64 == head, query_gain, 0.0)
    r.sums[3:4, :] = jnp.where(wide // 64 == head, key_gain, 0.0)
    same = jnp.sum(r.bias_s[0:1, :], axis=1, keepdims=True)
    every = jnp.sum(r.bias_s[1:2, :], axis=1, keepdims=True)
    row_bias = jnp.where(wide == head, same, 0.0)
    r.sums[4:5, :] = jnp.where(wide == 16 + head, every - same, row_bias)
    for k in range(8):
        r.s_acc[0, k] = r.sums[:, 128 * k : 128 * (k + 1)]
    s_steps = [net.send(r.s_acc.at[0], r.s_land.at[k], f) for k, f in enumerate(CHIP_FLIPS)]

    r.gw[...] = r.gate[:, :, :192].astype(bf).reshape(2, 8, 2, 32, 192)
    w_zh = net.send(r.gw.at[1 - zh], r.w_land, ("zh",))
    trees[0].forward(("y",))
    trees[0].forward(("zl",))
    trees[1].forward(("x",))
    tree_o.forward(("y",))
    for copy in reduced[1]:
        copy.wait_recv()
    total = r.kept[4] + r.resid[...]
    for k in range(3):
        total = total + r.red_land[1, k].astype(f32)
    r.out[...] = total.astype(bf)
    trees[1].forward(("zl",))
    w_zh.wait_recv()
    r.w_t[...] = (r.gw[zh].astype(f32) + r.w_land[...].astype(f32)).astype(bf)
    w_c = net.send(r.w_t.at[:, 1 - c], r.wp.at[:, c], ("c",))
    r.wp[:, c] = r.w_t[:, c]
    r.n_half[...] = trees[0].result().astype(bf)
    n_step = net.send(r.n_half, r.n_half_land, ("zh",))
    feed_sum(1)
    total = r.s_acc[0]
    for k, copy in enumerate(s_steps):
        copy.wait_recv()
        total = total + r.s_land[k]
    r.s_acc[1] = total
    s_step = net.send(r.s_acc.at[1], r.s_land.at[7], ("zh",))
    w_c.wait_recv()
    w_steps = []
    for flips in CHIP_FLIPS:
        w_steps.append(net.send(r.wp.at[net.index(CHIPS, flips)], r.wl.at[my_chip], flips))
    r.wl[my_chip] = r.wp[my_chip]
    total = tree_o.result()
    r.kept[3, :32] = total[0]
    r.kept[4, :32] = total[1]
    r.o_half[...] = r.kept[4 - zh, :32].astype(bf)
    o_step = net.send(r.o_half, r.o_half_land, ("zh",))
    r.kept[1 + zh, :64] = trees[1].result()
    s_step.wait_recv()
    r.s_acc[2] = r.s_acc[1] + r.s_land[7]
    s_step = net.send(r.s_acc.at[2], r.s_land.at[8], ("c",))
    y_near[2].wait_recv()
    h_steps[2].wait_recv()
    r.gwdown[...] = r.gwd[zh, y].astype(f32) + r.y_wd[0].astype(f32) + r.h_wd_land[...].astype(f32)
    feed_sibling(0)
    feed_sibling(1)
    n_step.wait_recv()
    r.kept[2 - zh, :64] = r.n_half_land[...].astype(f32)
    for b in range(2):
        value = r.tok[b].astype(f32)
        scale = row_scale(value)
        weighted = r.kept[1 + b, :64] * gain_attn
        mean = jnp.mean(weighted * value, axis=1, keepdims=True)
        back = scale * weighted - value * (scale * scale * scale) * mean
        r.gtok[b] = (r.kept[0, 64 * b : 64 * (b + 1), :] + back).astype(bf)
    for copy in w_steps:
        copy.wait_recv()
    for h in range(16):
        r.gwqkv[:, 192 * h : 192 * (h + 1)] = r.wl[h // 2, h % 2].astype(f32)
    o_step.wait_recv()
    r.gwout[...] = r.kept[3 + zh, :32] + r.o_half_land[...].astype(f32)
    for k, out in ((0, r.gwgate), (1, r.gwup)):
        f_c[k].wait_recv()
        for pair in range(4):
            for cc in range(2):
                for part in range(4):
                    idx = (part // 2) * 16 + pair * 4 + (part % 2) * 2 + cc
                    out[:, 128 * idx : 128 * (idx + 1)] = r.f2[
                        k, pair, cc, :, 128 * part : 128 * (part + 1)
                    ].astype(f32)
    s_step.wait_recv()
    r.gsmall[...] = r.s_acc[2] + r.s_land[8]
    net.drain()


def layer(*arrays):
    sm = pl.BlockSpec(memory_space=pltpu.SMEM)
    vm = pl.BlockSpec(memory_space=pltpu.VMEM)
    outs = layer_outputs()
    return pl.pallas_call(
        layer_kernel,
        out_shape=[jax.ShapeDtypeStruct(*spec) for spec in outs.values()],
        in_specs=[sm, sm] + [vm] * (len(layer_inputs()) - 2),
        out_specs=[vm] * len(outs),
        scratch_shapes=[pltpu.VMEM(*spec) for spec in layer_scratch().values()]
        + [
            pltpu.SemaphoreType.DMA((N_COPIES,)),
            pltpu.SemaphoreType.DMA((N_COPIES,)),
            pltpu.SemaphoreType.DMA((2,)),
        ],
        compiler_params=pltpu.CompilerParams(
            collective_id=1, has_side_effects=True, vmem_limit_bytes=VMEM_BYTES
        ),
        name="layer",
    )(*arrays)


def give_out_kernel(small, *refs):
    n = (len(refs) - 5) // 2
    gains, bias = refs[2 * n : 2 * n + 4], refs[-1]
    for source, dest in zip(refs[:n], refs[n : 2 * n]):
        dest[...] = source[...]
    rank = jnp.int32(0)
    for name in AXES:
        rank = rank * 2 + lax.axis_index(name)
    held = small[rank // 4]
    mine = held
    for k in range(1, 4):
        mine = jnp.where(rank % 4 == k, pltpu.roll(held, 128 - 32 * k, 1), mine)
    for k, gain in enumerate(gains):
        gain[...] = mine[k : k + 1, :32]
    first = small[0]
    bias[0:1, :] = first[4:5, :16]
    bias[1:2, :] = pltpu.roll(first, 112, 1)[4:5, :16]


def give_out(small, *large):
    f32 = jnp.float32
    vm = pl.BlockSpec(memory_space=pltpu.VMEM)
    n = len(large)
    return pl.pallas_call(
        give_out_kernel,
        out_shape=[jax.ShapeDtypeStruct(a.shape, a.dtype) for a in large]
        + [jax.ShapeDtypeStruct((1, 32), f32)] * 4
        + [jax.ShapeDtypeStruct((2, 16), f32)],
        in_specs=[vm] * (n + 1),
        out_specs=[vm] * (n + 5),
        name="give_out",
    )(small, *large)


def frequencies():
    index = np.arange(32, dtype=np.float32)
    return (THETA ** (-2.0 * index / 64.0)).astype(np.float32)[:, None]


def on_device_cube(
    tokens,
    cotangent,
    w_qkv,
    w_out,
    w_gate,
    w_up,
    w_down,
    norm_attn,
    norm_ffn,
    q_gain,
    k_gain,
    var_bias,
    doc_lengths,
    variate,
    times,
):
    results = layer(
        doc_lengths, var_bias.T, tokens, cotangent, w_qkv, w_out, w_gate, w_up, w_down,
        *(gain.reshape(1, 32) for gain in (norm_attn, norm_ffn, q_gain, k_gain)),
        variate, times, jnp.asarray(frequencies()),
    )
    *large, small = results
    out, gtok, gwqkv, gwout, gwgate, gwup, gwdown, *gains, bias = give_out(small, *large)
    return (
        out.reshape(2, 64, 1024),
        gtok,
        gwqkv,
        gwout,
        gwgate,
        gwup,
        gwdown,
        *(gain.reshape(32) for gain in gains),
        bias.T,
    )


def run_parts(mesh, body, split):
    rows, cut = P(split, None), P(split)
    part = P(None, split, None)
    return jax.shard_map(
        body,
        mesh=mesh,
        in_specs=(part, part) + (rows,) * 5 + (cut,) * 4 + (P(), P(), P(None, split), P(None, split)),
        out_specs=(part, part) + (rows,) * 5 + (cut,) * 4 + (P(),),
        check_vma=False,
    )


def solution(mesh):
    sizes = (mesh.shape["head"], mesh.shape["blk"])
    general = run_parts(mesh, on_device, ("head", "blk"))
    if sizes != (8, 4):
        return general
    cube = jax.sharding.Mesh(mesh.devices.reshape(2, 2, 2, 2, 2), AXES)
    special = run_parts(cube, on_device_cube, AXES)

    def chosen(*arrays):
        tokens, w_gate, var_bias, lengths = arrays[0], arrays[4], arrays[11], arrays[12]
        shapes = (tokens.shape, w_gate.shape, var_bias.shape, lengths.shape)
        if shapes == ((2, 2048, 1024), (1024, 4096), (16, 2), (2, 8)):
            return special(*arrays)
        return general(*arrays)

    return chosen
```
